32 devices in a mesh: gene: 8 (over z, x), cell: 4 (over y, core).
Axes of the slice: x: 2, y: 2, z: 4, core: 2. Of those that a mesh axis runs over, the one named last changes fastest.
Arguments:
- counts: int32 [16384, 20000], P('cell', 'gene'), may hold values from 0 to 63, as said below
- batch_index: int32 [16384], P('cell'), may hold values from 0 to 31
- valid_mask: int32 [16384], P('cell'), may hold values from 0 to 1, as said below
- noise_draw: float32 [16384, 10], P('cell'), may hold values from -5 to 5
- encoder_weight: float32 [20000, 128], P('gene'), may hold values from -0.0390625 to 0.0390625
- output_weight: float32 [2, 128, 20000], P(None, None, 'gene'), may hold values from -0.5 to 0.5
- gene_vectors: float32 [3, 20000], P(None, 'gene'), may hold values from -3 to 3
- batch_shift: float32 [32, 128], replicated, may hold values from -3 to 3
- layer_norm_params: float32 [4, 128], replicated, may hold values from 0.1 to 1.9
- head_weight: float32 [128, 20], replicated, may hold values from -0.5 to 0.5
- head_bias: float32 [20], replicated, may hold values from -1.5 to 1.5
- decoder_input: float32 [42, 128], replicated, may hold values from -2 to 2
- encoder_weight_momentum: float32 [20000, 128], P('gene'), may hold values from -0.00036621094 to 0.00036621094
- output_weight_momentum: float32 [2, 128, 20000], P(None, None, 'gene'), may hold values from -0.0029296875 to 0.0029296875
- gene_vectors_momentum: float32 [3, 20000], P(None, 'gene'), may hold values from -0.0014648438 to 0.0014648438
- batch_shift_momentum: float32 [32, 128], replicated, may hold values from -3.8146973e-05 to 3.8146973e-05
- norm_params_momentum: float32 [4, 128], replicated, may hold values from -0.00021362305 to 0.00021362305
- head_weight_momentum: float32 [128, 20], replicated, may hold values from -0.00012207031 to 0.00012207031
- head_bias_momentum: float32 [20], replicated, may hold values from -0.00021362305 to 0.00021362305
- decoder_input_momentum: float32 [42, 128], replicated, may hold values from -0.00021362305 to 0.00021362305
- encoder_weight_average: float32 [20000, 128], P('gene'), may hold values from -0.0390625 to 0.0390625
- output_weight_average: float32 [2, 128, 20000], P(None, None, 'gene'), may hold values from -0.5 to 0.5
- gene_vectors_average: float32 [3, 20000], P(None, 'gene'), may hold values from -3 to 3
- batch_shift_average: float32 [32, 128], replicated, may hold values from -3 to 3
- norm_params_average: float32 [4, 128], replicated, may hold values from 0.1 to 1.9
- head_weight_average: float32 [128, 20], replicated, may hold values from -0.5 to 0.5
- head_bias_average: float32 [20], replicated, may hold values from -1.5 to 1.5
- decoder_input_average: float32 [42, 128], replicated, may hold values from -2 to 2
Outputs:
- cell_loss: float32 [16384], P('cell')
- input_grad: float32 [16384, 20000], P('cell', 'gene')
- new_encoder_weight: float32 [20000, 128], P('gene')
- new_output_weight: float32 [2, 128, 20000], P(None, None, 'gene')
- new_gene_vectors: float32 [3, 20000], P(None, 'gene')
- new_batch_shift: float32 [32, 128], replicated
- new_norm_params: float32 [4, 128], replicated
- new_head_weight: float32 [128, 20], replicated
- new_head_bias: float32 [20], replicated
- new_decoder_input: float32 [42, 128], replicated
- new_encoder_weight_momentum: float32 [20000, 128], P('gene')
- new_output_weight_momentum: float32 [2, 128, 20000], P(None, None, 'gene')
- new_gene_vectors_momentum: float32 [3, 20000], P(None, 'gene')
- new_batch_shift_momentum: float32 [32, 128], replicated
- new_norm_params_momentum: float32 [4, 128], replicated
- new_head_weight_momentum: float32 [128, 20], replicated
- new_head_bias_momentum: float32 [20], replicated
- new_decoder_input_momentum: float32 [42, 128], replicated
- new_encoder_weight_average: float32 [20000, 128], P('gene')
- new_output_weight_average: float32 [2, 128, 20000], P(None, None, 'gene')
- new_gene_vectors_average: float32 [3, 20000], P(None, 'gene')
- new_batch_shift_average: float32 [32, 128], replicated
- new_norm_params_average: float32 [4, 128], replicated
- new_head_weight_average: float32 [128, 20], replicated
- new_head_bias_average: float32 [20], replicated
- new_decoder_input_average: float32 [42, 128], replicated
The draws below stay inside these ranges and needn't reach their ends.
Inputs may be any that keep to these rules, and one draw needn't show every extreme that they name: `counts`: counts are whole numbers; about half of them are zero. `valid_mask`: each index of cell and each run of 4096 // 8 rows within it has its own share of real cells.
All inputs are finite; a program needn't handle non-finite values.
Results may differ from the reference program's by a relative error of at most 0.0022.
The reference program's roundings to bfloat16 on the way count: a program that leaves them out, or rounds other values in their place, can miss the bound.
Values may be sent and summed in bfloat16 or wider, within the bound.
A program may use at most 512 MiB of HBM per device.

```python
import math
import jax
import jax.numpy as jnp
from jax import lax

G = 20000
H = 128
L = 10
NB = 32
CELL_DEV = 4096
CELLS = 16384
N_GENE = 8
N_CELL = 4


def draw_counts(key, part):
    first_key, second_key, third_key, fourth_key, fifth_key, sixth_key = jax.random.split(key, 6)
    element_level = jax.random.randint(first_key, (CELLS, G), 1, 7)
    cell_level = jax.random.randint(fourth_key, (CELLS, 1), 0, 2)
    exponent = jnp.minimum(element_level + cell_level, 6)
    ceiling = jnp.left_shift(jnp.ones((CELLS, G), jnp.int32), exponent)
    values = jax.random.randint(second_key, (CELLS, G), 0, ceiling)
    keeper = jax.random.randint(third_key, (CELLS, G), 0, 10) >= 4
    drawn = jnp.where(keeper, values, 0)
    top_row = jax.random.randint(fifth_key, (), 0, CELLS)
    top_gene = jax.random.randint(sixth_key, (), 0, G)
    marked = (jnp.arange(CELLS)[:, None] == top_row) & (jnp.arange(G)[None, :] == top_gene)
    return jnp.where(marked, 63, drawn).astype(jnp.int32)


def draw_valid_mask(key, part):
    rows = jnp.arange(CELLS)
    block_index = rows // CELL_DEV
    slab_index = rows % CELL_DEV // (CELL_DEV // N_GENE)
    limit = (N_GENE - 1 + 2 * slab_index) * (N_CELL - 1 + 2 * block_index)
    drawn = jax.random.randint(key, (CELLS,), 0, 9 * (N_GENE - 1) * (N_CELL - 1))
    return (drawn < limit).astype(jnp.int32)


def touch_ends(result, own_key, least, top_value):
    extent = result.shape
    place = [jax.random.randint(jax.random.fold_in(own_key, axis), (), 0, extent[axis]) for axis in range(len(extent))]
    result = result.at[tuple(place)].set(least)
    longest = extent.index(max(extent))
    place[longest] = (place[longest] + 1) % extent[longest]
    return result.at[tuple(place)].set(top_value)


def block_scale(own_key, shape, cuts, smallest, largest):
    factor_of = 1.0
    for dim, shards_of in cuts:
        steps = jax.random.uniform(jax.random.fold_in(jax.random.fold_in(own_key, 6), dim), (shards_of,), jnp.float32, smallest / len(cuts), largest / len(cuts))
        factor_of = factor_of * jnp.repeat(jnp.exp(steps), shape[dim] // shards_of).reshape((-1,) + (1,) * (len(shape) - 1 - dim))
    return factor_of


def normal_values(key, extent, deviation, most, pieces=(), held_as=jnp.bfloat16):
    loudness = block_scale(key, extent, pieces, -0.22, 0.18) if pieces else 1.0
    values = jax.random.normal(key, extent, jnp.float32) * deviation * loudness
    return jnp.minimum(jnp.maximum(values, -most), most).astype(held_as)


def setup_inputs(seed: int = 0) -> dict:
    streams_of = jax.random.split(jax.random.key(seed), 29)
    counts = draw_counts(jax.random.fold_in(streams_of[28], 71), 0)
    batch_index = touch_ends(jax.random.randint(streams_of[1], (CELLS,), 0, NB), jax.random.fold_in(streams_of[1], 1), 0, NB - 1).astype(jnp.int32)
    valid_mask = draw_valid_mask(jax.random.fold_in(streams_of[28], 71), 0)
    noise_draw = normal_values(streams_of[3], (CELLS, L), 1.0, 5.0, ((0, 4),), jnp.float32)
    encoder_weight = normal_values(streams_of[4], (G, H), G ** -0.5, 0.0390625, ((0, 8),), jnp.float32)
    output_weight = normal_values(streams_of[5], (2, H, G), H ** -0.5, 0.5, ((2, 8),), jnp.float32)
    gene_vectors = normal_values(streams_of[6], (3, G), 1.0, 3.0, ((1, 8),), jnp.float32)
    batch_shift = normal_values(streams_of[7], (NB, H), 0.5, 3.0, (), jnp.float32)
    layer_norm_params = jnp.clip(1.0 + 0.18 * jax.random.normal(streams_of[8], (4, H), jnp.float32), 0.1, 1.9)
    head_weight = normal_values(streams_of[9], (H, 2 * L), H ** -0.5, 0.5, (), jnp.float32)
    head_bias = normal_values(streams_of[10], (2 * L,), 0.3, 1.5, (), jnp.float32)
    decoder_input = normal_values(streams_of[11], (L + NB, H), L ** -0.5, 2.0, (), jnp.float32)
    encoder_weight_momentum = normal_values(streams_of[12], (G, H), (40 * (0.44 * CELLS) ** -0.5 / G), 0.00036621094, ((0, 8),), jnp.float32)
    output_weight_momentum = normal_values(streams_of[13], (2, H, G), (4.0 / G), 0.0029296875, ((2, 8),), jnp.float32)
    gene_vectors_momentum = normal_values(streams_of[14], (3, G), (2.0 / G), 0.0014648438, ((1, 8),), jnp.float32)
    batch_shift_momentum = normal_values(streams_of[15], (NB, H), (25 * (0.44 * CELLS / NB) ** 0.5 / (0.44 * CELLS * G)), 3.814697265625e-05, (), jnp.float32)
    norm_params_momentum = normal_values(streams_of[16], (4, H), (25 * (0.44 * CELLS) ** -0.5 / G), 0.00021362305, (), jnp.float32)
    head_weight_momentum = normal_values(streams_of[17], (H, 2 * L), (15 * (0.44 * CELLS) ** -0.5 / G), 0.00012207031, (), jnp.float32)
    head_bias_momentum = normal_values(streams_of[18], (2 * L,), (25 * (0.44 * CELLS) ** -0.5 / G), 0.00021362305, (), jnp.float32)
    decoder_input_momentum = normal_values(streams_of[19], (L + NB, H), (25 * (0.44 * CELLS) ** -0.5 / G), 0.00021362305, (), jnp.float32)
    encoder_weight_average = normal_values(streams_of[20], (G, H), G ** -0.5, 0.0390625, ((0, 8),), jnp.float32)
    output_weight_average = normal_values(streams_of[21], (2, H, G), H ** -0.5, 0.5, ((2, 8),), jnp.float32)
    gene_vectors_average = normal_values(streams_of[22], (3, G), 1.0, 3.0, ((1, 8),), jnp.float32)
    batch_shift_average = normal_values(streams_of[23], (NB, H), 0.5, 3.0, (), jnp.float32)
    norm_params_average = jnp.clip(1.0 + 0.18 * jax.random.normal(streams_of[24], (4, H), jnp.float32), 0.1, 1.9)
    head_weight_average = normal_values(streams_of[25], (H, 2 * L), H ** -0.5, 0.5, (), jnp.float32)
    head_bias_average = normal_values(streams_of[26], (2 * L,), 0.3, 1.5, (), jnp.float32)
    decoder_input_average = normal_values(streams_of[27], (L + NB, H), L ** -0.5, 2.0, (), jnp.float32)
    return {"counts": counts, "batch_index": batch_index, "valid_mask": valid_mask, "noise_draw": noise_draw, "encoder_weight": encoder_weight, "output_weight": output_weight, "gene_vectors": gene_vectors, "batch_shift": batch_shift, "layer_norm_params": layer_norm_params, "head_weight": head_weight, "head_bias": head_bias, "decoder_input": decoder_input, "encoder_weight_momentum": encoder_weight_momentum, "output_weight_momentum": output_weight_momentum, "gene_vectors_momentum": gene_vectors_momentum, "batch_shift_momentum": batch_shift_momentum, "norm_params_momentum": norm_params_momentum, "head_weight_momentum": head_weight_momentum, "head_bias_momentum": head_bias_momentum, "decoder_input_momentum": decoder_input_momentum, "encoder_weight_average": encoder_weight_average, "output_weight_average": output_weight_average, "gene_vectors_average": gene_vectors_average, "batch_shift_average": batch_shift_average, "norm_params_average": norm_params_average, "head_weight_average": head_weight_average, "head_bias_average": head_bias_average, "decoder_input_average": decoder_input_average}


@jax.custom_vjp
def low(v):
    return lax.optimization_barrier(v.astype(jnp.bfloat16)).astype(jnp.float32)

@jax.custom_vjp
def low_back(v):
    return v

def low_keep(v):
    return (low(v), None)

def low_pass(kept, grad):
    return (grad,)

def back_keep(v):
    return (v, None)

def back_low(kept, grad):
    return (low(grad),)
low.defvjp(low_keep, low_pass)
low_back.defvjp(back_keep, back_low)
momentum_decay = 0.9
average_decay = 0.99
norm_epsilon = 0.001
rate_epsilon = 1e-08
step_rates = (110.0, 46000.0, 300000.0, 70000.0, 13000.0, 3700.0, 7600.0, 8000.0)

def negative_loglik(counted, rate, theta, dropout):
    softplus_pi = jax.nn.softplus(-dropout)
    log_theta = jnp.log(theta + rate_epsilon)
    log_both = jnp.log(theta + rate + rate_epsilon)
    pi_theta = -dropout + theta * (log_theta - log_both)
    zero_case = jax.nn.softplus(pi_theta) - softplus_pi
    other_case = -softplus_pi + pi_theta + counted * (jnp.log(rate + rate_epsilon) - log_both) + lax.lgamma(counted + theta) - lax.lgamma(theta) - lax.lgamma(counted + 1.0)
    return -jnp.where(counted < 0.5, zero_case, other_case)

def encode_hot(index, width):
    return (index[:, None] == jnp.arange(width)[None, :]).astype(jnp.float32)

def batch_norm(values, gain, shift, valid, valid_count):
    mean = lax.optimization_barrier(jnp.sum(valid[:, None] * values, axis=0)) / valid_count
    spread = lax.optimization_barrier(jnp.sum(valid[:, None] * values * values, axis=0)) / valid_count - mean * mean
    return (values - mean) * lax.rsqrt(spread + norm_epsilon) * gain + shift

def nesterov(weight, momentum, average, grad, rate):
    moment = momentum_decay * momentum + grad
    fresh = weight - rate * (grad + momentum_decay * moment)
    return (fresh, moment, average_decay * average + (1.0 - average_decay) * fresh)

def reference(counts, batch_index, valid_mask, noise_draw, encoder_weight, output_weight, gene_vectors, batch_shift, layer_norm_params, head_weight, head_bias, decoder_input, encoder_weight_momentum, output_weight_momentum, gene_vectors_momentum, batch_shift_momentum, norm_params_momentum, head_weight_momentum, head_bias_momentum, decoder_input_momentum, encoder_weight_average, output_weight_average, gene_vectors_average, batch_shift_average, norm_params_average, head_weight_average, head_bias_average, decoder_input_average):
    cells, genes = counts.shape
    hidden_width = encoder_weight.shape[1]
    latent_width = head_bias.shape[0] // 2
    block = math.gcd(cells, 1024)
    blocks = cells // block
    valid_all = valid_mask.astype(jnp.float32)
    valid_count = jnp.maximum(jnp.sum(valid_all), 1.0)
    scale = 1.0 / (valid_count * genes)
    library = lax.optimization_barrier(jnp.sum(counts.astype(jnp.float32), axis=1))
    hot = encode_hot(batch_index, batch_shift.shape[0])
    inputs = jnp.log1p(counts.astype(jnp.float32))
    counts_blocks = counts.reshape(blocks, block, genes)
    valid_blocks = valid_all.reshape(blocks, block)
    library_blocks = library.reshape(blocks, block)

    def forward(inputs, enc_w, out_w, gene_v, shift_w, norm_p, head_w, head_b, mixing):
        weight16 = low(enc_w)

        def encode_block(part):
            return jnp.dot(low(part), weight16, precision=lax.Precision.HIGHEST)
        encoded = lax.map(jax.checkpoint(encode_block), inputs.reshape(blocks, block, genes))
        encoded = low_back(encoded.reshape(cells, hidden_width))
        encoder_preactivation = encoded + jnp.dot(hot, shift_w, precision=lax.Precision.HIGHEST)
        hidden1 = jax.nn.silu(batch_norm(encoder_preactivation, norm_p[0], norm_p[1], valid_all, valid_count))
        heads = jnp.dot(hidden1, head_w, precision=lax.Precision.HIGHEST) + head_b
        mean_z = heads[:, :latent_width]
        log_var = heads[:, latent_width:]
        latent = mean_z + jnp.exp(0.5 * log_var) * noise_draw
        diverge = 0.5 * lax.optimization_barrier(jnp.sum(mean_z * mean_z + jnp.exp(log_var) - log_var - 1.0, axis=1))
        decoder_preactivation = jnp.dot(jnp.concatenate([latent, hot], axis=1), mixing, precision=lax.Precision.HIGHEST)
        hidden2 = low(jax.nn.silu(batch_norm(decoder_preactivation, norm_p[2], norm_p[3], valid_all, valid_count)))
        out16 = low(out_w)

        def decode_block(items):
            rows, counted_int, valid_rows, library_rows = items
            logits = low_back(jnp.einsum('rh,khg->rkg', rows, out16, precision=lax.Precision.HIGHEST)) + gene_v[None, :2, :]
            rate = library_rows[:, None] * jax.nn.softmax(logits[:, 0], axis=1)
            terms = negative_loglik(counted_int.astype(jnp.float32), rate, jnp.exp(gene_v[2])[None, :], logits[:, 1])
            return lax.optimization_barrier(jnp.sum(valid_rows[:, None] * terms, axis=1))
        recon = lax.map(jax.checkpoint(decode_block), (hidden2.reshape(blocks, block, hidden_width), counts_blocks, valid_blocks, library_blocks))
        row_totals = recon.reshape(cells) + valid_all * diverge
        return (jnp.sum(row_totals) * scale, row_totals / genes)
    objective, pull, cell_loss = jax.vjp(forward, inputs, encoder_weight, output_weight, gene_vectors, batch_shift, layer_norm_params, head_weight, head_bias, decoder_input, has_aux=True)
    grads = pull(jnp.ones_like(objective))
    input_grad = grads[0]
    new_encoder_weight, new_encoder_weight_momentum, new_encoder_weight_average = nesterov(encoder_weight, encoder_weight_momentum, encoder_weight_average, grads[1], step_rates[0])
    new_output_weight, new_output_weight_momentum, new_output_weight_average = nesterov(output_weight, output_weight_momentum, output_weight_average, grads[2], step_rates[1])
    new_gene_vectors, new_gene_vectors_momentum, new_gene_vectors_average = nesterov(gene_vectors, gene_vectors_momentum, gene_vectors_average, grads[3], step_rates[2])
    new_batch_shift, new_batch_shift_momentum, new_batch_shift_average = nesterov(batch_shift, batch_shift_momentum, batch_shift_average, grads[4], step_rates[3])
    new_norm_params, new_norm_params_momentum, new_norm_params_average = nesterov(layer_norm_params, norm_params_momentum, norm_params_average, grads[5], step_rates[4])
    new_head_weight, new_head_weight_momentum, new_head_weight_average = nesterov(head_weight, head_weight_momentum, head_weight_average, grads[6], step_rates[5])
    new_head_bias, new_head_bias_momentum, new_head_bias_average = nesterov(head_bias, head_bias_momentum, head_bias_average, grads[7], step_rates[6])
    new_decoder_input, new_decoder_input_momentum, new_decoder_input_average = nesterov(decoder_input, decoder_input_momentum, decoder_input_average, grads[8], step_rates[7])
    return (cell_loss, input_grad, new_encoder_weight, new_output_weight, new_gene_vectors, new_batch_shift, new_norm_params, new_head_weight, new_head_bias, new_decoder_input, new_encoder_weight_momentum, new_output_weight_momentum, new_gene_vectors_momentum, new_batch_shift_momentum, new_norm_params_momentum, new_head_weight_momentum, new_head_bias_momentum, new_decoder_input_momentum, new_encoder_weight_average, new_output_weight_average, new_gene_vectors_average, new_batch_shift_average, new_norm_params_average, new_head_weight_average, new_head_bias_average, new_decoder_input_average)
```

```python
import functools

import jax
import jax.numpy as jnp
from jax import lax
from jax.experimental import pallas as pl
from jax.experimental.pallas import tpu as pltpu
from jax.sharding import PartitionSpec as P

momentum_decay = 0.9
average_decay = 0.99
norm_epsilon = 0.001
rate_epsilon = 1e-08
step_rates = (110.0, 46000.0, 300000.0, 70000.0, 13000.0, 3700.0, 7600.0, 8000.0)
ln2 = 0.6931471805599453
f32 = jnp.float32
bf16 = jnp.bfloat16
LANES = 128
ROWS = 16
HOT_DEPTH = 144
PARAMS = pltpu.CompilerParams(vmem_limit_bytes=60 << 20)


def silu_slope(value):
    sigma = jax.nn.sigmoid(value)
    return sigma * (1.0 + value * (1.0 - sigma))


def nesterov(weight, momentum, average, grad, rate):
    moment = momentum_decay * momentum + grad
    fresh = weight - rate * (grad + momentum_decay * moment)
    return (fresh, moment, average_decay * average + (1.0 - average_decay) * fresh)


def three_parts(value):
    high = lax.reduce_precision(value, 8, 7)
    rest = value - high
    middle = lax.reduce_precision(rest, 8, 7)
    return high, middle, lax.reduce_precision(rest - middle, 8, 7)


def whole(array):
    return pl.BlockSpec(array.shape, lambda i: (0,) * array.ndim)


def column_blocks(rows, chunk):
    return pl.BlockSpec((rows, chunk), lambda i: (0, i))


def split_rows(genes):
    full = genes // ROWS
    groups = max(d for d in range(1, 14) if full % d == 0)
    return full, groups, genes - full * ROWS


def padded(genes):
    return -(-genes // ROWS) * ROWS


def pick_chunk(cells, most):
    chunk = LANES
    while chunk * 2 <= most and cells % (chunk * 2) == 0:
        chunk *= 2
    return chunk


def tail_rows(ref, start, stop, columns, dtype):
    piece = ref[start:stop, columns]
    filler = jnp.zeros((ROWS - (stop - start), piece.shape[1]), dtype)
    return jnp.concatenate([piece, filler], axis=0)


def encode_kernel(counts_ref, weight_ref, out_ref, library_ref, inputs_ref, *, genes, chunk):
    full, groups, tail = split_rows(genes)

    def group(counted, rows, total):
        inputs_ref[rows, :] = jnp.log(counted + 1.0).astype(bf16)
        return total + counted[:8] + counted[8:]

    def step(i, total):
        rows = pl.ds(pl.multiple_of(i * ROWS, ROWS), ROWS)
        return group(counts_ref[rows, :].astype(f32), rows, total)

    total = lax.fori_loop(0, full, step, jnp.zeros((8, chunk), f32), unroll=4)
    if tail:
        rows = pl.ds(full * ROWS, ROWS)
        counted = tail_rows(counts_ref, full * ROWS, genes, slice(None), jnp.int32).astype(f32)
        total = group(counted, rows, total)
    library_ref[...] = jnp.sum(total, axis=0, keepdims=True)
    out_ref[...] = jnp.dot(weight_ref[...], inputs_ref[...], preferred_element_type=f32)


def encode(counts_t, weight_t):
    genes, cells = counts_t.shape
    chunk = pick_chunk(cells, 512)
    width = weight_t.shape[0]
    return pl.pallas_call(
        functools.partial(encode_kernel, genes=genes, chunk=chunk),
        grid=(cells // chunk,),
        in_specs=[column_blocks(genes, chunk), whole(weight_t)],
        out_specs=[column_blocks(width, chunk), column_blocks(1, chunk)],
        out_shape=[
            jax.ShapeDtypeStruct((width, cells), f32),
            jax.ShapeDtypeStruct((1, cells), f32),
        ],
        scratch_shapes=[pltpu.VMEM((padded(genes), chunk), bf16)],
        compiler_params=PARAMS,
        name="encode",
    )(counts_t, weight_t)


def fill_hidden(long_ref, hidden_ref, top):
    width, chunk = hidden_ref.shape
    long_ref[0:width, :] = hidden_ref[...]
    index = lax.broadcasted_iota(jnp.int32, (HOT_DEPTH - width, chunk), 0)
    extra = jnp.where(index < 3, 1.0, 0.0)
    if top is not None:
        high = (-top).astype(bf16).astype(f32)
        middle = (-top - high).astype(bf16).astype(f32)
        low = (-top - high - middle).astype(bf16).astype(f32)
        extra = jnp.where(index == 3, high, extra)
        extra = jnp.where(index == 4, middle, extra)
        extra = jnp.where(index == 5, low, extra)
    long_ref[width:HOT_DEPTH, :] = extra.astype(bf16)


def totals_kernel(hidden_ref, weight_ref, top_ref, total_ref, long_ref, value_ref, *, genes, chunk):
    size = weight_ref.shape[0]
    fill_hidden(long_ref, hidden_ref, None)
    value_ref[...] = jnp.dot(weight_ref[...], long_ref[...], preferred_element_type=f32)
    count = size // ROWS

    def highest(i, best):
        part = value_ref[pl.ds(pl.multiple_of(i * ROWS, ROWS), ROWS), :]
        return jnp.maximum(best, jnp.maximum(part[:8], part[8:]))

    best = lax.fori_loop(0, count, highest, jnp.full((8, chunk), -jnp.inf, f32), unroll=4)
    top = jnp.max(best, axis=0, keepdims=True)

    def add(i, total):
        part = jnp.exp(value_ref[pl.ds(pl.multiple_of(i * ROWS, ROWS), ROWS), :] - top)
        return total + part[:8] + part[8:]

    total = lax.fori_loop(0, count, add, jnp.zeros((8, chunk), f32), unroll=4)
    top_ref[...] = top
    total_ref[...] = jnp.sum(total, axis=0, keepdims=True)


def totals(hidden, weight, genes):
    width, cells = hidden.shape
    chunk = pick_chunk(cells, 512)
    return pl.pallas_call(
        functools.partial(totals_kernel, genes=genes, chunk=chunk),
        grid=(cells // chunk,),
        in_specs=[column_blocks(width, chunk), whole(weight)],
        out_specs=[column_blocks(1, chunk)] * 2,
        out_shape=[jax.ShapeDtypeStruct((1, cells), f32)] * 2,
        scratch_shapes=[
            pltpu.VMEM((HOT_DEPTH, chunk), bf16),
            pltpu.VMEM((weight.shape[0], chunk), f32),
        ],
        compiler_params=PARAMS,
        name="totals",
    )(hidden, weight)


def likelihood_kernel(
    counts_ref,
    hidden_ref,
    top_ref,
    ratio_ref,
    share_ref,
    weight_ref,
    back_ref,
    theta_ref,
    log_ref,
    slope_ref,
    table_ref,
    slopes_ref,
    loss_ref,
    total_ref,
    grad_hidden_ref,
    grad_weight_ref,
    grad_bias_ref,
    grad_theta_ref,
    long_ref,
    value_ref,
    second_ref,
    *,
    genes,
    chunk,
):
    full, groups, tail = split_rows(genes)
    block = ROWS * groups
    width = hidden_ref.shape[0]

    @pl.when(pl.program_id(0) == 0)
    def _():
        for ref in (grad_weight_ref, grad_bias_ref, grad_theta_ref):
            ref[...] = jnp.zeros_like(ref)

    fill_hidden(long_ref, hidden_ref, top_ref[...])
    tiles = [slice(j, j + LANES) for j in range(0, chunk, LANES)]
    ratio_all = ratio_ref[...]
    share_all = share_ref[...]

    def group(held, rows, read, carry):
        losses, sums = [], []
        theta = theta_ref[rows, :]
        log_theta = log_ref[rows, :]
        log_slope = slope_ref[rows, :]
        table = table_ref[rows, :]
        grad_bias = grad_bias_ref[rows, :]
        grad_theta = grad_theta_ref[rows, :]
        for j, columns in enumerate(tiles):
            count = read(columns)
            counted = count.astype(f32)
            first = value_ref[0, held, columns]
            dropout = value_ref[1, held, columns]
            ratio, share = ratio_all[:, columns], share_all[:, columns]
            rate = jnp.exp(first) * ratio
            near = rate + rate_epsilon
            both = theta + near
            inverse = pl.reciprocal(near * both)
            inverse_both = inverse * near
            inverse_near = inverse * both
            log_fraction = jnp.log2(near * inverse_both)
            log_both = jnp.log2(both)
            pi_theta = (theta * ln2) * (log_theta - log_both) - dropout
            small_pi = jnp.exp(-jnp.abs(dropout))
            small_theta = jnp.exp(-jnp.abs(pi_theta))
            one_pi = 1.0 + small_pi
            one_theta = 1.0 + small_theta
            inverse_ones = pl.reciprocal(one_pi * one_theta)
            sigma_pi = jnp.where(dropout >= 0.0, small_pi, 1.0) * (inverse_ones * one_theta)
            inverse_theta = inverse_ones * one_pi
            zero = count < 1
            sigma_theta = jnp.where(pi_theta >= 0.0, 1.0, small_theta) * inverse_theta
            sigma = jnp.where(zero, sigma_theta, 1.0)
            log_ones = jnp.log2(one_pi * jnp.where(zero, inverse_theta, 1.0))
            upper = jnp.where(zero, jnp.maximum(pi_theta, 0.0), pi_theta)
            gammas = jnp.take_along_axis(table, count, axis=1)
            digammas = jnp.take_along_axis(table, count + LANES // 2, axis=1)
            loss = (jnp.maximum(-dropout, 0.0) - upper) + (
                ln2 * (log_ones - counted * log_fraction) - gammas
            )
            pull = (sigma * theta + counted) * inverse_both
            slope = rate * (pull - counted * inverse_near)
            slopes_ref[rows, columns] = slope
            grad_dropout = (sigma - sigma_pi) * share
            second_ref[rows, columns] = grad_dropout.astype(bf16)
            grad_bias = grad_bias + grad_dropout
            grad_theta = grad_theta + share * (
                pull - ln2 * (sigma * (log_slope - log_both)) - digammas
            )
            losses.append(carry[0][j] + loss[:8] + loss[8:])
            sums.append(carry[1][j] + slope[:8] + slope[8:])
        grad_bias_ref[rows, :] = grad_bias
        grad_theta_ref[rows, :] = grad_theta
        return tuple(losses), tuple(sums)

    def logits(rows, size):
        for k in range(2):
            value_ref[k, 0:size, :] = jnp.dot(
                weight_ref[k, rows, :], long_ref[...], preferred_element_type=f32
            )

    def step(b, carry):
        start = pl.multiple_of(b * block, ROWS)
        logits(pl.ds(start, block), block)

        def inner(i, carry):
            held = pl.multiple_of(i * ROWS, ROWS)
            rows = pl.ds(pl.multiple_of(start + held, ROWS), ROWS)
            return group(pl.ds(held, ROWS), rows, lambda cols: counts_ref[rows, cols], carry)

        return lax.fori_loop(0, groups, inner, carry, unroll=4)

    zeros = tuple(jnp.zeros((8, LANES), f32) for _ in tiles)
    carry = lax.fori_loop(0, full // groups, step, (zeros, zeros))
    if tail:
        rows = pl.ds(full * ROWS, ROWS)
        logits(rows, ROWS)
        carry = group(
            pl.ds(0, ROWS),
            rows,
            lambda cols: tail_rows(counts_ref, full * ROWS, genes, cols, jnp.int32),
            carry,
        )
    for j, columns in enumerate(tiles):
        loss_ref[:, columns] = jnp.sum(carry[0][j], axis=0, keepdims=True)
        total_ref[:, columns] = jnp.sum(carry[1][j], axis=0, keepdims=True)
    grad_weight_ref[...] += lax.dot_general(
        second_ref[...], hidden_ref[...], (((1,), (1,)), ((), ())), preferred_element_type=f32
    )
    grad_hidden_ref[...] = jnp.dot(back_ref[...], second_ref[...], preferred_element_type=f32)


def likelihood(counts_t, hidden, top, ratio, share, weights, back, gene_tables):
    genes, cells = counts_t.shape
    size = weights.shape[1]
    width = hidden.shape[0]
    chunk = pick_chunk(cells, 512)
    groups = split_rows(genes)[1]
    row = column_blocks(1, chunk)
    per_gene = pl.BlockSpec((size, LANES), lambda i: (0, 0))
    return pl.pallas_call(
        functools.partial(likelihood_kernel, genes=genes, chunk=chunk),
        grid=(cells // chunk,),
        in_specs=[column_blocks(genes, chunk), column_blocks(width, chunk), row, row, row]
        + [whole(weights), whole(back)]
        + [whole(a) for a in gene_tables],
        out_specs=[column_blocks(size, chunk), row, row, column_blocks(width, chunk)]
        + [per_gene] * 3,
        out_shape=[
            jax.ShapeDtypeStruct((size, cells), f32),
            jax.ShapeDtypeStruct((1, cells), f32),
            jax.ShapeDtypeStruct((1, cells), f32),
            jax.ShapeDtypeStruct((width, cells), f32),
        ]
        + [jax.ShapeDtypeStruct((size, LANES), f32)] * 3,
        scratch_shapes=[
            pltpu.VMEM((HOT_DEPTH, chunk), bf16),
            pltpu.VMEM((2, ROWS * groups, chunk), f32),
            pltpu.VMEM((size, chunk), bf16),
        ],
        compiler_params=PARAMS,
        name="likelihood",
    )(counts_t, hidden, top, ratio, share, weights, back, *gene_tables)


def frequency_kernel(
    slopes_ref,
    hidden_ref,
    top_ref,
    pull_ref,
    share_ref,
    other_ref,
    weight_ref,
    back_ref,
    grad_hidden_ref,
    grad_weight_ref,
    grad_bias_ref,
    long_ref,
    value_ref,
    first_ref,
    *,
    chunk,
):
    size = weight_ref.shape[0]

    @pl.when(pl.program_id(0) == 0)
    def _():
        for ref in (grad_weight_ref, grad_bias_ref):
            ref[...] = jnp.zeros_like(ref)

    fill_hidden(long_ref, hidden_ref, top_ref[...])
    value_ref[...] = jnp.dot(weight_ref[...], long_ref[...], preferred_element_type=f32)
    tiles = [slice(j, j + LANES) for j in range(0, chunk, LANES)]
    pull_all = pull_ref[...]
    share_all = share_ref[...]

    def step(i, carry):
        rows = pl.ds(pl.multiple_of(i * ROWS, ROWS), ROWS)
        bias = grad_bias_ref[rows, :]
        for columns in tiles:
            grad = share_all[:, columns] * (
                slopes_ref[rows, columns] - jnp.exp(value_ref[rows, columns]) * pull_all[:, columns]
            )
            first_ref[rows, columns] = grad.astype(bf16)
            bias = bias + grad
        grad_bias_ref[rows, :] = bias
        return carry

    lax.fori_loop(0, size // ROWS, step, 0, unroll=2)
    grad_weight_ref[...] += lax.dot_general(
        first_ref[...], hidden_ref[...], (((1,), (1,)), ((), ())), preferred_element_type=f32
    )
    grad_hidden_ref[...] = other_ref[...] + jnp.dot(
        back_ref[...], first_ref[...], preferred_element_type=f32
    )


def frequency(slopes, hidden, top, pull, share, other, weight, back):
    size, cells = slopes.shape
    width = hidden.shape[0]
    chunk = pick_chunk(cells, 512)
    row = column_blocks(1, chunk)
    wide = column_blocks(width, chunk)
    per_gene = pl.BlockSpec((size, LANES), lambda i: (0, 0))
    return pl.pallas_call(
        functools.partial(frequency_kernel, chunk=chunk),
        grid=(cells // chunk,),
        in_specs=[column_blocks(size, chunk), wide, row, row, row, wide]
        + [whole(weight), whole(back)],
        out_specs=[wide, per_gene, per_gene],
        out_shape=[jax.ShapeDtypeStruct((width, cells), f32)]
        + [jax.ShapeDtypeStruct((size, LANES), f32)] * 2,
        scratch_shapes=[
            pltpu.VMEM((HOT_DEPTH, chunk), bf16),
            pltpu.VMEM((size, chunk), f32),
            pltpu.VMEM((size, chunk), bf16),
        ],
        compiler_params=PARAMS,
        name="frequency",
    )(slopes, hidden, top, pull, share, other, weight, back)


def encoder_back_kernel(counts_ref, grad_ref, weight_ref, input_ref, weight_grad_ref):
    inputs = jnp.log(counts_ref[...].astype(f32) + 1.0).astype(bf16)
    weight_grad_ref[...] = lax.dot_general(
        inputs, grad_ref[...], (((1,), (1,)), ((), ())), preferred_element_type=f32
    )
    input_ref[...] = jnp.dot(weight_ref[...], grad_ref[...], preferred_element_type=f32)


def encoder_back(counts_t, grad, weight16):
    genes, cells = counts_t.shape
    width = grad.shape[0]
    block = LANES
    return pl.pallas_call(
        encoder_back_kernel,
        grid=(pl.cdiv(genes, block),),
        in_specs=[
            pl.BlockSpec((block, cells), lambda i: (i, 0)),
            whole(grad),
            pl.BlockSpec((block, width), lambda i: (i, 0)),
        ],
        out_specs=[
            pl.BlockSpec((block, cells), lambda i: (i, 0)),
            pl.BlockSpec((block, width), lambda i: (i, 0)),
        ],
        out_shape=[
            jax.ShapeDtypeStruct((genes, cells), f32),
            jax.ShapeDtypeStruct((genes, width), f32),
        ],
        compiler_params=PARAMS,
        name="encoder_back",
    )(counts_t, grad, weight16)


def local(
    counts,
    batch_index,
    valid_mask,
    noise_draw,
    encoder_weight,
    output_weight,
    gene_vectors,
    batch_shift,
    layer_norm_params,
    head_weight,
    head_bias,
    decoder_input,
    encoder_weight_momentum,
    output_weight_momentum,
    gene_vectors_momentum,
    batch_shift_momentum,
    norm_params_momentum,
    head_weight_momentum,
    head_bias_momentum,
    decoder_input_momentum,
    encoder_weight_average,
    output_weight_average,
    gene_vectors_average,
    batch_shift_average,
    norm_params_average,
    head_weight_average,
    head_bias_average,
    decoder_input_average,
):
    cells, genes = counts.shape
    gene_devices = lax.axis_size("gene")
    genes_all = genes * gene_devices
    slab = cells // gene_devices
    first = lax.axis_index("gene") * slab
    latent = head_bias.shape[0] // 2
    batches = batch_shift.shape[0]
    size = padded(genes)
    gap = size - genes
    everyone = ("gene", "cell")
    dot = functools.partial(jnp.dot, precision=lax.Precision.HIGHEST)

    def dot_nt(left, right):
        return lax.dot_general(
            left, right, (((1,), (1,)), ((), ())), precision=lax.Precision.HIGHEST
        )

    def mine(array):
        return lax.dynamic_slice_in_dim(array, first, slab, 1)

    counts_t = counts.T
    weight16 = encoder_weight.astype(bf16)
    encoder_t = jnp.pad(weight16, ((0, gap), (0, 0))).T

    theta = jnp.pad(jnp.exp(gene_vectors[2]), (0, gap), constant_values=1.0)
    log_theta = jnp.log2(theta + rate_epsilon)

    def spread(column):
        return jnp.broadcast_to(column[:, None], (size, LANES))

    steps = jnp.arange(LANES // 2, dtype=f32)[None, :]
    column = theta[:, None]
    table = jnp.concatenate(
        [
            lax.lgamma(steps + column) - lax.lgamma(column) - lax.lgamma(steps + 1.0),
            lax.digamma(steps + column) - lax.digamma(column),
        ],
        axis=1,
    )
    gene_tables = (
        spread(theta),
        spread(log_theta),
        spread(log_theta + theta / (theta + rate_epsilon) / ln2),
        table,
    )
    genes_first = jnp.transpose(output_weight, (2, 0, 1))
    out16 = jnp.pad(genes_first.astype(bf16), ((0, gap), (0, 0), (0, 0)))
    bias = jnp.pad(gene_vectors[:2].T, ((0, gap), (0, 0)))
    off = (jnp.arange(size) >= genes)[:, None] & (jnp.arange(2) == 0)[None, :]
    bias = jnp.where(off, -1e30, bias)
    parts = jnp.stack(three_parts(bias), axis=2).astype(bf16)
    ones = jnp.broadcast_to((jnp.arange(2) == 0).astype(bf16)[None, :, None], (size, 2, 3))
    rest = jnp.zeros((size, 2, HOT_DEPTH - LANES - 6), bf16)
    weights = jnp.transpose(jnp.concatenate([out16, parts, ones, rest], axis=2), (1, 0, 2))
    backs = jnp.transpose(out16, (1, 2, 0))

    encoded, library = encode(counts_t, encoder_t)
    valid = valid_mask.astype(f32)[None, :]
    hot = (jnp.arange(batches)[:, None] == batch_index[None, :]).astype(f32)
    valid_mine, hot_mine, noise = mine(valid), mine(hot), mine(noise_draw.T)
    pre1 = lax.psum_scatter(encoded, "gene", scatter_dimension=1, tiled=True)
    pre1 = pre1 + dot(batch_shift.T, hot_mine)
    library = lax.psum(library, "gene")
    sum1, square1, tally = lax.psum(
        (
            jnp.sum(valid_mine * pre1, axis=1),
            jnp.sum(valid_mine * pre1 * pre1, axis=1),
            jnp.sum(valid_mine),
        ),
        everyone,
    )
    count = jnp.maximum(tally, 1.0)
    scale = 1.0 / (count * genes_all)
    norms = layer_norm_params[:, :, None]
    mean1 = sum1 / count
    inverse1 = lax.rsqrt(square1 / count - mean1 * mean1 + norm_epsilon)[:, None]
    centered1 = (pre1 - mean1[:, None]) * inverse1
    normed1 = centered1 * norms[0] + norms[1]
    hidden1 = jax.nn.silu(normed1)
    heads = dot(head_weight.T, hidden1) + head_bias[:, None]
    mean_z, log_var = heads[:latent], heads[latent:]
    spread_z = jnp.exp(0.5 * log_var)
    sample = mean_z + spread_z * noise
    diverge = 0.5 * jnp.sum(
        mean_z * mean_z + jnp.exp(log_var) - log_var - 1.0, axis=0, keepdims=True
    )

    pre2_mine = dot(decoder_input.T, jnp.concatenate([sample, hot_mine], axis=0))
    sum2, square2 = lax.psum(
        (jnp.sum(valid_mine * pre2_mine, axis=1), jnp.sum(valid_mine * pre2_mine**2, axis=1)),
        everyone,
    )
    sample_all = lax.all_gather(sample, "gene", axis=1, tiled=True)
    mixed = jnp.concatenate([sample_all, hot], axis=0)
    mean2 = sum2 / count
    inverse2 = lax.rsqrt(square2 / count - mean2 * mean2 + norm_epsilon)[:, None]

    def normed_of(values):
        centered = (values - mean2[:, None]) * inverse2
        return centered, centered * norms[2] + norms[3]

    centered2, normed2 = normed_of(dot(decoder_input.T, mixed))
    hidden2 = jax.nn.silu(normed2).astype(bf16)

    top_here, total_here = totals(hidden2, weights[0], genes)
    tops = lax.all_gather(jnp.concatenate([top_here, total_here], axis=0), "gene")
    top = jnp.max(tops[:, 0], axis=0, keepdims=True)
    total = jnp.sum(tops[:, 1] * jnp.exp(tops[:, 0] - top), axis=0, keepdims=True)
    share = scale * valid
    slopes, loss, pull, grad_hidden2, grad_out1, grad_bias1, grad_theta = likelihood(
        counts_t, hidden2, top, library / total, share, weights, backs[1], gene_tables
    )
    pull, loss = lax.psum((pull, loss), "gene")
    diverge_all = lax.all_gather(diverge, "gene", axis=1, tiled=True)
    cell_loss = (valid * (loss + diverge_all) / genes_all)[0]
    grad_hidden2, grad_out0, grad_bias0 = frequency(
        slopes, hidden2, top, pull / total, share, grad_hidden2, weights[0], backs[0]
    )
    grad_genes = jnp.stack(
        [
            jnp.sum(grad_bias0, axis=1),
            jnp.sum(grad_bias1, axis=1),
            jnp.sum(grad_theta, axis=1) * theta,
        ]
    )[:, :genes]

    grad_normed2 = grad_hidden2 * silu_slope(normed2)
    gain2_grad, shift2_grad = lax.psum(
        (jnp.sum(grad_normed2 * centered2, axis=1), jnp.sum(grad_normed2, axis=1)), everyone
    )
    factor2 = inverse2 * norms[2]
    latent_rows = decoder_input[:latent]
    grad_sample = lax.psum_scatter(
        dot(latent_rows, factor2 * grad_normed2), "gene", scatter_dimension=1, tiled=True
    )
    centered2_mine, _ = normed_of(pre2_mine)
    grad_sample = grad_sample - valid_mine / count * dot(
        latent_rows,
        factor2 * (shift2_grad[:, None] + centered2_mine * gain2_grad[:, None]),
    )
    mixed_mine = valid_mine * jnp.concatenate([sample, hot_mine], axis=0)
    grad_mixing = factor2[:, 0] * (
        dot_nt(mixed, grad_normed2)
        - (
            jnp.sum(mixed_mine, axis=1, keepdims=True) * shift2_grad
            + dot_nt(mixed_mine, centered2_mine) * gain2_grad
        )
        / count
    )
    grad_mean = grad_sample + scale * valid_mine * mean_z
    grad_log = (
        grad_sample * noise * spread_z * 0.5
        + scale * valid_mine * (jnp.exp(log_var) - 1.0) * 0.5
    )
    grad_heads_out = jnp.concatenate([grad_mean, grad_log], axis=0)
    grad_heads = dot_nt(hidden1, grad_heads_out)
    grad_head_bias = jnp.sum(grad_heads_out, axis=1)
    grad_normed1 = dot(head_weight, grad_heads_out) * silu_slope(normed1)
    gain1_grad, shift1_grad = lax.psum(
        (jnp.sum(grad_normed1 * centered1, axis=1), jnp.sum(grad_normed1, axis=1)), everyone
    )
    grad_pre1 = (inverse1 * norms[0]) * (
        grad_normed1
        - valid_mine / count * (shift1_grad[:, None] + centered1 * gain1_grad[:, None])
    )
    grad_shift = dot_nt(hot_mine, grad_pre1)
    grad_pre16 = lax.all_gather(grad_pre1.astype(bf16), "gene", axis=1, tiled=True)
    input_grad, grad_encoder = encoder_back(counts_t, grad_pre16, weight16)
    grad_shift, grad_heads, grad_head_bias, grad_mixing = lax.psum(
        (grad_shift, grad_heads, grad_head_bias, grad_mixing), everyone
    )
    grad_norms = jnp.stack([gain1_grad, shift1_grad, gain2_grad, shift2_grad])
    grad_encoder, grad_out0, grad_out1, grad_genes = lax.psum(
        (grad_encoder, grad_out0[:genes], grad_out1[:genes], grad_genes), "cell"
    )
    grad_output = jnp.transpose(jnp.stack([grad_out0, grad_out1], axis=1), (1, 2, 0))
    weights_in = (
        encoder_weight,
        output_weight,
        gene_vectors,
        batch_shift,
        layer_norm_params,
        head_weight,
        head_bias,
        decoder_input,
    )
    momenta = (
        encoder_weight_momentum,
        output_weight_momentum,
        gene_vectors_momentum,
        batch_shift_momentum,
        norm_params_momentum,
        head_weight_momentum,
        head_bias_momentum,
        decoder_input_momentum,
    )
    averages = (
        encoder_weight_average,
        output_weight_average,
        gene_vectors_average,
        batch_shift_average,
        norm_params_average,
        head_weight_average,
        head_bias_average,
        decoder_input_average,
    )
    grads = (
        grad_encoder,
        grad_output,
        grad_genes,
        grad_shift,
        grad_norms,
        grad_heads,
        grad_head_bias,
        grad_mixing,
    )
    fresh, moments, means = zip(
        *[nesterov(*group) for group in zip(weights_in, momenta, averages, grads, step_rates)]
    )
    return (cell_loss, input_grad.T, *fresh, *moments, *means)


def solution(mesh):
    cells, genes = P("cell"), P("gene", None)
    weight_specs = (genes, P(None, None, "gene"), P(None, "gene"), P(), P(), P(), P(), P())
    return jax.shard_map(
        local,
        mesh=mesh,
        in_specs=(P("cell", "gene"), cells, cells, P("cell", None)) + weight_specs * 3,
        out_specs=(cells, P("cell", "gene")) + weight_specs * 3,
        check_vma=False,
    )
```

```python
import functools

import jax
import jax.numpy as jnp
from jax import lax
from jax.experimental import pallas as pl
from jax.experimental.pallas import tpu as pltpu
from jax.sharding import PartitionSpec as P

momentum_decay = 0.9
average_decay = 0.99
norm_epsilon = 0.001
rate_epsilon = 1e-08
step_rates = (110.0, 46000.0, 300000.0, 70000.0, 13000.0, 3700.0, 7600.0, 8000.0)
ln2 = 0.6931471805599453
f32 = jnp.float32
bf16 = jnp.bfloat16
LANES = 128
ROWS = 16
HOT_DEPTH = 144
PARAMS = pltpu.CompilerParams(vmem_limit_bytes=60 << 20)
IN_VMEM = pl.BlockSpec(memory_space=pltpu.VMEM)
MESH = pl.DeviceIdType.MESH


def talking(number):
    return pltpu.CompilerParams(
        collective_id=number, has_side_effects=True, vmem_limit_bytes=60 << 20
    )


def nesterov(weight, momentum, average, grad, rate):
    moment = momentum_decay * momentum + grad
    fresh = weight - rate * (grad + momentum_decay * moment)
    return (fresh, moment, average_decay * average + (1.0 - average_decay) * fresh)


def three_parts(value):
    high = lax.reduce_precision(value, 8, 7)
    rest = value - high
    middle = lax.reduce_precision(rest, 8, 7)
    return high, middle, lax.reduce_precision(rest - middle, 8, 7)


def whole(array):
    return pl.BlockSpec(array.shape, lambda i: (0,) * array.ndim)


def column_blocks(rows, chunk):
    return pl.BlockSpec((rows, chunk), lambda i: (0, i))


def split_rows(genes):
    full = genes // ROWS
    groups = max(d for d in range(1, 14) if full % d == 0)
    return full, groups, genes - full * ROWS


def padded(genes):
    return -(-genes // ROWS) * ROWS


def pick_chunk(cells, most):
    chunk = LANES
    while chunk * 2 <= most and cells % (chunk * 2) == 0:
        chunk *= 2
    return chunk


def tail_rows(ref, start, stop, columns, dtype):
    piece = ref[start:stop, columns]
    filler = jnp.zeros((ROWS - (stop - start), piece.shape[1]), dtype)
    return jnp.concatenate([piece, filler], axis=0)


def encode_kernel(counts_ref, weight_ref, out_ref, inputs_ref, *, genes, chunk):
    full, groups, tail = split_rows(genes)

    def group(counted, rows, total):
        inputs_ref[rows, :] = jnp.log(counted + 1.0).astype(bf16)
        return total + counted[:8] + counted[8:]

    def step(i, total):
        rows = pl.ds(pl.multiple_of(i * ROWS, ROWS), ROWS)
        return group(counts_ref[rows, :].astype(f32), rows, total)

    total = lax.fori_loop(0, full, step, jnp.zeros((8, chunk), f32), unroll=4)
    if tail:
        rows = pl.ds(full * ROWS, ROWS)
        counted = tail_rows(counts_ref, full * ROWS, genes, slice(None), jnp.int32).astype(f32)
        total = group(counted, rows, total)
    width = weight_ref.shape[0]
    out_ref[0:width, :] = jnp.dot(weight_ref[...], inputs_ref[...], preferred_element_type=f32)
    row = lax.broadcasted_iota(jnp.int32, (8, chunk), 0)
    library = jnp.sum(total, axis=0, keepdims=True)
    out_ref[width : width + 8, :] = jnp.where(row == 0, library, 0.0)


def encode(counts_t, weight_t):
    genes, cells = counts_t.shape
    chunk = pick_chunk(cells, 512)
    width = weight_t.shape[0]
    return pl.pallas_call(
        functools.partial(encode_kernel, genes=genes, chunk=chunk),
        grid=(cells // chunk,),
        in_specs=[column_blocks(genes, chunk), whole(weight_t)],
        out_specs=column_blocks(width + 8, chunk),
        out_shape=jax.ShapeDtypeStruct((width + 8, cells), f32),
        scratch_shapes=[pltpu.VMEM((padded(genes), chunk), bf16)],
        compiler_params=PARAMS,
        name="encode",
    )(counts_t, weight_t)


class Team:
    def __init__(self, gene_only):
        self.genes, self.cells = lax.axis_size("gene"), lax.axis_size("cell")
        self.gene, self.cell = lax.axis_index("gene"), lax.axis_index("cell")
        self.gene_only = gene_only
        self.size = self.genes if gene_only else self.genes * self.cells
        self.me = self.gene if gene_only else self.gene * self.cells + self.cell

    def others(self, act):
        def one(step, carry):
            other = lax.rem(self.me + step, self.size)
            if self.gene_only:
                act(other, (other, self.cell))
            else:
                act(other, (other // self.cells, lax.rem(other, self.cells)))
            return carry

        lax.fori_loop(1, self.size, one, 0)

    def greet(self):
        barrier = pltpu.get_barrier_semaphore()

        def act(other, place):
            pl.semaphore_signal(barrier, inc=1, device_id=place, device_id_type=MESH)

        self.others(act)
        pl.semaphore_wait(barrier, self.size - 1)

    def send(self, source, target, sems):
        def act(other, place):
            pltpu.make_async_remote_copy(
                src_ref=source(other),
                dst_ref=target,
                send_sem=sems.at[0],
                recv_sem=sems.at[1],
                device_id=place,
                device_id_type=MESH,
            ).start()

        self.others(act)


def await_bytes(ref, sem):
    pltpu.make_async_copy(ref, ref, sem).wait()


def fold_lanes(values):
    return sum(values[:, j : j + LANES] for j in range(0, values.shape[1], LANES))


def row_sums(folded):
    return jnp.sum(jnp.transpose(folded), axis=0, keepdims=True)


def box_sum(box):
    def add(i, total):
        return total + box[i]

    return lax.fori_loop(1, box.shape[0], add, box[0])


def eight_rows(rows):
    filler = jnp.zeros((8 - len(rows), LANES), f32)
    return jnp.concatenate([*rows, filler], axis=0) if len(rows) < 8 else jnp.concatenate(rows, 0)


def columns_of(rows):
    turned = jnp.transpose(jnp.concatenate([eight_rows(rows), jnp.zeros((120, LANES), f32)], 0))
    return [turned[:, i : i + 1] for i in range(len(rows))]


def exact(left, right, left_dim, right_dim):
    return lax.dot_general(
        left,
        right,
        (((left_dim,), (right_dim,)), ((), ())),
        precision=lax.Precision.HIGHEST,
        preferred_element_type=f32,
    )


def hot_rows(index, batches):
    rows = lax.broadcasted_iota(jnp.int32, (batches, index.shape[1]), 0)
    return jnp.where(rows == index, 1.0, 0.0)


def sigmoid(value):
    return 1.0 / (1.0 + jnp.exp(-value))


def slope_of(value):
    sigma = sigmoid(value)
    return sigma * (1.0 + value * (1.0 - sigma))


def pack_layout(latent_pad, batches):
    mixing = slice(8, 8 + latent_pad + batches)
    heads = slice(mixing.stop, mixing.stop + 2 * latent_pad)
    return mixing, heads, slice(heads.stop, heads.stop + batches)


def middle_kernel(
    encoded_ref,
    index_ref,
    valid_ref,
    noise_ref,
    pack_ref,
    hidden_ref,
    centered_ref,
    sample_ref,
    share_ref,
    stats_ref,
    first_ref,
    heads_ref,
    rest_ref,
    slab_box,
    box1,
    box2,
    slab_sems,
    sems1,
    sems2,
    sample_sems,
    *,
    batches,
    latent,
    genes_all,
):
    group, everyone = Team(True), Team(False)
    width, slab = first_ref.shape
    cells = hidden_ref.shape[1]
    pad = sample_ref.shape[0]
    mixing_rows, heads_rows, shift_rows = pack_layout(pad, batches)
    mixing = pack_ref[mixing_rows, :]

    def part(other):
        return pl.ds(pl.multiple_of(other * slab, LANES), slab)

    mine = part(group.me)
    everyone.greet()
    group.send(lambda other: encoded_ref.at[:, part(other)], slab_box.at[group.me], slab_sems)
    slab_box[group.me] = encoded_ref[:, mine]
    hot = hot_rows(index_ref[:, mine], batches)
    valid = valid_ref[:, mine].astype(f32)
    shift = exact(pack_ref[shift_rows, :], hot, 0, 0)
    gain1, bias1, gain2, bias2, head_bias = columns_of([pack_ref[i : i + 1, :] for i in range(5)])
    others = slab_box.at[pl.ds(0, group.size - 1)]
    await_bytes(others, slab_sems.at[0])
    await_bytes(others, slab_sems.at[1])
    total = box_sum(slab_box)
    rest_ref[0:1, :] = total[width : width + 1, :]
    pre1 = total[0:width, :] + shift

    def reduced(rows, box, sems):
        box[everyone.me] = eight_rows(rows)
        everyone.send(lambda other: box.at[everyone.me], box.at[everyone.me], sems)
        others = box.at[pl.ds(0, everyone.size - 1)]

        def finish():
            await_bytes(others, sems.at[0])
            await_bytes(others, sems.at[1])
            return box_sum(box)

        return finish

    weighed = valid * pre1
    sums = reduced(
        [
            row_sums(fold_lanes(weighed)),
            row_sums(fold_lanes(weighed * pre1)),
            jnp.broadcast_to(jnp.sum(valid, axis=1, keepdims=True), (1, LANES)),
        ],
        box1,
        sems1,
    )()
    count = jnp.maximum(sums[2:3], 1.0)
    mean1 = sums[0:1] / count
    inverse1 = lax.rsqrt(sums[1:2] / count - mean1 * mean1 + norm_epsilon)
    mean_col, inverse_col = columns_of([mean1, inverse1])
    centered1 = (pre1 - mean_col) * inverse_col
    first_ref[...] = centered1
    normed1 = centered1 * gain1 + bias1
    hidden1 = normed1 * sigmoid(normed1)
    heads = exact(pack_ref[heads_rows, :], hidden1, 1, 0) + head_bias[0 : 2 * pad]
    heads_ref[...] = heads
    mean_z, log_var = heads[0:pad], heads[pad : 2 * pad]
    noise = jnp.concatenate([noise_ref[:, mine], jnp.zeros((pad - latent, slab), f32)], axis=0)
    sample = mean_z + jnp.exp(0.5 * log_var) * noise
    rest_ref[1:2, :] = 0.5 * jnp.sum(
        mean_z * mean_z + jnp.exp(log_var) - log_var - 1.0, axis=0, keepdims=True
    )
    sample_ref[:, mine] = sample
    group.send(lambda other: sample_ref.at[:, mine], sample_ref.at[:, mine], sample_sems)
    pre2 = exact(mixing, jnp.concatenate([sample, hot], axis=0), 0, 0)
    weighed = valid * pre2
    finish = reduced(
        [row_sums(fold_lanes(weighed)), row_sums(fold_lanes(weighed * pre2))], box2, sems2
    )
    scale = 1.0 / (count * genes_all)
    share_ref[...] = valid_ref[...].astype(f32) * scale[:, 0:1]
    sums = finish()
    mean2 = sums[0:1] / count
    inverse2 = lax.rsqrt(sums[1:2] / count - mean2 * mean2 + norm_epsilon)
    stats_ref[...] = eight_rows([inverse1, inverse2, count, scale])
    mean_col, inverse_col = columns_of([mean2, inverse2])
    others = sample_ref.at[:, pl.ds(0, (group.size - 1) * slab)]
    await_bytes(others, sample_sems.at[0])
    await_bytes(others, sample_sems.at[1])
    piece = pick_chunk(cells, 512)

    def decode(i, carry):
        columns = pl.ds(pl.multiple_of(i * piece, LANES), piece)
        mixed = jnp.concatenate(
            [sample_ref[:, columns], hot_rows(index_ref[:, columns], batches)], axis=0
        )
        centered = (exact(mixing, mixed, 0, 0) - mean_col) * inverse_col
        centered_ref[:, columns] = centered
        normed = centered * gain2 + bias2
        hidden_ref[:, columns] = (normed * sigmoid(normed)).astype(bf16)
        return carry

    lax.fori_loop(0, cells // piece, decode, 0)


def middle(encoded, index, valid, noise, pack, batches, pad, genes_all):
    cells = index.shape[1]
    width = LANES
    genes_axis = lax.axis_size("gene")
    devices = genes_axis * lax.axis_size("cell")
    slab = cells // genes_axis
    return pl.pallas_call(
        functools.partial(
            middle_kernel, batches=batches, latent=noise.shape[0], genes_all=genes_all
        ),
        out_shape=[
            jax.ShapeDtypeStruct((width, cells), bf16),
            jax.ShapeDtypeStruct((width, cells), f32),
            jax.ShapeDtypeStruct((pad, cells), f32),
            jax.ShapeDtypeStruct((1, cells), f32),
            jax.ShapeDtypeStruct((8, LANES), f32),
            jax.ShapeDtypeStruct((width, slab), f32),
            jax.ShapeDtypeStruct((2 * pad, slab), f32),
            jax.ShapeDtypeStruct((2, slab), f32),
        ],
        in_specs=[IN_VMEM] * 5,
        out_specs=[IN_VMEM] * 8,
        scratch_shapes=[
            pltpu.VMEM((genes_axis, width + 8, slab), f32),
            pltpu.VMEM((devices, 8, LANES), f32),
            pltpu.VMEM((devices, 8, LANES), f32),
        ]
        + [pltpu.SemaphoreType.DMA((2,))] * 4,
        compiler_params=talking(1),
        name="middle",
    )(encoded, index, valid, noise, pack)


def tops_kernel(tops_ref, rest_ref, out_ref, box, sems, back_sems):
    group = Team(True)
    slab = rest_ref.shape[1]

    def part(other):
        return pl.ds(pl.multiple_of(other * slab, LANES), slab)

    mine = part(group.me)
    group.greet()
    group.send(lambda other: tops_ref.at[:, part(other)], box.at[group.me], sems)
    box[group.me] = tops_ref[:, mine]
    others = box.at[pl.ds(0, group.size - 1)]
    await_bytes(others, sems.at[0])
    await_bytes(others, sems.at[1])

    def highest(i, best):
        return jnp.maximum(best, box[i, 0:1, :])

    top = lax.fori_loop(1, group.size, highest, box[0, 0:1, :])

    def add(i, total):
        return total + box[i, 1:2, :] * jnp.exp(box[i, 0:1, :] - top)

    total = lax.fori_loop(0, group.size, add, jnp.zeros_like(top))
    inverse = 1.0 / total
    out_ref[0:1, mine] = top
    out_ref[1:2, mine] = rest_ref[0:1, :] * inverse
    out_ref[2:3, mine] = inverse
    out_ref[3:4, mine] = inverse
    group.send(lambda other: out_ref.at[:, mine], out_ref.at[:, mine], back_sems)
    others = out_ref.at[:, pl.ds(0, (group.size - 1) * slab)]
    await_bytes(others, back_sems.at[0])
    await_bytes(others, back_sems.at[1])


def combine_tops(tops, rest):
    group = lax.axis_size("gene")
    slab = rest.shape[1]
    return pl.pallas_call(
        tops_kernel,
        out_shape=jax.ShapeDtypeStruct((4, tops.shape[1]), f32),
        in_specs=[IN_VMEM] * 2,
        out_specs=IN_VMEM,
        scratch_shapes=[pltpu.VMEM((group, 2, slab), f32)] + [pltpu.SemaphoreType.DMA((2,))] * 2,
        compiler_params=talking(2),
        name="combine_tops",
    )(tops, rest)


def sums_kernel(sums_ref, rows_ref, rest_ref, valid_ref, out_ref, box, sems, back_sems, *, genes_all):
    group = Team(True)
    slab = rest_ref.shape[1]

    def part(other):
        return pl.ds(pl.multiple_of(other * slab, LANES), slab)

    mine = part(group.me)
    group.greet()
    group.send(lambda other: sums_ref.at[:, part(other)], box.at[group.me], sems)
    box[group.me] = sums_ref[:, mine]
    others = box.at[pl.ds(0, group.size - 1)]
    await_bytes(others, sems.at[0])
    await_bytes(others, sems.at[1])
    total = box_sum(box)
    out_ref[0:1, mine] = total[0:1] * rows_ref[2:3, mine]
    out_ref[1:2, mine] = (
        valid_ref[:, mine].astype(f32) * (total[1:2] + rest_ref[1:2, :]) / genes_all
    )
    group.send(lambda other: out_ref.at[:, mine], out_ref.at[:, mine], back_sems)
    others = out_ref.at[:, pl.ds(0, (group.size - 1) * slab)]
    await_bytes(others, back_sems.at[0])
    await_bytes(others, back_sems.at[1])


def combine_sums(sums, rows, rest, valid, genes_all):
    group = lax.axis_size("gene")
    slab = rest.shape[1]
    return pl.pallas_call(
        functools.partial(sums_kernel, genes_all=genes_all),
        out_shape=jax.ShapeDtypeStruct((2, sums.shape[1]), f32),
        in_specs=[IN_VMEM] * 4,
        out_specs=IN_VMEM,
        scratch_shapes=[pltpu.VMEM((group, 2, slab), f32)] + [pltpu.SemaphoreType.DMA((2,))] * 2,
        compiler_params=talking(3),
        name="combine_sums",
    )(sums, rows, rest, valid)


def middle_back_kernel(
    grad_ref,
    centered_ref,
    sample_ref,
    index_ref,
    valid_ref,
    noise_ref,
    pack_ref,
    stats_ref,
    first_ref,
    heads_ref,
    grad16_ref,
    small_ref,
    norms_ref,
    part_ref,
    slab_box,
    box1,
    box2,
    slab_sems,
    sems1,
    sems2,
    grad_sems,
    *,
    batches,
    latent,
):
    group, everyone = Team(True), Team(False)
    width, slab = first_ref.shape
    cells = grad_ref.shape[1]
    pad = sample_ref.shape[0]
    mixing_rows, heads_rows, _ = pack_layout(pad, batches)
    depth = pad + batches

    def part(other):
        return pl.ds(pl.multiple_of(other * slab, LANES), slab)

    mine = part(group.me)
    inverse1, inverse2 = stats_ref[0:1, :], stats_ref[1:2, :]
    count, scale = stats_ref[2:3, 0:1], stats_ref[3:4, 0:1]
    factor2 = inverse2 * pack_ref[2:3, :]
    gain1, bias1, gain2, bias2, factor1 = columns_of(
        [pack_ref[i : i + 1, :] for i in range(4)] + [inverse1 * pack_ref[0:1, :]]
    )
    latent_rows = pack_ref[8 : 8 + pad, :] * factor2
    piece = pick_chunk(cells, 512)

    def gather(i, carry):
        gains, shifts, products = carry
        columns = pl.ds(pl.multiple_of(i * piece, LANES), piece)
        centered = centered_ref[:, columns]
        grad = grad_ref[:, columns] * slope_of(centered * gain2 + bias2)
        part_ref[:, columns] = exact(latent_rows, grad, 1, 0)
        mixed = jnp.concatenate(
            [sample_ref[:, columns], hot_rows(index_ref[:, columns], batches)], axis=0
        )
        return (
            gains + fold_lanes(grad * centered),
            shifts + fold_lanes(grad),
            products + exact(mixed, grad, 1, 1),
        )

    zeros = jnp.zeros((width, LANES), f32)
    gains, shifts, products = lax.fori_loop(
        0, cells // piece, gather, (zeros, zeros, jnp.zeros((depth, width), f32))
    )
    everyone.greet()

    def reduced(rows, box, sems):
        box[everyone.me] = eight_rows(rows)
        everyone.send(lambda other: box.at[everyone.me], box.at[everyone.me], sems)
        others = box.at[pl.ds(0, everyone.size - 1)]

        def finish():
            await_bytes(others, sems.at[0])
            await_bytes(others, sems.at[1])
            return box_sum(box)

        return finish

    finish = reduced([row_sums(gains), row_sums(shifts)], box1, sems1)
    group.send(lambda other: part_ref.at[:, part(other)], slab_box.at[group.me], slab_sems)
    slab_box[group.me] = part_ref[:, mine]
    hot = hot_rows(index_ref[:, mine], batches)
    valid = valid_ref[:, mine].astype(f32)
    mixed = valid * jnp.concatenate([sample_ref[:, mine], hot], axis=0)
    centered2 = centered_ref[:, mine]
    share = valid / count
    mixed_sum = jnp.sum(mixed, axis=1, keepdims=True)
    mixed_product = exact(mixed, centered2, 1, 1)
    noise = jnp.concatenate([noise_ref[:, mine], jnp.zeros((pad - latent, slab), f32)], axis=0)
    mean_z, log_var = heads_ref[0:pad, :], heads_ref[pad : 2 * pad, :]
    log_factor = 0.5 * noise * jnp.exp(0.5 * log_var)
    scaled = valid * scale
    grad_log_own = scaled * (jnp.exp(log_var) - 1.0) * 0.5
    centered1 = first_ref[...]
    normed1 = centered1 * gain1 + bias1
    sigma1 = sigmoid(normed1)
    hidden1 = normed1 * sigma1
    slope1 = sigma1 * (1.0 + normed1 * (1.0 - sigma1))

    sums = finish()
    gain2_grad, shift2_grad = sums[0:1], sums[1:2]
    small_ref[0:depth, :] = factor2 * (
        products - (mixed_sum * shift2_grad + mixed_product * gain2_grad) / count
    )
    gain_col, shift_col = columns_of([gain2_grad, shift2_grad])
    pulled = exact(latent_rows, shift_col + centered2 * gain_col, 1, 0)
    others = slab_box.at[pl.ds(0, group.size - 1)]
    await_bytes(others, slab_sems.at[0])
    await_bytes(others, slab_sems.at[1])
    grad_sample = box_sum(slab_box) - share * pulled
    grad_heads = jnp.concatenate(
        [grad_sample + scaled * mean_z, grad_sample * log_factor + grad_log_own], axis=0
    )
    grad_normed1 = exact(pack_ref[heads_rows, :], grad_heads, 0, 0) * slope1
    finish = reduced(
        [row_sums(fold_lanes(grad_normed1 * centered1)), row_sums(fold_lanes(grad_normed1))],
        box2,
        sems2,
    )
    small_ref[depth : depth + 2 * pad, :] = exact(grad_heads, hidden1, 1, 1)
    small_ref[depth + 2 * pad : depth + 4 * pad, :] = fold_lanes(grad_heads)
    sums = finish()
    gain1_grad, shift1_grad = sums[0:1], sums[1:2]
    norms_ref[...] = eight_rows([gain1_grad, shift1_grad, gain2_grad, shift2_grad])
    gain_col, shift_col = columns_of([gain1_grad, shift1_grad])
    grad_pre1 = factor1 * (grad_normed1 - share * (shift_col + centered1 * gain_col))
    grad16_ref[:, mine] = grad_pre1.astype(bf16)
    group.send(lambda other: grad16_ref.at[:, mine], grad16_ref.at[:, mine], grad_sems)
    small_ref[depth + 4 * pad :, :] = exact(hot, grad_pre1, 1, 1)
    others = grad16_ref.at[:, pl.ds(0, (group.size - 1) * slab)]
    await_bytes(others, grad_sems.at[0])
    await_bytes(others, grad_sems.at[1])


def middle_back(grad, centered, sample, index, valid, noise, pack, stats, first, heads, batches):
    cells = index.shape[1]
    width, slab = first.shape
    pad = sample.shape[0]
    genes_axis = lax.axis_size("gene")
    devices = genes_axis * lax.axis_size("cell")
    return pl.pallas_call(
        functools.partial(middle_back_kernel, batches=batches, latent=noise.shape[0]),
        out_shape=[
            jax.ShapeDtypeStruct((width, cells), bf16),
            jax.ShapeDtypeStruct((5 * pad + 2 * batches, LANES), f32),
            jax.ShapeDtypeStruct((8, LANES), f32),
        ],
        in_specs=[IN_VMEM] * 10,
        out_specs=[IN_VMEM] * 3,
        scratch_shapes=[
            pltpu.VMEM((pad, cells), f32),
            pltpu.VMEM((genes_axis, pad, slab), f32),
            pltpu.VMEM((devices, 8, LANES), f32),
            pltpu.VMEM((devices, 8, LANES), f32),
        ]
        + [pltpu.SemaphoreType.DMA((2,))] * 4,
        compiler_params=talking(4),
        name="middle_back",
    )(grad, centered, sample, index, valid, noise, pack, stats, first, heads)


def fill_hidden(long_ref, hidden_ref, top):
    width, chunk = hidden_ref.shape
    long_ref[0:width, :] = hidden_ref[...]
    index = lax.broadcasted_iota(jnp.int32, (HOT_DEPTH - width, chunk), 0)
    extra = jnp.where(index < 3, 1.0, 0.0)
    if top is not None:
        high = (-top).astype(bf16).astype(f32)
        middle = (-top - high).astype(bf16).astype(f32)
        low = (-top - high - middle).astype(bf16).astype(f32)
        extra = jnp.where(index == 3, high, extra)
        extra = jnp.where(index == 4, middle, extra)
        extra = jnp.where(index == 5, low, extra)
    long_ref[width:HOT_DEPTH, :] = extra.astype(bf16)


def totals_kernel(hidden_ref, weight_ref, out_ref, long_ref, value_ref, *, chunk):
    size = weight_ref.shape[0]
    fill_hidden(long_ref, hidden_ref, None)
    value_ref[...] = jnp.dot(weight_ref[...], long_ref[...], preferred_element_type=f32)
    count = size // ROWS

    def highest(i, best):
        part = value_ref[pl.ds(pl.multiple_of(i * ROWS, ROWS), ROWS), :]
        return jnp.maximum(best, jnp.maximum(part[:8], part[8:]))

    best = lax.fori_loop(0, count, highest, jnp.full((8, chunk), -jnp.inf, f32), unroll=4)
    top = jnp.max(best, axis=0, keepdims=True)

    def add(i, total):
        part = jnp.exp(value_ref[pl.ds(pl.multiple_of(i * ROWS, ROWS), ROWS), :] - top)
        return total + part[:8] + part[8:]

    total = lax.fori_loop(0, count, add, jnp.zeros((8, chunk), f32), unroll=4)
    out_ref[0:1, :] = top
    out_ref[1:2, :] = jnp.sum(total, axis=0, keepdims=True)


def totals(hidden, weight):
    width, cells = hidden.shape
    chunk = pick_chunk(cells, 512)
    return pl.pallas_call(
        functools.partial(totals_kernel, chunk=chunk),
        grid=(cells // chunk,),
        in_specs=[column_blocks(width, chunk), whole(weight)],
        out_specs=column_blocks(2, chunk),
        out_shape=jax.ShapeDtypeStruct((2, cells), f32),
        scratch_shapes=[
            pltpu.VMEM((HOT_DEPTH, chunk), bf16),
            pltpu.VMEM((weight.shape[0], chunk), f32),
        ],
        compiler_params=PARAMS,
        name="totals",
    )(hidden, weight)


def likelihood_kernel(
    counts_ref,
    hidden_ref,
    rows_ref,
    share_ref,
    weight_ref,
    back_ref,
    theta_ref,
    log_ref,
    slope_ref,
    table_ref,
    slopes_ref,
    sums_ref,
    grad_hidden_ref,
    grad_weight_ref,
    grad_bias_ref,
    grad_theta_ref,
    long_ref,
    value_ref,
    second_ref,
    *,
    genes,
    chunk,
):
    full, groups, tail = split_rows(genes)
    block = ROWS * groups
    width = hidden_ref.shape[0]

    @pl.when(pl.program_id(0) == 0)
    def _():
        for ref in (grad_weight_ref, grad_bias_ref, grad_theta_ref):
            ref[...] = jnp.zeros_like(ref)

    fill_hidden(long_ref, hidden_ref, rows_ref[0:1, :])
    tiles = [slice(j, j + LANES) for j in range(0, chunk, LANES)]
    ratio_all = rows_ref[1:2, :]
    share_all = share_ref[...]

    def group(held, rows, read, carry):
        losses, sums = [], []
        theta = theta_ref[rows, :]
        log_theta = log_ref[rows, :]
        log_slope = slope_ref[rows, :]
        table = table_ref[rows, :]
        grad_bias = grad_bias_ref[rows, :]
        grad_theta = grad_theta_ref[rows, :]
        for j, columns in enumerate(tiles):
            count = read(columns)
            counted = count.astype(f32)
            first = value_ref[0, held, columns]
            dropout = value_ref[1, held, columns]
            ratio, share = ratio_all[:, columns], share_all[:, columns]
            rate = jnp.exp(first) * ratio
            near = rate + rate_epsilon
            both = theta + near
            inverse = pl.reciprocal(near * both)
            inverse_both = inverse * near
            inverse_near = inverse * both
            log_fraction = jnp.log2(near * inverse_both)
            log_both = jnp.log2(both)
            pi_theta = (theta * ln2) * (log_theta - log_both) - dropout
            small_pi = jnp.exp(-jnp.abs(dropout))
            small_theta = jnp.exp(-jnp.abs(pi_theta))
            one_pi = 1.0 + small_pi
            one_theta = 1.0 + small_theta
            inverse_ones = pl.reciprocal(one_pi * one_theta)
            sigma_pi = jnp.where(dropout >= 0.0, small_pi, 1.0) * (inverse_ones * one_theta)
            inverse_theta = inverse_ones * one_pi
            zero = count < 1
            sigma_theta = jnp.where(pi_theta >= 0.0, 1.0, small_theta) * inverse_theta
            sigma = jnp.where(zero, sigma_theta, 1.0)
            log_ones = jnp.log2(one_pi * jnp.where(zero, inverse_theta, 1.0))
            upper = jnp.where(zero, jnp.maximum(pi_theta, 0.0), pi_theta)
            gammas = jnp.take_along_axis(table, count, axis=1)
            digammas = jnp.take_along_axis(table, count + LANES // 2, axis=1)
            loss = (jnp.maximum(-dropout, 0.0) - upper) + (
                ln2 * (log_ones - counted * log_fraction) - gammas
            )
            pull = (sigma * theta + counted) * inverse_both
            slope = rate * (pull - counted * inverse_near)
            slopes_ref[rows, columns] = slope
            grad_dropout = (sigma - sigma_pi) * share
            second_ref[rows, columns] = grad_dropout.astype(bf16)
            grad_bias = grad_bias + grad_dropout
            grad_theta = grad_theta + share * (
                pull - ln2 * (sigma * (log_slope - log_both)) - digammas
            )
            losses.append(carry[0][j] + loss[:8] + loss[8:])
            sums.append(carry[1][j] + slope[:8] + slope[8:])
        grad_bias_ref[rows, :] = grad_bias
        grad_theta_ref[rows, :] = grad_theta
        return tuple(losses), tuple(sums)

    def logits(rows, size):
        for k in range(2):
            value_ref[k, 0:size, :] = jnp.dot(
                weight_ref[k, rows, :], long_ref[...], preferred_element_type=f32
            )

    def step(b, carry):
        start = pl.multiple_of(b * block, ROWS)
        logits(pl.ds(start, block), block)

        def inner(i, carry):
            held = pl.multiple_of(i * ROWS, ROWS)
            rows = pl.ds(pl.multiple_of(start + held, ROWS), ROWS)
            return group(pl.ds(held, ROWS), rows, lambda cols: counts_ref[rows, cols], carry)

        return lax.fori_loop(0, groups, inner, carry, unroll=4)

    zeros = tuple(jnp.zeros((8, LANES), f32) for _ in tiles)
    carry = lax.fori_loop(0, full // groups, step, (zeros, zeros))
    if tail:
        rows = pl.ds(full * ROWS, ROWS)
        logits(rows, ROWS)
        carry = group(
            pl.ds(0, ROWS),
            rows,
            lambda cols: tail_rows(counts_ref, full * ROWS, genes, cols, jnp.int32),
            carry,
        )
    for j, columns in enumerate(tiles):
        sums_ref[0:1, columns] = jnp.sum(carry[1][j], axis=0, keepdims=True)
        sums_ref[1:2, columns] = jnp.sum(carry[0][j], axis=0, keepdims=True)
    grad_weight_ref[...] += lax.dot_general(
        second_ref[...], hidden_ref[...], (((1,), (1,)), ((), ())), preferred_element_type=f32
    )
    grad_hidden_ref[...] = jnp.dot(back_ref[...], second_ref[...], preferred_element_type=f32)


def likelihood(counts_t, hidden, rows, share, weights, back, gene_tables):
    genes, cells = counts_t.shape
    size = weights.shape[1]
    width = hidden.shape[0]
    chunk = pick_chunk(cells, 512)
    groups = split_rows(genes)[1]
    row = column_blocks(1, chunk)
    per_gene = pl.BlockSpec((size, LANES), lambda i: (0, 0))
    return pl.pallas_call(
        functools.partial(likelihood_kernel, genes=genes, chunk=chunk),
        grid=(cells // chunk,),
        in_specs=[column_blocks(genes, chunk), column_blocks(width, chunk)]
        + [column_blocks(rows.shape[0], chunk), row, whole(weights), whole(back)]
        + [whole(a) for a in gene_tables],
        out_specs=[
            column_blocks(size, chunk),
            column_blocks(2, chunk),
            column_blocks(width, chunk),
        ]
        + [per_gene] * 3,
        out_shape=[
            jax.ShapeDtypeStruct((size, cells), f32),
            jax.ShapeDtypeStruct((2, cells), f32),
            jax.ShapeDtypeStruct((width, cells), f32),
        ]
        + [jax.ShapeDtypeStruct((size, LANES), f32)] * 3,
        scratch_shapes=[
            pltpu.VMEM((HOT_DEPTH, chunk), bf16),
            pltpu.VMEM((2, ROWS * groups, chunk), f32),
            pltpu.VMEM((size, chunk), bf16),
        ],
        compiler_params=PARAMS,
        name="likelihood",
    )(counts_t, hidden, rows, share, weights, back, *gene_tables)


def frequency_kernel(
    slopes_ref,
    hidden_ref,
    rows_ref,
    pull_ref,
    share_ref,
    other_ref,
    weight_ref,
    back_ref,
    grad_hidden_ref,
    grad_weight_ref,
    grad_bias_ref,
    long_ref,
    value_ref,
    first_ref,
    *,
    chunk,
):
    size = weight_ref.shape[0]

    @pl.when(pl.program_id(0) == 0)
    def _():
        for ref in (grad_weight_ref, grad_bias_ref):
            ref[...] = jnp.zeros_like(ref)

    fill_hidden(long_ref, hidden_ref, rows_ref[0:1, :])
    value_ref[...] = jnp.dot(weight_ref[...], long_ref[...], preferred_element_type=f32)
    tiles = [slice(j, j + LANES) for j in range(0, chunk, LANES)]
    pull_all = pull_ref[0:1, :]
    share_all = share_ref[...]

    def step(i, carry):
        rows = pl.ds(pl.multiple_of(i * ROWS, ROWS), ROWS)
        bias = grad_bias_ref[rows, :]
        for columns in tiles:
            grad = share_all[:, columns] * (
                slopes_ref[rows, columns] - jnp.exp(value_ref[rows, columns]) * pull_all[:, columns]
            )
            first_ref[rows, columns] = grad.astype(bf16)
            bias = bias + grad
        grad_bias_ref[rows, :] = bias
        return carry

    lax.fori_loop(0, size // ROWS, step, 0, unroll=2)
    grad_weight_ref[...] += lax.dot_general(
        first_ref[...], hidden_ref[...], (((1,), (1,)), ((), ())), preferred_element_type=f32
    )
    grad_hidden_ref[...] = other_ref[...] + jnp.dot(
        back_ref[...], first_ref[...], preferred_element_type=f32
    )


def frequency(slopes, hidden, rows, pull, share, other, weight, back):
    size, cells = slopes.shape
    width = hidden.shape[0]
    chunk = pick_chunk(cells, 512)
    row = column_blocks(1, chunk)
    wide = column_blocks(width, chunk)
    per_gene = pl.BlockSpec((size, LANES), lambda i: (0, 0))
    return pl.pallas_call(
        functools.partial(frequency_kernel, chunk=chunk),
        grid=(cells // chunk,),
        in_specs=[column_blocks(size, chunk), wide, column_blocks(rows.shape[0], chunk)]
        + [column_blocks(2, chunk), row, wide, whole(weight), whole(back)],
        out_specs=[wide, per_gene, per_gene],
        out_shape=[jax.ShapeDtypeStruct((width, cells), f32)]
        + [jax.ShapeDtypeStruct((size, LANES), f32)] * 2,
        scratch_shapes=[
            pltpu.VMEM((HOT_DEPTH, chunk), bf16),
            pltpu.VMEM((size, chunk), f32),
            pltpu.VMEM((size, chunk), bf16),
        ],
        compiler_params=PARAMS,
        name="frequency",
    )(slopes, hidden, rows, pull, share, other, weight, back)


def encoder_back_kernel(counts_ref, grad_ref, weight_ref, input_ref, weight_grad_ref):
    inputs = jnp.log(counts_ref[...].astype(f32) + 1.0).astype(bf16)
    weight_grad_ref[...] = lax.dot_general(
        inputs, grad_ref[...], (((1,), (1,)), ((), ())), preferred_element_type=f32
    )
    input_ref[...] = jnp.dot(weight_ref[...], grad_ref[...], preferred_element_type=f32)


def encoder_back(counts_t, grad, weight16):
    genes, cells = counts_t.shape
    width = grad.shape[0]
    block = LANES
    return pl.pallas_call(
        encoder_back_kernel,
        grid=(pl.cdiv(genes, block),),
        in_specs=[
            pl.BlockSpec((block, cells), lambda i: (i, 0)),
            whole(grad),
            pl.BlockSpec((block, width), lambda i: (i, 0)),
        ],
        out_specs=[
            pl.BlockSpec((block, cells), lambda i: (i, 0)),
            pl.BlockSpec((block, width), lambda i: (i, 0)),
        ],
        out_shape=[
            jax.ShapeDtypeStruct((genes, cells), f32),
            jax.ShapeDtypeStruct((genes, width), f32),
        ],
        compiler_params=PARAMS,
        name="encoder_back",
    )(counts_t, grad, weight16)


def local(
    counts,
    batch_index,
    valid_mask,
    noise_draw,
    encoder_weight,
    output_weight,
    gene_vectors,
    batch_shift,
    layer_norm_params,
    head_weight,
    head_bias,
    decoder_input,
    encoder_weight_momentum,
    output_weight_momentum,
    gene_vectors_momentum,
    batch_shift_momentum,
    norm_params_momentum,
    head_weight_momentum,
    head_bias_momentum,
    decoder_input_momentum,
    encoder_weight_average,
    output_weight_average,
    gene_vectors_average,
    batch_shift_average,
    norm_params_average,
    head_weight_average,
    head_bias_average,
    decoder_input_average,
):
    cells, genes = counts.shape
    gene_devices = lax.axis_size("gene")
    genes_all = genes * gene_devices
    latent = head_bias.shape[0] // 2
    batches = batch_shift.shape[0]
    size = padded(genes)
    gap = size - genes
    counts_t = counts.T
    weight16 = encoder_weight.astype(bf16)
    encoder_t = jnp.pad(weight16, ((0, gap), (0, 0))).T

    theta = jnp.pad(jnp.exp(gene_vectors[2]), (0, gap), constant_values=1.0)
    log_theta = jnp.log2(theta + rate_epsilon)

    def spread(column):
        return jnp.broadcast_to(column[:, None], (size, LANES))

    steps = jnp.arange(LANES // 2, dtype=f32)[None, :]
    column = theta[:, None]
    table = jnp.concatenate(
        [
            lax.lgamma(steps + column) - lax.lgamma(column) - lax.lgamma(steps + 1.0),
            lax.digamma(steps + column) - lax.digamma(column),
        ],
        axis=1,
    )
    gene_tables = (
        spread(theta),
        spread(log_theta),
        spread(log_theta + theta / (theta + rate_epsilon) / ln2),
        table,
    )
    genes_first = jnp.transpose(output_weight, (2, 0, 1))
    out16 = jnp.pad(genes_first.astype(bf16), ((0, gap), (0, 0), (0, 0)))
    bias = jnp.pad(gene_vectors[:2].T, ((0, gap), (0, 0)))
    off = (jnp.arange(size) >= genes)[:, None] & (jnp.arange(2) == 0)[None, :]
    bias = jnp.where(off, -1e30, bias)
    parts = jnp.stack(three_parts(bias), axis=2).astype(bf16)
    ones = jnp.broadcast_to((jnp.arange(2) == 0).astype(bf16)[None, :, None], (size, 2, 3))
    rest = jnp.zeros((size, 2, HOT_DEPTH - LANES - 6), bf16)
    weights = jnp.transpose(jnp.concatenate([out16, parts, ones, rest], axis=2), (1, 0, 2))
    backs = jnp.transpose(out16, (1, 2, 0))

    pad = 16
    heads_t = jnp.pad(head_weight.T.reshape(2, latent, -1), ((0, 0), (0, pad - latent), (0, 0)))
    bias_row = jnp.pad(head_bias.reshape(2, latent), ((0, 0), (0, pad - latent))).reshape(1, -1)
    bias_row = jnp.pad(bias_row, ((0, 0), (0, LANES - 2 * pad)))
    pack = jnp.concatenate(
        [
            layer_norm_params,
            bias_row,
            jnp.zeros((3, LANES), f32),
            decoder_input[:latent],
            jnp.zeros((pad - latent, LANES), f32),
            decoder_input[latent:],
            heads_t.reshape(2 * pad, -1),
            batch_shift,
        ],
        axis=0,
    )
    index, valid, noise = batch_index[None, :], valid_mask[None, :], noise_draw.T

    encoded = encode(counts_t, encoder_t)
    hidden2, centered2, sample, share, stats, centered1, heads, rest_rows = middle(
        encoded, index, valid, noise, pack, batches, pad, genes_all
    )
    rows = combine_tops(totals(hidden2, weights[0]), rest_rows)
    slopes, sums, grad_hidden2, grad_out1, grad_bias1, grad_theta = likelihood(
        counts_t, hidden2, rows, share, weights, backs[1], gene_tables
    )
    pull = combine_sums(sums, rows, rest_rows, valid, genes_all)
    cell_loss = pull[1]

    grad_hidden2, grad_out0, grad_bias0 = frequency(
        slopes, hidden2, rows, pull, share, grad_hidden2, weights[0], backs[0]
    )
    grad_genes = jnp.stack(
        [
            jnp.sum(grad_bias0, axis=1),
            jnp.sum(grad_bias1, axis=1),
            jnp.sum(grad_theta, axis=1) * theta,
        ]
    )[:, :genes]
    grad_pre16, small, norm_rows = middle_back(
        grad_hidden2, centered2, sample, index, valid, noise, pack, stats, centered1, heads, batches
    )
    input_grad, grad_encoder = encoder_back(counts_t, grad_pre16, weight16)
    small = lax.psum(small, ("gene", "cell"))
    depth = pad + batches
    grad_mixing = jnp.concatenate([small[:latent], small[pad:depth]], axis=0)
    grad_heads = small[depth : depth + 2 * pad].reshape(2, pad, -1)[:, :latent]
    grad_heads = grad_heads.reshape(2 * latent, -1).T
    grad_head_bias = jnp.sum(small[depth + 2 * pad : depth + 4 * pad], axis=1)
    grad_head_bias = grad_head_bias.reshape(2, pad)[:, :latent].reshape(-1)
    grad_shift = small[depth + 4 * pad :]
    grad_norms = norm_rows[:4]
    grad_encoder, grad_out0, grad_out1, grad_genes = lax.psum(
        (grad_encoder, grad_out0[:genes], grad_out1[:genes], grad_genes), "cell"
    )
    grad_output = jnp.transpose(jnp.stack([grad_out0, grad_out1], axis=1), (1, 2, 0))
    weights_in = (
        encoder_weight,
        output_weight,
        gene_vectors,
        batch_shift,
        layer_norm_params,
        head_weight,
        head_bias,
        decoder_input,
    )
    momenta = (
        encoder_weight_momentum,
        output_weight_momentum,
        gene_vectors_momentum,
        batch_shift_momentum,
        norm_params_momentum,
        head_weight_momentum,
        head_bias_momentum,
        decoder_input_momentum,
    )
    averages = (
        encoder_weight_average,
        output_weight_average,
        gene_vectors_average,
        batch_shift_average,
        norm_params_average,
        head_weight_average,
        head_bias_average,
        decoder_input_average,
    )
    grads = (
        grad_encoder,
        grad_output,
        grad_genes,
        grad_shift,
        grad_norms,
        grad_heads,
        grad_head_bias,
        grad_mixing,
    )
    fresh, moments, means = zip(
        *[nesterov(*group) for group in zip(weights_in, momenta, averages, grads, step_rates)]
    )
    return (cell_loss, input_grad.T, *fresh, *moments, *means)


def solution(mesh):
    cells, genes = P("cell"), P("gene", None)
    weight_specs = (genes, P(None, None, "gene"), P(None, "gene"), P(), P(), P(), P(), P())
    return jax.shard_map(
        local,
        mesh=mesh,
        in_specs=(P("cell", "gene"), cells, cells, P("cell", None)) + weight_specs * 3,
        out_specs=(cells, P("cell", "gene")) + weight_specs * 3,
        check_vma=False,
    )
```

```python
import functools

import jax
import jax.numpy as jnp
from jax import lax
from jax.experimental import pallas as pl
from jax.experimental.pallas import tpu as pltpu
from jax.sharding import PartitionSpec as P

momentum_decay = 0.9
average_decay = 0.99
norm_epsilon = 0.001
rate_epsilon = 1e-08
step_rates = (110.0, 46000.0, 300000.0, 70000.0, 13000.0, 3700.0, 7600.0, 8000.0)
ln2 = 0.6931471805599453
f32 = jnp.float32
bf16 = jnp.bfloat16
LANES = 128
ROWS = 16
WIDE = 2 * LANES
HOT_DEPTH = 2 * LANES
PARAMS = pltpu.CompilerParams(vmem_limit_bytes=60 << 20)
IN_VMEM = pl.BlockSpec(memory_space=pltpu.VMEM)
MESH = pl.DeviceIdType.MESH


def talking(number):
    return pltpu.CompilerParams(
        collective_id=number, has_side_effects=True, vmem_limit_bytes=60 << 20
    )


def nesterov(weight, momentum, average, grad, rate):
    moment = momentum_decay * momentum + grad
    fresh = weight - rate * (grad + momentum_decay * moment)
    return (fresh, moment, average_decay * average + (1.0 - average_decay) * fresh)


def whole(array):
    return pl.BlockSpec(array.shape, lambda i: (0,) * array.ndim)


def column_blocks(rows, chunk):
    return pl.BlockSpec((rows, chunk), lambda i: (0, i))


def split_rows(genes):
    full = genes // ROWS
    groups = max(d for d in range(1, 14) if full % d == 0)
    return full, groups, genes - full * ROWS


def padded(genes):
    return -(-genes // ROWS) * ROWS


def pick_chunk(cells, most):
    chunk = LANES
    while chunk * 2 <= most and cells % (chunk * 2) == 0:
        chunk *= 2
    return chunk


def tail_rows(ref, start, stop, columns, dtype):
    piece = ref[start:stop, columns]
    filler = jnp.zeros((ROWS - (stop - start), piece.shape[1]), dtype)
    return jnp.concatenate([piece, filler], axis=0)


def prepare_kernel(
    output_ref,
    vectors_ref,
    weights_ref,
    theta_ref,
    log_ref,
    slope_ref,
    gammas_ref,
    digammas_ref,
    *,
    genes,
):
    block = theta_ref.shape[0]
    turned = jnp.transpose(
        jnp.concatenate([vectors_ref[...], jnp.zeros((block - 3, block), f32)], axis=0)
    )
    row = pl.program_id(0) * block + lax.broadcasted_iota(jnp.int32, (block, 1), 0)
    inside = row < genes
    lane = lax.broadcasted_iota(jnp.int32, (block, LANES), 1)
    for k in range(2):
        weight = jnp.where(inside, output_ref[pl.ds(k, block, stride=2), :], 0.0)
        weights_ref[k, :, 0:LANES] = weight.astype(bf16)
        bias = jnp.where(inside, turned[:, k : k + 1], 0.0 if k else -1e30)
        high = bias.astype(bf16).astype(f32)
        middle = (bias - high).astype(bf16).astype(f32)
        low = (bias - high - middle).astype(bf16).astype(f32)
        extra = jnp.where(lane == 0, high, jnp.where(lane == 1, middle, 0.0))
        extra = jnp.where(lane == 2, low, extra)
        if k == 0:
            extra = jnp.where((lane >= 3) & (lane < 6), 1.0, extra)
        weights_ref[k, :, LANES : 2 * LANES] = extra.astype(bf16)
    theta = jnp.where(inside, jnp.exp(turned[:, 2:3]), 1.0) + jnp.zeros((block, LANES), f32)
    log_theta = jnp.log2(theta + rate_epsilon)
    theta_ref[...] = theta
    log_ref[...] = log_theta
    slope_ref[...] = ln2 * log_theta + theta / (theta + rate_epsilon)
    step = lane.astype(f32)
    climb = theta + step
    upper = jnp.where(
        lax.broadcasted_iota(jnp.int32, (LANES, LANES), 0)
        < lax.broadcasted_iota(jnp.int32, (LANES, LANES), 1),
        1.0,
        0.0,
    )
    gammas_ref[...] = exact(jnp.log2(climb / (step + 1.0)), upper, 1, 0)
    digammas_ref[...] = exact(1.0 / climb, upper, 1, 0)


def prepare(output_rows, vectors, genes):
    size = padded(genes)
    block = LANES
    table = pl.BlockSpec((block, LANES), lambda i: (i, 0))
    return pl.pallas_call(
        functools.partial(prepare_kernel, genes=genes),
        grid=(pl.cdiv(size, block),),
        in_specs=[
            pl.BlockSpec((2 * block, LANES), lambda i: (i, 0)),
            pl.BlockSpec((3, block), lambda i: (0, i)),
        ],
        out_specs=[pl.BlockSpec((2, block, HOT_DEPTH), lambda i: (0, i, 0))] + [table] * 5,
        out_shape=[jax.ShapeDtypeStruct((2, size, HOT_DEPTH), bf16)]
        + [jax.ShapeDtypeStruct((size, LANES), f32)] * 5,
        compiler_params=PARAMS,
        name="prepare",
    )(output_rows, vectors)


def encode_kernel(counts_ref, encoder_ref, out_ref, inputs_ref, weight_ref, *, genes, chunk):
    full, groups, tail = split_rows(genes)
    width = encoder_ref.shape[1]

    @pl.when(pl.program_id(0) == 0)
    def _():
        weight_ref[0 : full * ROWS, :] = encoder_ref[0 : full * ROWS, :].astype(bf16)
        if tail:
            weight_ref[full * ROWS :, :] = tail_rows(
                encoder_ref, full * ROWS, genes, slice(None), f32
            ).astype(bf16)

    def group(counted, rows, total):
        inputs_ref[rows, :] = jnp.log(counted + 1.0).astype(bf16)
        return total + counted[:8] + counted[8:]

    def step(i, total):
        rows = pl.ds(pl.multiple_of(i * ROWS, ROWS), ROWS)
        return group(counts_ref[rows, :].astype(f32), rows, total)

    total = lax.fori_loop(0, full, step, jnp.zeros((8, chunk), f32), unroll=4)
    if tail:
        rows = pl.ds(full * ROWS, ROWS)
        counted = tail_rows(counts_ref, full * ROWS, genes, slice(None), jnp.int32).astype(f32)
        total = group(counted, rows, total)
    out_ref[0:width, :] = lax.dot_general(
        weight_ref[...], inputs_ref[...], (((0,), (0,)), ((), ())), preferred_element_type=f32
    )
    row = lax.broadcasted_iota(jnp.int32, (8, chunk), 0)
    library = jnp.sum(total, axis=0, keepdims=True)
    out_ref[width : width + 8, :] = jnp.where(row == 0, library, 0.0)


def encode(counts_t, weight):
    genes, cells = counts_t.shape
    chunk = pick_chunk(cells, 512)
    width = weight.shape[1]
    return pl.pallas_call(
        functools.partial(encode_kernel, genes=genes, chunk=chunk),
        grid=(cells // chunk,),
        in_specs=[column_blocks(genes, chunk), whole(weight)],
        out_specs=column_blocks(width + 8, chunk),
        out_shape=jax.ShapeDtypeStruct((width + 8, cells), f32),
        scratch_shapes=[
            pltpu.VMEM((padded(genes), chunk), bf16),
            pltpu.VMEM((padded(genes), width), bf16),
        ],
        compiler_params=PARAMS,
        name="encode",
    )(counts_t, weight)


class Team:
    def __init__(self, gene_only):
        self.genes, self.cells = lax.axis_size("gene"), lax.axis_size("cell")
        self.gene, self.cell = lax.axis_index("gene"), lax.axis_index("cell")
        self.gene_only = gene_only
        self.size = self.genes if gene_only else self.genes * self.cells
        self.me = self.gene if gene_only else self.gene * self.cells + self.cell

    def others(self, act):
        def one(step, carry):
            other = lax.rem(self.me + step, self.size)
            if self.gene_only:
                act(other, (other, self.cell))
            else:
                act(other, (other // self.cells, lax.rem(other, self.cells)))
            return carry

        lax.fori_loop(1, self.size, one, 0)

    def greet(self):
        barrier = pltpu.get_barrier_semaphore()

        def act(other, place):
            pl.semaphore_signal(barrier, inc=1, device_id=place, device_id_type=MESH)

        self.others(act)
        pl.semaphore_wait(barrier, self.size - 1)

    def send(self, source, target, sems):
        def act(other, place):
            pltpu.make_async_remote_copy(
                src_ref=source(other),
                dst_ref=target,
                send_sem=sems.at[0],
                recv_sem=sems.at[1],
                device_id=place,
                device_id_type=MESH,
            ).start()

        self.others(act)


def await_bytes(ref, sem):
    pltpu.make_async_copy(ref, ref, sem).wait()


def fold_lanes(values):
    return sum(values[:, j : j + LANES] for j in range(0, values.shape[1], LANES))


def row_sums(folded):
    return jnp.sum(jnp.transpose(folded), axis=0, keepdims=True)


def box_sum(box):
    def add(i, total):
        return total + box[i]

    return lax.fori_loop(1, box.shape[0], add, box[0])


def eight_rows(rows):
    filler = jnp.zeros((8 - len(rows), LANES), f32)
    return jnp.concatenate([*rows, filler], axis=0) if len(rows) < 8 else jnp.concatenate(rows, 0)


def columns_of(rows):
    turned = jnp.transpose(jnp.concatenate([eight_rows(rows), jnp.zeros((120, LANES), f32)], 0))
    return [turned[:, i : i + 1] for i in range(len(rows))]


def exact(left, right, left_dim, right_dim):
    return lax.dot_general(
        left,
        right,
        (((left_dim,), (right_dim,)), ((), ())),
        precision=lax.Precision.HIGHEST,
        preferred_element_type=f32,
    )


def hot_rows(index, batches):
    rows = lax.broadcasted_iota(jnp.int32, (batches, index.shape[1]), 0)
    return jnp.where(rows == index, 1.0, 0.0)


def sigmoid(value):
    return 1.0 / (1.0 + jnp.exp(-value))


def slope_of(value):
    sigma = sigmoid(value)
    return sigma * (1.0 + value * (1.0 - sigma))


def pack_layout(latent_pad, batches):
    mixing = slice(8, 8 + latent_pad + batches)
    heads = slice(mixing.stop, mixing.stop + 2 * latent_pad)
    return mixing, heads, slice(heads.stop, heads.stop + batches)


def middle_kernel(
    encoded_ref,
    index_ref,
    valid_ref,
    noise_ref,
    pack_ref,
    hidden_ref,
    centered_ref,
    sample_ref,
    share_ref,
    stats_ref,
    first_ref,
    heads_ref,
    rest_ref,
    slab_box,
    box1,
    box2,
    slab_sems,
    sems1,
    sems2,
    sample_sems,
    *,
    batches,
    latent,
    genes_all,
):
    group, everyone = Team(True), Team(False)
    width, slab = first_ref.shape
    cells = hidden_ref.shape[1]
    pad = sample_ref.shape[0]
    mixing_rows, heads_rows, shift_rows = pack_layout(pad, batches)
    mixing = pack_ref[mixing_rows, :]

    def part(other):
        return pl.ds(pl.multiple_of(other * slab, LANES), slab)

    mine = part(group.me)
    everyone.greet()
    group.send(lambda other: encoded_ref.at[:, part(other)], slab_box.at[group.me], slab_sems)
    slab_box[group.me] = encoded_ref[:, mine]
    hot = hot_rows(index_ref[:, mine], batches)
    valid = valid_ref[:, mine].astype(f32)
    shift = exact(pack_ref[shift_rows, :], hot, 0, 0)
    gain1, bias1, gain2, bias2, head_bias = columns_of([pack_ref[i : i + 1, :] for i in range(5)])
    others = slab_box.at[pl.ds(0, group.size - 1)]
    await_bytes(others, slab_sems.at[0])
    await_bytes(others, slab_sems.at[1])
    total = box_sum(slab_box)
    rest_ref[0:1, :] = total[width : width + 1, :]
    pre1 = total[0:width, :] + shift

    def reduced(rows, box, sems):
        box[everyone.me] = eight_rows(rows)
        everyone.send(lambda other: box.at[everyone.me], box.at[everyone.me], sems)
        others = box.at[pl.ds(0, everyone.size - 1)]

        def finish():
            await_bytes(others, sems.at[0])
            await_bytes(others, sems.at[1])
            return box_sum(box)

        return finish

    weighed = valid * pre1
    sums = reduced(
        [
            row_sums(fold_lanes(weighed)),
            row_sums(fold_lanes(weighed * pre1)),
            jnp.broadcast_to(jnp.sum(valid, axis=1, keepdims=True), (1, LANES)),
        ],
        box1,
        sems1,
    )()
    count = jnp.maximum(sums[2:3], 1.0)
    mean1 = sums[0:1] / count
    inverse1 = lax.rsqrt(sums[1:2] / count - mean1 * mean1 + norm_epsilon)
    mean_col, inverse_col = columns_of([mean1, inverse1])
    centered1 = (pre1 - mean_col) * inverse_col
    first_ref[...] = centered1
    normed1 = centered1 * gain1 + bias1
    hidden1 = normed1 * sigmoid(normed1)
    heads = exact(pack_ref[heads_rows, :], hidden1, 1, 0) + head_bias[0 : 2 * pad]
    heads_ref[...] = heads
    mean_z, log_var = heads[0:pad], heads[pad : 2 * pad]
    noise = jnp.concatenate([noise_ref[:, mine], jnp.zeros((pad - latent, slab), f32)], axis=0)
    sample = mean_z + jnp.exp(0.5 * log_var) * noise
    rest_ref[1:2, :] = 0.5 * jnp.sum(
        mean_z * mean_z + jnp.exp(log_var) - log_var - 1.0, axis=0, keepdims=True
    )
    sample_ref[:, mine] = sample
    group.send(lambda other: sample_ref.at[:, mine], sample_ref.at[:, mine], sample_sems)
    pre2 = exact(mixing, jnp.concatenate([sample, hot], axis=0), 0, 0)
    weighed = valid * pre2
    finish = reduced(
        [row_sums(fold_lanes(weighed)), row_sums(fold_lanes(weighed * pre2))], box2, sems2
    )
    scale = 1.0 / (count * genes_all)
    share_ref[...] = valid_ref[...].astype(f32) * scale[:, 0:1]
    sums = finish()
    mean2 = sums[0:1] / count
    inverse2 = lax.rsqrt(sums[1:2] / count - mean2 * mean2 + norm_epsilon)
    stats_ref[...] = eight_rows([inverse1, inverse2, count, scale])
    mean_col, inverse_col = columns_of([mean2, inverse2])
    others = sample_ref.at[:, pl.ds(0, (group.size - 1) * slab)]
    await_bytes(others, sample_sems.at[0])
    await_bytes(others, sample_sems.at[1])
    piece = pick_chunk(cells, 512)

    def decode(i, carry):
        columns = pl.ds(pl.multiple_of(i * piece, LANES), piece)
        mixed = jnp.concatenate(
            [sample_ref[:, columns], hot_rows(index_ref[:, columns], batches)], axis=0
        )
        centered = (exact(mixing, mixed, 0, 0) - mean_col) * inverse_col
        centered_ref[:, columns] = centered
        normed = centered * gain2 + bias2
        hidden_ref[:, columns] = (normed * sigmoid(normed)).astype(bf16)
        return carry

    lax.fori_loop(0, cells // piece, decode, 0)


def middle(encoded, index, valid, noise, pack, batches, pad, genes_all):
    cells = index.shape[1]
    width = LANES
    genes_axis = lax.axis_size("gene")
    devices = genes_axis * lax.axis_size("cell")
    slab = cells // genes_axis
    return pl.pallas_call(
        functools.partial(
            middle_kernel, batches=batches, latent=noise.shape[0], genes_all=genes_all
        ),
        out_shape=[
            jax.ShapeDtypeStruct((width, cells), bf16),
            jax.ShapeDtypeStruct((width, cells), f32),
            jax.ShapeDtypeStruct((pad, cells), f32),
            jax.ShapeDtypeStruct((1, cells), f32),
            jax.ShapeDtypeStruct((8, LANES), f32),
            jax.ShapeDtypeStruct((width, slab), f32),
            jax.ShapeDtypeStruct((2 * pad, slab), f32),
            jax.ShapeDtypeStruct((2, slab), f32),
        ],
        in_specs=[IN_VMEM] * 5,
        out_specs=[IN_VMEM] * 8,
        scratch_shapes=[
            pltpu.VMEM((genes_axis, width + 8, slab), f32),
            pltpu.VMEM((devices, 8, LANES), f32),
            pltpu.VMEM((devices, 8, LANES), f32),
        ]
        + [pltpu.SemaphoreType.DMA((2,))] * 4,
        compiler_params=talking(1),
        name="middle",
    )(encoded, index, valid, noise, pack)


def tops_kernel(tops_ref, rest_ref, out_ref, box, sems, back_sems):
    group = Team(True)
    slab = rest_ref.shape[1]

    def part(other):
        return pl.ds(pl.multiple_of(other * slab, LANES), slab)

    mine = part(group.me)
    group.greet()
    group.send(lambda other: tops_ref.at[:, part(other)], box.at[group.me], sems)
    box[group.me] = tops_ref[:, mine]
    others = box.at[pl.ds(0, group.size - 1)]
    await_bytes(others, sems.at[0])
    await_bytes(others, sems.at[1])

    def highest(i, best):
        return jnp.maximum(best, box[i, 0:1, :])

    top = lax.fori_loop(1, group.size, highest, box[0, 0:1, :])

    def add(i, total):
        return total + box[i, 1:2, :] * jnp.exp(box[i, 0:1, :] - top)

    total = lax.fori_loop(0, group.size, add, jnp.zeros_like(top))
    inverse = 1.0 / total
    out_ref[0:1, mine] = top
    out_ref[1:2, mine] = rest_ref[0:1, :] * inverse
    out_ref[2:3, mine] = inverse
    out_ref[3:4, mine] = inverse
    group.send(lambda other: out_ref.at[:, mine], out_ref.at[:, mine], back_sems)
    others = out_ref.at[:, pl.ds(0, (group.size - 1) * slab)]
    await_bytes(others, back_sems.at[0])
    await_bytes(others, back_sems.at[1])


def combine_tops(tops, rest):
    group = lax.axis_size("gene")
    slab = rest.shape[1]
    return pl.pallas_call(
        tops_kernel,
        out_shape=jax.ShapeDtypeStruct((4, tops.shape[1]), f32),
        in_specs=[IN_VMEM] * 2,
        out_specs=IN_VMEM,
        scratch_shapes=[pltpu.VMEM((group, 2, slab), f32)] + [pltpu.SemaphoreType.DMA((2,))] * 2,
        compiler_params=talking(2),
        name="combine_tops",
    )(tops, rest)


def sums_kernel(sums_ref, rows_ref, rest_ref, valid_ref, out_ref, box, sems, back_sems, *, genes_all):
    group = Team(True)
    slab = rest_ref.shape[1]

    def part(other):
        return pl.ds(pl.multiple_of(other * slab, LANES), slab)

    mine = part(group.me)
    group.greet()
    group.send(lambda other: sums_ref.at[:, part(other)], box.at[group.me], sems)
    box[group.me] = sums_ref[:, mine]
    others = box.at[pl.ds(0, group.size - 1)]
    await_bytes(others, sems.at[0])
    await_bytes(others, sems.at[1])
    total = box_sum(box)
    out_ref[0:1, mine] = total[0:1] * rows_ref[2:3, mine]
    out_ref[1:2, mine] = (
        valid_ref[:, mine].astype(f32) * (total[1:2] + rest_ref[1:2, :]) / genes_all
    )
    group.send(lambda other: out_ref.at[:, mine], out_ref.at[:, mine], back_sems)
    others = out_ref.at[:, pl.ds(0, (group.size - 1) * slab)]
    await_bytes(others, back_sems.at[0])
    await_bytes(others, back_sems.at[1])


def combine_sums(sums, rows, rest, valid, genes_all):
    group = lax.axis_size("gene")
    slab = rest.shape[1]
    return pl.pallas_call(
        functools.partial(sums_kernel, genes_all=genes_all),
        out_shape=jax.ShapeDtypeStruct((2, sums.shape[1]), f32),
        in_specs=[IN_VMEM] * 4,
        out_specs=IN_VMEM,
        scratch_shapes=[pltpu.VMEM((group, 2, slab), f32)] + [pltpu.SemaphoreType.DMA((2,))] * 2,
        compiler_params=talking(3),
        name="combine_sums",
    )(sums, rows, rest, valid)


def middle_back_kernel(
    grad_ref,
    centered_ref,
    sample_ref,
    index_ref,
    valid_ref,
    noise_ref,
    pack_ref,
    stats_ref,
    first_ref,
    heads_ref,
    output_ref,
    genes_ref,
    grad16_ref,
    small_ref,
    norms_ref,
    output_sum_ref,
    genes_sum_ref,
    part_ref,
    slab_box,
    box1,
    box2,
    output_box,
    half_box,
    half_give,
    genes_box,
    slab_sems,
    sems1,
    sems2,
    grad_sems,
    output_sems,
    genes_sems,
    *,
    batches,
    latent,
):
    group, everyone = Team(True), Team(False)
    cell = lax.axis_index("cell")
    bit, near, far = lax.rem(cell, 2), cell + 1 - 2 * lax.rem(cell, 2), lax.rem(cell + 2, 4)
    half = output_ref.shape[1] // 2

    def swap(source, target, other, number):
        copy = pltpu.make_async_remote_copy(
            src_ref=source,
            dst_ref=target,
            send_sem=output_sems.at[number, 0],
            recv_sem=output_sems.at[number, 1],
            device_id=(group.gene, other),
            device_id_type=MESH,
        )
        copy.start()
        return copy

    def rows_of(number):
        return pl.ds(pl.multiple_of(number * half, 8), half)
    width, slab = first_ref.shape
    cells = grad_ref.shape[1]
    pad = sample_ref.shape[0]
    mixing_rows, heads_rows, _ = pack_layout(pad, batches)
    depth = pad + batches

    def part(other):
        return pl.ds(pl.multiple_of(other * slab, LANES), slab)

    mine = part(group.me)
    everyone.greet()
    swap1 = swap(output_ref.at[1 - bit], output_box, near, 0)
    genes_box[cell] = genes_ref[...]

    def tell(step, carry):
        other = lax.rem(cell + step, group.cells)
        pltpu.make_async_remote_copy(
            src_ref=genes_ref,
            dst_ref=genes_box.at[cell],
            send_sem=genes_sems.at[0],
            recv_sem=genes_sems.at[1],
            device_id=(group.gene, other),
            device_id_type=MESH,
        ).start()
        return carry

    lax.fori_loop(1, group.cells, tell, 0)
    inverse1, inverse2 = stats_ref[0:1, :], stats_ref[1:2, :]
    count, scale = stats_ref[2:3, 0:1], stats_ref[3:4, 0:1]
    factor2 = inverse2 * pack_ref[2:3, :]
    gain1, bias1, gain2, bias2, factor1 = columns_of(
        [pack_ref[i : i + 1, :] for i in range(4)] + [inverse1 * pack_ref[0:1, :]]
    )
    latent_rows = pack_ref[8 : 8 + pad, :] * factor2
    piece = pick_chunk(cells, 512)

    def gather(i, carry):
        gains, shifts, products = carry
        columns = pl.ds(pl.multiple_of(i * piece, LANES), piece)
        centered = centered_ref[:, columns]
        grad = grad_ref[:, columns] * slope_of(centered * gain2 + bias2)
        part_ref[:, columns] = exact(latent_rows, grad, 1, 0)
        mixed = jnp.concatenate(
            [sample_ref[:, columns], hot_rows(index_ref[:, columns], batches)], axis=0
        )
        return (
            gains + fold_lanes(grad * centered),
            shifts + fold_lanes(grad),
            products + exact(mixed, grad, 1, 1),
        )

    zeros = jnp.zeros((width, LANES), f32)
    gains, shifts, products = lax.fori_loop(
        0, cells // piece, gather, (zeros, zeros, jnp.zeros((depth, width), f32))
    )

    def reduced(rows, box, sems):
        box[everyone.me] = eight_rows(rows)
        everyone.send(lambda other: box.at[everyone.me], box.at[everyone.me], sems)
        others = box.at[pl.ds(0, everyone.size - 1)]

        def finish():
            await_bytes(others, sems.at[0])
            await_bytes(others, sems.at[1])
            return box_sum(box)

        return finish

    finish = reduced([row_sums(gains), row_sums(shifts)], box1, sems1)
    group.send(lambda other: part_ref.at[:, part(other)], slab_box.at[group.me], slab_sems)
    slab_box[group.me] = part_ref[:, mine]
    swap1.wait()
    own, given = rows_of(far // 2), rows_of(cell // 2)
    half_give[...] = output_ref[bit, own] + output_box[own]
    swap2 = swap(half_give, half_box, far, 1)
    output_sum_ref[bit, given] = output_ref[bit, given] + output_box[given]
    hot = hot_rows(index_ref[:, mine], batches)
    valid = valid_ref[:, mine].astype(f32)
    mixed = valid * jnp.concatenate([sample_ref[:, mine], hot], axis=0)
    centered2 = centered_ref[:, mine]
    share = valid / count
    mixed_sum = jnp.sum(mixed, axis=1, keepdims=True)
    mixed_product = exact(mixed, centered2, 1, 1)
    noise = jnp.concatenate([noise_ref[:, mine], jnp.zeros((pad - latent, slab), f32)], axis=0)
    mean_z, log_var = heads_ref[0:pad, :], heads_ref[pad : 2 * pad, :]
    log_factor = 0.5 * noise * jnp.exp(0.5 * log_var)
    scaled = valid * scale
    grad_log_own = scaled * (jnp.exp(log_var) - 1.0) * 0.5
    centered1 = first_ref[...]
    normed1 = centered1 * gain1 + bias1
    sigma1 = sigmoid(normed1)
    hidden1 = normed1 * sigma1
    slope1 = sigma1 * (1.0 + normed1 * (1.0 - sigma1))

    sums = finish()
    gain2_grad, shift2_grad = sums[0:1], sums[1:2]
    small_ref[0:depth, :] = factor2 * (
        products - (mixed_sum * shift2_grad + mixed_product * gain2_grad) / count
    )
    gain_col, shift_col = columns_of([gain2_grad, shift2_grad])
    pulled = exact(latent_rows, shift_col + centered2 * gain_col, 1, 0)
    others = slab_box.at[pl.ds(0, group.size - 1)]
    await_bytes(others, slab_sems.at[0])
    await_bytes(others, slab_sems.at[1])
    grad_sample = box_sum(slab_box) - share * pulled
    grad_heads = jnp.concatenate(
        [grad_sample + scaled * mean_z, grad_sample * log_factor + grad_log_own], axis=0
    )
    grad_normed1 = exact(pack_ref[heads_rows, :], grad_heads, 0, 0) * slope1
    finish = reduced(
        [row_sums(fold_lanes(grad_normed1 * centered1)), row_sums(fold_lanes(grad_normed1))],
        box2,
        sems2,
    )
    swap2.wait()
    output_sum_ref[bit, given] = output_sum_ref[bit, given] + half_box[...]
    swap3 = swap(output_sum_ref.at[bit, given], output_sum_ref.at[bit, given], far, 2)
    small_ref[depth : depth + 2 * pad, :] = exact(grad_heads, hidden1, 1, 1)
    small_ref[depth + 2 * pad : depth + 4 * pad, :] = fold_lanes(grad_heads)
    sums = finish()
    gain1_grad, shift1_grad = sums[0:1], sums[1:2]
    norms_ref[...] = eight_rows([gain1_grad, shift1_grad, gain2_grad, shift2_grad])
    gain_col, shift_col = columns_of([gain1_grad, shift1_grad])
    grad_pre1 = factor1 * (grad_normed1 - share * (shift_col + centered1 * gain_col))
    grad16_ref[:, mine] = grad_pre1.astype(bf16)
    group.send(lambda other: grad16_ref.at[:, mine], grad16_ref.at[:, mine], grad_sems)
    small_ref[depth + 4 * pad :, :] = exact(hot, grad_pre1, 1, 1)
    others = genes_box.at[pl.ds(0, group.cells - 1)]
    await_bytes(others, genes_sems.at[0])
    await_bytes(others, genes_sems.at[1])
    genes_sum_ref[...] = box_sum(genes_box)
    swap3.wait()
    swap4 = swap(output_sum_ref.at[bit], output_sum_ref.at[bit], near, 3)
    swap4.wait()
    others = grad16_ref.at[:, pl.ds(0, (group.size - 1) * slab)]
    await_bytes(others, grad_sems.at[0])
    await_bytes(others, grad_sems.at[1])


def middle_back(
    grad,
    centered,
    sample,
    index,
    valid,
    noise,
    pack,
    stats,
    first,
    heads,
    output_grad,
    genes_grad,
    batches,
):
    cells = index.shape[1]
    width, slab = first.shape
    pad = sample.shape[0]
    genes_axis = lax.axis_size("gene")
    devices = genes_axis * lax.axis_size("cell")
    return pl.pallas_call(
        functools.partial(middle_back_kernel, batches=batches, latent=noise.shape[0]),
        out_shape=[
            jax.ShapeDtypeStruct((width, cells), bf16),
            jax.ShapeDtypeStruct((5 * pad + 2 * batches, LANES), f32),
            jax.ShapeDtypeStruct((8, LANES), f32),
            jax.ShapeDtypeStruct(output_grad.shape, f32),
            jax.ShapeDtypeStruct(genes_grad.shape, f32),
        ],
        in_specs=[IN_VMEM] * 12,
        out_specs=[IN_VMEM] * 5,
        scratch_shapes=[
            pltpu.VMEM((pad, cells), f32),
            pltpu.VMEM((genes_axis, pad, slab), f32),
            pltpu.VMEM((devices, 8, LANES), f32),
            pltpu.VMEM((devices, 8, LANES), f32),
            pltpu.VMEM(output_grad.shape[1:], f32),
            pltpu.VMEM((output_grad.shape[1] // 2, LANES), f32),
            pltpu.VMEM((output_grad.shape[1] // 2, LANES), f32),
            pltpu.VMEM((devices // genes_axis, *genes_grad.shape), f32),
        ]
        + [pltpu.SemaphoreType.DMA((2,))] * 4
        + [pltpu.SemaphoreType.DMA((4, 2)), pltpu.SemaphoreType.DMA((2,))],
        compiler_params=talking(4),
        name="middle_back",
    )(
        grad,
        centered,
        sample,
        index,
        valid,
        noise,
        pack,
        stats,
        first,
        heads,
        output_grad,
        genes_grad,
    )


def last_sums_kernel(
    grad_ref, small_ref, sum_ref, total_ref, box, half_box, half_give, small_box, sems, small_sems
):
    group, everyone = Team(True), Team(False)
    cell = lax.axis_index("cell")
    bit, near, far = lax.rem(cell, 2), cell + 1 - 2 * lax.rem(cell, 2), lax.rem(cell + 2, 4)
    high = cell // 2
    size = grad_ref.shape[0]
    half, quarter = size // 2, size // 4
    everyone.greet()

    def swap(source, target, other, sems):
        copy = pltpu.make_async_remote_copy(
            src_ref=source,
            dst_ref=target,
            send_sem=sems.at[0],
            recv_sem=sems.at[1],
            device_id=other,
            device_id_type=MESH,
        )
        copy.start()
        return copy

    total_ref[...] = small_ref[...]
    rounds = []
    for step in (1, 2):
        other = near if step == 1 else far
        rounds.append((group.gene, other))
    step = 1
    while step < group.genes:
        flip = group.gene + step - 2 * step * lax.rem(group.gene // step, 2)
        rounds.append((flip, cell))
        step *= 2

    def small_round(number):
        source = small_ref if number == 0 else small_box.at[1, number - 1]
        return swap(source, small_box.at[0, number], rounds[number], small_sems.at[number])

    def small_end(copy, number):
        copy.wait()
        source = small_ref[...] if number == 0 else small_box[1, number - 1]
        small_box[1, number] = source + small_box[0, number]

    def half_of(number):
        return pl.ds(pl.multiple_of(number * half, 8), half)

    def quarter_of(number):
        return pl.ds(pl.multiple_of(bit * half + number * quarter, 8), quarter)

    copy = swap(grad_ref.at[half_of(1 - bit)], box, (group.gene, near), sems.at[0])
    small = small_round(0)
    copy.wait()

    def inside(number):
        return pl.ds(pl.multiple_of(number * quarter, 8), quarter)

    half_give[...] = grad_ref[quarter_of(1 - high), :] + box[inside(1 - high), :]
    copy = swap(half_give, half_box, (group.gene, far), sems.at[1])
    small_end(small, 0)
    small = small_round(1)
    small_end(small, 1)
    small = small_round(2)
    copy.wait()
    mine = quarter_of(high)
    sum_ref[mine, :] = grad_ref[mine, :] + box[inside(high), :] + half_box[...]
    copy = swap(sum_ref.at[mine], sum_ref.at[mine], (group.gene, far), sems.at[2])
    small_end(small, 2)
    for number in range(3, len(rounds)):
        small_end(small_round(number), number)
    total_ref[...] = small_box[1, len(rounds) - 1]
    copy.wait()
    copy = swap(sum_ref.at[half_of(bit)], sum_ref.at[half_of(bit)], (group.gene, near), sems.at[3])
    copy.wait()


def last_sums(grad, small):
    rounds = 2
    while 2 ** (rounds - 2) < lax.axis_size("gene"):
        rounds += 1
    size = grad.shape[0]
    return pl.pallas_call(
        last_sums_kernel,
        out_shape=[
            jax.ShapeDtypeStruct(grad.shape, f32),
            jax.ShapeDtypeStruct(small.shape, f32),
        ],
        in_specs=[IN_VMEM] * 2,
        out_specs=[IN_VMEM] * 2,
        scratch_shapes=[
            pltpu.VMEM((size // 2, LANES), f32),
            pltpu.VMEM((size // 4, LANES), f32),
            pltpu.VMEM((size // 4, LANES), f32),
            pltpu.VMEM((2, rounds, *small.shape), f32),
            pltpu.SemaphoreType.DMA((4, 2)),
            pltpu.SemaphoreType.DMA((rounds, 2)),
        ],
        compiler_params=talking(5),
        name="last_sums",
    )(grad, small)


def update_kernel(*refs):
    groups, outs = refs[:8], refs[8:]
    encoder, output = groups[:4], groups[4:]
    fresh, moment, mean = nesterov(*[ref[...] for ref in encoder], step_rates[0])
    for ref, value in zip(outs[:3], (fresh, moment, mean)):
        ref[...] = value
    rows = output[3].shape[1]
    for k in range(2):
        here = pl.ds(k, rows, stride=2)
        old = [ref[here, :] for ref in output[:3]]
        for ref, value in zip(outs[3:], nesterov(*old, output[3][k], step_rates[1])):
            ref[here, :] = value


def update(encoder, encoder_grad, output, output_grad):
    genes = encoder[0].shape[0]
    block = 2 * LANES
    one = pl.BlockSpec((block, LANES), lambda i: (i, 0))
    two = pl.BlockSpec((2 * block, LANES), lambda i: (i, 0))
    both = pl.BlockSpec((2, block, LANES), lambda i: (0, i, 0))
    return pl.pallas_call(
        update_kernel,
        grid=(pl.cdiv(genes, block),),
        in_specs=[one] * 4 + [two] * 3 + [both],
        out_specs=[one] * 3 + [two] * 3,
        out_shape=[jax.ShapeDtypeStruct(encoder[0].shape, f32)] * 3
        + [jax.ShapeDtypeStruct(output[0].shape, f32)] * 3,
        compiler_params=PARAMS,
        name="update",
    )(*encoder, encoder_grad, *output, output_grad)


def fill_hidden(long_ref, hidden_ref, top):
    width, chunk = hidden_ref.shape
    long_ref[0:width, :] = hidden_ref[...]
    index = lax.broadcasted_iota(jnp.int32, (HOT_DEPTH - width, chunk), 0)
    extra = jnp.where(index < 3, 1.0, 0.0)
    if top is not None:
        high = (-top).astype(bf16).astype(f32)
        middle = (-top - high).astype(bf16).astype(f32)
        low = (-top - high - middle).astype(bf16).astype(f32)
        extra = jnp.where(index == 3, high, extra)
        extra = jnp.where(index == 4, middle, extra)
        extra = jnp.where(index == 5, low, extra)
    long_ref[width:HOT_DEPTH, :] = extra.astype(bf16)


def sweep(blocks, block, groups, pieces, logits, terms, back, carry):
    def rows_of(number):
        return pl.ds(pl.multiple_of(number * block, ROWS), block)

    logits(0, rows_of(0), block, pieces)

    def beside(i, later, earlier):
        acts = [
            lambda piece=piece: logits(1 - i, rows_of(later), block, [piece]) for piece in pieces
        ]
        if back is not None:
            acts.append(lambda: back(1 - i, rows_of(earlier), block))
        spaced = []
        for step in range(groups):
            spaced.append(acts.pop(0) if acts and step % 2 == 0 else lambda: None)
        return spaced + acts

    def pair(p, carry):
        first = 2 * p
        last, ahead = jnp.maximum(first - 1, 0), jnp.minimum(first + 2, blocks - 1)
        carry = terms(0, first, carry, beside(0, first + 1, last))
        return terms(1, first + 1, carry, beside(1, ahead, first))

    carry = lax.fori_loop(0, blocks // 2, pair, carry)
    if back is not None and blocks > 1:
        back(1, rows_of(blocks // 2 * 2 - 1), block)
    if blocks % 2:
        carry = terms(0, blocks - 1, carry, ())
        if back is not None:
            back(0, rows_of(blocks - 1), block)
    return carry


def logit_pieces(ks, chunk):
    width = min(chunk, WIDE)
    return [(k, slice(j, j + width)) for k in range(ks) for j in range(0, chunk, width)]


def totals_kernel(hidden_ref, weight_ref, out_ref, long_ref, even_ref, odd_ref, *, genes, chunk):
    full, groups, tail = split_rows(genes)
    block = ROWS * groups
    blocks = full // groups
    values = (even_ref, odd_ref)
    fill_hidden(long_ref, hidden_ref, None)
    pieces = logit_pieces(1, chunk)

    def logits(i, rows, size, which):
        for _, columns in which:
            values[i][0:size, columns] = jnp.dot(
                weight_ref[0, rows, :], long_ref[:, columns], preferred_element_type=f32
            )

    def online(value_ref, size, carry, beside=()):
        best, total = carry
        fresh = best
        for i in range(0, size, 8):
            fresh = jnp.maximum(fresh, value_ref[i : i + 8, :])
        total = total * jnp.exp2((best - fresh) * (1.0 / ln2))
        for i in range(0, size, 8):
            for act in beside[i // 8 :: size // 8]:
                act()
            total = total + jnp.exp2((value_ref[i : i + 8, :] - fresh) * (1.0 / ln2))
        return fresh, total

    def terms(i, number, carry, beside):
        return online(values[i], block, carry, beside)

    carry = (jnp.full((8, chunk), -jnp.inf, f32), jnp.zeros((8, chunk), f32))
    carry = sweep(blocks, block, groups, pieces, logits, terms, None, carry)
    if tail:
        logits(1, pl.ds(full * ROWS, ROWS), ROWS, pieces)
        carry = online(odd_ref, ROWS, carry)
    best, total = carry
    top = jnp.max(best, axis=0, keepdims=True)
    total = total * jnp.exp2((best - top) * (1.0 / ln2))
    out_ref[0:1, :] = top
    out_ref[1:2, :] = jnp.sum(total, axis=0, keepdims=True)


def totals(hidden, weights, genes):
    width, cells = hidden.shape
    chunk = pick_chunk(cells, 512)
    groups = split_rows(genes)[1]
    return pl.pallas_call(
        functools.partial(totals_kernel, genes=genes, chunk=chunk),
        grid=(cells // chunk,),
        in_specs=[column_blocks(width, chunk), whole(weights)],
        out_specs=column_blocks(2, chunk),
        out_shape=jax.ShapeDtypeStruct((2, cells), f32),
        scratch_shapes=[pltpu.VMEM((HOT_DEPTH, chunk), bf16)]
        + [pltpu.VMEM((ROWS * groups, chunk), f32)] * 2,
        compiler_params=PARAMS,
        name="totals",
    )(hidden, weights)


def likelihood_kernel(
    counts_ref,
    hidden_ref,
    rows_ref,
    share_ref,
    weight_ref,
    theta_ref,
    log_ref,
    slope_ref,
    gammas_ref,
    digammas_ref,
    slopes_ref,
    sums_ref,
    grad_hidden_ref,
    grad_weight_ref,
    grad_bias_ref,
    grad_theta_ref,
    long_ref,
    even_ref,
    odd_ref,
    even_grad_ref,
    odd_grad_ref,
    *,
    genes,
    chunk,
):
    full, groups, tail = split_rows(genes)
    block = ROWS * groups
    blocks = full // groups
    width = hidden_ref.shape[0]

    @pl.when(pl.program_id(0) == 0)
    def _():
        for ref in (grad_weight_ref, grad_bias_ref, grad_theta_ref):
            ref[...] = jnp.zeros_like(ref)

    fill_hidden(long_ref, hidden_ref, rows_ref[0:1, :])
    wide = min(WIDE, chunk)
    tiles = [slice(j, j + wide) for j in range(0, chunk, wide)]
    ratio_all = rows_ref[1:2, :]
    share_all = share_ref[...]

    def two(x):
        return jnp.concatenate([x] * (wide // LANES), axis=1)

    def look(t, c):
        return jnp.concatenate([jnp.take_along_axis(t, c[:, q:q+LANES], axis=1) for q in range(0, wide, LANES)], axis=1)

    def group(value_ref, grad_ref, held, span, read, carry):
        losses, sums = [], []
        theta = two(theta_ref.at[span][held, :])
        log_theta = two(log_ref.at[span][held, :])
        log_slope = two(slope_ref.at[span][held, :])
        gammas = gammas_ref.at[span][held, :]
        digammas = digammas_ref.at[span][held, :]
        grad_bias = grad_bias_ref.at[span][held, :]
        grad_theta = grad_theta_ref.at[span][held, :]
        for j, columns in enumerate(tiles):
            count = read(columns)
            counted = count.astype(f32)
            minus = value_ref[1, held, columns] * (-1.0 / ln2)
            share = share_all[:, columns]
            rate = jnp.exp2(value_ref[0, held, columns] * (1.0 / ln2)) * ratio_all[:, columns]
            near = rate + rate_epsilon
            both = theta + near
            inverse_both = 1.0 / both
            log_both = jnp.log2(both)
            upper = jnp.maximum(minus, 0.0)
            lower = jnp.minimum(minus, 0.0)
            one_pi = 1.0 + jnp.exp2(lower - upper)
            sigma_pi = jnp.exp2(lower) * (1.0 / one_pi)
            zero = count < 1
            pi_theta = theta * (log_theta - log_both) + minus
            inflated = jnp.where(zero, pi_theta, 1e30)
            small = jnp.exp2(-jnp.abs(inflated))
            inverse_theta = 1.0 / (1.0 + small)
            sigma = jnp.where(inflated >= 0.0, 1.0, small) * inverse_theta
            loss = (upper - jnp.where(zero, jnp.maximum(pi_theta, 0.0), pi_theta)) + (
                jnp.log2(one_pi * inverse_theta)
                - counted * (jnp.log2(near) - log_both)
                - look(gammas, count)
            )
            pull = (sigma * theta + counted) * inverse_both
            slope = rate * (pull - counted * (1.0 / near))
            slopes_ref.at[span][held, columns] = slope
            grad_dropout = (sigma - sigma_pi) * share
            grad_ref[held, columns] = grad_dropout.astype(bf16)
            grad_bias = grad_bias + fold_lanes(grad_dropout)
            grad_theta = grad_theta + fold_lanes(share * (
                (pull - sigma * (log_slope - ln2 * log_both))
                - look(digammas, count)
            ))
            losses.append(carry[0][j] + loss[:8] + loss[8:])
            sums.append(carry[1][j] + slope[:8] + slope[8:])
        grad_bias_ref.at[span][held, :] = grad_bias
        grad_theta_ref.at[span][held, :] = grad_theta
        return tuple(losses), tuple(sums)

    pieces = logit_pieces(2, chunk)
    values, grads = (even_ref, odd_ref), (even_grad_ref, odd_grad_ref)

    def logits(i, rows, size, which):
        for k, columns in which:
            values[i][k, 0:size, columns] = jnp.dot(
                weight_ref[k, rows, :], long_ref[:, columns], preferred_element_type=f32
            )

    def back(i, rows, size):
        grad = grads[i][0:size, :]
        grad_weight_ref[rows, :] += lax.dot_general(
            grad, hidden_ref[...], (((1,), (1,)), ((), ())), preferred_element_type=f32
        )
        grad_hidden_ref[...] += lax.dot_general(
            weight_ref[1, rows, 0:width],
            grad,
            (((0,), (0,)), ((), ())),
            preferred_element_type=f32,
        )

    def terms(buffer, number, carry, beside):
        span = pl.ds(pl.multiple_of(number * block, ROWS), block)
        for i in range(groups):
            for act in beside[i::groups]:
                act()
            held = slice(i * ROWS, (i + 1) * ROWS)
            carry = group(
                values[buffer],
                grads[buffer],
                held,
                span,
                lambda columns, held=held: counts_ref.at[span][held, columns],
                carry,
            )
        return carry

    grad_hidden_ref[...] = jnp.zeros_like(grad_hidden_ref)
    odd_grad_ref[...] = jnp.zeros_like(odd_grad_ref)
    carry = tuple(jnp.zeros((8, wide), f32) for _ in tiles)
    carry = sweep(blocks, block, groups, pieces, logits, terms, back, (carry, carry))
    if tail:
        rows = pl.ds(full * ROWS, ROWS)
        logits(1, rows, ROWS, pieces)
        carry = group(
            odd_ref,
            odd_grad_ref,
            slice(0, ROWS),
            rows,
            lambda cols: tail_rows(counts_ref, full * ROWS, genes, cols, jnp.int32),
            carry,
        )
        back(1, rows, ROWS)
    for j, columns in enumerate(tiles):
        sums_ref[0:1, columns] = jnp.sum(carry[1][j], axis=0, keepdims=True)
        sums_ref[1:2, columns] = jnp.sum(carry[0][j], axis=0, keepdims=True) * ln2


def likelihood(counts_t, hidden, rows, share, weights, gene_tables):
    genes, cells = counts_t.shape
    size = weights.shape[1]
    width = hidden.shape[0]
    chunk = pick_chunk(cells, 512)
    groups = split_rows(genes)[1]
    row = column_blocks(1, chunk)
    per_gene = pl.BlockSpec((size, LANES), lambda i: (0, 0))
    return pl.pallas_call(
        functools.partial(likelihood_kernel, genes=genes, chunk=chunk),
        grid=(cells // chunk,),
        in_specs=[column_blocks(genes, chunk), column_blocks(width, chunk)]
        + [column_blocks(rows.shape[0], chunk), row, whole(weights)]
        + [whole(a) for a in gene_tables],
        out_specs=[
            column_blocks(size, chunk),
            column_blocks(2, chunk),
            column_blocks(width, chunk),
        ]
        + [per_gene] * 3,
        out_shape=[
            jax.ShapeDtypeStruct((size, cells), f32),
            jax.ShapeDtypeStruct((2, cells), f32),
            jax.ShapeDtypeStruct((width, cells), f32),
        ]
        + [jax.ShapeDtypeStruct((size, LANES), f32)] * 3,
        scratch_shapes=[pltpu.VMEM((HOT_DEPTH, chunk), bf16)]
        + [pltpu.VMEM((2, ROWS * groups, chunk), f32)] * 2
        + [pltpu.VMEM((ROWS * groups, chunk), bf16)] * 2,
        compiler_params=PARAMS,
        name="likelihood",
    )(counts_t, hidden, rows, share, weights, *gene_tables)


def frequency_kernel(
    slopes_ref,
    hidden_ref,
    rows_ref,
    pull_ref,
    share_ref,
    other_ref,
    weight_ref,
    second_ref,
    dropout_ref,
    theta_ref,
    scale_ref,
    grad_hidden_ref,
    grad_weight_ref,
    genes_ref,
    long_ref,
    even_ref,
    odd_ref,
    even_grad_ref,
    odd_grad_ref,
    grad_bias_ref,
    *,
    genes,
    chunk,
):
    full, groups, tail = split_rows(genes)
    block = ROWS * groups
    blocks = full // groups
    size = weight_ref.shape[1]
    width = hidden_ref.shape[0]
    values, grads = (even_ref, odd_ref), (even_grad_ref, odd_grad_ref)

    @pl.when(pl.program_id(0) == 0)
    def _():
        grad_weight_ref[0] = jnp.zeros((size, LANES), f32)
        grad_weight_ref[1] = second_ref[...]
        grad_bias_ref[...] = jnp.zeros_like(grad_bias_ref)

    fill_hidden(long_ref, hidden_ref, rows_ref[0:1, :])
    pieces = logit_pieces(1, chunk)
    share = share_ref[...]
    pulled = pull_ref[0:1, :] * share

    def logits(i, rows, size, which):
        for _, columns in which:
            values[i][0:size, columns] = jnp.dot(
                weight_ref[0, rows, :], long_ref[:, columns], preferred_element_type=f32
            )

    def group(buffer, held, span):
        exponent = jnp.exp2(values[buffer][held, :] * (1.0 / ln2))
        grad = slopes_ref.at[span][held, :] * share - exponent * pulled
        grads[buffer][held, :] = grad.astype(bf16)
        grad_bias_ref.at[span][held, :] += fold_lanes(grad)

    def terms(buffer, number, carry, beside):
        span = pl.ds(pl.multiple_of(number * block, ROWS), block)
        for i in range(groups):
            for act in beside[i::groups]:
                act()
            group(buffer, slice(i * ROWS, (i + 1) * ROWS), span)
        return carry

    def back(i, rows, size):
        grad = grads[i][0:size, :]
        grad_weight_ref[0, rows, :] += lax.dot_general(
            grad, hidden_ref[...], (((1,), (1,)), ((), ())), preferred_element_type=f32
        )
        grad_hidden_ref[...] += lax.dot_general(
            weight_ref[0, rows, 0:width],
            grad,
            (((0,), (0,)), ((), ())),
            preferred_element_type=f32,
        )

    grad_hidden_ref[...] = other_ref[...]
    odd_grad_ref[...] = jnp.zeros_like(odd_grad_ref)
    sweep(blocks, block, groups, pieces, logits, terms, back, 0)
    if tail:
        rows = pl.ds(full * ROWS, ROWS)
        logits(1, rows, ROWS, pieces)
        group(1, slice(0, ROWS), rows)
        back(1, rows, ROWS)

    @pl.when(pl.program_id(0) == pl.num_programs(0) - 1)
    def _():
        ones = jnp.ones((8, LANES), f32)
        parts = (grad_bias_ref[...], dropout_ref[...], theta_ref[...] * scale_ref[...])
        for i, values in enumerate(parts):
            genes_ref[i : i + 1, :] = exact(ones, values, 1, 1)[0:1]
        genes_ref[3:4, :] = jnp.zeros((1, size), f32)


def frequency(slopes, hidden, rows, pull, share, other, weights, second, dropout, theta, scale, genes):
    size, cells = slopes.shape
    width = hidden.shape[0]
    chunk = pick_chunk(cells, 512)
    groups = split_rows(genes)[1]
    row = column_blocks(1, chunk)
    wide = column_blocks(width, chunk)
    return pl.pallas_call(
        functools.partial(frequency_kernel, genes=genes, chunk=chunk),
        grid=(cells // chunk,),
        in_specs=[column_blocks(size, chunk), wide, column_blocks(rows.shape[0], chunk)]
        + [column_blocks(2, chunk), row, wide, whole(weights)]
        + [whole(a) for a in (second, dropout, theta, scale)],
        out_specs=[
            wide,
            pl.BlockSpec((2, size, LANES), lambda i: (0, 0, 0)),
            pl.BlockSpec((4, size), lambda i: (0, 0)),
        ],
        out_shape=[
            jax.ShapeDtypeStruct((width, cells), f32),
            jax.ShapeDtypeStruct((2, size, LANES), f32),
            jax.ShapeDtypeStruct((4, size), f32),
        ],
        scratch_shapes=[pltpu.VMEM((HOT_DEPTH, chunk), bf16)]
        + [pltpu.VMEM((ROWS * groups, chunk), f32)] * 2
        + [pltpu.VMEM((ROWS * groups, chunk), bf16)] * 2
        + [pltpu.VMEM((size, LANES), f32)],
        compiler_params=PARAMS,
        name="frequency",
    )(slopes, hidden, rows, pull, share, other, weights, second, dropout, theta, scale)


def encoder_back_kernel(counts_ref, grad_ref, weight_ref, input_ref, weight_grad_ref):
    inputs = jnp.log(counts_ref[...].astype(f32) + 1.0).astype(bf16)
    weight_grad_ref[...] = lax.dot_general(
        inputs, grad_ref[...], (((1,), (1,)), ((), ())), preferred_element_type=f32
    )
    input_ref[...] = jnp.dot(
        weight_ref[...].astype(bf16), grad_ref[...], preferred_element_type=f32
    )


def encoder_back(counts_t, grad, weight):
    genes, cells = counts_t.shape
    width = grad.shape[0]
    block = LANES
    return pl.pallas_call(
        encoder_back_kernel,
        grid=(pl.cdiv(genes, block),),
        in_specs=[
            pl.BlockSpec((block, cells), lambda i: (i, 0)),
            whole(grad),
            pl.BlockSpec((block, width), lambda i: (i, 0)),
        ],
        out_specs=[
            pl.BlockSpec((block, cells), lambda i: (i, 0)),
            pl.BlockSpec((block, width), lambda i: (i, 0)),
        ],
        out_shape=[
            jax.ShapeDtypeStruct((genes, cells), f32),
            jax.ShapeDtypeStruct((-(-genes // 32) * 32, width), f32),
        ],
        compiler_params=PARAMS,
        name="encoder_back",
    )(counts_t, grad, weight)


def local(
    counts,
    batch_index,
    valid_mask,
    noise_draw,
    encoder_weight,
    output_weight,
    gene_vectors,
    batch_shift,
    layer_norm_params,
    head_weight,
    head_bias,
    decoder_input,
    encoder_weight_momentum,
    output_weight_momentum,
    gene_vectors_momentum,
    batch_shift_momentum,
    norm_params_momentum,
    head_weight_momentum,
    head_bias_momentum,
    decoder_input_momentum,
    encoder_weight_average,
    output_weight_average,
    gene_vectors_average,
    batch_shift_average,
    norm_params_average,
    head_weight_average,
    head_bias_average,
    decoder_input_average,
):
    cells, genes = counts.shape
    gene_devices = lax.axis_size("gene")
    genes_all = genes * gene_devices
    latent = head_bias.shape[0] // 2
    batches = batch_shift.shape[0]

    def by_gene(array):
        return jnp.transpose(array, (2, 0, 1)).reshape(2 * genes, -1)

    counts_t = counts.T
    output_rows = by_gene(output_weight)
    weights, *gene_tables = prepare(output_rows, gene_vectors, genes)

    pad = 16
    heads_t = jnp.pad(head_weight.T.reshape(2, latent, -1), ((0, 0), (0, pad - latent), (0, 0)))
    bias_row = jnp.pad(head_bias.reshape(2, latent), ((0, 0), (0, pad - latent))).reshape(1, -1)
    bias_row = jnp.pad(bias_row, ((0, 0), (0, LANES - 2 * pad)))
    pack = jnp.concatenate(
        [
            layer_norm_params,
            bias_row,
            jnp.zeros((3, LANES), f32),
            decoder_input[:latent],
            jnp.zeros((pad - latent, LANES), f32),
            decoder_input[latent:],
            heads_t.reshape(2 * pad, -1),
            batch_shift,
        ],
        axis=0,
    )
    index, valid, noise = batch_index[None, :], valid_mask[None, :], noise_draw.T

    encoded = encode(counts_t, encoder_weight)
    hidden2, centered2, sample, share, stats, centered1, heads, rest_rows = middle(
        encoded, index, valid, noise, pack, batches, pad, genes_all
    )
    rows = combine_tops(totals(hidden2, weights, genes), rest_rows)
    slopes, sums, grad_hidden2, grad_out1, grad_bias1, grad_theta = likelihood(
        counts_t, hidden2, rows, share, weights, gene_tables
    )
    pull = combine_sums(sums, rows, rest_rows, valid, genes_all)
    cell_loss = pull[1]

    grad_hidden2, grad_out, grad_genes = frequency(
        slopes,
        hidden2,
        rows,
        pull,
        share,
        grad_hidden2,
        weights,
        grad_out1,
        grad_bias1,
        grad_theta,
        gene_tables[0],
        genes,
    )
    grad_pre16, small, norm_rows, grad_out, grad_genes = middle_back(
        grad_hidden2,
        centered2,
        sample,
        index,
        valid,
        noise,
        pack,
        stats,
        centered1,
        heads,
        grad_out,
        grad_genes,
        batches,
    )
    input_grad, grad_encoder = encoder_back(counts_t, grad_pre16, encoder_weight)
    grad_encoder, small = last_sums(grad_encoder, small)
    depth = pad + batches
    grad_mixing = jnp.concatenate([small[:latent], small[pad:depth]], axis=0)
    grad_heads = small[depth : depth + 2 * pad].reshape(2, pad, -1)[:, :latent]
    grad_heads = grad_heads.reshape(2 * latent, -1).T
    grad_head_bias = jnp.sum(small[depth + 2 * pad : depth + 4 * pad], axis=1)
    grad_head_bias = grad_head_bias.reshape(2, pad)[:, :latent].reshape(-1)
    grad_shift = small[depth + 4 * pad :]

    updated = update(
        (encoder_weight, encoder_weight_momentum, encoder_weight_average),
        grad_encoder,
        (output_rows, by_gene(output_weight_momentum), by_gene(output_weight_average)),
        grad_out,
    )
    encoder_new = updated[:3]
    output_new = [jnp.transpose(a.reshape(genes, 2, -1), (1, 2, 0)) for a in updated[3:]]
    vectors = (gene_vectors, batch_shift, layer_norm_params, head_weight, head_bias, decoder_input)
    momenta = (
        gene_vectors_momentum,
        batch_shift_momentum,
        norm_params_momentum,
        head_weight_momentum,
        head_bias_momentum,
        decoder_input_momentum,
    )
    averages = (
        gene_vectors_average,
        batch_shift_average,
        norm_params_average,
        head_weight_average,
        head_bias_average,
        decoder_input_average,
    )
    grads = (
        grad_genes[:3, :genes],
        grad_shift,
        norm_rows[:4],
        grad_heads,
        grad_head_bias,
        grad_mixing,
    )
    small_new = zip(
        *[nesterov(*group) for group in zip(vectors, momenta, averages, grads, step_rates[2:])]
    )
    results = []
    for i, rest in enumerate(small_new):
        results += [encoder_new[i], output_new[i], *rest]
    return (cell_loss, input_grad.T, *results)


def solution(mesh):
    cells, genes = P("cell"), P("gene", None)
    weight_specs = (genes, P(None, None, "gene"), P(None, "gene"), P(), P(), P(), P(), P())
    return jax.shard_map(
        local,
        mesh=mesh,
        in_specs=(P("cell", "gene"), cells, cells, P("cell", None)) + weight_specs * 3,
        out_specs=(cells, P("cell", "gene")) + weight_specs * 3,
        check_vma=False,
    )
```

```python
import functools

import jax
import jax.numpy as jnp
from jax import lax
from jax.experimental import pallas as pl
from jax.experimental.pallas import tpu as pltpu
from jax.sharding import PartitionSpec as P

momentum_decay = 0.9
average_decay = 0.99
norm_epsilon = 0.001
rate_epsilon = 1e-08
step_rates = (110.0, 46000.0, 300000.0, 70000.0, 13000.0, 3700.0, 7600.0, 8000.0)
ln2 = 0.6931471805599453
f32 = jnp.float32
bf16 = jnp.bfloat16
LANES = 128
ROWS = 16
WIDE = 2 * LANES
HOT_DEPTH = 2 * LANES
PARAMS = pltpu.CompilerParams(vmem_limit_bytes=60 << 20)
IN_VMEM = pl.BlockSpec(memory_space=pltpu.VMEM)
MESH = pl.DeviceIdType.MESH


def talking(number):
    return pltpu.CompilerParams(
        collective_id=number, has_side_effects=True, vmem_limit_bytes=60 << 20
    )


def nesterov(weight, momentum, average, grad, rate):
    moment = momentum_decay * momentum + grad
    fresh = weight - rate * (grad + momentum_decay * moment)
    return (fresh, moment, average_decay * average + (1.0 - average_decay) * fresh)


def whole(array):
    return pl.BlockSpec(array.shape, lambda i: (0,) * array.ndim)


def column_blocks(rows, chunk):
    return pl.BlockSpec((rows, chunk), lambda i: (0, i))


def split_rows(genes, most=13):
    full = genes // ROWS
    groups = max(d for d in range(1, most + 1) if full % d == 0)
    return full, groups, genes - full * ROWS


def padded(genes):
    return -(-genes // ROWS) * ROWS


def pick_chunk(cells, most):
    chunk = LANES
    while chunk * 2 <= most and cells % (chunk * 2) == 0:
        chunk *= 2
    return chunk


def tail_rows(ref, start, stop, columns, dtype):
    piece = ref[start:stop, columns]
    filler = jnp.zeros((ROWS - (stop - start), piece.shape[1]), dtype)
    return jnp.concatenate([piece, filler], axis=0)


class Team:
    def __init__(self, axis):
        self.size, self.me = lax.axis_size(axis), lax.axis_index(axis)
        self.gene, self.cell = lax.axis_index("gene"), lax.axis_index("cell")
        self.axis = axis

    def place(self, other):
        return (other, self.cell) if self.axis == "gene" else (self.gene, other)

    def others(self, act):
        def one(step, carry):
            other = lax.rem(self.me + step, self.size)
            act(other, self.place(other))
            return carry

        lax.fori_loop(1, self.size, one, 0)

    def send(self, source, target, sems):
        def act(other, place):
            pltpu.make_async_remote_copy(
                src_ref=source(other),
                dst_ref=target,
                send_sem=sems.at[0],
                recv_sem=sems.at[1],
                device_id=place,
                device_id_type=MESH,
            ).start()

        self.others(act)


def greet(*teams):
    barrier = pltpu.get_barrier_semaphore()

    def act(other, place):
        pl.semaphore_signal(barrier, inc=1, device_id=place, device_id_type=MESH)

    for team in teams:
        team.others(act)
    pl.semaphore_wait(barrier, sum(team.size - 1 for team in teams))


def await_bytes(ref, sem):
    pltpu.make_async_copy(ref, ref, sem).wait()


def fold_lanes(values):
    return sum(values[:, j : j + LANES] for j in range(0, values.shape[1], LANES))


def row_sums(folded):
    return jnp.sum(jnp.transpose(folded), axis=0, keepdims=True)


def box_sum(box):
    def add(i, total):
        return total + box[i]

    return lax.fori_loop(1, box.shape[0], add, box[0])


def spread_box(team, box, value, sems):
    box[team.me] = value
    team.send(lambda other: box.at[team.me], box.at[team.me], sems)
    others = box.at[pl.ds(0, team.size - 1)]

    def finish():
        await_bytes(others, sems.at[0])
        await_bytes(others, sems.at[1])
        return box_sum(box)

    return finish


def row_boxes():
    shapes = [(lax.axis_size(axis), 8, LANES) for axis in ("cell", "gene")]
    return [pltpu.VMEM(shape, f32) for shape in shapes * 2]


def eight_rows(rows):
    filler = jnp.zeros((8 - len(rows), LANES), f32)
    return jnp.concatenate([*rows, filler], axis=0) if len(rows) < 8 else jnp.concatenate(rows, 0)


def columns_of(rows):
    turned = jnp.transpose(jnp.concatenate([eight_rows(rows), jnp.zeros((120, LANES), f32)], 0))
    return [turned[:, i : i + 1] for i in range(len(rows))]


def exact(left, right, left_dim, right_dim):
    return lax.dot_general(
        left,
        right,
        (((left_dim,), (right_dim,)), ((), ())),
        precision=lax.Precision.HIGHEST,
        preferred_element_type=f32,
    )


def hot_rows(index, batches):
    rows = lax.broadcasted_iota(jnp.int32, (batches, index.shape[1]), 0)
    return jnp.where(rows == index, 1.0, 0.0)


def sigmoid(value):
    return 1.0 / (1.0 + jnp.exp(-value))


def slope_of(value):
    sigma = sigmoid(value)
    return sigma * (1.0 + value * (1.0 - sigma))


def pack_layout(latent_pad, batches):
    mixing = slice(8, 8 + latent_pad + batches)
    heads = slice(mixing.stop, mixing.stop + 2 * latent_pad)
    return mixing, heads, slice(heads.stop, heads.stop + batches)


def prepare_tables(number, genes, output_ref, vectors_ref, weights_ref, tables):
    theta_ref, log_ref, slope_ref, gammas_ref, digammas_ref = tables
    lane = lax.broadcasted_iota(jnp.int32, (LANES, LANES), 1)
    below = lax.broadcasted_iota(jnp.int32, (LANES, LANES), 0)
    upper = jnp.where(below < lane, 1.0, 0.0)
    step = lane.astype(f32)
    block = theta_ref.shape[0]
    for at in range(0, block, LANES):
        here = slice(at, at + LANES)
        turned = jnp.transpose(
            jnp.concatenate([vectors_ref[:, here], jnp.zeros((LANES - 3, LANES), f32)], axis=0)
        )
        inside = number * block + at + below[:, 0:1] < genes
        for k in range(2):
            weight = output_ref[pl.ds(2 * at + k, LANES, stride=2), :]
            weights_ref[k, here, 0:LANES] = jnp.where(inside, weight, 0.0).astype(bf16)
            bias = jnp.where(inside, turned[:, k : k + 1], 0.0 if k else -1e30)
            high = bias.astype(bf16).astype(f32)
            middle = (bias - high).astype(bf16).astype(f32)
            low = (bias - high - middle).astype(bf16).astype(f32)
            extra = jnp.where(lane == 0, high, jnp.where(lane == 1, middle, 0.0))
            extra = jnp.where(lane == 2, low, extra)
            if k == 0:
                extra = jnp.where((lane >= 3) & (lane < 6), 1.0, extra)
            weights_ref[k, here, LANES : 2 * LANES] = extra.astype(bf16)
        theta = jnp.where(inside, jnp.exp(turned[:, 2:3]), 1.0) + jnp.zeros((LANES, LANES), f32)
        log_theta = jnp.log2(theta + rate_epsilon)
        theta_ref[here, :] = theta
        log_ref[here, :] = log_theta
        slope_ref[here, :] = ln2 * log_theta + theta / (theta + rate_epsilon)
        climb = theta + step
        gammas_ref[here, :] = exact(jnp.log2(climb / (step + 1.0)), upper, 1, 0)
        digammas_ref[here, :] = exact(1.0 / climb, upper, 1, 0)


def encode_kernel(
    counts_ref,
    encoder_ref,
    output_ref,
    vectors_ref,
    out_ref,
    weights_ref,
    theta_ref,
    log_ref,
    slope_ref,
    gammas_ref,
    digammas_ref,
    inputs_ref,
    weight_ref,
    near_give,
    near_box,
    far_give,
    far_box,
    near_sems,
    far_sems,
    *,
    genes,
    table_blocks,
):
    slab = counts_ref.shape[1]
    full, _, tail = split_rows(genes)
    width = encoder_ref.shape[1]
    group = Team("gene")
    pairs = group.size // 2
    high, low = group.me // 2, lax.rem(group.me, 2)
    step = pl.program_id(0)
    turn = step // 2

    def place(high, low):
        return (2 * high + low, group.cell)

    def copy(source, target, sems, where):
        return pltpu.make_async_remote_copy(
            src_ref=source,
            dst_ref=target,
            send_sem=sems.at[0],
            recv_sem=sems.at[1],
            device_id=where,
            device_id_type=MESH,
        )

    @pl.when(step == 0)
    def _():
        barrier = pltpu.get_barrier_semaphore()
        pl.semaphore_signal(barrier, inc=1, device_id=place(high, 1 - low), device_id_type=MESH)
        for d in range(1, pairs):
            where = place(lax.rem(high + d, pairs), low)
            pl.semaphore_signal(barrier, inc=1, device_id=where, device_id_type=MESH)
        weight_ref[0 : full * ROWS, :] = encoder_ref[0 : full * ROWS, :].astype(bf16)
        if tail:
            weight_ref[full * ROWS :, :] = tail_rows(
                encoder_ref, full * ROWS, genes, slice(None), f32
            ).astype(bf16)
        pl.semaphore_wait(barrier, pairs)

    def part(ref):
        def rows16(counted, rows, total):
            inputs_ref[rows, :] = jnp.log(counted + 1.0).astype(bf16)
            return total + counted[:8] + counted[8:]

        def one(i, total):
            rows = pl.ds(pl.multiple_of(i * ROWS, ROWS), ROWS)
            return rows16(counts_ref[rows, :].astype(f32), rows, total)

        total = lax.fori_loop(0, full, one, jnp.zeros((8, slab), f32), unroll=4)
        if tail:
            rows = pl.ds(full * ROWS, ROWS)
            counted = tail_rows(counts_ref, full * ROWS, genes, slice(None), jnp.int32)
            total = rows16(counted.astype(f32), rows, total)
        ref[0:width, :] = lax.dot_general(
            weight_ref[...], inputs_ref[...], (((0,), (0,)), ((), ())), preferred_element_type=f32
        )
        row = lax.broadcasted_iota(jnp.int32, (8, slab), 0)
        ref[width : width + 8, :] = jnp.where(row == 0, jnp.sum(total, axis=0, keepdims=True), 0.0)

    def near_copy(i):
        return copy(near_give.at[i], near_box.at[i], near_sems.at[i], place(high, 1 - low))

    def far_copy(i):
        target = lax.rem(high + 1 + i, pairs)
        return copy(far_give.at[i], far_box.at[i], far_sems.at[i], place(target, low))

    tables = (theta_ref, log_ref, slope_ref, gammas_ref, digammas_ref)

    @pl.when(step < table_blocks)
    def _():
        prepare_tables(step, genes, output_ref, vectors_ref, weights_ref, tables)

    @pl.when(lax.rem(step, 2) == 0)
    def _():
        part(near_give.at[turn])
        near_copy(turn).start()

    @pl.when(lax.rem(step, 2) == 1)
    def _():
        part(out_ref)
        near_copy(turn).wait_recv()
        total = out_ref[...] + near_box[turn]

        @pl.when(turn < pairs - 1)
        def _():
            far_give[turn] = total
            far_copy(turn).start()

        @pl.when(turn == pairs - 1)
        def _():
            def gather(i, total):
                far_copy(i).wait_recv()
                return total + far_box[i]

            out_ref[...] = lax.fori_loop(0, pairs - 1, gather, total)

            def drain(i, carry):
                far_copy(i).wait_send()
                return carry

            lax.fori_loop(0, pairs - 1, drain, 0)

            def drain_near(i, carry):
                near_copy(i).wait_send()
                return carry

            lax.fori_loop(0, pairs, drain_near, 0)


def encode(counts_t, weight, output_rows, vectors):
    genes, cells = counts_t.shape
    devices = lax.axis_size("gene")
    pairs = devices // 2
    slab = cells // devices
    width = weight.shape[1]

    def slab_of(i):
        me = lax.axis_index("gene")
        low = lax.rem(me + 1 + i, 2)
        return (0, 2 * lax.rem(me // 2 + 1 + i // 2, pairs) + low)

    box = pltpu.VMEM((pairs, width + 8, slab), f32)
    size = padded(genes)
    block = LANES * pl.cdiv(pl.cdiv(size, LANES), devices)
    table_blocks = pl.cdiv(size, block)

    def table_of(i):
        return jnp.minimum(i, table_blocks - 1)

    table = pl.BlockSpec((block, LANES), lambda i: (table_of(i), 0))
    return pl.pallas_call(
        functools.partial(encode_kernel, genes=genes, table_blocks=table_blocks),
        grid=(devices,),
        in_specs=[
            pl.BlockSpec((genes, slab), slab_of),
            whole(weight),
            pl.BlockSpec((2 * block, LANES), lambda i: (table_of(i), 0)),
            pl.BlockSpec((3, block), lambda i: (0, table_of(i))),
        ],
        out_specs=[
            pl.BlockSpec((width + 8, slab), lambda i: (0, 0)),
            pl.BlockSpec((2, block, HOT_DEPTH), lambda i: (0, table_of(i), 0)),
        ]
        + [table] * 5,
        out_shape=[
            jax.ShapeDtypeStruct((width + 8, slab), f32),
            jax.ShapeDtypeStruct((2, size, HOT_DEPTH), bf16),
        ]
        + [jax.ShapeDtypeStruct((size, LANES), f32)] * 5,
        scratch_shapes=[
            pltpu.VMEM((padded(genes), slab), bf16),
            pltpu.VMEM((padded(genes), width), bf16),
            box,
            box,
            box,
            box,
            pltpu.SemaphoreType.DMA((pairs, 2)),
            pltpu.SemaphoreType.DMA((pairs, 2)),
        ],
        compiler_params=talking(6),
        name="encode",
    )(counts_t, weight, output_rows, vectors)


def middle_kernel(
    encoded_ref,
    index_ref,
    valid_ref,
    noise_ref,
    norms_ref,
    bias_ref,
    mixing_ref,
    head_ref,
    shift_ref,
    hidden_ref,
    centered_ref,
    sample_ref,
    share_ref,
    stats_ref,
    first_ref,
    heads_ref,
    rest_ref,
    pack_ref,
    box1,
    box2,
    box3,
    box4,
    sems1,
    sems2,
    sems3,
    sems4,
    sample_sems,
    *,
    batches,
    latent,
    genes_all,
):
    group, team = Team("gene"), Team("cell")
    width, slab = first_ref.shape
    cells = hidden_ref.shape[1]
    pad = sample_ref.shape[0]
    mixing_rows, heads_rows, shift_rows = pack_layout(pad, batches)
    pack_ref[...] = jnp.zeros_like(pack_ref)
    pack_ref[0:4, :] = norms_ref[...]
    pack_ref[4:5, 0:latent] = bias_ref[:, 0:latent]
    pack_ref[4:5, pad : pad + latent] = bias_ref[:, latent : 2 * latent]
    at = mixing_rows.start
    pack_ref[at : at + latent, :] = mixing_ref[0:latent, :]
    pack_ref[at + pad : at + pad + batches, :] = mixing_ref[latent:, :]
    at = heads_rows.start
    pack_ref[at : at + latent, :] = head_ref[0:latent, :]
    pack_ref[at + pad : at + pad + latent, :] = head_ref[latent:, :]
    pack_ref[shift_rows, :] = shift_ref[...]
    mixing = pack_ref[mixing_rows, :]

    def part(other):
        return pl.ds(pl.multiple_of(other * slab, LANES), slab)

    mine = part(group.me)
    greet(group, team)
    hot = hot_rows(index_ref[:, mine], batches)
    valid = valid_ref[:, mine].astype(f32)
    shift = exact(pack_ref[shift_rows, :], hot, 0, 0)
    gain1, bias1, gain2, bias2, head_bias = columns_of([pack_ref[i : i + 1, :] for i in range(5)])
    total = encoded_ref[...]
    rest_ref[0:1, :] = total[width : width + 1, :]
    pre1 = total[0:width, :] + shift

    weighed = valid * pre1
    rows = [
        row_sums(fold_lanes(weighed)),
        row_sums(fold_lanes(weighed * pre1)),
        jnp.broadcast_to(jnp.sum(valid, axis=1, keepdims=True), (1, LANES)),
    ]
    sums = spread_box(team, box1, eight_rows(rows), sems1)()
    sums = spread_box(group, box2, sums, sems2)()
    count = jnp.maximum(sums[2:3], 1.0)
    mean1 = sums[0:1] / count
    inverse1 = lax.rsqrt(sums[1:2] / count - mean1 * mean1 + norm_epsilon)
    mean_col, inverse_col = columns_of([mean1, inverse1])
    centered1 = (pre1 - mean_col) * inverse_col
    first_ref[...] = centered1
    normed1 = centered1 * gain1 + bias1
    hidden1 = normed1 * sigmoid(normed1)
    heads = exact(pack_ref[heads_rows, :], hidden1, 1, 0) + head_bias[0 : 2 * pad]
    heads_ref[...] = heads
    mean_z, log_var = heads[0:pad], heads[pad : 2 * pad]
    noise = jnp.concatenate([noise_ref[:, mine], jnp.zeros((pad - latent, slab), f32)], axis=0)
    sample = mean_z + jnp.exp(0.5 * log_var) * noise
    rest_ref[1:2, :] = 0.5 * jnp.sum(
        mean_z * mean_z + jnp.exp(log_var) - log_var - 1.0, axis=0, keepdims=True
    )
    sample_ref[:, mine] = sample
    group.send(lambda other: sample_ref.at[:, mine], sample_ref.at[:, mine], sample_sems)
    pre2 = exact(mixing, jnp.concatenate([sample, hot], axis=0), 0, 0)
    weighed = valid * pre2
    rows = [row_sums(fold_lanes(weighed)), row_sums(fold_lanes(weighed * pre2))]
    sums = spread_box(team, box3, eight_rows(rows), sems3)()
    finish = spread_box(group, box4, sums, sems4)
    scale = 1.0 / (count * genes_all)
    share_ref[...] = valid_ref[...].astype(f32) * scale[:, 0:1]
    sums = finish()
    mean2 = sums[0:1] / count
    inverse2 = lax.rsqrt(sums[1:2] / count - mean2 * mean2 + norm_epsilon)
    stats_ref[...] = eight_rows([inverse1, inverse2, count, scale])
    mean_col, inverse_col = columns_of([mean2, inverse2])
    others = sample_ref.at[:, pl.ds(0, (group.size - 1) * slab)]
    await_bytes(others, sample_sems.at[0])
    await_bytes(others, sample_sems.at[1])
    piece = pick_chunk(cells, 512)

    def decode(i, carry):
        columns = pl.ds(pl.multiple_of(i * piece, LANES), piece)
        mixed = jnp.concatenate(
            [sample_ref[:, columns], hot_rows(index_ref[:, columns], batches)], axis=0
        )
        centered = (exact(mixing, mixed, 0, 0) - mean_col) * inverse_col
        centered_ref[:, columns] = centered
        normed = centered * gain2 + bias2
        hidden_ref[:, columns] = (normed * sigmoid(normed)).astype(bf16)
        return carry

    lax.fori_loop(0, cells // piece, decode, 0)


def middle(encoded, index, valid, noise, small_weights, batches, pad, genes_all):
    cells = index.shape[1]
    width = LANES
    genes_axis = lax.axis_size("gene")
    slab = cells // genes_axis
    return pl.pallas_call(
        functools.partial(
            middle_kernel, batches=batches, latent=noise.shape[0], genes_all=genes_all
        ),
        out_shape=[
            jax.ShapeDtypeStruct((width, cells), bf16),
            jax.ShapeDtypeStruct((width, cells), f32),
            jax.ShapeDtypeStruct((pad, cells), f32),
            jax.ShapeDtypeStruct((1, cells), f32),
            jax.ShapeDtypeStruct((8, LANES), f32),
            jax.ShapeDtypeStruct((width, slab), f32),
            jax.ShapeDtypeStruct((2 * pad, slab), f32),
            jax.ShapeDtypeStruct((2, slab), f32),
            jax.ShapeDtypeStruct((8 + 3 * pad + 2 * batches, LANES), f32),
        ],
        in_specs=[IN_VMEM] * 9,
        out_specs=[IN_VMEM] * 9,
        scratch_shapes=row_boxes() + [pltpu.SemaphoreType.DMA((2,))] * 5,
        compiler_params=talking(1),
        name="middle",
    )(encoded, index, valid, noise, *small_weights)


def tops_kernel(tops_ref, rest_ref, out_ref, box, sems, back_sems):
    group = Team("gene")
    slab = rest_ref.shape[1]

    def part(other):
        return pl.ds(pl.multiple_of(other * slab, LANES), slab)

    mine = part(group.me)
    greet(group)
    group.send(lambda other: tops_ref.at[:, part(other)], box.at[group.me], sems)
    box[group.me] = tops_ref[:, mine]
    others = box.at[pl.ds(0, group.size - 1)]
    await_bytes(others, sems.at[0])
    await_bytes(others, sems.at[1])

    def highest(i, best):
        return jnp.maximum(best, box[i, 0:1, :])

    top = lax.fori_loop(1, group.size, highest, box[0, 0:1, :])

    def add(i, total):
        return total + box[i, 1:2, :] * jnp.exp(box[i, 0:1, :] - top)

    total = lax.fori_loop(0, group.size, add, jnp.zeros_like(top))
    inverse = 1.0 / total
    out_ref[0:1, mine] = top
    out_ref[1:2, mine] = rest_ref[0:1, :] * inverse
    out_ref[2:3, mine] = inverse
    out_ref[3:4, mine] = inverse
    group.send(lambda other: out_ref.at[:, mine], out_ref.at[:, mine], back_sems)
    others = out_ref.at[:, pl.ds(0, (group.size - 1) * slab)]
    await_bytes(others, back_sems.at[0])
    await_bytes(others, back_sems.at[1])


def combine_tops(tops, rest):
    group = lax.axis_size("gene")
    slab = rest.shape[1]
    return pl.pallas_call(
        tops_kernel,
        out_shape=jax.ShapeDtypeStruct((4, tops.shape[1]), f32),
        in_specs=[IN_VMEM] * 2,
        out_specs=IN_VMEM,
        scratch_shapes=[pltpu.VMEM((group, 2, slab), f32)] + [pltpu.SemaphoreType.DMA((2,))] * 2,
        compiler_params=talking(2),
        name="combine_tops",
    )(tops, rest)


def sums_kernel(sums_ref, rows_ref, rest_ref, valid_ref, out_ref, box, sems, back_sems, *, genes_all):
    group = Team("gene")
    slab = rest_ref.shape[1]

    def part(other):
        return pl.ds(pl.multiple_of(other * slab, LANES), slab)

    mine = part(group.me)
    greet(group)
    group.send(lambda other: sums_ref.at[:, part(other)], box.at[group.me], sems)
    box[group.me] = sums_ref[:, mine]
    others = box.at[pl.ds(0, group.size - 1)]
    await_bytes(others, sems.at[0])
    await_bytes(others, sems.at[1])
    total = box_sum(box)
    out_ref[0:1, mine] = total[0:1] * rows_ref[2:3, mine]
    out_ref[1:2, mine] = (
        valid_ref[:, mine].astype(f32) * (total[1:2] + rest_ref[1:2, :]) / genes_all
    )
    group.send(lambda other: out_ref.at[:, mine], out_ref.at[:, mine], back_sems)
    others = out_ref.at[:, pl.ds(0, (group.size - 1) * slab)]
    await_bytes(others, back_sems.at[0])
    await_bytes(others, back_sems.at[1])


def combine_sums(sums, rows, rest, valid, genes_all):
    group = lax.axis_size("gene")
    slab = rest.shape[1]
    return pl.pallas_call(
        functools.partial(sums_kernel, genes_all=genes_all),
        out_shape=jax.ShapeDtypeStruct((2, sums.shape[1]), f32),
        in_specs=[IN_VMEM] * 4,
        out_specs=IN_VMEM,
        scratch_shapes=[pltpu.VMEM((group, 2, slab), f32)] + [pltpu.SemaphoreType.DMA((2,))] * 2,
        compiler_params=talking(3),
        name="combine_sums",
    )(sums, rows, rest, valid)


def middle_back_kernel(
    grad_ref,
    centered_ref,
    sample_ref,
    index_ref,
    valid_ref,
    noise_ref,
    pack_ref,
    stats_ref,
    first_ref,
    heads_ref,
    output_ref,
    genes_ref,
    grad16_ref,
    small_ref,
    norms_ref,
    output_sum_ref,
    genes_sum_ref,
    part_ref,
    slab_box,
    box1,
    box2,
    box3,
    box4,
    output_box,
    half_box,
    half_give,
    genes_box,
    slab_sems,
    sems1,
    sems2,
    sems3,
    sems4,
    grad_sems,
    output_sems,
    genes_sems,
    *,
    batches,
    latent,
):
    group, team = Team("gene"), Team("cell")
    cell = lax.axis_index("cell")
    bit, near, far = lax.rem(cell, 2), cell + 1 - 2 * lax.rem(cell, 2), lax.rem(cell + 2, 4)
    half = output_ref.shape[1] // 2

    def swap(source, target, other, number):
        copy = pltpu.make_async_remote_copy(
            src_ref=source,
            dst_ref=target,
            send_sem=output_sems.at[number, 0],
            recv_sem=output_sems.at[number, 1],
            device_id=(group.gene, other),
            device_id_type=MESH,
        )
        copy.start()
        return copy

    def rows_of(number):
        return pl.ds(pl.multiple_of(number * half, 8), half)
    width, slab = first_ref.shape
    cells = grad_ref.shape[1]
    pad = sample_ref.shape[0]
    mixing_rows, heads_rows, _ = pack_layout(pad, batches)
    depth = pad + batches

    def part(other):
        return pl.ds(pl.multiple_of(other * slab, LANES), slab)

    mine = part(group.me)
    greet(group, team)
    swap1 = swap(output_ref.at[1 - bit], output_box, near, 0)
    genes_box[cell] = genes_ref[...]

    def tell(step, carry):
        other = lax.rem(cell + step, team.size)
        pltpu.make_async_remote_copy(
            src_ref=genes_ref,
            dst_ref=genes_box.at[cell],
            send_sem=genes_sems.at[0],
            recv_sem=genes_sems.at[1],
            device_id=(group.gene, other),
            device_id_type=MESH,
        ).start()
        return carry

    lax.fori_loop(1, team.size, tell, 0)
    inverse1, inverse2 = stats_ref[0:1, :], stats_ref[1:2, :]
    count, scale = stats_ref[2:3, 0:1], stats_ref[3:4, 0:1]
    factor2 = inverse2 * pack_ref[2:3, :]
    gain1, bias1, gain2, bias2, factor1 = columns_of(
        [pack_ref[i : i + 1, :] for i in range(4)] + [inverse1 * pack_ref[0:1, :]]
    )
    latent_rows = pack_ref[8 : 8 + pad, :] * factor2
    piece = pick_chunk(cells, 512)

    def gather(i, carry):
        gains, shifts, products = carry
        columns = pl.ds(pl.multiple_of(i * piece, LANES), piece)
        centered = centered_ref[:, columns]
        grad = grad_ref[:, columns] * slope_of(centered * gain2 + bias2)
        part_ref[:, columns] = exact(latent_rows, grad, 1, 0)
        mixed = jnp.concatenate(
            [sample_ref[:, columns], hot_rows(index_ref[:, columns], batches)], axis=0
        )
        return (
            gains + fold_lanes(grad * centered),
            shifts + fold_lanes(grad),
            products + exact(mixed, grad, 1, 1),
        )

    zeros = jnp.zeros((width, LANES), f32)
    gains, shifts, products = lax.fori_loop(
        0, cells // piece, gather, (zeros, zeros, jnp.zeros((depth, width), f32))
    )

    finish = spread_box(team, box1, eight_rows([row_sums(gains), row_sums(shifts)]), sems1)
    group.send(lambda other: part_ref.at[:, part(other)], slab_box.at[group.me], slab_sems)
    slab_box[group.me] = part_ref[:, mine]
    finish = spread_box(group, box2, finish(), sems2)
    swap1.wait()
    own, given = rows_of(far // 2), rows_of(cell // 2)
    half_give[...] = output_ref[bit, own] + output_box[own]
    swap2 = swap(half_give, half_box, far, 1)
    output_sum_ref[bit, given] = output_ref[bit, given] + output_box[given]
    hot = hot_rows(index_ref[:, mine], batches)
    valid = valid_ref[:, mine].astype(f32)
    mixed = valid * jnp.concatenate([sample_ref[:, mine], hot], axis=0)
    centered2 = centered_ref[:, mine]
    share = valid / count
    mixed_sum = jnp.sum(mixed, axis=1, keepdims=True)
    mixed_product = exact(mixed, centered2, 1, 1)
    noise = jnp.concatenate([noise_ref[:, mine], jnp.zeros((pad - latent, slab), f32)], axis=0)
    mean_z, log_var = heads_ref[0:pad, :], heads_ref[pad : 2 * pad, :]
    log_factor = 0.5 * noise * jnp.exp(0.5 * log_var)
    scaled = valid * scale
    grad_log_own = scaled * (jnp.exp(log_var) - 1.0) * 0.5
    centered1 = first_ref[...]
    normed1 = centered1 * gain1 + bias1
    sigma1 = sigmoid(normed1)
    hidden1 = normed1 * sigma1
    slope1 = sigma1 * (1.0 + normed1 * (1.0 - sigma1))

    sums = finish()
    gain2_grad, shift2_grad = sums[0:1], sums[1:2]
    small_ref[0:depth, :] = factor2 * (
        products - (mixed_sum * shift2_grad + mixed_product * gain2_grad) / count
    )
    gain_col, shift_col = columns_of([gain2_grad, shift2_grad])
    pulled = exact(latent_rows, shift_col + centered2 * gain_col, 1, 0)
    others = slab_box.at[pl.ds(0, group.size - 1)]
    await_bytes(others, slab_sems.at[0])
    await_bytes(others, slab_sems.at[1])
    grad_sample = box_sum(slab_box) - share * pulled
    grad_heads = jnp.concatenate(
        [grad_sample + scaled * mean_z, grad_sample * log_factor + grad_log_own], axis=0
    )
    grad_normed1 = exact(pack_ref[heads_rows, :], grad_heads, 0, 0) * slope1
    rows = [row_sums(fold_lanes(grad_normed1 * centered1)), row_sums(fold_lanes(grad_normed1))]
    finish = spread_box(group, box4, spread_box(team, box3, eight_rows(rows), sems3)(), sems4)
    swap2.wait()
    output_sum_ref[bit, given] = output_sum_ref[bit, given] + half_box[...]
    swap3 = swap(output_sum_ref.at[bit, given], output_sum_ref.at[bit, given], far, 2)
    small_ref[depth : depth + 2 * pad, :] = exact(grad_heads, hidden1, 1, 1)
    small_ref[depth + 2 * pad : depth + 4 * pad, :] = fold_lanes(grad_heads)
    sums = finish()
    gain1_grad, shift1_grad = sums[0:1], sums[1:2]
    norms_ref[...] = eight_rows([gain1_grad, shift1_grad, gain2_grad, shift2_grad])
    gain_col, shift_col = columns_of([gain1_grad, shift1_grad])
    grad_pre1 = factor1 * (grad_normed1 - share * (shift_col + centered1 * gain_col))
    grad16_ref[:, mine] = grad_pre1.astype(bf16)
    group.send(lambda other: grad16_ref.at[:, mine], grad16_ref.at[:, mine], grad_sems)
    small_ref[depth + 4 * pad :, :] = exact(hot, grad_pre1, 1, 1)
    others = genes_box.at[pl.ds(0, team.size - 1)]
    await_bytes(others, genes_sems.at[0])
    await_bytes(others, genes_sems.at[1])
    genes_sum_ref[...] = box_sum(genes_box)
    swap3.wait()
    swap4 = swap(output_sum_ref.at[bit], output_sum_ref.at[bit], near, 3)
    swap4.wait()
    others = grad16_ref.at[:, pl.ds(0, (group.size - 1) * slab)]
    await_bytes(others, grad_sems.at[0])
    await_bytes(others, grad_sems.at[1])


def middle_back(
    grad,
    centered,
    sample,
    index,
    valid,
    noise,
    pack,
    stats,
    first,
    heads,
    output_grad,
    genes_grad,
    batches,
):
    cells = index.shape[1]
    width, slab = first.shape
    pad = sample.shape[0]
    genes_axis = lax.axis_size("gene")
    return pl.pallas_call(
        functools.partial(middle_back_kernel, batches=batches, latent=noise.shape[0]),
        out_shape=[
            jax.ShapeDtypeStruct((width, cells), bf16),
            jax.ShapeDtypeStruct((5 * pad + 2 * batches, LANES), f32),
            jax.ShapeDtypeStruct((8, LANES), f32),
            jax.ShapeDtypeStruct(output_grad.shape, f32),
            jax.ShapeDtypeStruct(genes_grad.shape, f32),
        ],
        in_specs=[IN_VMEM] * 12,
        out_specs=[IN_VMEM] * 5,
        scratch_shapes=[
            pltpu.VMEM((pad, cells), f32),
            pltpu.VMEM((genes_axis, pad, slab), f32),
            *row_boxes(),
            pltpu.VMEM(output_grad.shape[1:], f32),
            pltpu.VMEM((output_grad.shape[1] // 2, LANES), f32),
            pltpu.VMEM((output_grad.shape[1] // 2, LANES), f32),
            pltpu.VMEM((lax.axis_size("cell"), *genes_grad.shape), f32),
        ]
        + [pltpu.SemaphoreType.DMA((2,))] * 6
        + [pltpu.SemaphoreType.DMA((4, 2)), pltpu.SemaphoreType.DMA((2,))],
        compiler_params=talking(4),
        name="middle_back",
    )(
        grad,
        centered,
        sample,
        index,
        valid,
        noise,
        pack,
        stats,
        first,
        heads,
        output_grad,
        genes_grad,
    )


def encoder_grad_kernel(
    counts_ref,
    grad_ref,
    small_ref,
    sum_ref,
    total_ref,
    near_give,
    near_box,
    far_give,
    far_box,
    whole_box,
    small_box,
    near_sems,
    far_sems,
    last_sems,
    small_sems,
):
    gene, cell = lax.axis_index("gene"), lax.axis_index("cell")
    bit, high = lax.rem(cell, 2), cell // 2
    near, far = cell + 1 - 2 * bit, lax.rem(cell + 2, 4)
    quarter, cells = counts_ref.shape
    step = pl.program_id(0)

    def copy(source, target, sems, where):
        return pltpu.make_async_remote_copy(
            src_ref=source,
            dst_ref=target,
            send_sem=sems.at[0],
            recv_sem=sems.at[1],
            device_id=where,
            device_id_type=MESH,
        )

    rounds = [(gene, near), (gene, far)]
    size = 1
    while size < lax.axis_size("gene"):
        rounds.append((gene + size - 2 * size * lax.rem(gene // size, 2), cell))
        size *= 2

    def small_copy(number):
        source = small_ref if number == 0 else small_box.at[1, number - 1]
        return copy(source, small_box.at[0, number], small_sems.at[number], rounds[number])

    def small_end(number):
        small_copy(number).wait()
        source = small_ref[...] if number == 0 else small_box[1, number - 1]
        small_box[1, number] = source + small_box[0, number]

    def rows_of(bit, high):
        return pl.ds(pl.multiple_of((2 * bit + high) * quarter, ROWS), quarter)

    def near_copy(number):
        return copy(near_give.at[number], near_box.at[number], near_sems.at[number], (gene, near))

    far_copy = copy(far_give, far_box, far_sems, (gene, far))

    def last_copy(number, high, other):
        rows = rows_of(bit, high)
        return copy(whole_box.at[rows], whole_box.at[rows], last_sems.at[number], (gene, other))

    @pl.when(step == 0)
    def _():
        barrier = pltpu.get_barrier_semaphore()
        for where in rounds:
            pl.semaphore_signal(barrier, inc=1, device_id=where, device_id_type=MESH)
        pl.semaphore_wait(barrier, len(rounds))
        small_copy(0).start()

    piece = pick_chunk(cells, 512)

    def part():
        total = jnp.zeros((quarter, LANES), f32)
        for at in range(0, cells, piece):
            columns = slice(at, at + piece)
            inputs = jnp.log(counts_ref[:, columns].astype(f32) + 1.0).astype(bf16)
            total = total + lax.dot_general(
                inputs,
                grad_ref[:, columns],
                (((1,), (1,)), ((), ())),
                preferred_element_type=f32,
            )
        return total

    value = part()

    @pl.when(step < 2)
    def _():
        near_give[step] = value
        near_copy(step).start()

    @pl.when(step == 1)
    def _():
        small_end(0)
        small_copy(1).start()

    @pl.when(step == 2)
    def _():
        near_copy(0).wait()
        far_give[...] = value + near_box[0]
        far_copy.start()
        small_end(1)
        small_copy(2).start()

    @pl.when(step == 3)
    def _():
        near_copy(1).wait()
        total = value + near_box[1]
        small_end(2)
        if len(rounds) > 3:
            small_copy(3).start()
        far_copy.wait()
        whole_box[rows_of(bit, high), :] = total + far_box[...]
        own_far, own_near = last_copy(0, high, far), last_copy(1, high, near)
        own_far.start()
        own_near.start()
        for number in range(3, len(rounds)):
            small_end(number)
            if number + 1 < len(rounds):
                small_copy(number + 1).start()
        total_ref[...] = small_box[1, len(rounds) - 1]
        own_far.wait()
        passed = last_copy(2, 1 - high, near)
        passed.start()
        own_near.wait()
        passed.wait()
        sum_ref[...] = whole_box[...]


def encoder_grad(counts_t, grad, small):
    genes, cells = counts_t.shape
    quarter = ROWS * pl.cdiv(genes, 4 * ROWS)
    rounds = 2
    while 2 ** (rounds - 2) < lax.axis_size("gene"):
        rounds += 1

    def quarter_of(i):
        cell = lax.axis_index("cell")
        bit, high = lax.rem(cell, 2), cell // 2
        half = lax.rem(bit + 1 + i // 2, 2)
        return (2 * half + lax.rem(high + 1 + i, 2), 0)

    box = pltpu.VMEM((2, quarter, LANES), f32)
    one = pltpu.VMEM((quarter, LANES), f32)
    return pl.pallas_call(
        encoder_grad_kernel,
        grid=(4,),
        in_specs=[pl.BlockSpec((quarter, cells), quarter_of), whole(grad), whole(small)],
        out_specs=[
            pl.BlockSpec((4 * quarter, LANES), lambda i: (0, 0)),
            pl.BlockSpec(small.shape, lambda i: (0, 0)),
        ],
        out_shape=[
            jax.ShapeDtypeStruct((4 * quarter, LANES), f32),
            jax.ShapeDtypeStruct(small.shape, f32),
        ],
        scratch_shapes=[
            box,
            box,
            one,
            one,
            pltpu.VMEM((4 * quarter, LANES), f32),
            pltpu.VMEM((2, rounds, *small.shape), f32),
            pltpu.SemaphoreType.DMA((2, 2)),
            pltpu.SemaphoreType.DMA((2,)),
            pltpu.SemaphoreType.DMA((3, 2)),
            pltpu.SemaphoreType.DMA((rounds, 2)),
        ],
        compiler_params=talking(5),
        name="encoder_grad",
    )(counts_t, grad, small)


def update_kernel(*refs):
    groups, outs = refs[:8], refs[8:]
    encoder, output = groups[:4], groups[4:]
    fresh, moment, mean = nesterov(*[ref[...] for ref in encoder], step_rates[0])
    for ref, value in zip(outs[:3], (fresh, moment, mean)):
        ref[...] = value
    rows = output[3].shape[1]
    for k in range(2):
        here = pl.ds(k, rows, stride=2)
        old = [ref[here, :] for ref in output[:3]]
        for ref, value in zip(outs[3:], nesterov(*old, output[3][k], step_rates[1])):
            ref[here, :] = value


def update(encoder, encoder_grad, output, output_grad):
    genes = encoder[0].shape[0]
    block = 2 * LANES
    one = pl.BlockSpec((block, LANES), lambda i: (i, 0))
    two = pl.BlockSpec((2 * block, LANES), lambda i: (i, 0))
    both = pl.BlockSpec((2, block, LANES), lambda i: (0, i, 0))
    return pl.pallas_call(
        update_kernel,
        grid=(pl.cdiv(genes, block),),
        in_specs=[one] * 4 + [two] * 3 + [both],
        out_specs=[one] * 3 + [two] * 3,
        out_shape=[jax.ShapeDtypeStruct(encoder[0].shape, f32)] * 3
        + [jax.ShapeDtypeStruct(output[0].shape, f32)] * 3,
        compiler_params=PARAMS,
        name="update",
    )(*encoder, encoder_grad, *output, output_grad)


def fill_hidden(long_ref, hidden_ref, top):
    width, chunk = hidden_ref.shape
    long_ref[0:width, :] = hidden_ref[...]
    index = lax.broadcasted_iota(jnp.int32, (HOT_DEPTH - width, chunk), 0)
    extra = jnp.where(index < 3, 1.0, 0.0)
    if top is not None:
        high = (-top).astype(bf16).astype(f32)
        middle = (-top - high).astype(bf16).astype(f32)
        low = (-top - high - middle).astype(bf16).astype(f32)
        extra = jnp.where(index == 3, high, extra)
        extra = jnp.where(index == 4, middle, extra)
        extra = jnp.where(index == 5, low, extra)
    long_ref[width:HOT_DEPTH, :] = extra.astype(bf16)


def sweep(blocks, block, groups, pieces, logits, terms, back, carry):
    def rows_of(number):
        return pl.ds(pl.multiple_of(number * block, ROWS), block)

    logits(0, rows_of(0), block, pieces)

    def beside(i, later, earlier):
        acts = [
            lambda piece=piece: logits(1 - i, rows_of(later), block, [piece]) for piece in pieces
        ]
        if back is not None:
            acts.append(lambda: back(1 - i, rows_of(earlier), block))
        spaced = []
        for step in range(groups):
            spaced.append(acts.pop(0) if acts and step % 2 == 0 else lambda: None)
        return spaced + acts

    def pair(p, carry):
        first = 2 * p
        last, ahead = jnp.maximum(first - 1, 0), jnp.minimum(first + 2, blocks - 1)
        carry = terms(0, first, carry, beside(0, first + 1, last))
        return terms(1, first + 1, carry, beside(1, ahead, first))

    carry = lax.fori_loop(0, blocks // 2, pair, carry)
    if back is not None and blocks > 1:
        back(1, rows_of(blocks // 2 * 2 - 1), block)
    if blocks % 2:
        carry = terms(0, blocks - 1, carry, ())
        if back is not None:
            back(0, rows_of(blocks - 1), block)
    return carry


def logit_pieces(ks, chunk):
    width = min(chunk, WIDE)
    return [(k, slice(j, j + width)) for k in range(ks) for j in range(0, chunk, width)]


def totals_kernel(hidden_ref, weight_ref, out_ref, long_ref, even_ref, odd_ref, *, genes, chunk):
    full, groups, tail = split_rows(genes, 26)
    block = ROWS * groups
    blocks = full // groups
    values = (even_ref, odd_ref)
    fill_hidden(long_ref, hidden_ref, None)
    pieces = logit_pieces(1, chunk)

    def logits(i, rows, size, which):
        for _, columns in which:
            values[i][0:size, columns] = jnp.dot(
                weight_ref[0, rows, :], long_ref[:, columns], preferred_element_type=f32
            )

    def online(value_ref, size, carry, beside=()):
        best, total = carry
        fresh = best
        for i in range(0, size, 8):
            fresh = jnp.maximum(fresh, value_ref[i : i + 8, :])
        total = total * jnp.exp2((best - fresh) * (1.0 / ln2))
        for i in range(0, size, 8):
            for act in beside[i // 8 :: size // 8]:
                act()
            total = total + jnp.exp2((value_ref[i : i + 8, :] - fresh) * (1.0 / ln2))
        return fresh, total

    def terms(i, number, carry, beside):
        return online(values[i], block, carry, beside)

    carry = (jnp.full((8, chunk), -jnp.inf, f32), jnp.zeros((8, chunk), f32))
    carry = sweep(blocks, block, groups, pieces, logits, terms, None, carry)
    if tail:
        logits(1, pl.ds(full * ROWS, ROWS), ROWS, pieces)
        carry = online(odd_ref, ROWS, carry)
    best, total = carry
    top = jnp.max(best, axis=0, keepdims=True)
    total = total * jnp.exp2((best - top) * (1.0 / ln2))
    out_ref[0:1, :] = top
    out_ref[1:2, :] = jnp.sum(total, axis=0, keepdims=True)


def totals(hidden, weights, genes):
    width, cells = hidden.shape
    chunk = pick_chunk(cells, 2048)
    groups = split_rows(genes, 26)[1]
    return pl.pallas_call(
        functools.partial(totals_kernel, genes=genes, chunk=chunk),
        grid=(cells // chunk,),
        in_specs=[column_blocks(width, chunk), whole(weights)],
        out_specs=column_blocks(2, chunk),
        out_shape=jax.ShapeDtypeStruct((2, cells), f32),
        scratch_shapes=[pltpu.VMEM((HOT_DEPTH, chunk), bf16)]
        + [pltpu.VMEM((ROWS * groups, chunk), f32)] * 2,
        compiler_params=PARAMS,
        name="totals",
    )(hidden, weights)


def likelihood_kernel(
    counts_ref,
    hidden_ref,
    rows_ref,
    share_ref,
    weight_ref,
    theta_ref,
    log_ref,
    slope_ref,
    gammas_ref,
    digammas_ref,
    slopes_ref,
    sums_ref,
    grad_hidden_ref,
    grad_weight_ref,
    grad_bias_ref,
    grad_theta_ref,
    long_ref,
    even_ref,
    odd_ref,
    even_grad_ref,
    odd_grad_ref,
    *,
    genes,
    chunk,
):
    full, groups, tail = split_rows(genes)
    block = ROWS * groups
    blocks = full // groups
    width = hidden_ref.shape[0]

    @pl.when(pl.program_id(0) == 0)
    def _():
        for ref in (grad_weight_ref, grad_bias_ref, grad_theta_ref):
            ref[...] = jnp.zeros_like(ref)

    fill_hidden(long_ref, hidden_ref, rows_ref[0:1, :])
    wide = min(WIDE, chunk)
    tiles = [slice(j, j + wide) for j in range(0, chunk, wide)]
    ratio_all = rows_ref[1:2, :]
    share_all = share_ref[...]

    def two(x):
        return jnp.concatenate([x] * (wide // LANES), axis=1)

    def look(t, c):
        return jnp.concatenate([jnp.take_along_axis(t, c[:, q:q+LANES], axis=1) for q in range(0, wide, LANES)], axis=1)

    def group(value_ref, grad_ref, held, span, read, carry):
        losses, sums = [], []
        theta = two(theta_ref.at[span][held, :])
        log_theta = two(log_ref.at[span][held, :])
        log_slope = two(slope_ref.at[span][held, :])
        gammas = gammas_ref.at[span][held, :]
        digammas = digammas_ref.at[span][held, :]
        grad_bias = grad_bias_ref.at[span][held, :]
        grad_theta = grad_theta_ref.at[span][held, :]
        for j, columns in enumerate(tiles):
            count = read(columns)
            counted = count.astype(f32)
            minus = value_ref[1, held, columns] * (-1.0 / ln2)
            share = share_all[:, columns]
            rate = jnp.exp2(value_ref[0, held, columns] * (1.0 / ln2)) * ratio_all[:, columns]
            near = rate + rate_epsilon
            both = theta + near
            inverse_both = 1.0 / both
            log_both = jnp.log2(both)
            upper = jnp.maximum(minus, 0.0)
            lower = jnp.minimum(minus, 0.0)
            one_pi = 1.0 + jnp.exp2(lower - upper)
            sigma_pi = jnp.exp2(lower) * (1.0 / one_pi)
            zero = count < 1
            pi_theta = theta * (log_theta - log_both) + minus
            inflated = jnp.where(zero, pi_theta, 1e30)
            small = jnp.exp2(-jnp.abs(inflated))
            inverse_theta = 1.0 / (1.0 + small)
            sigma = jnp.where(inflated >= 0.0, 1.0, small) * inverse_theta
            loss = (upper - jnp.where(zero, jnp.maximum(pi_theta, 0.0), pi_theta)) + (
                jnp.log2(one_pi * inverse_theta)
                - counted * (jnp.log2(near) - log_both)
                - look(gammas, count)
            )
            pull = (sigma * theta + counted) * inverse_both
            slope = rate * (pull - counted * (1.0 / near))
            slopes_ref.at[span][held, columns] = slope
            grad_dropout = (sigma - sigma_pi) * share
            grad_ref[held, columns] = grad_dropout.astype(bf16)
            grad_bias = grad_bias + fold_lanes(grad_dropout)
            grad_theta = grad_theta + fold_lanes(share * (
                (pull - sigma * (log_slope - ln2 * log_both))
                - look(digammas, count)
            ))
            losses.append(carry[0][j] + loss[:8] + loss[8:])
            sums.append(carry[1][j] + slope[:8] + slope[8:])
        grad_bias_ref.at[span][held, :] = grad_bias
        grad_theta_ref.at[span][held, :] = grad_theta
        return tuple(losses), tuple(sums)

    pieces = logit_pieces(2, chunk)
    values, grads = (even_ref, odd_ref), (even_grad_ref, odd_grad_ref)

    def logits(i, rows, size, which):
        for k, columns in which:
            values[i][k, 0:size, columns] = jnp.dot(
                weight_ref[k, rows, :], long_ref[:, columns], preferred_element_type=f32
            )

    def back(i, rows, size):
        grad = grads[i][0:size, :]
        grad_weight_ref[rows, :] += lax.dot_general(
            grad, hidden_ref[...], (((1,), (1,)), ((), ())), preferred_element_type=f32
        )
        grad_hidden_ref[...] += lax.dot_general(
            weight_ref[1, rows, 0:width],
            grad,
            (((0,), (0,)), ((), ())),
            preferred_element_type=f32,
        )

    def terms(buffer, number, carry, beside):
        span = pl.ds(pl.multiple_of(number * block, ROWS), block)
        for i in range(groups):
            for act in beside[i::groups]:
                act()
            held = slice(i * ROWS, (i + 1) * ROWS)
            carry = group(
                values[buffer],
                grads[buffer],
                held,
                span,
                lambda columns, held=held: counts_ref.at[span][held, columns],
                carry,
            )
        return carry

    grad_hidden_ref[...] = jnp.zeros_like(grad_hidden_ref)
    odd_grad_ref[...] = jnp.zeros_like(odd_grad_ref)
    carry = tuple(jnp.zeros((8, wide), f32) for _ in tiles)
    carry = sweep(blocks, block, groups, pieces, logits, terms, back, (carry, carry))
    if tail:
        rows = pl.ds(full * ROWS, ROWS)
        logits(1, rows, ROWS, pieces)
        carry = group(
            odd_ref,
            odd_grad_ref,
            slice(0, ROWS),
            rows,
            lambda cols: tail_rows(counts_ref, full * ROWS, genes, cols, jnp.int32),
            carry,
        )
        back(1, rows, ROWS)
    for j, columns in enumerate(tiles):
        sums_ref[0:1, columns] = jnp.sum(carry[1][j], axis=0, keepdims=True)
        sums_ref[1:2, columns] = jnp.sum(carry[0][j], axis=0, keepdims=True) * ln2


def likelihood(counts_t, hidden, rows, share, weights, gene_tables):
    genes, cells = counts_t.shape
    size = weights.shape[1]
    width = hidden.shape[0]
    chunk = pick_chunk(cells, 512)
    groups = split_rows(genes)[1]
    row = column_blocks(1, chunk)
    per_gene = pl.BlockSpec((size, LANES), lambda i: (0, 0))
    return pl.pallas_call(
        functools.partial(likelihood_kernel, genes=genes, chunk=chunk),
        grid=(cells // chunk,),
        in_specs=[column_blocks(genes, chunk), column_blocks(width, chunk)]
        + [column_blocks(rows.shape[0], chunk), row, whole(weights)]
        + [whole(a) for a in gene_tables],
        out_specs=[
            column_blocks(size, chunk),
            column_blocks(2, chunk),
            column_blocks(width, chunk),
        ]
        + [per_gene] * 3,
        out_shape=[
            jax.ShapeDtypeStruct((size, cells), f32),
            jax.ShapeDtypeStruct((2, cells), f32),
            jax.ShapeDtypeStruct((width, cells), f32),
        ]
        + [jax.ShapeDtypeStruct((size, LANES), f32)] * 3,
        scratch_shapes=[pltpu.VMEM((HOT_DEPTH, chunk), bf16)]
        + [pltpu.VMEM((2, ROWS * groups, chunk), f32)] * 2
        + [pltpu.VMEM((ROWS * groups, chunk), bf16)] * 2,
        compiler_params=PARAMS,
        name="likelihood",
    )(counts_t, hidden, rows, share, weights, *gene_tables)


def frequency_kernel(
    slopes_ref,
    hidden_ref,
    rows_ref,
    pull_ref,
    share_ref,
    other_ref,
    weight_ref,
    second_ref,
    dropout_ref,
    theta_ref,
    scale_ref,
    grad_hidden_ref,
    grad_weight_ref,
    genes_ref,
    long_ref,
    even_ref,
    odd_ref,
    even_grad_ref,
    odd_grad_ref,
    grad_bias_ref,
    *,
    genes,
    chunk,
):
    full, groups, tail = split_rows(genes, 26)
    block = ROWS * groups
    blocks = full // groups
    size = weight_ref.shape[1]
    width = hidden_ref.shape[0]
    values, grads = (even_ref, odd_ref), (even_grad_ref, odd_grad_ref)

    @pl.when(pl.program_id(0) == 0)
    def _():
        grad_weight_ref[0] = jnp.zeros((size, LANES), f32)
        grad_weight_ref[1] = second_ref[...]
        grad_bias_ref[...] = jnp.zeros_like(grad_bias_ref)

    fill_hidden(long_ref, hidden_ref, rows_ref[0:1, :])
    pieces = logit_pieces(1, chunk)
    share = share_ref[...]
    pulled = pull_ref[0:1, :] * share

    def logits(i, rows, size, which):
        for _, columns in which:
            values[i][0:size, columns] = jnp.dot(
                weight_ref[0, rows, :], long_ref[:, columns], preferred_element_type=f32
            )

    def group(buffer, held, span):
        exponent = jnp.exp2(values[buffer][held, :] * (1.0 / ln2))
        grad = slopes_ref.at[span][held, :] * share - exponent * pulled
        grads[buffer][held, :] = grad.astype(bf16)
        grad_bias_ref.at[span][held, :] += fold_lanes(grad)

    def terms(buffer, number, carry, beside):
        span = pl.ds(pl.multiple_of(number * block, ROWS), block)
        for i in range(groups):
            for act in beside[i::groups]:
                act()
            group(buffer, slice(i * ROWS, (i + 1) * ROWS), span)
        return carry

    def back(i, rows, size):
        grad = grads[i][0:size, :]
        grad_weight_ref[0, rows, :] += lax.dot_general(
            grad, hidden_ref[...], (((1,), (1,)), ((), ())), preferred_element_type=f32
        )
        grad_hidden_ref[...] += lax.dot_general(
            weight_ref[0, rows, 0:width],
            grad,
            (((0,), (0,)), ((), ())),
            preferred_element_type=f32,
        )

    grad_hidden_ref[...] = other_ref[...]
    odd_grad_ref[...] = jnp.zeros_like(odd_grad_ref)
    sweep(blocks, block, groups, pieces, logits, terms, back, 0)
    if tail:
        rows = pl.ds(full * ROWS, ROWS)
        logits(1, rows, ROWS, pieces)
        group(1, slice(0, ROWS), rows)
        back(1, rows, ROWS)

    @pl.when(pl.program_id(0) == pl.num_programs(0) - 1)
    def _():
        ones = jnp.ones((8, LANES), f32)
        parts = (grad_bias_ref[...], dropout_ref[...], theta_ref[...] * scale_ref[...])
        for i, values in enumerate(parts):
            genes_ref[i : i + 1, :] = exact(ones, values, 1, 1)[0:1]
        genes_ref[3:4, :] = jnp.zeros((1, size), f32)


def frequency(slopes, hidden, rows, pull, share, other, weights, second, dropout, theta, scale, genes):
    size, cells = slopes.shape
    width = hidden.shape[0]
    chunk = pick_chunk(cells, 1024)
    groups = split_rows(genes, 26)[1]
    row = column_blocks(1, chunk)
    wide = column_blocks(width, chunk)
    return pl.pallas_call(
        functools.partial(frequency_kernel, genes=genes, chunk=chunk),
        grid=(cells // chunk,),
        in_specs=[column_blocks(size, chunk), wide, column_blocks(rows.shape[0], chunk)]
        + [column_blocks(2, chunk), row, wide, whole(weights)]
        + [whole(a) for a in (second, dropout, theta, scale)],
        out_specs=[
            wide,
            pl.BlockSpec((2, size, LANES), lambda i: (0, 0, 0)),
            pl.BlockSpec((4, size), lambda i: (0, 0)),
        ],
        out_shape=[
            jax.ShapeDtypeStruct((width, cells), f32),
            jax.ShapeDtypeStruct((2, size, LANES), f32),
            jax.ShapeDtypeStruct((4, size), f32),
        ],
        scratch_shapes=[pltpu.VMEM((HOT_DEPTH, chunk), bf16)]
        + [pltpu.VMEM((ROWS * groups, chunk), f32)] * 2
        + [pltpu.VMEM((ROWS * groups, chunk), bf16)] * 2
        + [pltpu.VMEM((size, LANES), f32)],
        compiler_params=PARAMS,
        name="frequency",
    )(slopes, hidden, rows, pull, share, other, weights, second, dropout, theta, scale)


def input_grad_kernel(grad_ref, weight_ref, input_ref):
    input_ref[...] = jnp.dot(
        weight_ref[...].astype(bf16), grad_ref[...], preferred_element_type=f32
    )


def encoder_input_grad(grad, weight):
    width, cells = grad.shape
    genes = weight.shape[0]
    block = 2 * LANES
    return pl.pallas_call(
        input_grad_kernel,
        grid=(pl.cdiv(genes, block),),
        in_specs=[whole(grad), pl.BlockSpec((block, width), lambda i: (i, 0))],
        out_specs=pl.BlockSpec((block, cells), lambda i: (i, 0)),
        out_shape=jax.ShapeDtypeStruct((genes, cells), f32),
        compiler_params=PARAMS,
        name="input_grad",
    )(grad, weight)


def local(
    counts,
    batch_index,
    valid_mask,
    noise_draw,
    encoder_weight,
    output_weight,
    gene_vectors,
    batch_shift,
    layer_norm_params,
    head_weight,
    head_bias,
    decoder_input,
    encoder_weight_momentum,
    output_weight_momentum,
    gene_vectors_momentum,
    batch_shift_momentum,
    norm_params_momentum,
    head_weight_momentum,
    head_bias_momentum,
    decoder_input_momentum,
    encoder_weight_average,
    output_weight_average,
    gene_vectors_average,
    batch_shift_average,
    norm_params_average,
    head_weight_average,
    head_bias_average,
    decoder_input_average,
):
    cells, genes = counts.shape
    gene_devices = lax.axis_size("gene")
    genes_all = genes * gene_devices
    latent = head_bias.shape[0] // 2
    batches = batch_shift.shape[0]

    def by_gene(array):
        return jnp.transpose(array, (2, 0, 1)).reshape(2 * genes, -1)

    counts_t = counts.T
    output_rows = by_gene(output_weight)

    pad = 16
    small_weights = (
        layer_norm_params,
        head_bias[None, :],
        decoder_input,
        head_weight.T,
        batch_shift,
    )
    index, valid, noise = batch_index[None, :], valid_mask[None, :], noise_draw.T

    encoded, weights, *gene_tables = encode(counts_t, encoder_weight, output_rows, gene_vectors)
    hidden2, centered2, sample, share, stats, centered1, heads, rest_rows, pack = middle(
        encoded, index, valid, noise, small_weights, batches, pad, genes_all
    )
    rows = combine_tops(totals(hidden2, weights, genes), rest_rows)
    slopes, sums, grad_hidden2, grad_out1, grad_bias1, grad_theta = likelihood(
        counts_t, hidden2, rows, share, weights, gene_tables
    )
    pull = combine_sums(sums, rows, rest_rows, valid, genes_all)
    cell_loss = pull[1]

    grad_hidden2, grad_out, grad_genes = frequency(
        slopes,
        hidden2,
        rows,
        pull,
        share,
        grad_hidden2,
        weights,
        grad_out1,
        grad_bias1,
        grad_theta,
        gene_tables[0],
        genes,
    )
    grad_pre16, small, norm_rows, grad_out, grad_genes = middle_back(
        grad_hidden2,
        centered2,
        sample,
        index,
        valid,
        noise,
        pack,
        stats,
        centered1,
        heads,
        grad_out,
        grad_genes,
        batches,
    )
    grad_encoder, small = encoder_grad(counts_t, grad_pre16, small)
    input_grad = encoder_input_grad(grad_pre16, encoder_weight)
    depth = pad + batches
    grad_mixing = jnp.concatenate([small[:latent], small[pad:depth]], axis=0)
    grad_heads = small[depth : depth + 2 * pad].reshape(2, pad, -1)[:, :latent]
    grad_heads = grad_heads.reshape(2 * latent, -1).T
    grad_head_bias = jnp.sum(small[depth + 2 * pad : depth + 4 * pad], axis=1)
    grad_head_bias = grad_head_bias.reshape(2, pad)[:, :latent].reshape(-1)
    grad_shift = small[depth + 4 * pad :]

    updated = update(
        (encoder_weight, encoder_weight_momentum, encoder_weight_average),
        grad_encoder,
        (output_rows, by_gene(output_weight_momentum), by_gene(output_weight_average)),
        grad_out,
    )
    encoder_new = updated[:3]
    output_new = [jnp.transpose(a.reshape(genes, 2, -1), (1, 2, 0)) for a in updated[3:]]
    vectors = (gene_vectors, batch_shift, layer_norm_params, head_weight, head_bias, decoder_input)
    momenta = (
        gene_vectors_momentum,
        batch_shift_momentum,
        norm_params_momentum,
        head_weight_momentum,
        head_bias_momentum,
        decoder_input_momentum,
    )
    averages = (
        gene_vectors_average,
        batch_shift_average,
        norm_params_average,
        head_weight_average,
        head_bias_average,
        decoder_input_average,
    )
    grads = (
        grad_genes[:3, :genes],
        grad_shift,
        norm_rows[:4],
        grad_heads,
        grad_head_bias,
        grad_mixing,
    )
    small_new = zip(
        *[nesterov(*group) for group in zip(vectors, momenta, averages, grads, step_rates[2:])]
    )
    results = []
    for i, rest in enumerate(small_new):
        results += [encoder_new[i], output_new[i], *rest]
    return (cell_loss, input_grad.T, *results)


def solution(mesh):
    cells, genes = P("cell"), P("gene", None)
    weight_specs = (genes, P(None, None, "gene"), P(None, "gene"), P(), P(), P(), P(), P())
    return jax.shard_map(
        local,
        mesh=mesh,
        in_specs=(P("cell", "gene"), cells, cells, P("cell", None)) + weight_specs * 3,
        out_specs=(cells, P("cell", "gene")) + weight_specs * 3,
        check_vma=False,
    )
```

```python
import functools

import jax
import jax.numpy as jnp
from jax import lax
from jax.experimental import pallas as pl
from jax.experimental.pallas import tpu as pltpu
from jax.sharding import PartitionSpec as P

momentum_decay = 0.9
average_decay = 0.99
norm_epsilon = 0.001
rate_epsilon = 1e-08
step_rates = (110.0, 46000.0, 300000.0, 70000.0, 13000.0, 3700.0, 7600.0, 8000.0)
ln2 = 0.6931471805599453
f32 = jnp.float32
bf16 = jnp.bfloat16
LANES = 128
ROWS = 16
WIDE = 2 * LANES
HOT_DEPTH = 2 * LANES
PARAMS = pltpu.CompilerParams(vmem_limit_bytes=60 << 20)
IN_VMEM = pl.BlockSpec(memory_space=pltpu.VMEM)
MESH = pl.DeviceIdType.MESH


def talking(number):
    return pltpu.CompilerParams(
        collective_id=number, has_side_effects=True, vmem_limit_bytes=60 << 20
    )


def nesterov(weight, momentum, average, grad, rate):
    moment = momentum_decay * momentum + grad
    fresh = weight - rate * (grad + momentum_decay * moment)
    return (fresh, moment, average_decay * average + (1.0 - average_decay) * fresh)


def whole(array):
    return pl.BlockSpec(array.shape, lambda i: (0,) * array.ndim)


def column_blocks(rows, chunk):
    return pl.BlockSpec((rows, chunk), lambda i: (0, i))


def split_rows(genes, most=13):
    full = genes // ROWS
    groups = max(d for d in range(1, most + 1) if full % d == 0)
    return full, groups, genes - full * ROWS


def padded(genes):
    return -(-genes // ROWS) * ROWS


def pick_chunk(cells, most):
    chunk = LANES
    while chunk * 2 <= most and cells % (chunk * 2) == 0:
        chunk *= 2
    return chunk


def tail_rows(ref, start, stop, columns, dtype):
    piece = ref[start:stop, columns]
    filler = jnp.zeros((ROWS - (stop - start), piece.shape[1]), dtype)
    return jnp.concatenate([piece, filler], axis=0)


class Team:
    def __init__(self, axis):
        self.size, self.me = lax.axis_size(axis), lax.axis_index(axis)
        self.gene, self.cell = lax.axis_index("gene"), lax.axis_index("cell")
        self.axis = axis

    def place(self, other):
        return (other, self.cell) if self.axis == "gene" else (self.gene, other)

    def others(self, act):
        def one(step, carry):
            other = lax.rem(self.me + step, self.size)
            act(other, self.place(other))
            return carry

        lax.fori_loop(1, self.size, one, 0)

    def send(self, source, target, sems):
        def act(other, place):
            pltpu.make_async_remote_copy(
                src_ref=source(other),
                dst_ref=target,
                send_sem=sems.at[0],
                recv_sem=sems.at[1],
                device_id=place,
                device_id_type=MESH,
            ).start()

        self.others(act)


def greet(*teams):
    barrier = pltpu.get_barrier_semaphore()

    def act(other, place):
        pl.semaphore_signal(barrier, inc=1, device_id=place, device_id_type=MESH)

    for team in teams:
        team.others(act)
    pl.semaphore_wait(barrier, sum(team.size - 1 for team in teams))


def await_bytes(ref, sem):
    pltpu.make_async_copy(ref, ref, sem).wait()


def fold_lanes(values):
    return sum(values[:, j : j + LANES] for j in range(0, values.shape[1], LANES))


def row_sums(folded):
    return jnp.sum(jnp.transpose(folded), axis=0, keepdims=True)


def box_sum(box):
    def add(i, total):
        return total + box[i]

    return lax.fori_loop(1, box.shape[0], add, box[0])


def spread_box(team, box, value, sems):
    box[team.me] = value
    team.send(lambda other: box.at[team.me], box.at[team.me], sems)
    others = box.at[pl.ds(0, team.size - 1)]

    def finish():
        await_bytes(others, sems.at[0])
        await_bytes(others, sems.at[1])
        return box_sum(box)

    return finish


def row_boxes():
    shapes = [(lax.axis_size(axis), 8, LANES) for axis in ("cell", "gene")]
    return [pltpu.VMEM(shape, f32) for shape in shapes * 2]


class Gather:
    def __init__(self, ref, slab, far_sems, near_sems):
        self.ref, self.slab = ref, slab
        self.gene, self.cell = lax.axis_index("gene"), lax.axis_index("cell")
        self.pairs = lax.axis_size("gene") // 2
        self.high, self.low = self.gene // 2, lax.rem(self.gene, 2)
        self.far_sems, self.near_sems = far_sems, near_sems

    def copy(self, source_high, target, sems):
        columns = pl.ds(
            pl.multiple_of((2 * source_high + self.low) * self.slab, LANES), self.slab
        )
        return pltpu.make_async_remote_copy(
            src_ref=self.ref.at[:, columns],
            dst_ref=self.ref.at[:, columns],
            send_sem=sems.at[0],
            recv_sem=sems.at[1],
            device_id=(target, self.cell),
            device_id_type=MESH,
        )

    def far(self, d):
        target = 2 * lax.rem(self.high + d, self.pairs) + self.low
        return self.copy(self.high, target, self.far_sems.at[d - 1])

    def near(self, d):
        source = lax.rem(self.high - d + self.pairs, self.pairs)
        return self.copy(source, 2 * self.high + 1 - self.low, self.near_sems.at[d])

    def start(self):
        self.near(0).start()

        def one(d, carry):
            self.far(d).start()
            return carry

        lax.fori_loop(1, self.pairs, one, 0)

    def finish(self):
        def one(d, carry):
            self.far(d).wait_recv()
            self.near(d).start()
            return carry

        lax.fori_loop(1, self.pairs, one, 0)

        def drain(d, carry):
            self.near(d).wait()
            return carry

        lax.fori_loop(0, self.pairs, drain, 0)

        def drain_far(d, carry):
            self.far(d).wait_send()
            return carry

        lax.fori_loop(1, self.pairs, drain_far, 0)


def gather_sems():
    pairs = lax.axis_size("gene") // 2
    return [pltpu.SemaphoreType.DMA((pairs, 2))] * 2


class Shared:
    def __init__(self, box, sems, chunk):
        self.box, self.sems, self.team = box, sems, Team("gene")
        start = pl.multiple_of(pl.program_id(0) * chunk, LANES)
        self.here = pl.ds(start, chunk)

    def send(self, first, second):
        me = self.team.me
        self.box[me, 0:1, self.here] = first
        self.box[me, 1:2, self.here] = second
        place = self.box.at[me, :, self.here]
        self.team.send(lambda other: place, place, self.sems)

    def finish(self):
        others = self.box.at[pl.ds(0, self.team.size - 1)]
        await_bytes(others, self.sems.at[0])
        await_bytes(others, self.sems.at[1])


def eight_rows(rows):
    filler = jnp.zeros((8 - len(rows), LANES), f32)
    return jnp.concatenate([*rows, filler], axis=0) if len(rows) < 8 else jnp.concatenate(rows, 0)


def columns_of(rows):
    turned = jnp.transpose(jnp.concatenate([eight_rows(rows), jnp.zeros((120, LANES), f32)], 0))
    return [turned[:, i : i + 1] for i in range(len(rows))]


def exact(left, right, left_dim, right_dim):
    return lax.dot_general(
        left,
        right,
        (((left_dim,), (right_dim,)), ((), ())),
        precision=lax.Precision.HIGHEST,
        preferred_element_type=f32,
    )


def hot_rows(index, batches):
    rows = lax.broadcasted_iota(jnp.int32, (batches, index.shape[1]), 0)
    return jnp.where(rows == index, 1.0, 0.0)


def sigmoid(value):
    return 1.0 / (1.0 + jnp.exp(-value))


def slope_of(value):
    sigma = sigmoid(value)
    return sigma * (1.0 + value * (1.0 - sigma))


def pack_layout(latent_pad, batches):
    mixing = slice(8, 8 + latent_pad + batches)
    heads = slice(mixing.stop, mixing.stop + 2 * latent_pad)
    return mixing, heads, slice(heads.stop, heads.stop + batches)


def prepare_tables(number, genes, output_ref, vectors_ref, weights_ref, tables):
    theta_ref, log_ref, slope_ref, gammas_ref, digammas_ref = tables
    lane = lax.broadcasted_iota(jnp.int32, (LANES, LANES), 1)
    below = lax.broadcasted_iota(jnp.int32, (LANES, LANES), 0)
    upper = jnp.where(below < lane, 1.0, 0.0).astype(bf16)
    step = lane.astype(f32)
    block = theta_ref.shape[0]
    for at in range(0, block, LANES):
        here = slice(at, at + LANES)
        turned = jnp.transpose(
            jnp.concatenate([vectors_ref[:, here], jnp.zeros((LANES - 3, LANES), f32)], axis=0)
        )
        inside = number * block + at + below[:, 0:1] < genes
        for k in range(2):
            weight = output_ref[pl.ds(2 * at + k, LANES, stride=2), :]
            weights_ref[k, here, 0:LANES] = jnp.where(inside, weight, 0.0).astype(bf16)
            bias = jnp.where(inside, turned[:, k : k + 1], 0.0 if k else -1e30)
            high = bias.astype(bf16).astype(f32)
            middle = (bias - high).astype(bf16).astype(f32)
            low = (bias - high - middle).astype(bf16).astype(f32)
            extra = jnp.where(lane == 0, high, jnp.where(lane == 1, middle, 0.0))
            extra = jnp.where(lane == 2, low, extra)
            if k == 0:
                extra = jnp.where((lane >= 3) & (lane < 6), 1.0, extra)
            weights_ref[k, here, LANES : 2 * LANES] = extra.astype(bf16)
        theta = jnp.where(inside, jnp.exp(turned[:, 2:3]), 1.0) + jnp.zeros((LANES, LANES), f32)
        log_theta = jnp.log2(theta + rate_epsilon)
        theta_ref[here, :] = theta
        log_ref[here, :] = log_theta
        slope_ref[here, :] = ln2 * log_theta + theta / (theta + rate_epsilon)
        climb = theta + step
        terms = jnp.concatenate([jnp.log2(climb / (step + 1.0)), 1.0 / climb], axis=0)
        high = terms.astype(bf16)
        rest = terms - high.astype(f32)
        middle = rest.astype(bf16)
        low = (rest - middle.astype(f32)).astype(bf16)
        total = jnp.zeros((2 * LANES, LANES), f32)
        for piece in (low, middle, high):
            total = total + jnp.dot(piece, upper, preferred_element_type=f32)
        gammas_ref[here, :] = total[0:LANES]
        digammas_ref[here, :] = total[LANES:]


def encode_order(step, steps):
    last = step // (steps - 1)
    given = 1 - (step + steps - 1) // steps + lax.rem(step, 2) * (1 - last)
    return given, given * ((step + 1) // 2) + (1 - given) * (step // 2 - 1 + last)


def encode_kernel(
    counts_ref,
    encoder_ref,
    output_ref,
    vectors_ref,
    out_ref,
    weights_ref,
    theta_ref,
    log_ref,
    slope_ref,
    gammas_ref,
    digammas_ref,
    inputs_ref,
    weight_ref,
    near_give,
    near_box,
    far_give,
    far_box,
    near_sems,
    far_sems,
    *,
    genes,
    table_blocks,
):
    slab = counts_ref.shape[1]
    width = encoder_ref.shape[1]
    group = Team("gene")
    pairs = group.size // 2
    high, low = group.me // 2, lax.rem(group.me, 2)
    step = pl.program_id(0)
    given, turn = encode_order(step, group.size)

    def place(high, low):
        return (2 * high + low, group.cell)

    def copy(source, target, sems, where):
        return pltpu.make_async_remote_copy(
            src_ref=source,
            dst_ref=target,
            send_sem=sems.at[0],
            recv_sem=sems.at[1],
            device_id=where,
            device_id_type=MESH,
        )

    @pl.when(step == 0)
    def _():
        barrier = pltpu.get_barrier_semaphore()
        pl.semaphore_signal(barrier, inc=1, device_id=place(high, 1 - low), device_id_type=MESH)
        for d in range(1, pairs):
            where = place(lax.rem(high + d, pairs), low)
            pl.semaphore_signal(barrier, inc=1, device_id=where, device_id_type=MESH)
        for at in range(0, weight_ref.shape[1], LANES):
            stop = min(at + LANES, genes)
            piece = encoder_ref[at:stop, :]
            if stop < at + LANES:
                filler = jnp.zeros((at + LANES - stop, width), f32)
                piece = jnp.concatenate([piece, filler], axis=0)
            weight_ref[:, at : at + LANES] = jnp.transpose(piece).astype(bf16)
        pl.semaphore_wait(barrier, pairs)

    def part(ref):
        depth = 3 * LANES
        total = jnp.zeros((8, slab), f32)
        for number, at in enumerate(range(0, genes, depth)):
            held = inputs_ref.at[number % 2]
            stop = min(at + depth, genes)
            for row in range(at, stop, ROWS):
                if row + ROWS <= genes:
                    counted = counts_ref[row : row + ROWS, :].astype(f32)
                else:
                    counted = tail_rows(counts_ref, row, genes, slice(None), jnp.int32).astype(f32)
                held[row - at : row - at + ROWS, :] = jnp.log(counted + 1.0).astype(bf16)
                total = total + counted[:8] + counted[8:]
            here = padded(stop - at)
            product = jnp.dot(
                weight_ref[:, at : at + here], held[0:here, :], preferred_element_type=f32
            )
            if at == 0:
                ref[0:width, :] = product
            else:
                ref[0:width, :] += product
        row = lax.broadcasted_iota(jnp.int32, (8, slab), 0)
        ref[width : width + 8, :] = jnp.where(row == 0, jnp.sum(total, axis=0, keepdims=True), 0.0)

    def near_copy(i):
        return copy(near_give.at[i], near_box.at[i], near_sems.at[i], place(high, 1 - low))

    def far_copy(i):
        target = lax.rem(high + 1 + i, pairs)
        return copy(far_give.at[i], far_box.at[i], far_sems.at[i], place(target, low))

    tables = (theta_ref, log_ref, slope_ref, gammas_ref, digammas_ref)

    @pl.when(step < table_blocks)
    def _():
        prepare_tables(step, genes, output_ref, vectors_ref, weights_ref, tables)

    @pl.when(given == 1)
    def _():
        part(near_give.at[turn])
        near_copy(turn).start()

    @pl.when(given == 0)
    def _():
        part(out_ref)
        near_copy(turn).wait_recv()
        total = out_ref[...] + near_box[turn]

        @pl.when(turn < pairs - 1)
        def _():
            far_give[turn] = total
            far_copy(turn).start()

        @pl.when(turn == pairs - 1)
        def _():
            def gather(i, total):
                far_copy(i).wait_recv()
                return total + far_box[i]

            out_ref[...] = lax.fori_loop(0, pairs - 1, gather, total)

            def drain(i, carry):
                far_copy(i).wait_send()
                return carry

            lax.fori_loop(0, pairs - 1, drain, 0)

            def drain_near(i, carry):
                near_copy(i).wait_send()
                return carry

            lax.fori_loop(0, pairs, drain_near, 0)


def encode(counts_t, weight, output_rows, vectors):
    genes, cells = counts_t.shape
    devices = lax.axis_size("gene")
    pairs = devices // 2
    slab = cells // devices
    width = weight.shape[1]

    def slab_of(i):
        me = lax.axis_index("gene")
        given, turn = encode_order(i, devices)
        return (0, 2 * lax.rem(me // 2 + 1 + turn, pairs) + lax.rem(me + given, 2))

    box = pltpu.VMEM((pairs, width + 8, slab), f32)
    size = 2 * ROWS * pl.cdiv(genes, 2 * ROWS)
    block = LANES * pl.cdiv(pl.cdiv(size, LANES), devices)
    table_blocks = pl.cdiv(size, block)

    def table_of(i):
        return jnp.minimum(i, table_blocks - 1)

    table = pl.BlockSpec((block, LANES), lambda i: (table_of(i), 0))
    return pl.pallas_call(
        functools.partial(encode_kernel, genes=genes, table_blocks=table_blocks),
        grid=(devices,),
        in_specs=[
            pl.BlockSpec((genes, slab), slab_of),
            whole(weight),
            pl.BlockSpec((2 * block, LANES), lambda i: (table_of(i), 0)),
            pl.BlockSpec((3, block), lambda i: (0, table_of(i))),
        ],
        out_specs=[
            pl.BlockSpec((width + 8, slab), lambda i: (0, 0)),
            pl.BlockSpec((2, block, HOT_DEPTH), lambda i: (0, table_of(i), 0)),
        ]
        + [table] * 5,
        out_shape=[
            jax.ShapeDtypeStruct((width + 8, slab), f32),
            jax.ShapeDtypeStruct((2, size, HOT_DEPTH), bf16),
        ]
        + [jax.ShapeDtypeStruct((size, LANES), f32)] * 5,
        scratch_shapes=[
            pltpu.VMEM((2, 3 * LANES, slab), bf16),
            pltpu.VMEM((width, LANES * pl.cdiv(genes, LANES)), bf16),
            box,
            box,
            box,
            box,
            pltpu.SemaphoreType.DMA((pairs, 2)),
            pltpu.SemaphoreType.DMA((pairs, 2)),
        ],
        compiler_params=talking(6),
        name="encode",
    )(counts_t, weight, output_rows, vectors)


def middle_kernel(
    encoded_ref,
    index_ref,
    valid_ref,
    noise_ref,
    norms_ref,
    bias_ref,
    mixing_ref,
    head_ref,
    shift_ref,
    hidden_ref,
    centered_ref,
    sample_ref,
    share_ref,
    stats_ref,
    first_ref,
    heads_ref,
    pack_ref,
    box1,
    box2,
    box3,
    box4,
    sems1,
    sems2,
    sems3,
    sems4,
    sample_far,
    sample_near,
    *,
    batches,
    latent,
    genes_all,
):
    group, team = Team("gene"), Team("cell")
    width, slab = first_ref.shape
    cells = hidden_ref.shape[1]
    pad = sample_ref.shape[0]
    mixing_rows, heads_rows, shift_rows = pack_layout(pad, batches)
    pack_ref[...] = jnp.zeros_like(pack_ref)
    pack_ref[0:4, :] = norms_ref[...]
    pack_ref[4:5, 0:latent] = bias_ref[:, 0:latent]
    pack_ref[4:5, pad : pad + latent] = bias_ref[:, latent : 2 * latent]
    at = mixing_rows.start
    pack_ref[at : at + latent, :] = mixing_ref[0:latent, :]
    pack_ref[at + pad : at + pad + batches, :] = mixing_ref[latent:, :]
    at = heads_rows.start
    pack_ref[at : at + latent, :] = head_ref[0:latent, :]
    pack_ref[at + pad : at + pad + latent, :] = head_ref[latent:, :]
    pack_ref[shift_rows, :] = shift_ref[...]
    mixing = pack_ref[mixing_rows, :]

    def part(other):
        return pl.ds(pl.multiple_of(other * slab, LANES), slab)

    mine = part(group.me)
    greet(group, team)
    hot = hot_rows(index_ref[:, mine], batches)
    valid = valid_ref[:, mine].astype(f32)
    shift = exact(pack_ref[shift_rows, :], hot, 0, 0)
    gain1, bias1, gain2, bias2, head_bias = columns_of([pack_ref[i : i + 1, :] for i in range(5)])
    total = encoded_ref[...]
    library = total[width : width + 1, :]
    pre1 = total[0:width, :] + shift

    weighed = valid * pre1
    rows = [
        row_sums(fold_lanes(weighed)),
        row_sums(fold_lanes(weighed * pre1)),
        jnp.broadcast_to(jnp.sum(valid, axis=1, keepdims=True), (1, LANES)),
    ]
    sums = spread_box(team, box1, eight_rows(rows), sems1)()
    sums = spread_box(group, box2, sums, sems2)()
    count = jnp.maximum(sums[2:3], 1.0)
    mean1 = sums[0:1] / count
    inverse1 = lax.rsqrt(sums[1:2] / count - mean1 * mean1 + norm_epsilon)
    mean_col, inverse_col = columns_of([mean1, inverse1])
    centered1 = (pre1 - mean_col) * inverse_col
    first_ref[...] = centered1
    normed1 = centered1 * gain1 + bias1
    hidden1 = normed1 * sigmoid(normed1)
    heads = exact(pack_ref[heads_rows, :], hidden1, 1, 0) + head_bias[0 : 2 * pad]
    heads_ref[...] = heads
    mean_z, log_var = heads[0:pad], heads[pad : 2 * pad]
    noise = jnp.concatenate([noise_ref[:, mine], jnp.zeros((pad - latent, slab), f32)], axis=0)
    sample = mean_z + jnp.exp(0.5 * log_var) * noise
    sample_ref[:, mine] = sample
    sample_ref[pad - 2 : pad - 1, mine] = 0.5 * jnp.sum(
        mean_z * mean_z + jnp.exp(log_var) - log_var - 1.0, axis=0, keepdims=True
    )
    sample_ref[pad - 1 : pad, mine] = library
    gathering = Gather(sample_ref, slab, sample_far, sample_near)
    gathering.start()
    pre2 = exact(mixing, jnp.concatenate([sample, hot], axis=0), 0, 0)
    weighed = valid * pre2
    rows = [row_sums(fold_lanes(weighed)), row_sums(fold_lanes(weighed * pre2))]
    sums = spread_box(team, box3, eight_rows(rows), sems3)()
    finish = spread_box(group, box4, sums, sems4)
    scale = 1.0 / (count * genes_all)
    share_ref[...] = valid_ref[...].astype(f32) * scale[:, 0:1]
    sums = finish()
    mean2 = sums[0:1] / count
    inverse2 = lax.rsqrt(sums[1:2] / count - mean2 * mean2 + norm_epsilon)
    stats_ref[...] = eight_rows([inverse1, inverse2, count, scale])
    mean_col, inverse_col = columns_of([mean2, inverse2])
    gathering.finish()
    piece = pick_chunk(cells, 512)

    def decode(i, carry):
        columns = pl.ds(pl.multiple_of(i * piece, LANES), piece)
        mixed = jnp.concatenate(
            [sample_ref[:, columns], hot_rows(index_ref[:, columns], batches)], axis=0
        )
        centered = (exact(mixing, mixed, 0, 0) - mean_col) * inverse_col
        centered_ref[:, columns] = centered
        normed = centered * gain2 + bias2
        hidden_ref[:, columns] = (normed * sigmoid(normed)).astype(bf16)
        return carry

    lax.fori_loop(0, cells // piece, decode, 0)


def middle(encoded, index, valid, noise, small_weights, batches, pad, genes_all):
    cells = index.shape[1]
    width = LANES
    genes_axis = lax.axis_size("gene")
    slab = cells // genes_axis
    return pl.pallas_call(
        functools.partial(
            middle_kernel, batches=batches, latent=noise.shape[0], genes_all=genes_all
        ),
        out_shape=[
            jax.ShapeDtypeStruct((width, cells), bf16),
            jax.ShapeDtypeStruct((width, cells), f32),
            jax.ShapeDtypeStruct((pad, cells), f32),
            jax.ShapeDtypeStruct((1, cells), f32),
            jax.ShapeDtypeStruct((8, LANES), f32),
            jax.ShapeDtypeStruct((width, slab), f32),
            jax.ShapeDtypeStruct((2 * pad, slab), f32),
            jax.ShapeDtypeStruct((8 + 3 * pad + 2 * batches, LANES), f32),
        ],
        in_specs=[IN_VMEM] * 9,
        out_specs=[IN_VMEM] * 8,
        scratch_shapes=row_boxes() + [pltpu.SemaphoreType.DMA((2,))] * 4 + gather_sems(),
        compiler_params=talking(1),
        name="middle",
    )(encoded, index, valid, noise, *small_weights)


def middle_back_kernel(
    grad_ref,
    centered_ref,
    sample_ref,
    index_ref,
    valid_ref,
    noise_ref,
    pack_ref,
    stats_ref,
    first_ref,
    heads_ref,
    output_ref,
    genes_ref,
    grad16_ref,
    small_ref,
    norms_ref,
    output_sum_ref,
    genes_sum_ref,
    part_ref,
    slab_box,
    box1,
    box2,
    box3,
    box4,
    output_box,
    half_box,
    half_give,
    genes_box,
    slab_sems,
    sems1,
    sems2,
    sems3,
    sems4,
    grad_far,
    grad_near,
    output_sems,
    genes_sems,
    *,
    batches,
    latent,
):
    group, team = Team("gene"), Team("cell")
    cell = lax.axis_index("cell")
    bit, near, far = lax.rem(cell, 2), cell + 1 - 2 * lax.rem(cell, 2), lax.rem(cell + 2, 4)
    half = output_ref.shape[1] // 2

    def swap(source, target, other, number):
        copy = pltpu.make_async_remote_copy(
            src_ref=source,
            dst_ref=target,
            send_sem=output_sems.at[number, 0],
            recv_sem=output_sems.at[number, 1],
            device_id=(group.gene, other),
            device_id_type=MESH,
        )
        copy.start()
        return copy

    def rows_of(number):
        return pl.ds(pl.multiple_of(number * half, 8), half)
    width, slab = first_ref.shape
    cells = grad_ref.shape[1]
    pad = sample_ref.shape[0]
    mixing_rows, heads_rows, _ = pack_layout(pad, batches)
    depth = pad + batches

    def part(other):
        return pl.ds(pl.multiple_of(other * slab, LANES), slab)

    mine = part(group.me)
    greet(group, team)
    swap1 = swap(output_ref.at[1 - bit], output_box, near, 0)
    genes_box[cell] = genes_ref[...]

    def tell(step, carry):
        other = lax.rem(cell + step, team.size)
        pltpu.make_async_remote_copy(
            src_ref=genes_ref,
            dst_ref=genes_box.at[cell],
            send_sem=genes_sems.at[0],
            recv_sem=genes_sems.at[1],
            device_id=(group.gene, other),
            device_id_type=MESH,
        ).start()
        return carry

    lax.fori_loop(1, team.size, tell, 0)
    inverse1, inverse2 = stats_ref[0:1, :], stats_ref[1:2, :]
    count, scale = stats_ref[2:3, 0:1], stats_ref[3:4, 0:1]
    factor2 = inverse2 * pack_ref[2:3, :]
    gain1, bias1, gain2, bias2, factor1 = columns_of(
        [pack_ref[i : i + 1, :] for i in range(4)] + [inverse1 * pack_ref[0:1, :]]
    )
    latent_rows = pack_ref[8 : 8 + pad, :] * factor2
    piece = pick_chunk(cells, 512)

    def gather(i, carry):
        gains, shifts, products = carry
        columns = pl.ds(pl.multiple_of(i * piece, LANES), piece)
        centered = centered_ref[:, columns]
        grad = grad_ref[:, columns] * slope_of(centered * gain2 + bias2)
        part_ref[:, columns] = exact(latent_rows, grad, 1, 0)
        mixed = jnp.concatenate(
            [sample_ref[:, columns], hot_rows(index_ref[:, columns], batches)], axis=0
        )
        return (
            gains + fold_lanes(grad * centered),
            shifts + fold_lanes(grad),
            products + exact(mixed, grad, 1, 1),
        )

    zeros = jnp.zeros((width, LANES), f32)
    gains, shifts, products = lax.fori_loop(
        0, cells // piece, gather, (zeros, zeros, jnp.zeros((depth, width), f32))
    )

    finish = spread_box(team, box1, eight_rows([row_sums(gains), row_sums(shifts)]), sems1)
    group.send(lambda other: part_ref.at[:, part(other)], slab_box.at[group.me], slab_sems)
    slab_box[group.me] = part_ref[:, mine]
    finish = spread_box(group, box2, finish(), sems2)
    swap1.wait()
    own, given = rows_of(far // 2), rows_of(cell // 2)
    half_give[...] = output_ref[bit, own] + output_box[own]
    swap2 = swap(half_give, half_box, far, 1)
    output_sum_ref[given] = output_ref[bit, given] + output_box[given]
    hot = hot_rows(index_ref[:, mine], batches)
    valid = valid_ref[:, mine].astype(f32)
    mixed = valid * jnp.concatenate([sample_ref[:, mine], hot], axis=0)
    centered2 = centered_ref[:, mine]
    share = valid / count
    mixed_sum = jnp.sum(mixed, axis=1, keepdims=True)
    mixed_product = exact(mixed, centered2, 1, 1)
    noise = jnp.concatenate([noise_ref[:, mine], jnp.zeros((pad - latent, slab), f32)], axis=0)
    mean_z, log_var = heads_ref[0:pad, :], heads_ref[pad : 2 * pad, :]
    log_factor = 0.5 * noise * jnp.exp(0.5 * log_var)
    scaled = valid * scale
    grad_log_own = scaled * (jnp.exp(log_var) - 1.0) * 0.5
    centered1 = first_ref[...]
    normed1 = centered1 * gain1 + bias1
    sigma1 = sigmoid(normed1)
    hidden1 = normed1 * sigma1
    slope1 = sigma1 * (1.0 + normed1 * (1.0 - sigma1))

    sums = finish()
    gain2_grad, shift2_grad = sums[0:1], sums[1:2]
    small_ref[0:depth, :] = factor2 * (
        products - (mixed_sum * shift2_grad + mixed_product * gain2_grad) / count
    )
    gain_col, shift_col = columns_of([gain2_grad, shift2_grad])
    pulled = exact(latent_rows, shift_col + centered2 * gain_col, 1, 0)
    others = slab_box.at[pl.ds(0, group.size - 1)]
    await_bytes(others, slab_sems.at[0])
    await_bytes(others, slab_sems.at[1])
    grad_sample = box_sum(slab_box) - share * pulled
    grad_heads = jnp.concatenate(
        [grad_sample + scaled * mean_z, grad_sample * log_factor + grad_log_own], axis=0
    )
    grad_normed1 = exact(pack_ref[heads_rows, :], grad_heads, 0, 0) * slope1
    rows = [row_sums(fold_lanes(grad_normed1 * centered1)), row_sums(fold_lanes(grad_normed1))]
    finish = spread_box(group, box4, spread_box(team, box3, eight_rows(rows), sems3)(), sems4)
    swap2.wait()
    output_sum_ref[given] = output_sum_ref[given] + half_box[...]
    swap3 = swap(output_sum_ref.at[given], output_sum_ref.at[given], far, 2)
    small_ref[depth : depth + 2 * pad, :] = exact(grad_heads, hidden1, 1, 1)
    small_ref[depth + 2 * pad : depth + 4 * pad, :] = fold_lanes(grad_heads)
    sums = finish()
    gain1_grad, shift1_grad = sums[0:1], sums[1:2]
    norms_ref[...] = eight_rows([gain1_grad, shift1_grad, gain2_grad, shift2_grad])
    gain_col, shift_col = columns_of([gain1_grad, shift1_grad])
    grad_pre1 = factor1 * (grad_normed1 - share * (shift_col + centered1 * gain_col))
    grad16_ref[:, mine] = grad_pre1.astype(bf16)
    gathering = Gather(grad16_ref, slab, grad_far, grad_near)
    gathering.start()
    small_ref[depth + 4 * pad :, :] = exact(hot, grad_pre1, 1, 1)
    gathering.finish()
    others = genes_box.at[pl.ds(0, team.size - 1)]
    await_bytes(others, genes_sems.at[0])
    await_bytes(others, genes_sems.at[1])
    genes_sum_ref[...] = box_sum(genes_box)
    swap3.wait()


def middle_back(
    grad,
    centered,
    sample,
    index,
    valid,
    noise,
    pack,
    stats,
    first,
    heads,
    output_grad,
    genes_grad,
    batches,
):
    cells = index.shape[1]
    width, slab = first.shape
    pad = sample.shape[0]
    genes_axis = lax.axis_size("gene")
    return pl.pallas_call(
        functools.partial(middle_back_kernel, batches=batches, latent=noise.shape[0]),
        out_shape=[
            jax.ShapeDtypeStruct((width, cells), bf16),
            jax.ShapeDtypeStruct((5 * pad + 2 * batches, LANES), f32),
            jax.ShapeDtypeStruct((8, LANES), f32),
            jax.ShapeDtypeStruct(output_grad.shape[1:], f32),
            jax.ShapeDtypeStruct(genes_grad.shape, f32),
        ],
        in_specs=[IN_VMEM] * 12,
        out_specs=[IN_VMEM] * 5,
        scratch_shapes=[
            pltpu.VMEM((pad, cells), f32),
            pltpu.VMEM((genes_axis, pad, slab), f32),
            *row_boxes(),
            pltpu.VMEM(output_grad.shape[1:], f32),
            pltpu.VMEM((output_grad.shape[1] // 2, LANES), f32),
            pltpu.VMEM((output_grad.shape[1] // 2, LANES), f32),
            pltpu.VMEM((lax.axis_size("cell"), *genes_grad.shape), f32),
        ]
        + [pltpu.SemaphoreType.DMA((2,))] * 5
        + gather_sems()
        + [pltpu.SemaphoreType.DMA((3, 2)), pltpu.SemaphoreType.DMA((2,))],
        compiler_params=talking(4),
        name="middle_back",
    )(
        grad,
        centered,
        sample,
        index,
        valid,
        noise,
        pack,
        stats,
        first,
        heads,
        output_grad,
        genes_grad,
    )


def encoder_grad_kernel(
    counts_ref,
    grad_ref,
    small_ref,
    output_ref,
    sum_ref,
    total_ref,
    output_sum_ref,
    near_give,
    near_box,
    far_give,
    far_box,
    whole_box,
    small_box,
    near_sems,
    far_sems,
    last_sems,
    small_sems,
    output_box,
    output_sems,
):
    gene, cell = lax.axis_index("gene"), lax.axis_index("cell")
    bit, high = lax.rem(cell, 2), cell // 2
    near, far = cell + 1 - 2 * bit, lax.rem(cell + 2, 4)
    quarter, cells = counts_ref.shape
    step = pl.program_id(0)

    def copy(source, target, sems, where):
        return pltpu.make_async_remote_copy(
            src_ref=source,
            dst_ref=target,
            send_sem=sems.at[0],
            recv_sem=sems.at[1],
            device_id=where,
            device_id_type=MESH,
        )

    rounds = [(gene, near), (gene, far)]
    size = 1
    while size < lax.axis_size("gene"):
        rounds.append((gene + size - 2 * size * lax.rem(gene // size, 2), cell))
        size *= 2

    def small_copy(number):
        source = small_ref if number == 0 else small_box.at[1, number - 1]
        return copy(source, small_box.at[0, number], small_sems.at[number], rounds[number])

    def small_end(number):
        small_copy(number).wait()
        source = small_ref[...] if number == 0 else small_box[1, number - 1]
        small_box[1, number] = source + small_box[0, number]

    def rows_of(bit, high):
        return pl.ds(pl.multiple_of((2 * bit + high) * quarter, ROWS), quarter)

    def near_copy(number):
        return copy(near_give.at[number], near_box.at[number], near_sems.at[number], (gene, near))

    far_copy = copy(far_give, far_box, far_sems, (gene, far))

    def last_copy(number, high, other):
        rows = rows_of(bit, high)
        return copy(whole_box.at[rows], whole_box.at[rows], last_sems.at[number], (gene, other))

    output_copy = copy(output_box.at[bit], output_box.at[bit], output_sems, (gene, near))

    @pl.when(step == 0)
    def _():
        output_box[bit] = output_ref[...]
        barrier = pltpu.get_barrier_semaphore()
        for where in rounds:
            pl.semaphore_signal(barrier, inc=1, device_id=where, device_id_type=MESH)
        pl.semaphore_wait(barrier, len(rounds))
        small_copy(0).start()
        output_copy.start()

    piece = pick_chunk(cells, 512)

    def part():
        total = jnp.zeros((quarter, LANES), f32)
        for at in range(0, cells, piece):
            columns = slice(at, at + piece)
            inputs = jnp.log(counts_ref[:, columns].astype(f32) + 1.0).astype(bf16)
            total = total + lax.dot_general(
                inputs,
                grad_ref[:, columns],
                (((1,), (1,)), ((), ())),
                preferred_element_type=f32,
            )
        return total

    value = part()

    @pl.when(step < 2)
    def _():
        near_give[step] = value
        near_copy(step).start()

    @pl.when(step == 1)
    def _():
        small_end(0)
        small_copy(1).start()

    @pl.when(step == 2)
    def _():
        near_copy(0).wait()
        far_give[...] = value + near_box[0]
        far_copy.start()
        small_end(1)
        small_copy(2).start()

    @pl.when(step == 3)
    def _():
        near_copy(1).wait()
        total = value + near_box[1]
        small_end(2)
        if len(rounds) > 3:
            small_copy(3).start()
        far_copy.wait()
        whole_box[rows_of(bit, high), :] = total + far_box[...]
        own_far, own_near = last_copy(0, high, far), last_copy(1, high, near)
        own_far.start()
        own_near.start()
        for number in range(3, len(rounds)):
            small_end(number)
            if number + 1 < len(rounds):
                small_copy(number + 1).start()
        total_ref[...] = small_box[1, len(rounds) - 1]
        own_far.wait()
        passed = last_copy(2, 1 - high, near)
        passed.start()
        own_near.wait()
        passed.wait()
        sum_ref[...] = whole_box[...]
        output_copy.wait()
        output_sum_ref[...] = output_box[...]


def encoder_grad(counts_t, grad, small, output):
    genes, cells = counts_t.shape
    quarter = ROWS * pl.cdiv(genes, 4 * ROWS)
    rounds = 2
    while 2 ** (rounds - 2) < lax.axis_size("gene"):
        rounds += 1

    def quarter_of(i):
        cell = lax.axis_index("cell")
        bit, high = lax.rem(cell, 2), cell // 2
        half = lax.rem(bit + 1 + i // 2, 2)
        return (2 * half + lax.rem(high + 1 + i, 2), 0)

    box = pltpu.VMEM((2, quarter, LANES), f32)
    one = pltpu.VMEM((quarter, LANES), f32)
    return pl.pallas_call(
        encoder_grad_kernel,
        grid=(4,),
        in_specs=[pl.BlockSpec((quarter, cells), quarter_of)]
        + [whole(array) for array in (grad, small, output)],
        out_specs=[
            pl.BlockSpec((4 * quarter, LANES), lambda i: (0, 0)),
            pl.BlockSpec(small.shape, lambda i: (0, 0)),
            pl.BlockSpec((2, *output.shape), lambda i: (0, 0, 0)),
        ],
        out_shape=[
            jax.ShapeDtypeStruct((4 * quarter, LANES), f32),
            jax.ShapeDtypeStruct(small.shape, f32),
            jax.ShapeDtypeStruct((2, *output.shape), f32),
        ],
        scratch_shapes=[
            box,
            box,
            one,
            one,
            pltpu.VMEM((4 * quarter, LANES), f32),
            pltpu.VMEM((2, rounds, *small.shape), f32),
            pltpu.SemaphoreType.DMA((2, 2)),
            pltpu.SemaphoreType.DMA((2,)),
            pltpu.SemaphoreType.DMA((3, 2)),
            pltpu.SemaphoreType.DMA((rounds, 2)),
            pltpu.VMEM((2, *output.shape), f32),
            pltpu.SemaphoreType.DMA((2,)),
        ],
        compiler_params=talking(5),
        name="encoder_grad",
    )(counts_t, grad, small, output)


def finish_kernel(*refs, pad, latent, batches):
    grad16_ref, encoder_grad_ref, output_grad_ref, genes_grad_ref, small_ref, norms_ref = refs[:6]
    ins, input_ref, outs = refs[6:30], refs[30], refs[31:]

    def group(number):
        return [part[8 * i + number] for part in (ins, outs) for i in range(3)]

    def step(number, here, grad):
        weight, momentum, average, *results = group(number)
        old = [ref[here] for ref in (weight, momentum, average)]
        for ref, value in zip(results, nesterov(*old, grad, step_rates[number])):
            ref[here] = value

    input_ref[...] = jnp.dot(
        ins[0][...].astype(bf16), grad16_ref[...], preferred_element_type=f32
    )
    step(0, (slice(None), slice(None)), encoder_grad_ref[...])
    for k in range(2):
        rows = pl.ds(k, output_grad_ref.shape[1], stride=2)
        step(1, (rows, slice(None)), output_grad_ref[k])
    step(2, (slice(None), slice(None)), genes_grad_ref[0:3, :])

    @pl.when(pl.program_id(0) == 0)
    def _():
        depth = pad + batches
        columns = slice(None)
        step(3, (columns, columns), small_ref[depth + 4 * pad :, :])
        step(4, (columns, columns), norms_ref[0:4, :])
        step(7, (slice(0, latent), columns), small_ref[0:latent, :])
        step(7, (slice(latent, None), columns), small_ref[pad:depth, :])
        bias = exact(
            jnp.ones((8, LANES), f32), small_ref[depth + 2 * pad : depth + 4 * pad, :], 1, 1
        )
        for half in range(2):
            rows = slice(half * latent, (half + 1) * latent)
            at = half * pad
            step(5, (rows, columns), small_ref[depth + at : depth + at + latent, :])
            step(6, (slice(None), rows), bias[0:1, at : at + latent])


def finish(grad16, encoder_grad, output_grad, genes_grad, small, norms, states, pad, latent, batches):
    width, cells = grad16.shape
    genes = states[0][0].shape[0]
    block = 2 * LANES
    one = pl.BlockSpec((block, LANES), lambda i: (i, 0))
    two = pl.BlockSpec((2 * block, LANES), lambda i: (i, 0))
    both = pl.BlockSpec((2, block, LANES), lambda i: (0, i, 0))

    def rows(count):
        return pl.BlockSpec((count, block), lambda i: (0, i))

    specs = [spec for state in states for spec in [one, two, rows(3), *map(whole, state[3:])]]
    flat = [array for state in states for array in state]
    results = pl.pallas_call(
        functools.partial(finish_kernel, pad=pad, latent=latent, batches=batches),
        grid=(pl.cdiv(genes, block),),
        in_specs=[whole(grad16), one, both, rows(4), whole(small), whole(norms)] + specs,
        out_specs=[pl.BlockSpec((block, cells), lambda i: (i, 0))] + specs,
        out_shape=[jax.ShapeDtypeStruct((genes, cells), f32)]
        + [jax.ShapeDtypeStruct(array.shape, f32) for array in flat],
        compiler_params=PARAMS,
        name="finish",
    )(grad16, encoder_grad, output_grad, genes_grad, small, norms, *flat)
    return results[0], [results[1 + 8 * i : 9 + 8 * i] for i in range(3)]


def fill_hidden(long_ref, hidden_ref, top):
    width, chunk = hidden_ref.shape
    long_ref[0:width, :] = hidden_ref[...]
    index = lax.broadcasted_iota(jnp.int32, (HOT_DEPTH - width, chunk), 0)
    extra = jnp.where(index < 3, 1.0, 0.0)
    if top is not None:
        high = (-top).astype(bf16).astype(f32)
        middle = (-top - high).astype(bf16).astype(f32)
        low = (-top - high - middle).astype(bf16).astype(f32)
        extra = jnp.where(index == 3, high, extra)
        extra = jnp.where(index == 4, middle, extra)
        extra = jnp.where(index == 5, low, extra)
    long_ref[width:HOT_DEPTH, :] = extra.astype(bf16)


def sweep(blocks, block, groups, pieces, logits, terms, back, carry):
    def rows_of(number):
        return pl.ds(pl.multiple_of(number * block, ROWS), block)

    logits(0, rows_of(0), block, pieces)

    def beside(i, later, earlier):
        acts = [
            lambda piece=piece: logits(1 - i, rows_of(later), block, [piece]) for piece in pieces
        ]
        if back is not None:
            acts.append(lambda: back(1 - i, rows_of(earlier), block))
        spaced = []
        for step in range(groups):
            spaced.append(acts.pop(0) if acts and step % 2 == 0 else lambda: None)
        return spaced + acts

    def pair(p, carry):
        first = 2 * p
        last, ahead = jnp.maximum(first - 1, 0), jnp.minimum(first + 2, blocks - 1)
        carry = terms(0, first, carry, beside(0, first + 1, last))
        return terms(1, first + 1, carry, beside(1, ahead, first))

    carry = lax.fori_loop(0, blocks // 2, pair, carry)
    if back is not None and blocks > 1:
        back(1, rows_of(blocks // 2 * 2 - 1), block)
    if blocks % 2:
        carry = terms(0, blocks - 1, carry, ())
        if back is not None:
            back(0, rows_of(blocks - 1), block)
    return carry


def logit_pieces(ks, chunk):
    width = min(chunk, WIDE)
    return [(k, slice(j, j + width)) for k in range(ks) for j in range(0, chunk, width)]


def totals_kernel(
    hidden_ref, weight_ref, sample_ref, out_ref, long_ref, even_ref, odd_ref, box, sems, *, genes, chunk
):
    full, groups, tail = split_rows(genes, 26)
    block = ROWS * groups
    blocks = full // groups
    values = (even_ref, odd_ref)
    fill_hidden(long_ref, hidden_ref, None)
    pieces = logit_pieces(1, chunk)

    @pl.when(pl.program_id(0) == 0)
    def _():
        greet(Team("gene"))

    def logits(i, rows, size, which):
        for _, columns in which:
            values[i][0:size, columns] = jnp.dot(
                weight_ref[0, rows, :], long_ref[:, columns], preferred_element_type=f32
            )

    def online(value_ref, size, carry, beside=()):
        best, total = carry
        fresh = best
        for i in range(0, size, 8):
            fresh = jnp.maximum(fresh, value_ref[i : i + 8, :])
        total = total * jnp.exp2((best - fresh) * (1.0 / ln2))
        for i in range(0, size, 8):
            for act in beside[i // 8 :: size // 8]:
                act()
            total = total + jnp.exp2((value_ref[i : i + 8, :] - fresh) * (1.0 / ln2))
        return fresh, total

    def terms(i, number, carry, beside):
        return online(values[i], block, carry, beside)

    carry = (jnp.full((8, chunk), -jnp.inf, f32), jnp.zeros((8, chunk), f32))
    carry = sweep(blocks, block, groups, pieces, logits, terms, None, carry)
    if tail:
        logits(1, pl.ds(full * ROWS, ROWS), ROWS, pieces)
        carry = online(odd_ref, ROWS, carry)
    best, total = carry
    top = jnp.max(best, axis=0, keepdims=True)
    total = total * jnp.exp2((best - top) * (1.0 / ln2))
    shared = Shared(box, sems, chunk)
    shared.send(top, jnp.sum(total, axis=0, keepdims=True))

    @pl.when(pl.program_id(0) == pl.num_programs(0) - 1)
    def _():
        shared.finish()
        top = box[0, 0:1, :]
        for i in range(1, box.shape[0]):
            top = jnp.maximum(top, box[i, 0:1, :])
        total = jnp.zeros_like(top)
        for i in range(box.shape[0]):
            total = total + box[i, 1:2, :] * jnp.exp(box[i, 0:1, :] - top)
        inverse = 1.0 / total
        out_ref[0:1, :] = top
        out_ref[1:2, :] = sample_ref[sample_ref.shape[0] - 1 :, :] * inverse
        out_ref[2:3, :] = inverse
        out_ref[3:4, :] = inverse


def totals(hidden, weights, sample, genes):
    width, cells = hidden.shape
    chunk = pick_chunk(cells, 2048)
    groups = split_rows(genes, 26)[1]
    return pl.pallas_call(
        functools.partial(totals_kernel, genes=genes, chunk=chunk),
        grid=(cells // chunk,),
        in_specs=[column_blocks(width, chunk), whole(weights), whole(sample)],
        out_specs=pl.BlockSpec((4, cells), lambda i: (0, 0)),
        out_shape=jax.ShapeDtypeStruct((4, cells), f32),
        scratch_shapes=[pltpu.VMEM((HOT_DEPTH, chunk), bf16)]
        + [pltpu.VMEM((ROWS * groups, chunk), f32)] * 2
        + [pltpu.VMEM((lax.axis_size("gene"), 2, cells), f32), pltpu.SemaphoreType.DMA((2,))],
        compiler_params=talking(2),
        name="totals",
    )(hidden, weights, sample)


def likelihood_kernel(
    counts_ref,
    hidden_ref,
    rows_ref,
    share_ref,
    all_rows_ref,
    sample_ref,
    valid_ref,
    weight_ref,
    theta_ref,
    log_ref,
    slope_ref,
    gammas_ref,
    digammas_ref,
    slopes_ref,
    sums_ref,
    grad_hidden_ref,
    grad_weight_ref,
    grad_bias_ref,
    grad_theta_ref,
    long_ref,
    even_ref,
    odd_ref,
    even_grad_ref,
    odd_grad_ref,
    box,
    sems,
    *,
    genes,
    chunk,
    genes_all,
):
    full, groups, tail = split_rows(genes, 12)
    block = ROWS * groups
    blocks = full // groups
    width = hidden_ref.shape[0]

    @pl.when(pl.program_id(0) == 0)
    def _():
        for ref in (grad_weight_ref, grad_bias_ref, grad_theta_ref):
            ref[...] = jnp.zeros_like(ref)
        greet(Team("gene"))

    fill_hidden(long_ref, hidden_ref, rows_ref[0:1, :])
    wide = min(WIDE, chunk)
    tiles = [slice(j, j + wide) for j in range(0, chunk, wide)]
    ratio_all = rows_ref[1:2, :]
    share_all = share_ref[...]

    def two(x):
        return jnp.concatenate([x] * (wide // LANES), axis=1)

    def look(t, c):
        return jnp.concatenate([jnp.take_along_axis(t, c[:, q:q+LANES], axis=1) for q in range(0, wide, LANES)], axis=1)

    def group(value_ref, grad_ref, held, span, read, carry):
        losses, sums = [], []
        theta = two(theta_ref.at[span][held, :])
        log_theta = two(log_ref.at[span][held, :])
        log_slope = two(slope_ref.at[span][held, :])
        gammas = gammas_ref.at[span][held, :]
        digammas = digammas_ref.at[span][held, :]
        grad_bias = grad_bias_ref.at[span][held, :]
        grad_theta = grad_theta_ref.at[span][held, :]
        for j, columns in enumerate(tiles):
            count = read(columns)
            counted = count.astype(f32)
            minus = value_ref[1, held, columns] * (-1.0 / ln2)
            share = share_all[:, columns]
            rate = jnp.exp2(value_ref[0, held, columns] * (1.0 / ln2)) * ratio_all[:, columns]
            near = rate + rate_epsilon
            both = theta + near
            inverse_both = 1.0 / both
            log_both = jnp.log2(both)
            upper = jnp.maximum(minus, 0.0)
            lower = jnp.minimum(minus, 0.0)
            one_pi = 1.0 + jnp.exp2(lower - upper)
            sigma_pi = jnp.exp2(lower) * (1.0 / one_pi)
            zero = count < 1
            pi_theta = theta * (log_theta - log_both) + minus
            inflated = jnp.where(zero, pi_theta, 1e30)
            small = jnp.exp2(-jnp.abs(inflated))
            inverse_theta = 1.0 / (1.0 + small)
            sigma = jnp.where(inflated >= 0.0, 1.0, small) * inverse_theta
            loss = (upper - jnp.where(zero, jnp.maximum(pi_theta, 0.0), pi_theta)) + (
                jnp.log2(one_pi * inverse_theta)
                - counted * (jnp.log2(near) - log_both)
                - look(gammas, count)
            )
            pull = (sigma * theta + counted) * inverse_both
            slope = rate * (pull - counted * (1.0 / near))
            slopes_ref.at[span][held, columns] = slope
            grad_dropout = (sigma - sigma_pi) * share
            grad_ref[held, columns] = grad_dropout.astype(bf16)
            grad_bias = grad_bias + fold_lanes(grad_dropout)
            grad_theta = grad_theta + fold_lanes(share * (
                (pull - sigma * (log_slope - ln2 * log_both))
                - look(digammas, count)
            ))
            losses.append(carry[0][j] + loss[:8] + loss[8:])
            sums.append(carry[1][j] + slope[:8] + slope[8:])
        grad_bias_ref.at[span][held, :] = grad_bias
        grad_theta_ref.at[span][held, :] = grad_theta
        return tuple(losses), tuple(sums)

    pieces = logit_pieces(2, chunk)
    values, grads = (even_ref, odd_ref), (even_grad_ref, odd_grad_ref)

    def logits(i, rows, size, which):
        for k, columns in which:
            values[i][k, 0:size, columns] = jnp.dot(
                weight_ref[k, rows, :], long_ref[:, columns], preferred_element_type=f32
            )

    def back(i, rows, size):
        grad = grads[i][0:size, :]
        grad_weight_ref[rows, :] += lax.dot_general(
            grad, hidden_ref[...], (((1,), (1,)), ((), ())), preferred_element_type=f32
        )
        grad_hidden_ref[...] += lax.dot_general(
            weight_ref[1, rows, 0:width],
            grad,
            (((0,), (0,)), ((), ())),
            preferred_element_type=f32,
        )

    def terms(buffer, number, carry, beside):
        span = pl.ds(pl.multiple_of(number * block, ROWS), block)
        for i in range(groups):
            for act in beside[i::groups]:
                act()
            held = slice(i * ROWS, (i + 1) * ROWS)
            carry = group(
                values[buffer],
                grads[buffer],
                held,
                span,
                lambda columns, held=held: counts_ref.at[span][held, columns],
                carry,
            )
        return carry

    grad_hidden_ref[...] = jnp.zeros_like(grad_hidden_ref)
    odd_grad_ref[...] = jnp.zeros_like(odd_grad_ref)
    carry = tuple(jnp.zeros((8, wide), f32) for _ in tiles)
    carry = sweep(blocks, block, groups, pieces, logits, terms, back, (carry, carry))
    if tail:
        rows = pl.ds(full * ROWS, ROWS)
        logits(1, rows, ROWS, pieces)
        carry = group(
            odd_ref,
            odd_grad_ref,
            slice(0, ROWS),
            rows,
            lambda cols: tail_rows(counts_ref, full * ROWS, genes, cols, jnp.int32),
            carry,
        )
        back(1, rows, ROWS)
    shared = Shared(box, sems, chunk)
    rows = [
        jnp.concatenate([jnp.sum(part, axis=0, keepdims=True) for part in carry[i]], axis=1)
        for i in (1, 0)
    ]
    shared.send(rows[0], rows[1] * ln2)

    @pl.when(pl.program_id(0) == pl.num_programs(0) - 1)
    def _():
        shared.finish()
        total = box_sum(box)
        at = sample_ref.shape[0] - 2
        sums_ref[0:1, :] = total[0:1] * all_rows_ref[2:3, :]
        sums_ref[1:2, :] = (
            valid_ref[...].astype(f32) * (total[1:2] + sample_ref[at : at + 1, :]) / genes_all
        )


def likelihood(counts_t, hidden, rows, share, sample, valid, weights, gene_tables, genes_all):
    genes, cells = counts_t.shape
    size = weights.shape[1]
    width = hidden.shape[0]
    chunk = pick_chunk(cells, 512)
    groups = split_rows(genes, 12)[1]
    row = column_blocks(1, chunk)
    per_gene = pl.BlockSpec((size, LANES), lambda i: (0, 0))
    return pl.pallas_call(
        functools.partial(likelihood_kernel, genes=genes, chunk=chunk, genes_all=genes_all),
        grid=(cells // chunk,),
        in_specs=[column_blocks(genes, chunk), column_blocks(width, chunk)]
        + [column_blocks(rows.shape[0], chunk), row]
        + [whole(a) for a in (rows, sample, valid, weights)]
        + [whole(a) for a in gene_tables],
        out_specs=[
            column_blocks(size, chunk),
            pl.BlockSpec((2, cells), lambda i: (0, 0)),
            column_blocks(width, chunk),
        ]
        + [per_gene] * 3,
        out_shape=[
            jax.ShapeDtypeStruct((size, cells), f32),
            jax.ShapeDtypeStruct((2, cells), f32),
            jax.ShapeDtypeStruct((width, cells), f32),
        ]
        + [jax.ShapeDtypeStruct((size, LANES), f32)] * 3,
        scratch_shapes=[pltpu.VMEM((HOT_DEPTH, chunk), bf16)]
        + [pltpu.VMEM((2, ROWS * groups, chunk), f32)] * 2
        + [pltpu.VMEM((ROWS * groups, chunk), bf16)] * 2
        + [pltpu.VMEM((lax.axis_size("gene"), 2, cells), f32), pltpu.SemaphoreType.DMA((2,))],
        compiler_params=talking(3),
        name="likelihood",
    )(counts_t, hidden, rows, share, rows, sample, valid, weights, *gene_tables)


def frequency_kernel(
    slopes_ref,
    hidden_ref,
    rows_ref,
    pull_ref,
    share_ref,
    other_ref,
    weight_ref,
    second_ref,
    dropout_ref,
    theta_ref,
    scale_ref,
    grad_hidden_ref,
    grad_weight_ref,
    genes_ref,
    long_ref,
    even_ref,
    odd_ref,
    even_grad_ref,
    odd_grad_ref,
    grad_bias_ref,
    *,
    genes,
    chunk,
):
    full, groups, tail = split_rows(genes, 26)
    block = ROWS * groups
    blocks = full // groups
    size = weight_ref.shape[1]
    width = hidden_ref.shape[0]
    values, grads = (even_ref, odd_ref), (even_grad_ref, odd_grad_ref)

    @pl.when(pl.program_id(0) == 0)
    def _():
        grad_weight_ref[0] = jnp.zeros((size, LANES), f32)
        grad_weight_ref[1] = second_ref[...]
        grad_bias_ref[...] = jnp.zeros_like(grad_bias_ref)

    fill_hidden(long_ref, hidden_ref, rows_ref[0:1, :])
    pieces = logit_pieces(1, chunk)
    share = share_ref[...]
    pulled = pull_ref[0:1, :] * share

    def logits(i, rows, size, which):
        for _, columns in which:
            values[i][0:size, columns] = jnp.dot(
                weight_ref[0, rows, :], long_ref[:, columns], preferred_element_type=f32
            )

    def group(buffer, held, span):
        exponent = jnp.exp2(values[buffer][held, :] * (1.0 / ln2))
        grad = slopes_ref.at[span][held, :] * share - exponent * pulled
        grads[buffer][held, :] = grad.astype(bf16)
        grad_bias_ref.at[span][held, :] += fold_lanes(grad)

    def terms(buffer, number, carry, beside):
        span = pl.ds(pl.multiple_of(number * block, ROWS), block)
        for i in range(groups):
            for act in beside[i::groups]:
                act()
            group(buffer, slice(i * ROWS, (i + 1) * ROWS), span)
        return carry

    def back(i, rows, size):
        grad = grads[i][0:size, :]
        grad_weight_ref[0, rows, :] += lax.dot_general(
            grad, hidden_ref[...], (((1,), (1,)), ((), ())), preferred_element_type=f32
        )
        grad_hidden_ref[...] += lax.dot_general(
            weight_ref[0, rows, 0:width],
            grad,
            (((0,), (0,)), ((), ())),
            preferred_element_type=f32,
        )

    grad_hidden_ref[...] = other_ref[...]
    odd_grad_ref[...] = jnp.zeros_like(odd_grad_ref)
    sweep(blocks, block, groups, pieces, logits, terms, back, 0)
    if tail:
        rows = pl.ds(full * ROWS, ROWS)
        logits(1, rows, ROWS, pieces)
        group(1, slice(0, ROWS), rows)
        back(1, rows, ROWS)

    @pl.when(pl.program_id(0) == pl.num_programs(0) - 1)
    def _():
        ones = jnp.ones((8, LANES), f32)
        parts = (grad_bias_ref[...], dropout_ref[...], theta_ref[...] * scale_ref[...])
        for i, values in enumerate(parts):
            genes_ref[i : i + 1, :] = exact(ones, values, 1, 1)[0:1]
        genes_ref[3:4, :] = jnp.zeros((1, size), f32)


def frequency(slopes, hidden, rows, pull, share, other, weights, second, dropout, theta, scale, genes):
    size, cells = slopes.shape
    width = hidden.shape[0]
    chunk = pick_chunk(cells, 1024)
    groups = split_rows(genes, 26)[1]
    row = column_blocks(1, chunk)
    wide = column_blocks(width, chunk)
    return pl.pallas_call(
        functools.partial(frequency_kernel, genes=genes, chunk=chunk),
        grid=(cells // chunk,),
        in_specs=[column_blocks(size, chunk), wide, column_blocks(rows.shape[0], chunk)]
        + [column_blocks(2, chunk), row, wide, whole(weights)]
        + [whole(a) for a in (second, dropout, theta, scale)],
        out_specs=[
            wide,
            pl.BlockSpec((2, size, LANES), lambda i: (0, 0, 0)),
            pl.BlockSpec((4, size), lambda i: (0, 0)),
        ],
        out_shape=[
            jax.ShapeDtypeStruct((width, cells), f32),
            jax.ShapeDtypeStruct((2, size, LANES), f32),
            jax.ShapeDtypeStruct((4, size), f32),
        ],
        scratch_shapes=[pltpu.VMEM((HOT_DEPTH, chunk), bf16)]
        + [pltpu.VMEM((ROWS * groups, chunk), f32)] * 2
        + [pltpu.VMEM((ROWS * groups, chunk), bf16)] * 2
        + [pltpu.VMEM((size, LANES), f32)],
        compiler_params=PARAMS,
        name="frequency",
    )(slopes, hidden, rows, pull, share, other, weights, second, dropout, theta, scale)


def local(
    counts,
    batch_index,
    valid_mask,
    noise_draw,
    encoder_weight,
    output_weight,
    gene_vectors,
    batch_shift,
    layer_norm_params,
    head_weight,
    head_bias,
    decoder_input,
    encoder_weight_momentum,
    output_weight_momentum,
    gene_vectors_momentum,
    batch_shift_momentum,
    norm_params_momentum,
    head_weight_momentum,
    head_bias_momentum,
    decoder_input_momentum,
    encoder_weight_average,
    output_weight_average,
    gene_vectors_average,
    batch_shift_average,
    norm_params_average,
    head_weight_average,
    head_bias_average,
    decoder_input_average,
):
    cells, genes = counts.shape
    gene_devices = lax.axis_size("gene")
    genes_all = genes * gene_devices
    latent = head_bias.shape[0] // 2
    batches = batch_shift.shape[0]

    def by_gene(array):
        return jnp.transpose(array, (2, 0, 1)).reshape(2 * genes, -1)

    counts_t = counts.T
    output_rows = by_gene(output_weight)

    pad = 16
    small_weights = (
        layer_norm_params,
        head_bias[None, :],
        decoder_input,
        head_weight.T,
        batch_shift,
    )
    index, valid, noise = batch_index[None, :], valid_mask[None, :], noise_draw.T

    encoded, weights, *gene_tables = encode(counts_t, encoder_weight, output_rows, gene_vectors)
    hidden2, centered2, sample, share, stats, centered1, heads, pack = middle(
        encoded, index, valid, noise, small_weights, batches, pad, genes_all
    )
    rows = totals(hidden2, weights, sample, genes)
    slopes, pull, grad_hidden2, grad_out1, grad_bias1, grad_theta = likelihood(
        counts_t, hidden2, rows, share, sample, valid, weights, gene_tables, genes_all
    )
    cell_loss = pull[1]

    grad_hidden2, grad_out, grad_genes = frequency(
        slopes,
        hidden2,
        rows,
        pull,
        share,
        grad_hidden2,
        weights,
        grad_out1,
        grad_bias1,
        grad_theta,
        gene_tables[0],
        genes,
    )
    grad_pre16, small, norm_rows, grad_out, grad_genes = middle_back(
        grad_hidden2,
        centered2,
        sample,
        index,
        valid,
        noise,
        pack,
        stats,
        centered1,
        heads,
        grad_out,
        grad_genes,
        batches,
    )
    grad_encoder, small, grad_out = encoder_grad(counts_t, grad_pre16, small, grad_out)
    states = [
        (encoder, by_gene(output), vectors, shift, norms, head.T, bias[None, :], mixing)
        for encoder, output, vectors, shift, norms, head, bias, mixing in (
            (
                encoder_weight,
                output_weight,
                gene_vectors,
                batch_shift,
                layer_norm_params,
                head_weight,
                head_bias,
                decoder_input,
            ),
            (
                encoder_weight_momentum,
                output_weight_momentum,
                gene_vectors_momentum,
                batch_shift_momentum,
                norm_params_momentum,
                head_weight_momentum,
                head_bias_momentum,
                decoder_input_momentum,
            ),
            (
                encoder_weight_average,
                output_weight_average,
                gene_vectors_average,
                batch_shift_average,
                norm_params_average,
                head_weight_average,
                head_bias_average,
                decoder_input_average,
            ),
        )
    ]
    input_grad, fresh = finish(
        grad_pre16,
        grad_encoder,
        grad_out,
        grad_genes,
        small,
        norm_rows,
        states,
        pad,
        latent,
        batches,
    )
    results = []
    for encoder, output, vectors, shift, norms, head, bias, mixing in fresh:
        output = jnp.transpose(output.reshape(genes, 2, -1), (1, 2, 0))
        results += [encoder, output, vectors, shift, norms, head.T, bias[0], mixing]
    return (cell_loss, input_grad.T, *results)


def solution(mesh):
    cells, genes = P("cell"), P("gene", None)
    weight_specs = (genes, P(None, None, "gene"), P(None, "gene"), P(), P(), P(), P(), P())
    return jax.shard_map(
        local,
        mesh=mesh,
        in_specs=(P("cell", "gene"), cells, cells, P("cell", None)) + weight_specs * 3,
        out_specs=(cells, P("cell", "gene")) + weight_specs * 3,
        check_vma=False,
    )
```

```python
import functools

import jax
import jax.numpy as jnp
from jax import lax
from jax.experimental import pallas as pl
from jax.experimental.pallas import tpu as pltpu
from jax.sharding import PartitionSpec as P

momentum_decay = 0.9
average_decay = 0.99
norm_epsilon = 0.001
rate_epsilon = 1e-08
step_rates = (110.0, 46000.0, 300000.0, 70000.0, 13000.0, 3700.0, 7600.0, 8000.0)
ln2 = 0.6931471805599453
f32 = jnp.float32
bf16 = jnp.bfloat16
LANES = 128
ROWS = 16
WIDE = 2 * LANES
HOT_DEPTH = 2 * LANES
PARAMS = pltpu.CompilerParams(vmem_limit_bytes=60 << 20)
IN_VMEM = pl.BlockSpec(memory_space=pltpu.VMEM)
MESH = pl.DeviceIdType.MESH


def talking(number):
    return pltpu.CompilerParams(
        collective_id=number, has_side_effects=True, vmem_limit_bytes=60 << 20
    )


def nesterov(weight, momentum, average, grad, rate):
    moment = momentum_decay * momentum + grad
    fresh = weight - rate * (grad + momentum_decay * moment)
    return (fresh, moment, average_decay * average + (1.0 - average_decay) * fresh)


def whole(array):
    return pl.BlockSpec(array.shape, lambda i: (0,) * array.ndim)


def column_blocks(rows, chunk):
    return pl.BlockSpec((rows, chunk), lambda i: (0, i))


def split_rows(genes, most=13):
    full = genes // ROWS
    groups = max(d for d in range(1, most + 1) if full % d == 0)
    return full, groups, genes - full * ROWS


def padded(genes):
    return -(-genes // ROWS) * ROWS


def pick_chunk(cells, most):
    chunk = LANES
    while chunk * 2 <= most and cells % (chunk * 2) == 0:
        chunk *= 2
    return chunk


def tail_rows(ref, start, stop, columns, dtype):
    piece = ref[start:stop, columns]
    filler = jnp.zeros((ROWS - (stop - start), piece.shape[1]), dtype)
    return jnp.concatenate([piece, filler], axis=0)


class Team:
    def __init__(self, axis):
        self.size, self.me = lax.axis_size(axis), lax.axis_index(axis)
        self.gene, self.cell = lax.axis_index("gene"), lax.axis_index("cell")
        self.axis = axis

    def place(self, other):
        return (other, self.cell) if self.axis == "gene" else (self.gene, other)

    def others(self, act):
        def one(step, carry):
            other = lax.rem(self.me + step, self.size)
            act(other, self.place(other))
            return carry

        lax.fori_loop(1, self.size, one, 0)

    def send(self, source, target, sems):
        def act(other, place):
            pltpu.make_async_remote_copy(
                src_ref=source(other),
                dst_ref=target,
                send_sem=sems.at[0],
                recv_sem=sems.at[1],
                device_id=place,
                device_id_type=MESH,
            ).start()

        self.others(act)


def greet(*teams):
    barrier = pltpu.get_barrier_semaphore()

    def act(other, place):
        pl.semaphore_signal(barrier, inc=1, device_id=place, device_id_type=MESH)

    for team in teams:
        team.others(act)
    return lambda: pl.semaphore_wait(barrier, sum(team.size - 1 for team in teams))


def await_bytes(ref, sem):
    pltpu.make_async_copy(ref, ref, sem).wait()


def fold_lanes(values):
    return sum(values[:, j : j + LANES] for j in range(0, values.shape[1], LANES))


def row_sums(folded):
    return jnp.sum(jnp.transpose(folded), axis=0, keepdims=True)


def box_sum(box):
    def add(i, total):
        return total + box[i]

    return lax.fori_loop(1, box.shape[0], add, box[0])


def spread_box(team, box, value, sems):
    box[team.me] = value
    team.send(lambda other: box.at[team.me], box.at[team.me], sems)
    others = box.at[pl.ds(0, team.size - 1)]

    def finish():
        await_bytes(others, sems.at[0])
        await_bytes(others, sems.at[1])
        return box_sum(box)

    return finish


def row_boxes():
    shapes = [(lax.axis_size(axis), 8, LANES) for axis in ("cell", "gene")]
    return [pltpu.VMEM(shape, f32) for shape in shapes * 2]


class Gather:
    def __init__(self, ref, slab, far_sems, near_sems):
        self.ref, self.slab = ref, slab
        self.gene, self.cell = lax.axis_index("gene"), lax.axis_index("cell")
        self.pairs = lax.axis_size("gene") // 2
        self.high, self.low = self.gene // 2, lax.rem(self.gene, 2)
        self.far_sems, self.near_sems = far_sems, near_sems

    def copy(self, source_high, target, sems):
        columns = pl.ds(
            pl.multiple_of((2 * source_high + self.low) * self.slab, LANES), self.slab
        )
        return pltpu.make_async_remote_copy(
            src_ref=self.ref.at[:, columns],
            dst_ref=self.ref.at[:, columns],
            send_sem=sems.at[0],
            recv_sem=sems.at[1],
            device_id=(target, self.cell),
            device_id_type=MESH,
        )

    def far(self, d):
        target = 2 * lax.rem(self.high + d, self.pairs) + self.low
        return self.copy(self.high, target, self.far_sems.at[d - 1])

    def near(self, d):
        source = lax.rem(self.high - d + self.pairs, self.pairs)
        return self.copy(source, 2 * self.high + 1 - self.low, self.near_sems.at[d])

    def start(self):
        self.near(0).start()

        def one(d, carry):
            self.far(d).start()
            return carry

        lax.fori_loop(1, self.pairs, one, 0)

    def finish(self):
        def one(d, carry):
            self.far(d).wait_recv()
            self.near(d).start()
            return carry

        lax.fori_loop(1, self.pairs, one, 0)

        def drain(d, carry):
            self.near(d).wait()
            return carry

        lax.fori_loop(0, self.pairs, drain, 0)

        def drain_far(d, carry):
            self.far(d).wait_send()
            return carry

        lax.fori_loop(1, self.pairs, drain_far, 0)


def gather_sems():
    pairs = lax.axis_size("gene") // 2
    return [pltpu.SemaphoreType.DMA((pairs, 2))] * 2


class Shared:
    def __init__(self, box, sems, chunk):
        self.box, self.sems, self.team = box, sems, Team("gene")
        start = pl.multiple_of(pl.program_id(0) * chunk, LANES)
        self.here = pl.ds(start, chunk)

    def send(self, first, second):
        me = self.team.me
        self.box[me, 0:1, self.here] = first
        self.box[me, 1:2, self.here] = second
        place = self.box.at[me, :, self.here]
        self.team.send(lambda other: place, place, self.sems)

    def finish(self):
        others = self.box.at[pl.ds(0, self.team.size - 1)]
        await_bytes(others, self.sems.at[0])
        await_bytes(others, self.sems.at[1])


def eight_rows(rows):
    filler = jnp.zeros((8 - len(rows), LANES), f32)
    return jnp.concatenate([*rows, filler], axis=0) if len(rows) < 8 else jnp.concatenate(rows, 0)


def columns_of(rows):
    turned = jnp.transpose(jnp.concatenate([eight_rows(rows), jnp.zeros((120, LANES), f32)], 0))
    return [turned[:, i : i + 1] for i in range(len(rows))]


def exact(left, right, left_dim, right_dim):
    return lax.dot_general(
        left,
        right,
        (((left_dim,), (right_dim,)), ((), ())),
        precision=lax.Precision.HIGHEST,
        preferred_element_type=f32,
    )


def hot_rows(index, batches):
    rows = lax.broadcasted_iota(jnp.int32, (batches, index.shape[1]), 0)
    return jnp.where(rows == index, 1.0, 0.0)


def sigmoid(value):
    return 1.0 / (1.0 + jnp.exp(-value))


def slope_of(value):
    sigma = sigmoid(value)
    return sigma * (1.0 + value * (1.0 - sigma))


def pack_layout(latent_pad, batches):
    mixing = slice(8, 8 + latent_pad + batches)
    heads = slice(mixing.stop, mixing.stop + 2 * latent_pad)
    return mixing, heads, slice(heads.stop, heads.stop + batches)


def prepare_tables(number, genes, output_ref, vectors_ref, weights_ref, tables):
    theta_ref, log_ref, slope_ref, gammas_ref, digammas_ref = tables
    lane = lax.broadcasted_iota(jnp.int32, (LANES, LANES), 1)
    below = lax.broadcasted_iota(jnp.int32, (LANES, LANES), 0)
    upper = jnp.where(below < lane, 1.0, 0.0).astype(bf16)
    step = lane.astype(f32)
    block = theta_ref.shape[0]
    for at in range(0, block, LANES):
        here = slice(at, at + LANES)
        turned = jnp.transpose(
            jnp.concatenate([vectors_ref[:, here], jnp.zeros((LANES - 3, LANES), f32)], axis=0)
        )
        inside = number * block + at + below[:, 0:1] < genes
        for k in range(2):
            weight = output_ref[pl.ds(2 * at + k, LANES, stride=2), :]
            weights_ref[k, here, 0:LANES] = jnp.where(inside, weight, 0.0).astype(bf16)
            bias = jnp.where(inside, turned[:, k : k + 1], 0.0 if k else -1e30)
            high = bias.astype(bf16).astype(f32)
            middle = (bias - high).astype(bf16).astype(f32)
            low = (bias - high - middle).astype(bf16).astype(f32)
            extra = jnp.where(lane == 0, high, jnp.where(lane == 1, middle, 0.0))
            extra = jnp.where(lane == 2, low, extra)
            if k == 0:
                extra = jnp.where((lane >= 3) & (lane < 6), 1.0, extra)
            weights_ref[k, here, LANES : 2 * LANES] = extra.astype(bf16)
        theta = jnp.where(inside, jnp.exp(turned[:, 2:3]), 1.0) + jnp.zeros((LANES, LANES), f32)
        log_theta = jnp.log2(theta + rate_epsilon)
        theta_ref[here, :] = theta
        log_ref[here, :] = log_theta
        slope_ref[here, :] = ln2 * log_theta + theta / (theta + rate_epsilon)
        climb = theta + step
        terms = jnp.concatenate([jnp.log2(climb / (step + 1.0)), 1.0 / climb], axis=0)
        high = terms.astype(bf16)
        rest = terms - high.astype(f32)
        middle = rest.astype(bf16)
        low = (rest - middle.astype(f32)).astype(bf16)
        total = jnp.zeros((2 * LANES, LANES), f32)
        for piece in (low, middle, high):
            total = total + jnp.dot(piece, upper, preferred_element_type=f32)
        gammas_ref[here, :] = total[0:LANES]
        digammas_ref[here, :] = total[LANES:]


def encode_order(step, steps):
    last = step // (steps - 1)
    given = 1 - (step + steps - 1) // steps + lax.rem(step, 2) * (1 - last)
    return given, given * ((step + 1) // 2) + (1 - given) * (step // 2 - 1 + last)


def encode_kernel(
    counts_ref,
    encoder_ref,
    output_ref,
    vectors_ref,
    out_ref,
    weights_ref,
    theta_ref,
    log_ref,
    slope_ref,
    gammas_ref,
    digammas_ref,
    inputs_ref,
    weight_ref,
    near_give,
    near_box,
    far_give,
    far_box,
    near_sems,
    far_sems,
    *,
    genes,
    table_blocks,
):
    slab = counts_ref.shape[1]
    width = encoder_ref.shape[1]
    group = Team("gene")
    pairs = group.size // 2
    high, low = group.me // 2, lax.rem(group.me, 2)
    step = pl.program_id(0)
    given, turn = encode_order(step, group.size)

    def place(high, low):
        return (2 * high + low, group.cell)

    def copy(source, target, sems, where):
        return pltpu.make_async_remote_copy(
            src_ref=source,
            dst_ref=target,
            send_sem=sems.at[0],
            recv_sem=sems.at[1],
            device_id=where,
            device_id_type=MESH,
        )

    @pl.when(step == 0)
    def _():
        barrier = pltpu.get_barrier_semaphore()
        pl.semaphore_signal(barrier, inc=1, device_id=place(high, 1 - low), device_id_type=MESH)
        for d in range(1, pairs):
            where = place(lax.rem(high + d, pairs), low)
            pl.semaphore_signal(barrier, inc=1, device_id=where, device_id_type=MESH)
        for at in range(0, weight_ref.shape[1], LANES):
            stop = min(at + LANES, genes)
            piece = encoder_ref[at:stop, :]
            if stop < at + LANES:
                filler = jnp.zeros((at + LANES - stop, width), f32)
                piece = jnp.concatenate([piece, filler], axis=0)
            weight_ref[:, at : at + LANES] = jnp.transpose(piece).astype(bf16)

    def part(ref):
        depth = 3 * LANES
        total = jnp.zeros((8, slab), f32)
        for number, at in enumerate(range(0, genes, depth)):
            held = inputs_ref.at[number % 2]
            stop = min(at + depth, genes)
            for row in range(at, stop, ROWS):
                if row + ROWS <= genes:
                    counted = counts_ref[row : row + ROWS, :].astype(f32)
                else:
                    counted = tail_rows(counts_ref, row, genes, slice(None), jnp.int32).astype(f32)
                held[row - at : row - at + ROWS, :] = jnp.log(counted + 1.0).astype(bf16)
                total = total + counted[:8] + counted[8:]
            here = padded(stop - at)
            product = jnp.dot(
                weight_ref[:, at : at + here], held[0:here, :], preferred_element_type=f32
            )
            if at == 0:
                ref[0:width, :] = product
            else:
                ref[0:width, :] += product
        row = lax.broadcasted_iota(jnp.int32, (8, slab), 0)
        ref[width : width + 8, :] = jnp.where(row == 0, jnp.sum(total, axis=0, keepdims=True), 0.0)

    def near_copy(i):
        return copy(near_give.at[i], near_box.at[i], near_sems.at[i], place(high, 1 - low))

    def far_copy(i):
        target = lax.rem(high + 1 + i, pairs)
        return copy(far_give.at[i], far_box.at[i], far_sems.at[i], place(target, low))

    tables = (theta_ref, log_ref, slope_ref, gammas_ref, digammas_ref)

    @pl.when(step < table_blocks)
    def _():
        prepare_tables(step, genes, output_ref, vectors_ref, weights_ref, tables)

    @pl.when(given == 1)
    def _():
        part(near_give.at[turn])

        @pl.when(step == 0)
        def _():
            pl.semaphore_wait(pltpu.get_barrier_semaphore(), pairs)

        near_copy(turn).start()

    @pl.when(given == 0)
    def _():
        part(out_ref)
        near_copy(turn).wait_recv()
        total = out_ref[...] + near_box[turn]

        @pl.when(turn < pairs - 1)
        def _():
            far_give[turn] = total
            far_copy(turn).start()

        @pl.when(turn == pairs - 1)
        def _():
            def gather(i, total):
                far_copy(i).wait_recv()
                return total + far_box[i]

            out_ref[...] = lax.fori_loop(0, pairs - 1, gather, total)

            def drain(i, carry):
                far_copy(i).wait_send()
                return carry

            lax.fori_loop(0, pairs - 1, drain, 0)

            def drain_near(i, carry):
                near_copy(i).wait_send()
                return carry

            lax.fori_loop(0, pairs, drain_near, 0)


def encode(counts_t, weight, output_rows, vectors):
    genes, cells = counts_t.shape
    devices = lax.axis_size("gene")
    pairs = devices // 2
    slab = cells // devices
    width = weight.shape[1]

    def slab_of(i):
        me = lax.axis_index("gene")
        given, turn = encode_order(i, devices)
        return (0, 2 * lax.rem(me // 2 + 1 + turn, pairs) + lax.rem(me + given, 2))

    box = pltpu.VMEM((pairs, width + 8, slab), f32)
    size = 2 * ROWS * pl.cdiv(genes, 2 * ROWS)
    block = LANES * pl.cdiv(pl.cdiv(size, LANES), devices)
    table_blocks = pl.cdiv(size, block)

    def table_of(i):
        return jnp.minimum(i, table_blocks - 1)

    table = pl.BlockSpec((block, LANES), lambda i: (table_of(i), 0))
    return pl.pallas_call(
        functools.partial(encode_kernel, genes=genes, table_blocks=table_blocks),
        grid=(devices,),
        in_specs=[
            pl.BlockSpec((genes, slab), slab_of),
            whole(weight),
            pl.BlockSpec((2 * block, LANES), lambda i: (table_of(i), 0)),
            pl.BlockSpec((3, block), lambda i: (0, table_of(i))),
        ],
        out_specs=[
            pl.BlockSpec((width + 8, slab), lambda i: (0, 0)),
            pl.BlockSpec((2, block, HOT_DEPTH), lambda i: (0, table_of(i), 0)),
        ]
        + [table] * 5,
        out_shape=[
            jax.ShapeDtypeStruct((width + 8, slab), f32),
            jax.ShapeDtypeStruct((2, size, HOT_DEPTH), bf16),
        ]
        + [jax.ShapeDtypeStruct((size, LANES), f32)] * 5,
        scratch_shapes=[
            pltpu.VMEM((2, 3 * LANES, slab), bf16),
            pltpu.VMEM((width, LANES * pl.cdiv(genes, LANES)), bf16),
            box,
            box,
            box,
            box,
            pltpu.SemaphoreType.DMA((pairs, 2)),
            pltpu.SemaphoreType.DMA((pairs, 2)),
        ],
        compiler_params=talking(6),
        name="encode",
    )(counts_t, weight, output_rows, vectors)


def middle_kernel(
    encoded_ref,
    index_ref,
    valid_ref,
    noise_ref,
    norms_ref,
    bias_ref,
    mixing_ref,
    head_ref,
    shift_ref,
    hidden_ref,
    centered_ref,
    sample_ref,
    share_ref,
    stats_ref,
    first_ref,
    heads_ref,
    pack_ref,
    box1,
    box2,
    box3,
    box4,
    sems1,
    sems2,
    sems3,
    sems4,
    sample_far,
    sample_near,
    *,
    batches,
    latent,
    genes_all,
):
    group, team = Team("gene"), Team("cell")
    width, slab = first_ref.shape
    cells = hidden_ref.shape[1]
    pad = sample_ref.shape[0]
    mixing_rows, heads_rows, shift_rows = pack_layout(pad, batches)
    pack_ref[...] = jnp.zeros_like(pack_ref)
    pack_ref[0:4, :] = norms_ref[...]
    pack_ref[4:5, 0:latent] = bias_ref[:, 0:latent]
    pack_ref[4:5, pad : pad + latent] = bias_ref[:, latent : 2 * latent]
    at = mixing_rows.start
    pack_ref[at : at + latent, :] = mixing_ref[0:latent, :]
    pack_ref[at + pad : at + pad + batches, :] = mixing_ref[latent:, :]
    at = heads_rows.start
    pack_ref[at : at + latent, :] = head_ref[0:latent, :]
    pack_ref[at + pad : at + pad + latent, :] = head_ref[latent:, :]
    pack_ref[shift_rows, :] = shift_ref[...]
    mixing = pack_ref[mixing_rows, :]

    def part(other):
        return pl.ds(pl.multiple_of(other * slab, LANES), slab)

    mine = part(group.me)
    greet(group, team)()
    hot = hot_rows(index_ref[:, mine], batches)
    valid = valid_ref[:, mine].astype(f32)
    shift = exact(pack_ref[shift_rows, :], hot, 0, 0)
    gain1, bias1, gain2, bias2, head_bias = columns_of([pack_ref[i : i + 1, :] for i in range(5)])
    total = encoded_ref[...]
    library = total[width : width + 1, :]
    pre1 = total[0:width, :] + shift

    weighed = valid * pre1
    rows = [
        row_sums(fold_lanes(weighed)),
        row_sums(fold_lanes(weighed * pre1)),
        jnp.broadcast_to(jnp.sum(valid, axis=1, keepdims=True), (1, LANES)),
    ]
    sums = spread_box(team, box1, eight_rows(rows), sems1)()
    sums = spread_box(group, box2, sums, sems2)()
    count = jnp.maximum(sums[2:3], 1.0)
    mean1 = sums[0:1] / count
    inverse1 = lax.rsqrt(sums[1:2] / count - mean1 * mean1 + norm_epsilon)
    mean_col, inverse_col = columns_of([mean1, inverse1])
    centered1 = (pre1 - mean_col) * inverse_col
    first_ref[...] = centered1
    normed1 = centered1 * gain1 + bias1
    hidden1 = normed1 * sigmoid(normed1)
    heads = exact(pack_ref[heads_rows, :], hidden1, 1, 0) + head_bias[0 : 2 * pad]
    heads_ref[...] = heads
    mean_z, log_var = heads[0:pad], heads[pad : 2 * pad]
    noise = jnp.concatenate([noise_ref[:, mine], jnp.zeros((pad - latent, slab), f32)], axis=0)
    sample = mean_z + jnp.exp(0.5 * log_var) * noise
    sample_ref[:, mine] = sample
    sample_ref[pad - 2 : pad - 1, mine] = 0.5 * jnp.sum(
        mean_z * mean_z + jnp.exp(log_var) - log_var - 1.0, axis=0, keepdims=True
    )
    sample_ref[pad - 1 : pad, mine] = library
    gathering = Gather(sample_ref, slab, sample_far, sample_near)
    gathering.start()
    pre2 = exact(mixing, jnp.concatenate([sample, hot], axis=0), 0, 0)
    weighed = valid * pre2
    rows = [row_sums(fold_lanes(weighed)), row_sums(fold_lanes(weighed * pre2))]
    sums = spread_box(team, box3, eight_rows(rows), sems3)()
    finish = spread_box(group, box4, sums, sems4)
    scale = 1.0 / (count * genes_all)
    share_ref[...] = valid_ref[...].astype(f32) * scale[:, 0:1]
    sums = finish()
    mean2 = sums[0:1] / count
    inverse2 = lax.rsqrt(sums[1:2] / count - mean2 * mean2 + norm_epsilon)
    stats_ref[...] = eight_rows([inverse1, inverse2, count, scale])
    mean_col, inverse_col = columns_of([mean2, inverse2])
    gathering.finish()
    piece = pick_chunk(cells, 512)

    def decode(i, carry):
        columns = pl.ds(pl.multiple_of(i * piece, LANES), piece)
        mixed = jnp.concatenate(
            [sample_ref[:, columns], hot_rows(index_ref[:, columns], batches)], axis=0
        )
        centered = (exact(mixing, mixed, 0, 0) - mean_col) * inverse_col
        centered_ref[:, columns] = centered
        normed = centered * gain2 + bias2
        hidden_ref[:, columns] = (normed * sigmoid(normed)).astype(bf16)
        return carry

    lax.fori_loop(0, cells // piece, decode, 0)


def middle(encoded, index, valid, noise, small_weights, batches, pad, genes_all):
    cells = index.shape[1]
    width = LANES
    genes_axis = lax.axis_size("gene")
    slab = cells // genes_axis
    return pl.pallas_call(
        functools.partial(
            middle_kernel, batches=batches, latent=noise.shape[0], genes_all=genes_all
        ),
        out_shape=[
            jax.ShapeDtypeStruct((width, cells), bf16),
            jax.ShapeDtypeStruct((width, cells), f32),
            jax.ShapeDtypeStruct((pad, cells), f32),
            jax.ShapeDtypeStruct((1, cells), f32),
            jax.ShapeDtypeStruct((8, LANES), f32),
            jax.ShapeDtypeStruct((width, slab), f32),
            jax.ShapeDtypeStruct((2 * pad, slab), f32),
            jax.ShapeDtypeStruct((8 + 3 * pad + 2 * batches, LANES), f32),
        ],
        in_specs=[IN_VMEM] * 9,
        out_specs=[IN_VMEM] * 8,
        scratch_shapes=row_boxes() + [pltpu.SemaphoreType.DMA((2,))] * 4 + gather_sems(),
        compiler_params=talking(1),
        name="middle",
    )(encoded, index, valid, noise, *small_weights)


def middle_back_kernel(
    grad_ref,
    centered_ref,
    sample_ref,
    index_ref,
    valid_ref,
    noise_ref,
    pack_ref,
    stats_ref,
    first_ref,
    heads_ref,
    output_ref,
    genes_ref,
    grad16_ref,
    small_ref,
    norms_ref,
    output_sum_ref,
    genes_sum_ref,
    part_ref,
    slab_box,
    box1,
    box2,
    box3,
    box4,
    output_box,
    half_box,
    half_give,
    genes_box,
    slab_sems,
    sems1,
    sems2,
    sems3,
    sems4,
    grad_far,
    grad_near,
    output_sems,
    genes_sems,
    *,
    batches,
    latent,
):
    group, team = Team("gene"), Team("cell")
    cell = lax.axis_index("cell")
    bit, near, far = lax.rem(cell, 2), cell + 1 - 2 * lax.rem(cell, 2), lax.rem(cell + 2, 4)
    half = output_ref.shape[1] // 2

    def swap(source, target, other, number):
        copy = pltpu.make_async_remote_copy(
            src_ref=source,
            dst_ref=target,
            send_sem=output_sems.at[number, 0],
            recv_sem=output_sems.at[number, 1],
            device_id=(group.gene, other),
            device_id_type=MESH,
        )
        copy.start()
        return copy

    def rows_of(number):
        return pl.ds(pl.multiple_of(number * half, 8), half)
    width, slab = first_ref.shape
    cells = grad_ref.shape[1]
    pad = sample_ref.shape[0]
    mixing_rows, heads_rows, _ = pack_layout(pad, batches)
    depth = pad + batches

    def part(other):
        return pl.ds(pl.multiple_of(other * slab, LANES), slab)

    mine = part(group.me)
    greet(group, team)()
    swap1 = swap(output_ref.at[1 - bit], output_box, near, 0)
    genes_box[cell] = genes_ref[...]

    def tell(step, carry):
        other = lax.rem(cell + step, team.size)
        pltpu.make_async_remote_copy(
            src_ref=genes_ref,
            dst_ref=genes_box.at[cell],
            send_sem=genes_sems.at[0],
            recv_sem=genes_sems.at[1],
            device_id=(group.gene, other),
            device_id_type=MESH,
        ).start()
        return carry

    lax.fori_loop(1, team.size, tell, 0)
    inverse1, inverse2 = stats_ref[0:1, :], stats_ref[1:2, :]
    count, scale = stats_ref[2:3, 0:1], stats_ref[3:4, 0:1]
    factor2 = inverse2 * pack_ref[2:3, :]
    gain1, bias1, gain2, bias2, factor1 = columns_of(
        [pack_ref[i : i + 1, :] for i in range(4)] + [inverse1 * pack_ref[0:1, :]]
    )
    latent_rows = pack_ref[8 : 8 + pad, :] * factor2
    piece = pick_chunk(cells, 512)

    def gather(i, carry):
        gains, shifts, products = carry
        columns = pl.ds(pl.multiple_of(i * piece, LANES), piece)
        centered = centered_ref[:, columns]
        grad = grad_ref[:, columns] * slope_of(centered * gain2 + bias2)
        part_ref[:, columns] = exact(latent_rows, grad, 1, 0)
        mixed = jnp.concatenate(
            [sample_ref[:, columns], hot_rows(index_ref[:, columns], batches)], axis=0
        )
        return (
            gains + fold_lanes(grad * centered),
            shifts + fold_lanes(grad),
            products + exact(mixed, grad, 1, 1),
        )

    zeros = jnp.zeros((width, LANES), f32)
    gains, shifts, products = lax.fori_loop(
        0, cells // piece, gather, (zeros, zeros, jnp.zeros((depth, width), f32))
    )

    finish = spread_box(team, box1, eight_rows([row_sums(gains), row_sums(shifts)]), sems1)
    group.send(lambda other: part_ref.at[:, part(other)], slab_box.at[group.me], slab_sems)
    slab_box[group.me] = part_ref[:, mine]
    finish = spread_box(group, box2, finish(), sems2)
    swap1.wait()
    own, given = rows_of(far // 2), rows_of(cell // 2)
    half_give[...] = output_ref[bit, own] + output_box[own]
    swap2 = swap(half_give, half_box, far, 1)
    output_sum_ref[given] = output_ref[bit, given] + output_box[given]
    hot = hot_rows(index_ref[:, mine], batches)
    valid = valid_ref[:, mine].astype(f32)
    mixed = valid * jnp.concatenate([sample_ref[:, mine], hot], axis=0)
    centered2 = centered_ref[:, mine]
    share = valid / count
    mixed_sum = jnp.sum(mixed, axis=1, keepdims=True)
    mixed_product = exact(mixed, centered2, 1, 1)
    noise = jnp.concatenate([noise_ref[:, mine], jnp.zeros((pad - latent, slab), f32)], axis=0)
    mean_z, log_var = heads_ref[0:pad, :], heads_ref[pad : 2 * pad, :]
    log_factor = 0.5 * noise * jnp.exp(0.5 * log_var)
    scaled = valid * scale
    grad_log_own = scaled * (jnp.exp(log_var) - 1.0) * 0.5
    centered1 = first_ref[...]
    normed1 = centered1 * gain1 + bias1
    sigma1 = sigmoid(normed1)
    hidden1 = normed1 * sigma1
    slope1 = sigma1 * (1.0 + normed1 * (1.0 - sigma1))

    sums = finish()
    gain2_grad, shift2_grad = sums[0:1], sums[1:2]
    small_ref[0:depth, :] = factor2 * (
        products - (mixed_sum * shift2_grad + mixed_product * gain2_grad) / count
    )
    gain_col, shift_col = columns_of([gain2_grad, shift2_grad])
    pulled = exact(latent_rows, shift_col + centered2 * gain_col, 1, 0)
    others = slab_box.at[pl.ds(0, group.size - 1)]
    await_bytes(others, slab_sems.at[0])
    await_bytes(others, slab_sems.at[1])
    grad_sample = box_sum(slab_box) - share * pulled
    grad_heads = jnp.concatenate(
        [grad_sample + scaled * mean_z, grad_sample * log_factor + grad_log_own], axis=0
    )
    grad_normed1 = exact(pack_ref[heads_rows, :], grad_heads, 0, 0) * slope1
    rows = [row_sums(fold_lanes(grad_normed1 * centered1)), row_sums(fold_lanes(grad_normed1))]
    finish = spread_box(group, box4, spread_box(team, box3, eight_rows(rows), sems3)(), sems4)
    swap2.wait()
    output_sum_ref[given] = output_sum_ref[given] + half_box[...]
    swap3 = swap(output_sum_ref.at[given], output_sum_ref.at[given], far, 2)
    small_ref[depth : depth + 2 * pad, :] = exact(grad_heads, hidden1, 1, 1)
    small_ref[depth + 2 * pad : depth + 4 * pad, :] = fold_lanes(grad_heads)
    sums = finish()
    gain1_grad, shift1_grad = sums[0:1], sums[1:2]
    norms_ref[...] = eight_rows([gain1_grad, shift1_grad, gain2_grad, shift2_grad])
    gain_col, shift_col = columns_of([gain1_grad, shift1_grad])
    grad_pre1 = factor1 * (grad_normed1 - share * (shift_col + centered1 * gain_col))
    grad16_ref[:, mine] = grad_pre1.astype(bf16)
    gathering = Gather(grad16_ref, slab, grad_far, grad_near)
    gathering.start()
    small_ref[depth + 4 * pad :, :] = exact(hot, grad_pre1, 1, 1)
    gathering.finish()
    others = genes_box.at[pl.ds(0, team.size - 1)]
    await_bytes(others, genes_sems.at[0])
    await_bytes(others, genes_sems.at[1])
    genes_sum_ref[...] = box_sum(genes_box)
    swap3.wait()


def middle_back(
    grad,
    centered,
    sample,
    index,
    valid,
    noise,
    pack,
    stats,
    first,
    heads,
    output_grad,
    genes_grad,
    batches,
):
    cells = index.shape[1]
    width, slab = first.shape
    pad = sample.shape[0]
    genes_axis = lax.axis_size("gene")
    return pl.pallas_call(
        functools.partial(middle_back_kernel, batches=batches, latent=noise.shape[0]),
        out_shape=[
            jax.ShapeDtypeStruct((width, cells), bf16),
            jax.ShapeDtypeStruct((5 * pad + 2 * batches, LANES), f32),
            jax.ShapeDtypeStruct((8, LANES), f32),
            jax.ShapeDtypeStruct(output_grad.shape[1:], f32),
            jax.ShapeDtypeStruct(genes_grad.shape, f32),
        ],
        in_specs=[IN_VMEM] * 12,
        out_specs=[IN_VMEM] * 5,
        scratch_shapes=[
            pltpu.VMEM((pad, cells), f32),
            pltpu.VMEM((genes_axis, pad, slab), f32),
            *row_boxes(),
            pltpu.VMEM(output_grad.shape[1:], f32),
            pltpu.VMEM((output_grad.shape[1] // 2, LANES), f32),
            pltpu.VMEM((output_grad.shape[1] // 2, LANES), f32),
            pltpu.VMEM((lax.axis_size("cell"), *genes_grad.shape), f32),
        ]
        + [pltpu.SemaphoreType.DMA((2,))] * 5
        + gather_sems()
        + [pltpu.SemaphoreType.DMA((3, 2)), pltpu.SemaphoreType.DMA((2,))],
        compiler_params=talking(4),
        name="middle_back",
    )(
        grad,
        centered,
        sample,
        index,
        valid,
        noise,
        pack,
        stats,
        first,
        heads,
        output_grad,
        genes_grad,
    )


def encoder_grad_kernel(
    counts_ref,
    grad_ref,
    small_ref,
    output_ref,
    sum_ref,
    total_ref,
    output_sum_ref,
    near_give,
    near_box,
    far_give,
    far_box,
    whole_box,
    small_box,
    near_sems,
    far_sems,
    last_sems,
    small_sems,
    output_box,
    output_sems,
):
    gene, cell = lax.axis_index("gene"), lax.axis_index("cell")
    bit, high = lax.rem(cell, 2), cell // 2
    near, far = cell + 1 - 2 * bit, lax.rem(cell + 2, 4)
    quarter, cells = counts_ref.shape
    step = pl.program_id(0)

    def copy(source, target, sems, where):
        return pltpu.make_async_remote_copy(
            src_ref=source,
            dst_ref=target,
            send_sem=sems.at[0],
            recv_sem=sems.at[1],
            device_id=where,
            device_id_type=MESH,
        )

    rounds = [(gene, near), (gene, far)]
    size = 1
    while size < lax.axis_size("gene"):
        rounds.append((gene + size - 2 * size * lax.rem(gene // size, 2), cell))
        size *= 2

    def small_copy(number):
        source = small_ref if number == 0 else small_box.at[1, number - 1]
        return copy(source, small_box.at[0, number], small_sems.at[number], rounds[number])

    def small_end(number):
        small_copy(number).wait()
        source = small_ref[...] if number == 0 else small_box[1, number - 1]
        small_box[1, number] = source + small_box[0, number]

    def rows_of(bit, high):
        return pl.ds(pl.multiple_of((2 * bit + high) * quarter, ROWS), quarter)

    def near_copy(number):
        return copy(near_give.at[number], near_box.at[number], near_sems.at[number], (gene, near))

    far_copy = copy(far_give, far_box, far_sems, (gene, far))

    def last_copy(number, high, other):
        rows = rows_of(bit, high)
        return copy(whole_box.at[rows], whole_box.at[rows], last_sems.at[number], (gene, other))

    output_copy = copy(output_box.at[bit], output_box.at[bit], output_sems, (gene, near))

    @pl.when(step == 0)
    def _():
        output_box[bit] = output_ref[...]
        barrier = pltpu.get_barrier_semaphore()
        for where in rounds:
            pl.semaphore_signal(barrier, inc=1, device_id=where, device_id_type=MESH)

    piece = pick_chunk(cells, 512)

    def part():
        total = jnp.zeros((quarter, LANES), f32)
        for at in range(0, cells, piece):
            columns = slice(at, at + piece)
            inputs = jnp.log(counts_ref[:, columns].astype(f32) + 1.0).astype(bf16)
            total = total + lax.dot_general(
                inputs,
                grad_ref[:, columns],
                (((1,), (1,)), ((), ())),
                preferred_element_type=f32,
            )
        return total

    value = part()

    @pl.when(step == 0)
    def _():
        pl.semaphore_wait(pltpu.get_barrier_semaphore(), len(rounds))
        small_copy(0).start()
        output_copy.start()

    @pl.when(step < 2)
    def _():
        near_give[step] = value
        near_copy(step).start()

    @pl.when(step == 1)
    def _():
        small_end(0)
        small_copy(1).start()

    @pl.when(step == 2)
    def _():
        near_copy(0).wait()
        far_give[...] = value + near_box[0]
        far_copy.start()
        small_end(1)
        small_copy(2).start()

    @pl.when(step == 3)
    def _():
        near_copy(1).wait()
        total = value + near_box[1]
        small_end(2)
        if len(rounds) > 3:
            small_copy(3).start()
        far_copy.wait()
        whole_box[rows_of(bit, high), :] = total + far_box[...]
        own_far, own_near = last_copy(0, high, far), last_copy(1, high, near)
        own_far.start()
        own_near.start()
        for number in range(3, len(rounds)):
            small_end(number)
            if number + 1 < len(rounds):
                small_copy(number + 1).start()
        total_ref[...] = small_box[1, len(rounds) - 1]
        own_far.wait()
        passed = last_copy(2, 1 - high, near)
        passed.start()
        own_near.wait()
        passed.wait()
        sum_ref[...] = whole_box[...]
        output_copy.wait()
        output_sum_ref[...] = output_box[...]


def encoder_grad(counts_t, grad, small, output):
    genes, cells = counts_t.shape
    quarter = ROWS * pl.cdiv(genes, 4 * ROWS)
    rounds = 2
    while 2 ** (rounds - 2) < lax.axis_size("gene"):
        rounds += 1

    def quarter_of(i):
        cell = lax.axis_index("cell")
        bit, high = lax.rem(cell, 2), cell // 2
        half = lax.rem(bit + 1 + i // 2, 2)
        return (2 * half + lax.rem(high + 1 + i, 2), 0)

    box = pltpu.VMEM((2, quarter, LANES), f32)
    one = pltpu.VMEM((quarter, LANES), f32)
    return pl.pallas_call(
        encoder_grad_kernel,
        grid=(4,),
        in_specs=[pl.BlockSpec((quarter, cells), quarter_of)]
        + [whole(array) for array in (grad, small, output)],
        out_specs=[
            pl.BlockSpec((4 * quarter, LANES), lambda i: (0, 0)),
            pl.BlockSpec(small.shape, lambda i: (0, 0)),
            pl.BlockSpec((2, *output.shape), lambda i: (0, 0, 0)),
        ],
        out_shape=[
            jax.ShapeDtypeStruct((4 * quarter, LANES), f32),
            jax.ShapeDtypeStruct(small.shape, f32),
            jax.ShapeDtypeStruct((2, *output.shape), f32),
        ],
        scratch_shapes=[
            box,
            box,
            one,
            one,
            pltpu.VMEM((4 * quarter, LANES), f32),
            pltpu.VMEM((2, rounds, *small.shape), f32),
            pltpu.SemaphoreType.DMA((2, 2)),
            pltpu.SemaphoreType.DMA((2,)),
            pltpu.SemaphoreType.DMA((3, 2)),
            pltpu.SemaphoreType.DMA((rounds, 2)),
            pltpu.VMEM((2, *output.shape), f32),
            pltpu.SemaphoreType.DMA((2,)),
        ],
        compiler_params=talking(5),
        name="encoder_grad",
    )(counts_t, grad, small, output)


def finish_kernel(*refs, pad, latent, batches):
    grad16_ref, encoder_grad_ref, output_grad_ref, genes_grad_ref, small_ref, norms_ref = refs[:6]
    ins, input_ref, outs = refs[6:30], refs[30], refs[31:]

    def group(number):
        return [part[8 * i + number] for part in (ins, outs) for i in range(3)]

    def step(number, here, grad):
        weight, momentum, average, *results = group(number)
        old = [ref[here] for ref in (weight, momentum, average)]
        for ref, value in zip(results, nesterov(*old, grad, step_rates[number])):
            ref[here] = value

    input_ref[...] = jnp.dot(
        ins[0][...].astype(bf16), grad16_ref[...], preferred_element_type=f32
    )
    step(0, (slice(None), slice(None)), encoder_grad_ref[...])
    for k in range(2):
        rows = pl.ds(k, output_grad_ref.shape[1], stride=2)
        step(1, (rows, slice(None)), output_grad_ref[k])
    step(2, (slice(None), slice(None)), genes_grad_ref[0:3, :])

    @pl.when(pl.program_id(0) == 0)
    def _():
        depth = pad + batches
        columns = slice(None)
        step(3, (columns, columns), small_ref[depth + 4 * pad :, :])
        step(4, (columns, columns), norms_ref[0:4, :])
        step(7, (slice(0, latent), columns), small_ref[0:latent, :])
        step(7, (slice(latent, None), columns), small_ref[pad:depth, :])
        bias = exact(
            jnp.ones((8, LANES), f32), small_ref[depth + 2 * pad : depth + 4 * pad, :], 1, 1
        )
        for half in range(2):
            rows = slice(half * latent, (half + 1) * latent)
            at = half * pad
            step(5, (rows, columns), small_ref[depth + at : depth + at + latent, :])
            step(6, (slice(None), rows), bias[0:1, at : at + latent])


def finish(grad16, encoder_grad, output_grad, genes_grad, small, norms, states, pad, latent, batches):
    width, cells = grad16.shape
    genes = states[0][0].shape[0]
    block = 4 * LANES
    one = pl.BlockSpec((block, LANES), lambda i: (i, 0))
    two = pl.BlockSpec((2 * block, LANES), lambda i: (i, 0))
    both = pl.BlockSpec((2, block, LANES), lambda i: (0, i, 0))

    def rows(count):
        return pl.BlockSpec((count, block), lambda i: (0, i))

    specs = [spec for state in states for spec in [one, two, rows(3), *map(whole, state[3:])]]
    flat = [array for state in states for array in state]
    results = pl.pallas_call(
        functools.partial(finish_kernel, pad=pad, latent=latent, batches=batches),
        grid=(pl.cdiv(genes, block),),
        in_specs=[whole(grad16), one, both, rows(4), whole(small), whole(norms)] + specs,
        out_specs=[pl.BlockSpec((block, cells), lambda i: (i, 0))] + specs,
        out_shape=[jax.ShapeDtypeStruct((genes, cells), f32)]
        + [jax.ShapeDtypeStruct(array.shape, f32) for array in flat],
        compiler_params=PARAMS,
        name="finish",
    )(grad16, encoder_grad, output_grad, genes_grad, small, norms, *flat)
    return results[0], [results[1 + 8 * i : 9 + 8 * i] for i in range(3)]


def fill_hidden(long_ref, hidden_ref, top):
    width, chunk = hidden_ref.shape
    long_ref[0:width, :] = hidden_ref[...]
    index = lax.broadcasted_iota(jnp.int32, (HOT_DEPTH - width, chunk), 0)
    extra = jnp.where(index < 3, 1.0, 0.0)
    if top is not None:
        high = (-top).astype(bf16).astype(f32)
        middle = (-top - high).astype(bf16).astype(f32)
        low = (-top - high - middle).astype(bf16).astype(f32)
        extra = jnp.where(index == 3, high, extra)
        extra = jnp.where(index == 4, middle, extra)
        extra = jnp.where(index == 5, low, extra)
    long_ref[width:HOT_DEPTH, :] = extra.astype(bf16)


def sweep(blocks, block, groups, pieces, logits, terms, back, carry):
    def rows_of(number):
        return pl.ds(pl.multiple_of(number * block, ROWS), block)

    logits(0, rows_of(0), block, pieces)

    def beside(i, later, earlier):
        acts = [
            lambda piece=piece: logits(1 - i, rows_of(later), block, [piece]) for piece in pieces
        ]
        if back is not None:
            acts.append(lambda: back(1 - i, rows_of(earlier), block))
        spaced = []
        for step in range(groups):
            spaced.append(acts.pop(0) if acts and step % 2 == 0 else lambda: None)
        return spaced + acts

    def pair(p, carry):
        first = 2 * p
        last, ahead = jnp.maximum(first - 1, 0), jnp.minimum(first + 2, blocks - 1)
        carry = terms(0, first, carry, beside(0, first + 1, last))
        return terms(1, first + 1, carry, beside(1, ahead, first))

    carry = lax.fori_loop(0, blocks // 2, pair, carry)
    if back is not None and blocks > 1:
        back(1, rows_of(blocks // 2 * 2 - 1), block)
    if blocks % 2:
        carry = terms(0, blocks - 1, carry, ())
        if back is not None:
            back(0, rows_of(blocks - 1), block)
    return carry


def logit_pieces(ks, chunk):
    width = min(chunk, WIDE)
    return [(k, slice(j, j + width)) for k in range(ks) for j in range(0, chunk, width)]


def totals_kernel(
    hidden_ref, weight_ref, sample_ref, out_ref, long_ref, even_ref, odd_ref, box, sems, *, genes, chunk
):
    full, groups, tail = split_rows(genes, 26)
    block = ROWS * groups
    blocks = full // groups
    values = (even_ref, odd_ref)
    fill_hidden(long_ref, hidden_ref, None)
    pieces = logit_pieces(1, chunk)

    @pl.when(pl.program_id(0) == 0)
    def _():
        greet(Team("gene"))

    def logits(i, rows, size, which):
        for _, columns in which:
            values[i][0:size, columns] = jnp.dot(
                weight_ref[0, rows, :], long_ref[:, columns], preferred_element_type=f32
            )

    def online(value_ref, size, carry, beside=()):
        best, total = carry
        fresh = best
        for i in range(0, size, 8):
            fresh = jnp.maximum(fresh, value_ref[i : i + 8, :])
        total = total * jnp.exp2((best - fresh) * (1.0 / ln2))
        for i in range(0, size, 8):
            for act in beside[i // 8 :: size // 8]:
                act()
            total = total + jnp.exp2((value_ref[i : i + 8, :] - fresh) * (1.0 / ln2))
        return fresh, total

    def terms(i, number, carry, beside):
        return online(values[i], block, carry, beside)

    carry = (jnp.full((8, chunk), -jnp.inf, f32), jnp.zeros((8, chunk), f32))
    carry = sweep(blocks, block, groups, pieces, logits, terms, None, carry)
    if tail:
        logits(1, pl.ds(full * ROWS, ROWS), ROWS, pieces)
        carry = online(odd_ref, ROWS, carry)
    best, total = carry
    top = jnp.max(best, axis=0, keepdims=True)
    total = total * jnp.exp2((best - top) * (1.0 / ln2))
    shared = Shared(box, sems, chunk)

    @pl.when(pl.program_id(0) == 0)
    def _():
        pl.semaphore_wait(pltpu.get_barrier_semaphore(), box.shape[0] - 1)

    shared.send(top, jnp.sum(total, axis=0, keepdims=True))

    @pl.when(pl.program_id(0) == pl.num_programs(0) - 1)
    def _():
        shared.finish()
        top = box[0, 0:1, :]
        for i in range(1, box.shape[0]):
            top = jnp.maximum(top, box[i, 0:1, :])
        total = jnp.zeros_like(top)
        for i in range(box.shape[0]):
            total = total + box[i, 1:2, :] * jnp.exp(box[i, 0:1, :] - top)
        inverse = 1.0 / total
        out_ref[0:1, :] = top
        out_ref[1:2, :] = sample_ref[sample_ref.shape[0] - 1 :, :] * inverse
        out_ref[2:3, :] = inverse
        out_ref[3:4, :] = inverse


def totals(hidden, weights, sample, genes):
    width, cells = hidden.shape
    chunk = pick_chunk(cells, 4096)
    groups = split_rows(genes, 26)[1]
    return pl.pallas_call(
        functools.partial(totals_kernel, genes=genes, chunk=chunk),
        grid=(cells // chunk,),
        in_specs=[column_blocks(width, chunk), whole(weights), whole(sample)],
        out_specs=pl.BlockSpec((4, cells), lambda i: (0, 0)),
        out_shape=jax.ShapeDtypeStruct((4, cells), f32),
        scratch_shapes=[pltpu.VMEM((HOT_DEPTH, chunk), bf16)]
        + [pltpu.VMEM((ROWS * groups, chunk), f32)] * 2
        + [pltpu.VMEM((lax.axis_size("gene"), 2, cells), f32), pltpu.SemaphoreType.DMA((2,))],
        compiler_params=talking(2),
        name="totals",
    )(hidden, weights, sample)


def likelihood_kernel(
    counts_ref,
    hidden_ref,
    rows_ref,
    share_ref,
    all_rows_ref,
    sample_ref,
    valid_ref,
    weight_ref,
    theta_ref,
    log_ref,
    slope_ref,
    gammas_ref,
    digammas_ref,
    slopes_ref,
    sums_ref,
    grad_hidden_ref,
    grad_weight_ref,
    grad_bias_ref,
    grad_theta_ref,
    long_ref,
    even_ref,
    odd_ref,
    even_grad_ref,
    odd_grad_ref,
    box,
    sems,
    *,
    genes,
    chunk,
    genes_all,
):
    full, groups, tail = split_rows(genes, 12)
    block = ROWS * groups
    blocks = full // groups
    width = hidden_ref.shape[0]

    @pl.when(pl.program_id(0) == 0)
    def _():
        for ref in (grad_weight_ref, grad_bias_ref, grad_theta_ref):
            ref[...] = jnp.zeros_like(ref)
        greet(Team("gene"))

    fill_hidden(long_ref, hidden_ref, rows_ref[0:1, :])
    wide = min(WIDE, chunk)
    tiles = [slice(j, j + wide) for j in range(0, chunk, wide)]
    ratio_all = rows_ref[1:2, :]
    share_all = share_ref[...]

    def two(x):
        return jnp.concatenate([x] * (wide // LANES), axis=1)

    def look(t, c):
        return jnp.concatenate([jnp.take_along_axis(t, c[:, q:q+LANES], axis=1) for q in range(0, wide, LANES)], axis=1)

    def group(value_ref, grad_ref, held, span, read, carry):
        losses, sums = [], []
        theta = two(theta_ref.at[span][held, :])
        log_theta = two(log_ref.at[span][held, :])
        log_slope = two(slope_ref.at[span][held, :])
        gammas = gammas_ref.at[span][held, :]
        digammas = digammas_ref.at[span][held, :]
        grad_bias = grad_bias_ref.at[span][held, :]
        grad_theta = grad_theta_ref.at[span][held, :]
        for j, columns in enumerate(tiles):
            count = read(columns)
            counted = count.astype(f32)
            minus = value_ref[1, held, columns] * (-1.0 / ln2)
            share = share_all[:, columns]
            rate = jnp.exp2(value_ref[0, held, columns] * (1.0 / ln2)) * ratio_all[:, columns]
            near = rate + rate_epsilon
            both = theta + near
            inverse_both = 1.0 / both
            log_both = jnp.log2(both)
            upper = jnp.maximum(minus, 0.0)
            lower = jnp.minimum(minus, 0.0)
            one_pi = 1.0 + jnp.exp2(lower - upper)
            sigma_pi = jnp.exp2(lower) * (1.0 / one_pi)
            zero = count < 1
            pi_theta = theta * (log_theta - log_both) + minus
            inflated = jnp.where(zero, pi_theta, 1e30)
            small = jnp.exp2(-jnp.abs(inflated))
            inverse_theta = 1.0 / (1.0 + small)
            sigma = jnp.where(inflated >= 0.0, 1.0, small) * inverse_theta
            loss = (upper - jnp.where(zero, jnp.maximum(pi_theta, 0.0), pi_theta)) + (
                jnp.log2(one_pi * inverse_theta)
                - counted * (jnp.log2(near) - log_both)
                - look(gammas, count)
            )
            pull = (sigma * theta + counted) * inverse_both
            slope = rate * (pull - counted * (1.0 / near))
            slopes_ref.at[span][held, columns] = slope
            grad_dropout = (sigma - sigma_pi) * share
            grad_ref[held, columns] = grad_dropout.astype(bf16)
            grad_bias = grad_bias + fold_lanes(grad_dropout)
            grad_theta = grad_theta + fold_lanes(share * (
                (pull - sigma * (log_slope - ln2 * log_both))
                - look(digammas, count)
            ))
            losses.append(carry[0][j] + loss[:8] + loss[8:])
            sums.append(carry[1][j] + slope[:8] + slope[8:])
        grad_bias_ref.at[span][held, :] = grad_bias
        grad_theta_ref.at[span][held, :] = grad_theta
        return tuple(losses), tuple(sums)

    pieces = logit_pieces(2, chunk)
    values, grads = (even_ref, odd_ref), (even_grad_ref, odd_grad_ref)

    def logits(i, rows, size, which):
        for k, columns in which:
            values[i][k, 0:size, columns] = jnp.dot(
                weight_ref[k, rows, :], long_ref[:, columns], preferred_element_type=f32
            )

    def back(i, rows, size):
        grad = grads[i][0:size, :]
        grad_weight_ref[rows, :] += lax.dot_general(
            grad, hidden_ref[...], (((1,), (1,)), ((), ())), preferred_element_type=f32
        )
        grad_hidden_ref[...] += lax.dot_general(
            weight_ref[1, rows, 0:width],
            grad,
            (((0,), (0,)), ((), ())),
            preferred_element_type=f32,
        )

    def terms(buffer, number, carry, beside):
        span = pl.ds(pl.multiple_of(number * block, ROWS), block)
        for i in range(groups):
            for act in beside[i::groups]:
                act()
            held = slice(i * ROWS, (i + 1) * ROWS)
            carry = group(
                values[buffer],
                grads[buffer],
                held,
                span,
                lambda columns, held=held: counts_ref.at[span][held, columns],
                carry,
            )
        return carry

    grad_hidden_ref[...] = jnp.zeros_like(grad_hidden_ref)
    odd_grad_ref[...] = jnp.zeros_like(odd_grad_ref)
    carry = tuple(jnp.zeros((8, wide), f32) for _ in tiles)
    carry = sweep(blocks, block, groups, pieces, logits, terms, back, (carry, carry))
    if tail:
        rows = pl.ds(full * ROWS, ROWS)
        logits(1, rows, ROWS, pieces)
        carry = group(
            odd_ref,
            odd_grad_ref,
            slice(0, ROWS),
            rows,
            lambda cols: tail_rows(counts_ref, full * ROWS, genes, cols, jnp.int32),
            carry,
        )
        back(1, rows, ROWS)
    shared = Shared(box, sems, chunk)

    @pl.when(pl.program_id(0) == 0)
    def _():
        pl.semaphore_wait(pltpu.get_barrier_semaphore(), box.shape[0] - 1)

    rows = [
        jnp.concatenate([jnp.sum(part, axis=0, keepdims=True) for part in carry[i]], axis=1)
        for i in (1, 0)
    ]
    shared.send(rows[0], rows[1] * ln2)

    @pl.when(pl.program_id(0) == pl.num_programs(0) - 1)
    def _():
        shared.finish()
        total = box_sum(box)
        at = sample_ref.shape[0] - 2
        sums_ref[0:1, :] = total[0:1] * all_rows_ref[2:3, :]
        sums_ref[1:2, :] = (
            valid_ref[...].astype(f32) * (total[1:2] + sample_ref[at : at + 1, :]) / genes_all
        )


def likelihood(counts_t, hidden, rows, share, sample, valid, weights, gene_tables, genes_all):
    genes, cells = counts_t.shape
    size = weights.shape[1]
    width = hidden.shape[0]
    chunk = pick_chunk(cells, 512)
    groups = split_rows(genes, 12)[1]
    row = column_blocks(1, chunk)
    per_gene = pl.BlockSpec((size, LANES), lambda i: (0, 0))
    return pl.pallas_call(
        functools.partial(likelihood_kernel, genes=genes, chunk=chunk, genes_all=genes_all),
        grid=(cells // chunk,),
        in_specs=[column_blocks(genes, chunk), column_blocks(width, chunk)]
        + [column_blocks(rows.shape[0], chunk), row]
        + [whole(a) for a in (rows, sample, valid, weights)]
        + [whole(a) for a in gene_tables],
        out_specs=[
            column_blocks(size, chunk),
            pl.BlockSpec((2, cells), lambda i: (0, 0)),
            column_blocks(width, chunk),
        ]
        + [per_gene] * 3,
        out_shape=[
            jax.ShapeDtypeStruct((size, cells), f32),
            jax.ShapeDtypeStruct((2, cells), f32),
            jax.ShapeDtypeStruct((width, cells), f32),
        ]
        + [jax.ShapeDtypeStruct((size, LANES), f32)] * 3,
        scratch_shapes=[pltpu.VMEM((HOT_DEPTH, chunk), bf16)]
        + [pltpu.VMEM((2, ROWS * groups, chunk), f32)] * 2
        + [pltpu.VMEM((ROWS * groups, chunk), bf16)] * 2
        + [pltpu.VMEM((lax.axis_size("gene"), 2, cells), f32), pltpu.SemaphoreType.DMA((2,))],
        compiler_params=talking(3),
        name="likelihood",
    )(counts_t, hidden, rows, share, rows, sample, valid, weights, *gene_tables)


def frequency_kernel(
    slopes_ref,
    hidden_ref,
    rows_ref,
    pull_ref,
    share_ref,
    other_ref,
    weight_ref,
    second_ref,
    dropout_ref,
    theta_ref,
    scale_ref,
    grad_hidden_ref,
    grad_weight_ref,
    genes_ref,
    long_ref,
    even_ref,
    odd_ref,
    even_grad_ref,
    odd_grad_ref,
    grad_bias_ref,
    *,
    genes,
    chunk,
):
    full, groups, tail = split_rows(genes, 26)
    block = ROWS * groups
    blocks = full // groups
    size = weight_ref.shape[1]
    width = hidden_ref.shape[0]
    values, grads = (even_ref, odd_ref), (even_grad_ref, odd_grad_ref)

    @pl.when(pl.program_id(0) == 0)
    def _():
        grad_weight_ref[0] = jnp.zeros((size, LANES), f32)
        grad_weight_ref[1] = second_ref[...]
        grad_bias_ref[...] = jnp.zeros_like(grad_bias_ref)

    fill_hidden(long_ref, hidden_ref, rows_ref[0:1, :])
    pieces = logit_pieces(1, chunk)
    share = share_ref[...]
    pulled = pull_ref[0:1, :] * share

    def logits(i, rows, size, which):
        for _, columns in which:
            values[i][0:size, columns] = jnp.dot(
                weight_ref[0, rows, :], long_ref[:, columns], preferred_element_type=f32
            )

    def group(buffer, held, span):
        exponent = jnp.exp2(values[buffer][held, :] * (1.0 / ln2))
        grad = slopes_ref.at[span][held, :] * share - exponent * pulled
        grads[buffer][held, :] = grad.astype(bf16)
        grad_bias_ref.at[span][held, :] += fold_lanes(grad)

    def terms(buffer, number, carry, beside):
        span = pl.ds(pl.multiple_of(number * block, ROWS), block)
        for i in range(groups):
            for act in beside[i::groups]:
                act()
            group(buffer, slice(i * ROWS, (i + 1) * ROWS), span)
        return carry

    def back(i, rows, size):
        grad = grads[i][0:size, :]
        grad_weight_ref[0, rows, :] += lax.dot_general(
            grad, hidden_ref[...], (((1,), (1,)), ((), ())), preferred_element_type=f32
        )
        grad_hidden_ref[...] += lax.dot_general(
            weight_ref[0, rows, 0:width],
            grad,
            (((0,), (0,)), ((), ())),
            preferred_element_type=f32,
        )

    grad_hidden_ref[...] = other_ref[...]
    odd_grad_ref[...] = jnp.zeros_like(odd_grad_ref)
    sweep(blocks, block, groups, pieces, logits, terms, back, 0)
    if tail:
        rows = pl.ds(full * ROWS, ROWS)
        logits(1, rows, ROWS, pieces)
        group(1, slice(0, ROWS), rows)
        back(1, rows, ROWS)

    @pl.when(pl.program_id(0) == pl.num_programs(0) - 1)
    def _():
        ones = jnp.ones((ROWS, LANES), bf16)
        parts = (grad_bias_ref[...], dropout_ref[...], theta_ref[...] * scale_ref[...])
        for i, values in enumerate(parts):
            total = jnp.zeros((1, size), f32)
            for _ in range(3):
                piece = values.astype(bf16)
                values = values - piece.astype(f32)
                total = total + lax.dot_general(
                    ones, piece, (((1,), (1,)), ((), ())), preferred_element_type=f32
                )[0:1]
            genes_ref[i : i + 1, :] = total
        genes_ref[3:4, :] = jnp.zeros((1, size), f32)


def frequency(slopes, hidden, rows, pull, share, other, weights, second, dropout, theta, scale, genes):
    size, cells = slopes.shape
    width = hidden.shape[0]
    chunk = pick_chunk(cells, 1024)
    groups = split_rows(genes, 26)[1]
    row = column_blocks(1, chunk)
    wide = column_blocks(width, chunk)
    return pl.pallas_call(
        functools.partial(frequency_kernel, genes=genes, chunk=chunk),
        grid=(cells // chunk,),
        in_specs=[column_blocks(size, chunk), wide, column_blocks(rows.shape[0], chunk)]
        + [column_blocks(2, chunk), row, wide, whole(weights)]
        + [whole(a) for a in (second, dropout, theta, scale)],
        out_specs=[
            wide,
            pl.BlockSpec((2, size, LANES), lambda i: (0, 0, 0)),
            pl.BlockSpec((4, size), lambda i: (0, 0)),
        ],
        out_shape=[
            jax.ShapeDtypeStruct((width, cells), f32),
            jax.ShapeDtypeStruct((2, size, LANES), f32),
            jax.ShapeDtypeStruct((4, size), f32),
        ],
        scratch_shapes=[pltpu.VMEM((HOT_DEPTH, chunk), bf16)]
        + [pltpu.VMEM((ROWS * groups, chunk), f32)] * 2
        + [pltpu.VMEM((ROWS * groups, chunk), bf16)] * 2
        + [pltpu.VMEM((size, LANES), f32)],
        compiler_params=PARAMS,
        name="frequency",
    )(slopes, hidden, rows, pull, share, other, weights, second, dropout, theta, scale)


def local(
    counts,
    batch_index,
    valid_mask,
    noise_draw,
    encoder_weight,
    output_weight,
    gene_vectors,
    batch_shift,
    layer_norm_params,
    head_weight,
    head_bias,
    decoder_input,
    encoder_weight_momentum,
    output_weight_momentum,
    gene_vectors_momentum,
    batch_shift_momentum,
    norm_params_momentum,
    head_weight_momentum,
    head_bias_momentum,
    decoder_input_momentum,
    encoder_weight_average,
    output_weight_average,
    gene_vectors_average,
    batch_shift_average,
    norm_params_average,
    head_weight_average,
    head_bias_average,
    decoder_input_average,
):
    cells, genes = counts.shape
    gene_devices = lax.axis_size("gene")
    genes_all = genes * gene_devices
    latent = head_bias.shape[0] // 2
    batches = batch_shift.shape[0]

    def by_gene(array):
        return jnp.transpose(array, (2, 0, 1)).reshape(2 * genes, -1)

    counts_t = counts.T
    output_rows = by_gene(output_weight)

    pad = 16
    small_weights = (
        layer_norm_params,
        head_bias[None, :],
        decoder_input,
        head_weight.T,
        batch_shift,
    )
    index, valid, noise = batch_index[None, :], valid_mask[None, :], noise_draw.T

    encoded, weights, *gene_tables = encode(counts_t, encoder_weight, output_rows, gene_vectors)
    hidden2, centered2, sample, share, stats, centered1, heads, pack = middle(
        encoded, index, valid, noise, small_weights, batches, pad, genes_all
    )
    rows = totals(hidden2, weights, sample, genes)
    slopes, pull, grad_hidden2, grad_out1, grad_bias1, grad_theta = likelihood(
        counts_t, hidden2, rows, share, sample, valid, weights, gene_tables, genes_all
    )
    cell_loss = pull[1]

    grad_hidden2, grad_out, grad_genes = frequency(
        slopes,
        hidden2,
        rows,
        pull,
        share,
        grad_hidden2,
        weights,
        grad_out1,
        grad_bias1,
        grad_theta,
        gene_tables[0],
        genes,
    )
    grad_pre16, small, norm_rows, grad_out, grad_genes = middle_back(
        grad_hidden2,
        centered2,
        sample,
        index,
        valid,
        noise,
        pack,
        stats,
        centered1,
        heads,
        grad_out,
        grad_genes,
        batches,
    )
    grad_encoder, small, grad_out = encoder_grad(counts_t, grad_pre16, small, grad_out)
    states = [
        (encoder, by_gene(output), vectors, shift, norms, head.T, bias[None, :], mixing)
        for encoder, output, vectors, shift, norms, head, bias, mixing in (
            (
                encoder_weight,
                output_weight,
                gene_vectors,
                batch_shift,
                layer_norm_params,
                head_weight,
                head_bias,
                decoder_input,
            ),
            (
                encoder_weight_momentum,
                output_weight_momentum,
                gene_vectors_momentum,
                batch_shift_momentum,
                norm_params_momentum,
                head_weight_momentum,
                head_bias_momentum,
                decoder_input_momentum,
            ),
            (
                encoder_weight_average,
                output_weight_average,
                gene_vectors_average,
                batch_shift_average,
                norm_params_average,
                head_weight_average,
                head_bias_average,
                decoder_input_average,
            ),
        )
    ]
    input_grad, fresh = finish(
        grad_pre16,
        grad_encoder,
        grad_out,
        grad_genes,
        small,
        norm_rows,
        states,
        pad,
        latent,
        batches,
    )
    results = []
    for encoder, output, vectors, shift, norms, head, bias, mixing in fresh:
        output = jnp.transpose(output.reshape(genes, 2, -1), (1, 2, 0))
        results += [encoder, output, vectors, shift, norms, head.T, bias[0], mixing]
    return (cell_loss, input_grad.T, *results)


def solution(mesh):
    cells, genes = P("cell"), P("gene", None)
    weight_specs = (genes, P(None, None, "gene"), P(None, "gene"), P(), P(), P(), P(), P())
    return jax.shard_map(
        local,
        mesh=mesh,
        in_specs=(P("cell", "gene"), cells, cells, P("cell", None)) + weight_specs * 3,
        out_specs=(cells, P("cell", "gene")) + weight_specs * 3,
        check_vma=False,
    )
```

```python
import functools

import jax
import jax.numpy as jnp
from jax import lax
from jax.experimental import pallas as pl
from jax.experimental.pallas import tpu as pltpu
from jax.sharding import PartitionSpec as P

momentum_decay = 0.9
average_decay = 0.99
norm_epsilon = 0.001
rate_epsilon = 1e-08
step_rates = (110.0, 46000.0, 300000.0, 70000.0, 13000.0, 3700.0, 7600.0, 8000.0)
ln2 = 0.6931471805599453
f32 = jnp.float32
bf16 = jnp.bfloat16
LANES = 128
ROWS = 16
WIDE = 2 * LANES
HOT_DEPTH = 2 * LANES
PARAMS = pltpu.CompilerParams(vmem_limit_bytes=60 << 20)
IN_VMEM = pl.BlockSpec(memory_space=pltpu.VMEM)
MESH = pl.DeviceIdType.MESH


def talking(number):
    return pltpu.CompilerParams(
        collective_id=number, has_side_effects=True, vmem_limit_bytes=60 << 20
    )


def nesterov(weight, momentum, average, grad, rate):
    moment = momentum_decay * momentum + grad
    fresh = weight - rate * (grad + momentum_decay * moment)
    return (fresh, moment, average_decay * average + (1.0 - average_decay) * fresh)


def whole(array):
    return pl.BlockSpec(array.shape, lambda i: (0,) * array.ndim)


def column_blocks(rows, chunk):
    return pl.BlockSpec((rows, chunk), lambda i: (0, i))


def split_rows(genes, most=13):
    full = genes // ROWS
    groups = max(d for d in range(1, most + 1) if full % d == 0)
    return full, groups, genes - full * ROWS


def padded(genes):
    return -(-genes // ROWS) * ROWS


def pick_chunk(cells, most):
    chunk = LANES
    while chunk * 2 <= most and cells % (chunk * 2) == 0:
        chunk *= 2
    return chunk


def tail_rows(ref, start, stop, columns, dtype):
    piece = ref[start:stop, columns]
    filler = jnp.zeros((ROWS - (stop - start), piece.shape[1]), dtype)
    return jnp.concatenate([piece, filler], axis=0)


class Team:
    def __init__(self, axis):
        self.size, self.me = lax.axis_size(axis), lax.axis_index(axis)
        self.gene, self.cell = lax.axis_index("gene"), lax.axis_index("cell")
        self.axis = axis

    def place(self, other):
        return (other, self.cell) if self.axis == "gene" else (self.gene, other)

    def others(self, act):
        def one(step, carry):
            other = lax.rem(self.me + step, self.size)
            act(other, self.place(other))
            return carry

        lax.fori_loop(1, self.size, one, 0)

    def send(self, source, target, sems):
        def act(other, place):
            pltpu.make_async_remote_copy(
                src_ref=source(other),
                dst_ref=target,
                send_sem=sems.at[0],
                recv_sem=sems.at[1],
                device_id=place,
                device_id_type=MESH,
            ).start()

        self.others(act)


def greet(*teams):
    barrier = pltpu.get_barrier_semaphore()

    def act(other, place):
        pl.semaphore_signal(barrier, inc=1, device_id=place, device_id_type=MESH)

    for team in teams:
        team.others(act)
    return lambda: pl.semaphore_wait(barrier, sum(team.size - 1 for team in teams))


def await_bytes(ref, sem):
    pltpu.make_async_copy(ref, ref, sem).wait()


def fold_lanes(values):
    return sum(values[:, j : j + LANES] for j in range(0, values.shape[1], LANES))


def row_sums(folded):
    return jnp.sum(jnp.transpose(folded), axis=0, keepdims=True)


def box_sum(box):
    def add(i, total):
        return total + box[i]

    return lax.fori_loop(1, box.shape[0], add, box[0])


def spread_box(team, box, value, sems):
    box[team.me] = value
    team.send(lambda other: box.at[team.me], box.at[team.me], sems)
    others = box.at[pl.ds(0, team.size - 1)]

    def finish():
        await_bytes(others, sems.at[0])
        await_bytes(others, sems.at[1])
        return box_sum(box)

    return finish


def row_boxes():
    shapes = [(lax.axis_size(axis), 8, LANES) for axis in ("cell", "gene")]
    return [pltpu.VMEM(shape, f32) for shape in shapes * 2]


class Gather:
    def __init__(self, ref, slab, far_sems, near_sems):
        self.ref, self.slab = ref, slab
        self.gene, self.cell = lax.axis_index("gene"), lax.axis_index("cell")
        self.pairs = lax.axis_size("gene") // 2
        self.high, self.low = self.gene // 2, lax.rem(self.gene, 2)
        self.far_sems, self.near_sems = far_sems, near_sems

    def copy(self, source_high, target, sems):
        columns = pl.ds(
            pl.multiple_of((2 * source_high + self.low) * self.slab, LANES), self.slab
        )
        return pltpu.make_async_remote_copy(
            src_ref=self.ref.at[:, columns],
            dst_ref=self.ref.at[:, columns],
            send_sem=sems.at[0],
            recv_sem=sems.at[1],
            device_id=(target, self.cell),
            device_id_type=MESH,
        )

    def far(self, d):
        target = 2 * lax.rem(self.high + d, self.pairs) + self.low
        return self.copy(self.high, target, self.far_sems.at[d - 1])

    def near(self, d):
        source = lax.rem(self.high - d + self.pairs, self.pairs)
        return self.copy(source, 2 * self.high + 1 - self.low, self.near_sems.at[d])

    def start(self):
        self.near(0).start()

        def one(d, carry):
            self.far(d).start()
            return carry

        lax.fori_loop(1, self.pairs, one, 0)

    def finish(self):
        def one(d, carry):
            self.far(d).wait_recv()
            self.near(d).start()
            return carry

        lax.fori_loop(1, self.pairs, one, 0)

        def drain(d, carry):
            self.near(d).wait()
            return carry

        lax.fori_loop(0, self.pairs, drain, 0)

        def drain_far(d, carry):
            self.far(d).wait_send()
            return carry

        lax.fori_loop(1, self.pairs, drain_far, 0)


def gather_sems():
    pairs = lax.axis_size("gene") // 2
    return [pltpu.SemaphoreType.DMA((pairs, 2))] * 2


class Shared:
    def __init__(self, box, sems, chunk):
        self.box, self.sems, self.team = box, sems, Team("gene")
        start = pl.multiple_of(pl.program_id(0) * chunk, LANES)
        self.here = pl.ds(start, chunk)

    def send(self, first, second):
        me = self.team.me
        self.box[me, 0:1, self.here] = first
        self.box[me, 1:2, self.here] = second
        place = self.box.at[me, :, self.here]
        self.team.send(lambda other: place, place, self.sems)

    def finish(self):
        others = self.box.at[pl.ds(0, self.team.size - 1)]
        await_bytes(others, self.sems.at[0])
        await_bytes(others, self.sems.at[1])


def eight_rows(rows):
    filler = jnp.zeros((8 - len(rows), LANES), f32)
    return jnp.concatenate([*rows, filler], axis=0) if len(rows) < 8 else jnp.concatenate(rows, 0)


def columns_of(rows):
    turned = jnp.transpose(jnp.concatenate([eight_rows(rows), jnp.zeros((120, LANES), f32)], 0))
    return [turned[:, i : i + 1] for i in range(len(rows))]


def exact(left, right, left_dim, right_dim):
    return lax.dot_general(
        left,
        right,
        (((left_dim,), (right_dim,)), ((), ())),
        precision=lax.Precision.HIGHEST,
        preferred_element_type=f32,
    )


def hot_rows(index, batches):
    rows = lax.broadcasted_iota(jnp.int32, (batches, index.shape[1]), 0)
    return jnp.where(rows == index, 1.0, 0.0)


def sigmoid(value):
    return 1.0 / (1.0 + jnp.exp(-value))


def slope_of(value):
    sigma = sigmoid(value)
    return sigma * (1.0 + value * (1.0 - sigma))


def pack_layout(latent_pad, batches):
    mixing = slice(8, 8 + latent_pad + batches)
    heads = slice(mixing.stop, mixing.stop + 2 * latent_pad)
    return mixing, heads, slice(heads.stop, heads.stop + batches)


def prepare_tables(number, genes, output_ref, vectors_ref, weights_ref, tables):
    theta_ref, log_ref, slope_ref, gammas_ref, digammas_ref = tables
    lane = lax.broadcasted_iota(jnp.int32, (LANES, LANES), 1)
    below = lax.broadcasted_iota(jnp.int32, (LANES, LANES), 0)
    upper = jnp.where(below < lane, 1.0, 0.0).astype(bf16)
    step = lane.astype(f32)
    block = theta_ref.shape[0]
    for at in range(0, block, LANES):
        here = slice(at, at + LANES)
        turned = jnp.transpose(
            jnp.concatenate([vectors_ref[:, here], jnp.zeros((LANES - 3, LANES), f32)], axis=0)
        )
        inside = number * block + at + below[:, 0:1] < genes
        for k in range(2):
            weight = output_ref[pl.ds(2 * at + k, LANES, stride=2), :]
            weights_ref[k, here, 0:LANES] = jnp.where(inside, weight, 0.0).astype(bf16)
            bias = jnp.where(inside, turned[:, k : k + 1], 0.0 if k else -1e30)
            high = bias.astype(bf16).astype(f32)
            middle = (bias - high).astype(bf16).astype(f32)
            low = (bias - high - middle).astype(bf16).astype(f32)
            extra = jnp.where(lane == 0, high, jnp.where(lane == 1, middle, 0.0))
            extra = jnp.where(lane == 2, low, extra)
            if k == 0:
                extra = jnp.where((lane >= 3) & (lane < 6), 1.0, extra)
            weights_ref[k, here, LANES : 2 * LANES] = extra.astype(bf16)
        theta = jnp.where(inside, jnp.exp(turned[:, 2:3]), 1.0) + jnp.zeros((LANES, LANES), f32)
        log_theta = jnp.log2(theta + rate_epsilon)
        theta_ref[here, :] = theta
        log_ref[here, :] = log_theta
        slope_ref[here, :] = ln2 * log_theta + theta / (theta + rate_epsilon)
        climb = theta + step
        terms = jnp.concatenate([jnp.log2(climb / (step + 1.0)), 1.0 / climb], axis=0)
        high = terms.astype(bf16)
        rest = terms - high.astype(f32)
        middle = rest.astype(bf16)
        low = (rest - middle.astype(f32)).astype(bf16)
        total = jnp.zeros((2 * LANES, LANES), f32)
        for piece in (low, middle, high):
            total = total + jnp.dot(piece, upper, preferred_element_type=f32)
        gammas_ref[here, :] = total[0:LANES]
        digammas_ref[here, :] = total[LANES:]


def encode_order(step, steps):
    last = step // (steps - 1)
    given = 1 - (step + steps - 1) // steps + lax.rem(step, 2) * (1 - last)
    return given, given * ((step + 1) // 2) + (1 - given) * (step // 2 - 1 + last)


def encode_kernel(
    counts_ref,
    encoder_ref,
    output_ref,
    vectors_ref,
    out_ref,
    weights_ref,
    theta_ref,
    log_ref,
    slope_ref,
    gammas_ref,
    digammas_ref,
    inputs_ref,
    weight_ref,
    near_give,
    near_box,
    far_give,
    far_box,
    near_sems,
    far_sems,
    *,
    genes,
    table_blocks,
):
    slab = counts_ref.shape[1]
    width = encoder_ref.shape[1]
    group = Team("gene")
    pairs = group.size // 2
    high, low = group.me // 2, lax.rem(group.me, 2)
    step = pl.program_id(0)
    given, turn = encode_order(step, group.size)

    def place(high, low):
        return (2 * high + low, group.cell)

    def copy(source, target, sems, where):
        return pltpu.make_async_remote_copy(
            src_ref=source,
            dst_ref=target,
            send_sem=sems.at[0],
            recv_sem=sems.at[1],
            device_id=where,
            device_id_type=MESH,
        )

    @pl.when(step == 0)
    def _():
        barrier = pltpu.get_barrier_semaphore()
        pl.semaphore_signal(barrier, inc=1, device_id=place(high, 1 - low), device_id_type=MESH)
        for d in range(1, pairs):
            where = place(lax.rem(high + d, pairs), low)
            pl.semaphore_signal(barrier, inc=1, device_id=where, device_id_type=MESH)
        for at in range(0, weight_ref.shape[1], LANES):
            stop = min(at + LANES, genes)
            piece = encoder_ref[at:stop, :]
            if stop < at + LANES:
                filler = jnp.zeros((at + LANES - stop, width), f32)
                piece = jnp.concatenate([piece, filler], axis=0)
            weight_ref[:, at : at + LANES] = jnp.transpose(piece).astype(bf16)

    def part(ref):
        depth = 3 * LANES
        total = jnp.zeros((8, slab), f32)
        for number, at in enumerate(range(0, genes, depth)):
            held = inputs_ref.at[number % 2]
            stop = min(at + depth, genes)
            for row in range(at, stop, ROWS):
                if row + ROWS <= genes:
                    counted = counts_ref[row : row + ROWS, :].astype(f32)
                else:
                    counted = tail_rows(counts_ref, row, genes, slice(None), jnp.int32).astype(f32)
                held[row - at : row - at + ROWS, :] = jnp.log(counted + 1.0).astype(bf16)
                total = total + counted[:8] + counted[8:]
            here = padded(stop - at)
            product = jnp.dot(
                weight_ref[:, at : at + here], held[0:here, :], preferred_element_type=f32
            )
            if at == 0:
                ref[0:width, :] = product
            else:
                ref[0:width, :] += product
        row = lax.broadcasted_iota(jnp.int32, (8, slab), 0)
        ref[width : width + 8, :] = jnp.where(row == 0, jnp.sum(total, axis=0, keepdims=True), 0.0)

    def near_copy(i):
        return copy(near_give.at[i], near_box.at[i], near_sems.at[i], place(high, 1 - low))

    def far_copy(i):
        target = lax.rem(high + 1 + i, pairs)
        return copy(far_give.at[i], far_box.at[i], far_sems.at[i], place(target, low))

    tables = (theta_ref, log_ref, slope_ref, gammas_ref, digammas_ref)

    @pl.when(step < table_blocks)
    def _():
        prepare_tables(step, genes, output_ref, vectors_ref, weights_ref, tables)

    @pl.when(given == 1)
    def _():
        part(near_give.at[turn])

        @pl.when(step == 0)
        def _():
            pl.semaphore_wait(pltpu.get_barrier_semaphore(), pairs)

        near_copy(turn).start()

    @pl.when(given == 0)
    def _():
        part(out_ref)
        near_copy(turn).wait_recv()
        total = out_ref[...] + near_box[turn]

        @pl.when(turn < pairs - 1)
        def _():
            far_give[turn] = total
            far_copy(turn).start()

        @pl.when(turn == pairs - 1)
        def _():
            def gather(i, total):
                far_copy(i).wait_recv()
                return total + far_box[i]

            out_ref[...] = lax.fori_loop(0, pairs - 1, gather, total)

            def drain(i, carry):
                far_copy(i).wait_send()
                return carry

            lax.fori_loop(0, pairs - 1, drain, 0)

            def drain_near(i, carry):
                near_copy(i).wait_send()
                return carry

            lax.fori_loop(0, pairs, drain_near, 0)


def encode(counts_t, weight, output_rows, vectors):
    genes, cells = counts_t.shape
    devices = lax.axis_size("gene")
    pairs = devices // 2
    slab = cells // devices
    width = weight.shape[1]

    def slab_of(i):
        me = lax.axis_index("gene")
        given, turn = encode_order(i, devices)
        return (0, 2 * lax.rem(me // 2 + 1 + turn, pairs) + lax.rem(me + given, 2))

    box = pltpu.VMEM((pairs, width + 8, slab), f32)
    size = 2 * ROWS * pl.cdiv(genes, 2 * ROWS)
    block = LANES * pl.cdiv(pl.cdiv(size, LANES), devices)
    table_blocks = pl.cdiv(size, block)

    def table_of(i):
        return jnp.minimum(i, table_blocks - 1)

    table = pl.BlockSpec((block, LANES), lambda i: (table_of(i), 0))
    return pl.pallas_call(
        functools.partial(encode_kernel, genes=genes, table_blocks=table_blocks),
        grid=(devices,),
        in_specs=[
            pl.BlockSpec((genes, slab), slab_of),
            whole(weight),
            pl.BlockSpec((2 * block, LANES), lambda i: (table_of(i), 0)),
            pl.BlockSpec((3, block), lambda i: (0, table_of(i))),
        ],
        out_specs=[
            pl.BlockSpec((width + 8, slab), lambda i: (0, 0)),
            pl.BlockSpec((2, block, HOT_DEPTH), lambda i: (0, table_of(i), 0)),
        ]
        + [table] * 5,
        out_shape=[
            jax.ShapeDtypeStruct((width + 8, slab), f32),
            jax.ShapeDtypeStruct((2, size, HOT_DEPTH), bf16),
        ]
        + [jax.ShapeDtypeStruct((size, LANES), f32)] * 5,
        scratch_shapes=[
            pltpu.VMEM((2, 3 * LANES, slab), bf16),
            pltpu.VMEM((width, LANES * pl.cdiv(genes, LANES)), bf16),
            box,
            box,
            box,
            box,
            pltpu.SemaphoreType.DMA((pairs, 2)),
            pltpu.SemaphoreType.DMA((pairs, 2)),
        ],
        compiler_params=talking(6),
        name="encode",
    )(counts_t, weight, output_rows, vectors)


def middle_kernel(
    encoded_ref,
    index_ref,
    valid_ref,
    noise_ref,
    norms_ref,
    bias_ref,
    mixing_ref,
    head_ref,
    shift_ref,
    hidden_ref,
    centered_ref,
    sample_ref,
    share_ref,
    stats_ref,
    first_ref,
    heads_ref,
    pack_ref,
    box1,
    box2,
    box3,
    box4,
    sems1,
    sems2,
    sems3,
    sems4,
    sample_far,
    sample_near,
    *,
    batches,
    latent,
    genes_all,
):
    group, team = Team("gene"), Team("cell")
    width, slab = first_ref.shape
    cells = hidden_ref.shape[1]
    pad = sample_ref.shape[0]
    mixing_rows, heads_rows, shift_rows = pack_layout(pad, batches)
    pack_ref[...] = jnp.zeros_like(pack_ref)
    pack_ref[0:4, :] = norms_ref[...]
    pack_ref[4:5, 0:latent] = bias_ref[:, 0:latent]
    pack_ref[4:5, pad : pad + latent] = bias_ref[:, latent : 2 * latent]
    at = mixing_rows.start
    pack_ref[at : at + latent, :] = mixing_ref[0:latent, :]
    pack_ref[at + pad : at + pad + batches, :] = mixing_ref[latent:, :]
    at = heads_rows.start
    pack_ref[at : at + latent, :] = head_ref[0:latent, :]
    pack_ref[at + pad : at + pad + latent, :] = head_ref[latent:, :]
    pack_ref[shift_rows, :] = shift_ref[...]
    mixing = pack_ref[mixing_rows, :]

    def part(other):
        return pl.ds(pl.multiple_of(other * slab, LANES), slab)

    mine = part(group.me)
    entered = greet(group, team)
    hot = hot_rows(index_ref[:, mine], batches)
    valid = valid_ref[:, mine].astype(f32)
    shift = exact(pack_ref[shift_rows, :], hot, 0, 0)
    gain1, bias1, gain2, bias2, head_bias = columns_of([pack_ref[i : i + 1, :] for i in range(5)])
    total = encoded_ref[...]
    library = total[width : width + 1, :]
    pre1 = total[0:width, :] + shift

    weighed = valid * pre1
    rows = [
        row_sums(fold_lanes(weighed)),
        row_sums(fold_lanes(weighed * pre1)),
        jnp.broadcast_to(jnp.sum(valid, axis=1, keepdims=True), (1, LANES)),
    ]
    entered()
    sums = spread_box(team, box1, eight_rows(rows), sems1)()
    sums = spread_box(group, box2, sums, sems2)()
    count = jnp.maximum(sums[2:3], 1.0)
    mean1 = sums[0:1] / count
    inverse1 = lax.rsqrt(sums[1:2] / count - mean1 * mean1 + norm_epsilon)
    mean_col, inverse_col = columns_of([mean1, inverse1])
    centered1 = (pre1 - mean_col) * inverse_col
    first_ref[...] = centered1
    normed1 = centered1 * gain1 + bias1
    hidden1 = normed1 * sigmoid(normed1)
    heads = exact(pack_ref[heads_rows, :], hidden1, 1, 0) + head_bias[0 : 2 * pad]
    heads_ref[...] = heads
    mean_z, log_var = heads[0:pad], heads[pad : 2 * pad]
    noise = jnp.concatenate([noise_ref[:, mine], jnp.zeros((pad - latent, slab), f32)], axis=0)
    sample = mean_z + jnp.exp(0.5 * log_var) * noise
    sample_ref[:, mine] = sample
    sample_ref[pad - 2 : pad - 1, mine] = 0.5 * jnp.sum(
        mean_z * mean_z + jnp.exp(log_var) - log_var - 1.0, axis=0, keepdims=True
    )
    sample_ref[pad - 1 : pad, mine] = library
    gathering = Gather(sample_ref, slab, sample_far, sample_near)
    gathering.start()
    pre2 = exact(mixing, jnp.concatenate([sample, hot], axis=0), 0, 0)
    weighed = valid * pre2
    rows = [row_sums(fold_lanes(weighed)), row_sums(fold_lanes(weighed * pre2))]
    sums = spread_box(team, box3, eight_rows(rows), sems3)()
    finish = spread_box(group, box4, sums, sems4)
    scale = 1.0 / (count * genes_all)
    share_ref[...] = valid_ref[...].astype(f32) * scale[:, 0:1]
    sums = finish()
    mean2 = sums[0:1] / count
    inverse2 = lax.rsqrt(sums[1:2] / count - mean2 * mean2 + norm_epsilon)
    stats_ref[...] = eight_rows([inverse1, inverse2, count, scale])
    mean_col, inverse_col = columns_of([mean2, inverse2])
    gathering.finish()
    piece = pick_chunk(cells, 512)

    def decode(i, carry):
        columns = pl.ds(pl.multiple_of(i * piece, LANES), piece)
        mixed = jnp.concatenate(
            [sample_ref[:, columns], hot_rows(index_ref[:, columns], batches)], axis=0
        )
        centered = (exact(mixing, mixed, 0, 0) - mean_col) * inverse_col
        centered_ref[:, columns] = centered
        normed = centered * gain2 + bias2
        hidden_ref[:, columns] = (normed * sigmoid(normed)).astype(bf16)
        return carry

    lax.fori_loop(0, cells // piece, decode, 0)


def middle(encoded, index, valid, noise, small_weights, batches, pad, genes_all):
    cells = index.shape[1]
    width = LANES
    genes_axis = lax.axis_size("gene")
    slab = cells // genes_axis
    return pl.pallas_call(
        functools.partial(
            middle_kernel, batches=batches, latent=noise.shape[0], genes_all=genes_all
        ),
        out_shape=[
            jax.ShapeDtypeStruct((width, cells), bf16),
            jax.ShapeDtypeStruct((width, cells), f32),
            jax.ShapeDtypeStruct((pad, cells), f32),
            jax.ShapeDtypeStruct((1, cells), f32),
            jax.ShapeDtypeStruct((8, LANES), f32),
            jax.ShapeDtypeStruct((width, slab), f32),
            jax.ShapeDtypeStruct((2 * pad, slab), f32),
            jax.ShapeDtypeStruct((8 + 3 * pad + 2 * batches, LANES), f32),
        ],
        in_specs=[IN_VMEM] * 9,
        out_specs=[IN_VMEM] * 8,
        scratch_shapes=row_boxes() + [pltpu.SemaphoreType.DMA((2,))] * 4 + gather_sems(),
        compiler_params=talking(1),
        name="middle",
    )(encoded, index, valid, noise, *small_weights)


def middle_back_kernel(
    grad_ref,
    centered_ref,
    sample_ref,
    index_ref,
    valid_ref,
    noise_ref,
    pack_ref,
    stats_ref,
    first_ref,
    heads_ref,
    output_ref,
    genes_ref,
    grad16_ref,
    small_ref,
    norms_ref,
    output_sum_ref,
    genes_sum_ref,
    part_ref,
    slab_box,
    box1,
    box2,
    box3,
    box4,
    output_box,
    half_box,
    half_give,
    genes_box,
    slab_sems,
    sems1,
    sems2,
    sems3,
    sems4,
    grad_far,
    grad_near,
    output_sems,
    genes_sems,
    *,
    batches,
    latent,
):
    group, team = Team("gene"), Team("cell")
    cell = lax.axis_index("cell")
    bit, near, far = lax.rem(cell, 2), cell + 1 - 2 * lax.rem(cell, 2), lax.rem(cell + 2, 4)
    half = output_ref.shape[1] // 2

    def swap(source, target, other, number):
        copy = pltpu.make_async_remote_copy(
            src_ref=source,
            dst_ref=target,
            send_sem=output_sems.at[number, 0],
            recv_sem=output_sems.at[number, 1],
            device_id=(group.gene, other),
            device_id_type=MESH,
        )
        copy.start()
        return copy

    def rows_of(number):
        return pl.ds(pl.multiple_of(number * half, 8), half)
    width, slab = first_ref.shape
    cells = grad_ref.shape[1]
    pad = sample_ref.shape[0]
    mixing_rows, heads_rows, _ = pack_layout(pad, batches)
    depth = pad + batches

    def part(other):
        return pl.ds(pl.multiple_of(other * slab, LANES), slab)

    mine = part(group.me)
    greet(group, team)()
    swap1 = swap(output_ref.at[1 - bit], output_box, near, 0)
    genes_box[cell] = genes_ref[...]

    def tell(step, carry):
        other = lax.rem(cell + step, team.size)
        pltpu.make_async_remote_copy(
            src_ref=genes_ref,
            dst_ref=genes_box.at[cell],
            send_sem=genes_sems.at[0],
            recv_sem=genes_sems.at[1],
            device_id=(group.gene, other),
            device_id_type=MESH,
        ).start()
        return carry

    lax.fori_loop(1, team.size, tell, 0)
    inverse1, inverse2 = stats_ref[0:1, :], stats_ref[1:2, :]
    count, scale = stats_ref[2:3, 0:1], stats_ref[3:4, 0:1]
    factor2 = inverse2 * pack_ref[2:3, :]
    gain1, bias1, gain2, bias2, factor1 = columns_of(
        [pack_ref[i : i + 1, :] for i in range(4)] + [inverse1 * pack_ref[0:1, :]]
    )
    latent_rows = pack_ref[8 : 8 + pad, :] * factor2
    piece = pick_chunk(cells, 512)

    def gather(i, carry):
        gains, shifts, products = carry
        columns = pl.ds(pl.multiple_of(i * piece, LANES), piece)
        centered = centered_ref[:, columns]
        grad = grad_ref[:, columns] * slope_of(centered * gain2 + bias2)
        part_ref[:, columns] = exact(latent_rows, grad, 1, 0)
        mixed = jnp.concatenate(
            [sample_ref[:, columns], hot_rows(index_ref[:, columns], batches)], axis=0
        )
        return (
            gains + fold_lanes(grad * centered),
            shifts + fold_lanes(grad),
            products + exact(mixed, grad, 1, 1),
        )

    zeros = jnp.zeros((width, LANES), f32)
    gains, shifts, products = lax.fori_loop(
        0, cells // piece, gather, (zeros, zeros, jnp.zeros((depth, width), f32))
    )

    finish = spread_box(team, box1, eight_rows([row_sums(gains), row_sums(shifts)]), sems1)
    group.send(lambda other: part_ref.at[:, part(other)], slab_box.at[group.me], slab_sems)
    slab_box[group.me] = part_ref[:, mine]
    finish = spread_box(group, box2, finish(), sems2)
    swap1.wait()
    own, given = rows_of(far // 2), rows_of(cell // 2)
    half_give[...] = output_ref[bit, own] + output_box[own]
    swap2 = swap(half_give, half_box, far, 1)
    output_sum_ref[given] = output_ref[bit, given] + output_box[given]
    hot = hot_rows(index_ref[:, mine], batches)
    valid = valid_ref[:, mine].astype(f32)
    mixed = valid * jnp.concatenate([sample_ref[:, mine], hot], axis=0)
    centered2 = centered_ref[:, mine]
    share = valid / count
    mixed_sum = jnp.sum(mixed, axis=1, keepdims=True)
    mixed_product = exact(mixed, centered2, 1, 1)
    noise = jnp.concatenate([noise_ref[:, mine], jnp.zeros((pad - latent, slab), f32)], axis=0)
    mean_z, log_var = heads_ref[0:pad, :], heads_ref[pad : 2 * pad, :]
    log_factor = 0.5 * noise * jnp.exp(0.5 * log_var)
    scaled = valid * scale
    grad_log_own = scaled * (jnp.exp(log_var) - 1.0) * 0.5
    centered1 = first_ref[...]
    normed1 = centered1 * gain1 + bias1
    sigma1 = sigmoid(normed1)
    hidden1 = normed1 * sigma1
    slope1 = sigma1 * (1.0 + normed1 * (1.0 - sigma1))

    sums = finish()
    gain2_grad, shift2_grad = sums[0:1], sums[1:2]
    small_ref[0:depth, :] = factor2 * (
        products - (mixed_sum * shift2_grad + mixed_product * gain2_grad) / count
    )
    gain_col, shift_col = columns_of([gain2_grad, shift2_grad])
    pulled = exact(latent_rows, shift_col + centered2 * gain_col, 1, 0)
    others = slab_box.at[pl.ds(0, group.size - 1)]
    await_bytes(others, slab_sems.at[0])
    await_bytes(others, slab_sems.at[1])
    grad_sample = box_sum(slab_box) - share * pulled
    grad_heads = jnp.concatenate(
        [grad_sample + scaled * mean_z, grad_sample * log_factor + grad_log_own], axis=0
    )
    grad_normed1 = exact(pack_ref[heads_rows, :], grad_heads, 0, 0) * slope1
    rows = [row_sums(fold_lanes(grad_normed1 * centered1)), row_sums(fold_lanes(grad_normed1))]
    finish = spread_box(group, box4, spread_box(team, box3, eight_rows(rows), sems3)(), sems4)
    swap2.wait()
    output_sum_ref[given] = output_sum_ref[given] + half_box[...]
    swap3 = swap(output_sum_ref.at[given], output_sum_ref.at[given], far, 2)
    small_ref[depth : depth + 2 * pad, :] = exact(grad_heads, hidden1, 1, 1)
    small_ref[depth + 2 * pad : depth + 4 * pad, :] = fold_lanes(grad_heads)
    sums = finish()
    gain1_grad, shift1_grad = sums[0:1], sums[1:2]
    norms_ref[...] = eight_rows([gain1_grad, shift1_grad, gain2_grad, shift2_grad])
    gain_col, shift_col = columns_of([gain1_grad, shift1_grad])
    grad_pre1 = factor1 * (grad_normed1 - share * (shift_col + centered1 * gain_col))
    grad16_ref[:, mine] = grad_pre1.astype(bf16)
    gathering = Gather(grad16_ref, slab, grad_far, grad_near)
    gathering.start()
    small_ref[depth + 4 * pad :, :] = exact(hot, grad_pre1, 1, 1)
    gathering.finish()
    others = genes_box.at[pl.ds(0, team.size - 1)]
    await_bytes(others, genes_sems.at[0])
    await_bytes(others, genes_sems.at[1])
    genes_sum_ref[...] = box_sum(genes_box)
    swap3.wait()


def middle_back(
    grad,
    centered,
    sample,
    index,
    valid,
    noise,
    pack,
    stats,
    first,
    heads,
    output_grad,
    genes_grad,
    batches,
):
    cells = index.shape[1]
    width, slab = first.shape
    pad = sample.shape[0]
    genes_axis = lax.axis_size("gene")
    return pl.pallas_call(
        functools.partial(middle_back_kernel, batches=batches, latent=noise.shape[0]),
        out_shape=[
            jax.ShapeDtypeStruct((width, cells), bf16),
            jax.ShapeDtypeStruct((5 * pad + 2 * batches, LANES), f32),
            jax.ShapeDtypeStruct((8, LANES), f32),
            jax.ShapeDtypeStruct(output_grad.shape[1:], f32),
            jax.ShapeDtypeStruct(genes_grad.shape, f32),
        ],
        in_specs=[IN_VMEM] * 12,
        out_specs=[IN_VMEM] * 5,
        scratch_shapes=[
            pltpu.VMEM((pad, cells), f32),
            pltpu.VMEM((genes_axis, pad, slab), f32),
            *row_boxes(),
            pltpu.VMEM(output_grad.shape[1:], f32),
            pltpu.VMEM((output_grad.shape[1] // 2, LANES), f32),
            pltpu.VMEM((output_grad.shape[1] // 2, LANES), f32),
            pltpu.VMEM((lax.axis_size("cell"), *genes_grad.shape), f32),
        ]
        + [pltpu.SemaphoreType.DMA((2,))] * 5
        + gather_sems()
        + [pltpu.SemaphoreType.DMA((3, 2)), pltpu.SemaphoreType.DMA((2,))],
        compiler_params=talking(4),
        name="middle_back",
    )(
        grad,
        centered,
        sample,
        index,
        valid,
        noise,
        pack,
        stats,
        first,
        heads,
        output_grad,
        genes_grad,
    )


def encoder_grad_kernel(
    counts_ref,
    grad_ref,
    small_ref,
    output_ref,
    sum_ref,
    total_ref,
    output_sum_ref,
    near_give,
    near_box,
    far_give,
    far_box,
    whole_box,
    small_box,
    near_sems,
    far_sems,
    last_sems,
    small_sems,
    output_box,
    output_sems,
):
    gene, cell = lax.axis_index("gene"), lax.axis_index("cell")
    bit, high = lax.rem(cell, 2), cell // 2
    near, far = cell + 1 - 2 * bit, lax.rem(cell + 2, 4)
    quarter, cells = counts_ref.shape
    step = pl.program_id(0)

    def copy(source, target, sems, where):
        return pltpu.make_async_remote_copy(
            src_ref=source,
            dst_ref=target,
            send_sem=sems.at[0],
            recv_sem=sems.at[1],
            device_id=where,
            device_id_type=MESH,
        )

    rounds = [(gene, near), (gene, far)]
    size = 1
    while size < lax.axis_size("gene"):
        rounds.append((gene + size - 2 * size * lax.rem(gene // size, 2), cell))
        size *= 2

    def small_copy(number):
        source = small_ref if number == 0 else small_box.at[1, number - 1]
        return copy(source, small_box.at[0, number], small_sems.at[number], rounds[number])

    def small_end(number):
        small_copy(number).wait()
        source = small_ref[...] if number == 0 else small_box[1, number - 1]
        small_box[1, number] = source + small_box[0, number]

    def rows_of(bit, high):
        return pl.ds(pl.multiple_of((2 * bit + high) * quarter, ROWS), quarter)

    def near_copy(number):
        return copy(near_give.at[number], near_box.at[number], near_sems.at[number], (gene, near))

    far_copy = copy(far_give, far_box, far_sems, (gene, far))

    def last_copy(number, high, other):
        rows = rows_of(bit, high)
        return copy(whole_box.at[rows], whole_box.at[rows], last_sems.at[number], (gene, other))

    output_copy = copy(output_box.at[bit], output_box.at[bit], output_sems, (gene, near))

    @pl.when(step == 0)
    def _():
        output_box[bit] = output_ref[...]
        barrier = pltpu.get_barrier_semaphore()
        for where in rounds:
            pl.semaphore_signal(barrier, inc=1, device_id=where, device_id_type=MESH)

    piece = pick_chunk(cells, 512)

    def part():
        total = jnp.zeros((quarter, LANES), f32)
        for at in range(0, cells, piece):
            columns = slice(at, at + piece)
            inputs = jnp.log(counts_ref[:, columns].astype(f32) + 1.0).astype(bf16)
            total = total + lax.dot_general(
                inputs,
                grad_ref[:, columns],
                (((1,), (1,)), ((), ())),
                preferred_element_type=f32,
            )
        return total

    value = part()

    @pl.when(step == 0)
    def _():
        pl.semaphore_wait(pltpu.get_barrier_semaphore(), len(rounds))
        small_copy(0).start()
        output_copy.start()

    @pl.when(step < 2)
    def _():
        near_give[step] = value
        near_copy(step).start()

    @pl.when(step == 1)
    def _():
        small_end(0)
        small_copy(1).start()

    @pl.when(step == 2)
    def _():
        near_copy(0).wait()
        far_give[...] = value + near_box[0]
        far_copy.start()
        small_end(1)
        small_copy(2).start()

    @pl.when(step == 3)
    def _():
        near_copy(1).wait()
        total = value + near_box[1]
        small_end(2)
        if len(rounds) > 3:
            small_copy(3).start()
        far_copy.wait()
        whole_box[rows_of(bit, high), :] = total + far_box[...]
        own_far, own_near = last_copy(0, high, far), last_copy(1, high, near)
        own_far.start()
        own_near.start()
        for number in range(3, len(rounds)):
            small_end(number)
            if number + 1 < len(rounds):
                small_copy(number + 1).start()
        total_ref[...] = small_box[1, len(rounds) - 1]
        own_far.wait()
        passed = last_copy(2, 1 - high, near)
        passed.start()
        own_near.wait()
        passed.wait()
        sum_ref[...] = whole_box[...]
        output_copy.wait()
        output_sum_ref[...] = output_box[...]


def encoder_grad(counts_t, grad, small, output):
    genes, cells = counts_t.shape
    quarter = ROWS * pl.cdiv(genes, 4 * ROWS)
    rounds = 2
    while 2 ** (rounds - 2) < lax.axis_size("gene"):
        rounds += 1

    def quarter_of(i):
        cell = lax.axis_index("cell")
        bit, high = lax.rem(cell, 2), cell // 2
        half = lax.rem(bit + 1 + i // 2, 2)
        return (2 * half + lax.rem(high + 1 + i, 2), 0)

    box = pltpu.VMEM((2, quarter, LANES), f32)
    one = pltpu.VMEM((quarter, LANES), f32)
    return pl.pallas_call(
        encoder_grad_kernel,
        grid=(4,),
        in_specs=[pl.BlockSpec((quarter, cells), quarter_of)]
        + [whole(array) for array in (grad, small, output)],
        out_specs=[
            pl.BlockSpec((4 * quarter, LANES), lambda i: (0, 0)),
            pl.BlockSpec(small.shape, lambda i: (0, 0)),
            pl.BlockSpec((2, *output.shape), lambda i: (0, 0, 0)),
        ],
        out_shape=[
            jax.ShapeDtypeStruct((4 * quarter, LANES), f32),
            jax.ShapeDtypeStruct(small.shape, f32),
            jax.ShapeDtypeStruct((2, *output.shape), f32),
        ],
        scratch_shapes=[
            box,
            box,
            one,
            one,
            pltpu.VMEM((4 * quarter, LANES), f32),
            pltpu.VMEM((2, rounds, *small.shape), f32),
            pltpu.SemaphoreType.DMA((2, 2)),
            pltpu.SemaphoreType.DMA((2,)),
            pltpu.SemaphoreType.DMA((3, 2)),
            pltpu.SemaphoreType.DMA((rounds, 2)),
            pltpu.VMEM((2, *output.shape), f32),
            pltpu.SemaphoreType.DMA((2,)),
        ],
        compiler_params=talking(5),
        name="encoder_grad",
    )(counts_t, grad, small, output)


def finish_kernel(*refs, pad, latent, batches):
    grad16_ref, encoder_grad_ref, output_grad_ref, genes_grad_ref, small_ref, norms_ref = refs[:6]
    ins, input_ref, outs = refs[6:30], refs[30], refs[31:]

    def group(number):
        return [part[8 * i + number] for part in (ins, outs) for i in range(3)]

    def step(number, here, grad):
        weight, momentum, average, *results = group(number)
        old = [ref[here] for ref in (weight, momentum, average)]
        for ref, value in zip(results, nesterov(*old, grad, step_rates[number])):
            ref[here] = value

    input_ref[...] = jnp.dot(
        ins[0][...].astype(bf16), grad16_ref[...], preferred_element_type=f32
    )
    step(0, (slice(None), slice(None)), encoder_grad_ref[...])
    for k in range(2):
        rows = pl.ds(k, output_grad_ref.shape[1], stride=2)
        step(1, (rows, slice(None)), output_grad_ref[k])
    step(2, (slice(None), slice(None)), genes_grad_ref[0:3, :])

    @pl.when(pl.program_id(0) == 0)
    def _():
        depth = pad + batches
        columns = slice(None)
        step(3, (columns, columns), small_ref[depth + 4 * pad :, :])
        step(4, (columns, columns), norms_ref[0:4, :])
        step(7, (slice(0, latent), columns), small_ref[0:latent, :])
        step(7, (slice(latent, None), columns), small_ref[pad:depth, :])
        bias = exact(
            jnp.ones((8, LANES), f32), small_ref[depth + 2 * pad : depth + 4 * pad, :], 1, 1
        )
        for half in range(2):
            rows = slice(half * latent, (half + 1) * latent)
            at = half * pad
            step(5, (rows, columns), small_ref[depth + at : depth + at + latent, :])
            step(6, (slice(None), rows), bias[0:1, at : at + latent])


def finish(grad16, encoder_grad, output_grad, genes_grad, small, norms, states, pad, latent, batches):
    width, cells = grad16.shape
    genes = states[0][0].shape[0]
    block = 4 * LANES
    one = pl.BlockSpec((block, LANES), lambda i: (i, 0))
    two = pl.BlockSpec((2 * block, LANES), lambda i: (i, 0))
    both = pl.BlockSpec((2, block, LANES), lambda i: (0, i, 0))

    def rows(count):
        return pl.BlockSpec((count, block), lambda i: (0, i))

    specs = [spec for state in states for spec in [one, two, rows(3), *map(whole, state[3:])]]
    flat = [array for state in states for array in state]
    results = pl.pallas_call(
        functools.partial(finish_kernel, pad=pad, latent=latent, batches=batches),
        grid=(pl.cdiv(genes, block),),
        in_specs=[whole(grad16), one, both, rows(4), whole(small), whole(norms)] + specs,
        out_specs=[pl.BlockSpec((block, cells), lambda i: (i, 0))] + specs,
        out_shape=[jax.ShapeDtypeStruct((genes, cells), f32)]
        + [jax.ShapeDtypeStruct(array.shape, f32) for array in flat],
        compiler_params=PARAMS,
        name="finish",
    )(grad16, encoder_grad, output_grad, genes_grad, small, norms, *flat)
    return results[0], [results[1 + 8 * i : 9 + 8 * i] for i in range(3)]


def fill_hidden(long_ref, hidden_ref, top):
    width, chunk = hidden_ref.shape
    long_ref[0:width, :] = hidden_ref[...]
    index = lax.broadcasted_iota(jnp.int32, (HOT_DEPTH - width, chunk), 0)
    extra = jnp.where(index < 3, 1.0, 0.0)
    if top is not None:
        high = (-top).astype(bf16).astype(f32)
        middle = (-top - high).astype(bf16).astype(f32)
        low = (-top - high - middle).astype(bf16).astype(f32)
        extra = jnp.where(index == 3, high, extra)
        extra = jnp.where(index == 4, middle, extra)
        extra = jnp.where(index == 5, low, extra)
    long_ref[width:HOT_DEPTH, :] = extra.astype(bf16)


def sweep(blocks, block, groups, pieces, logits, terms, back, carry):
    def rows_of(number):
        return pl.ds(pl.multiple_of(number * block, ROWS), block)

    logits(0, rows_of(0), block, pieces)

    def beside(i, later, earlier):
        acts = [
            lambda piece=piece: logits(1 - i, rows_of(later), block, [piece]) for piece in pieces
        ]
        if back is not None:
            acts.append(lambda: back(1 - i, rows_of(earlier), block))
        spaced = []
        for step in range(groups):
            spaced.append(acts.pop(0) if acts and step % 2 == 0 else lambda: None)
        return spaced + acts

    def pair(p, carry):
        first = 2 * p
        last, ahead = jnp.maximum(first - 1, 0), jnp.minimum(first + 2, blocks - 1)
        carry = terms(0, first, carry, beside(0, first + 1, last))
        return terms(1, first + 1, carry, beside(1, ahead, first))

    carry = lax.fori_loop(0, blocks // 2, pair, carry)
    if back is not None and blocks > 1:
        back(1, rows_of(blocks // 2 * 2 - 1), block)
    if blocks % 2:
        carry = terms(0, blocks - 1, carry, ())
        if back is not None:
            back(0, rows_of(blocks - 1), block)
    return carry


def logit_pieces(ks, chunk):
    width = min(chunk, WIDE)
    return [(k, slice(j, j + width)) for k in range(ks) for j in range(0, chunk, width)]


def totals_kernel(
    hidden_ref, weight_ref, sample_ref, out_ref, long_ref, even_ref, odd_ref, box, sems, *, genes, chunk
):
    full, groups, tail = split_rows(genes, 26)
    block = ROWS * groups
    blocks = full // groups
    values = (even_ref, odd_ref)
    fill_hidden(long_ref, hidden_ref, None)
    pieces = logit_pieces(1, chunk)

    @pl.when(pl.program_id(0) == 0)
    def _():
        greet(Team("gene"))

    def logits(i, rows, size, which):
        for _, columns in which:
            values[i][0:size, columns] = jnp.dot(
                weight_ref[0, rows, :], long_ref[:, columns], preferred_element_type=f32
            )

    def online(value_ref, size, carry, beside=()):
        best, total = carry
        fresh = best
        for i in range(0, size, 8):
            fresh = jnp.maximum(fresh, value_ref[i : i + 8, :])
        total = total * jnp.exp2((best - fresh) * (1.0 / ln2))
        for i in range(0, size, 8):
            for act in beside[i // 8 :: size // 8]:
                act()
            total = total + jnp.exp2((value_ref[i : i + 8, :] - fresh) * (1.0 / ln2))
        return fresh, total

    def terms(i, number, carry, beside):
        return online(values[i], block, carry, beside)

    carry = (jnp.full((8, chunk), -jnp.inf, f32), jnp.zeros((8, chunk), f32))
    carry = sweep(blocks, block, groups, pieces, logits, terms, None, carry)
    if tail:
        logits(1, pl.ds(full * ROWS, ROWS), ROWS, pieces)
        carry = online(odd_ref, ROWS, carry)
    best, total = carry
    top = jnp.max(best, axis=0, keepdims=True)
    total = total * jnp.exp2((best - top) * (1.0 / ln2))
    shared = Shared(box, sems, chunk)

    @pl.when(pl.program_id(0) == 0)
    def _():
        pl.semaphore_wait(pltpu.get_barrier_semaphore(), box.shape[0] - 1)

    shared.send(top, jnp.sum(total, axis=0, keepdims=True))

    @pl.when(pl.program_id(0) == pl.num_programs(0) - 1)
    def _():
        shared.finish()
        top = box[0, 0:1, :]
        for i in range(1, box.shape[0]):
            top = jnp.maximum(top, box[i, 0:1, :])
        total = jnp.zeros_like(top)
        for i in range(box.shape[0]):
            total = total + box[i, 1:2, :] * jnp.exp(box[i, 0:1, :] - top)
        inverse = 1.0 / total
        out_ref[0:1, :] = top
        out_ref[1:2, :] = sample_ref[sample_ref.shape[0] - 1 :, :] * inverse
        out_ref[2:3, :] = inverse
        out_ref[3:4, :] = inverse


def totals(hidden, weights, sample, genes):
    width, cells = hidden.shape
    chunk = pick_chunk(cells, 4096)
    groups = split_rows(genes, 26)[1]
    return pl.pallas_call(
        functools.partial(totals_kernel, genes=genes, chunk=chunk),
        grid=(cells // chunk,),
        in_specs=[column_blocks(width, chunk), whole(weights), whole(sample)],
        out_specs=pl.BlockSpec((4, cells), lambda i: (0, 0)),
        out_shape=jax.ShapeDtypeStruct((4, cells), f32),
        scratch_shapes=[pltpu.VMEM((HOT_DEPTH, chunk), bf16)]
        + [pltpu.VMEM((ROWS * groups, chunk), f32)] * 2
        + [pltpu.VMEM((lax.axis_size("gene"), 2, cells), f32), pltpu.SemaphoreType.DMA((2,))],
        compiler_params=talking(2),
        name="totals",
    )(hidden, weights, sample)


def likelihood_kernel(
    counts_ref,
    hidden_ref,
    rows_ref,
    share_ref,
    all_rows_ref,
    sample_ref,
    valid_ref,
    weight_ref,
    theta_ref,
    log_ref,
    slope_ref,
    gammas_ref,
    digammas_ref,
    slopes_ref,
    sums_ref,
    grad_hidden_ref,
    grad_weight_ref,
    grad_bias_ref,
    grad_theta_ref,
    long_ref,
    even_ref,
    odd_ref,
    even_grad_ref,
    odd_grad_ref,
    box,
    sems,
    *,
    genes,
    chunk,
    genes_all,
):
    full, groups, tail = split_rows(genes, 12)
    block = ROWS * groups
    blocks = full // groups
    width = hidden_ref.shape[0]

    @pl.when(pl.program_id(0) == 0)
    def _():
        for ref in (grad_weight_ref, grad_bias_ref, grad_theta_ref):
            ref[...] = jnp.zeros_like(ref)
        greet(Team("gene"))

    fill_hidden(long_ref, hidden_ref, rows_ref[0:1, :])
    wide = min(WIDE, chunk)
    tiles = [slice(j, j + wide) for j in range(0, chunk, wide)]
    ratio_all = rows_ref[1:2, :]
    share_all = share_ref[...]

    def two(x):
        return jnp.concatenate([x] * (wide // LANES), axis=1)

    def look(t, c):
        return jnp.concatenate([jnp.take_along_axis(t, c[:, q:q+LANES], axis=1) for q in range(0, wide, LANES)], axis=1)

    def group(value_ref, grad_ref, held, span, read, carry):
        losses, sums = [], []
        theta = two(theta_ref.at[span][held, :])
        log_theta = two(log_ref.at[span][held, :])
        log_slope = two(slope_ref.at[span][held, :])
        gammas = gammas_ref.at[span][held, :]
        digammas = digammas_ref.at[span][held, :]
        grad_bias = grad_bias_ref.at[span][held, :]
        grad_theta = grad_theta_ref.at[span][held, :]
        for j, columns in enumerate(tiles):
            count = read(columns)
            counted = count.astype(f32)
            minus = value_ref[1, held, columns] * (-1.0 / ln2)
            share = share_all[:, columns]
            rate = jnp.exp2(value_ref[0, held, columns] * (1.0 / ln2)) * ratio_all[:, columns]
            near = rate + rate_epsilon
            both = theta + near
            inverse_both = 1.0 / both
            log_both = jnp.log2(both)
            upper = jnp.maximum(minus, 0.0)
            lower = jnp.minimum(minus, 0.0)
            one_pi = 1.0 + jnp.exp2(lower - upper)
            sigma_pi = jnp.exp2(lower) * (1.0 / one_pi)
            zero = count < 1
            pi_theta = theta * (log_theta - log_both) + minus
            inflated = jnp.where(zero, pi_theta, 1e30)
            small = jnp.exp2(-jnp.abs(inflated))
            inverse_theta = 1.0 / (1.0 + small)
            sigma = jnp.where(inflated >= 0.0, 1.0, small) * inverse_theta
            loss = (upper - jnp.where(zero, jnp.maximum(pi_theta, 0.0), pi_theta)) + (
                jnp.log2(one_pi * inverse_theta)
                - counted * (jnp.log2(near) - log_both)
                - look(gammas, count)
            )
            pull = (sigma * theta + counted) * inverse_both
            slope = rate * (pull - counted * (1.0 / near))
            slopes_ref.at[span][held, columns] = slope
            grad_dropout = (sigma - sigma_pi) * share
            grad_ref[held, columns] = grad_dropout.astype(bf16)
            grad_bias = grad_bias + fold_lanes(grad_dropout)
            grad_theta = grad_theta + fold_lanes(share * (
                (pull - sigma * (log_slope - ln2 * log_both))
                - look(digammas, count)
            ))
            losses.append(carry[0][j] + loss[:8] + loss[8:])
            sums.append(carry[1][j] + slope[:8] + slope[8:])
        grad_bias_ref.at[span][held, :] = grad_bias
        grad_theta_ref.at[span][held, :] = grad_theta
        return tuple(losses), tuple(sums)

    pieces = logit_pieces(2, chunk)
    values, grads = (even_ref, odd_ref), (even_grad_ref, odd_grad_ref)

    def logits(i, rows, size, which):
        for k, columns in which:
            values[i][k, 0:size, columns] = jnp.dot(
                weight_ref[k, rows, :], long_ref[:, columns], preferred_element_type=f32
            )

    def back(i, rows, size):
        grad = grads[i][0:size, :]
        grad_weight_ref[rows, :] += lax.dot_general(
            grad, hidden_ref[...], (((1,), (1,)), ((), ())), preferred_element_type=f32
        )
        grad_hidden_ref[...] += lax.dot_general(
            weight_ref[1, rows, 0:width],
            grad,
            (((0,), (0,)), ((), ())),
            preferred_element_type=f32,
        )

    def terms(buffer, number, carry, beside):
        span = pl.ds(pl.multiple_of(number * block, ROWS), block)
        for i in range(groups):
            for act in beside[i::groups]:
                act()
            held = slice(i * ROWS, (i + 1) * ROWS)
            carry = group(
                values[buffer],
                grads[buffer],
                held,
                span,
                lambda columns, held=held: counts_ref.at[span][held, columns],
                carry,
            )
        return carry

    grad_hidden_ref[...] = jnp.zeros_like(grad_hidden_ref)
    odd_grad_ref[...] = jnp.zeros_like(odd_grad_ref)
    carry = tuple(jnp.zeros((8, wide), f32) for _ in tiles)
    carry = sweep(blocks, block, groups, pieces, logits, terms, back, (carry, carry))
    if tail:
        rows = pl.ds(full * ROWS, ROWS)
        logits(1, rows, ROWS, pieces)
        carry = group(
            odd_ref,
            odd_grad_ref,
            slice(0, ROWS),
            rows,
            lambda cols: tail_rows(counts_ref, full * ROWS, genes, cols, jnp.int32),
            carry,
        )
        back(1, rows, ROWS)
    shared = Shared(box, sems, chunk)

    @pl.when(pl.program_id(0) == 0)
    def _():
        pl.semaphore_wait(pltpu.get_barrier_semaphore(), box.shape[0] - 1)

    rows = [
        jnp.concatenate([jnp.sum(part, axis=0, keepdims=True) for part in carry[i]], axis=1)
        for i in (1, 0)
    ]
    shared.send(rows[0], rows[1] * ln2)

    @pl.when(pl.program_id(0) == pl.num_programs(0) - 1)
    def _():
        shared.finish()
        total = box_sum(box)
        at = sample_ref.shape[0] - 2
        sums_ref[0:1, :] = total[0:1] * all_rows_ref[2:3, :]
        sums_ref[1:2, :] = (
            valid_ref[...].astype(f32) * (total[1:2] + sample_ref[at : at + 1, :]) / genes_all
        )


def likelihood(counts_t, hidden, rows, share, sample, valid, weights, gene_tables, genes_all):
    genes, cells = counts_t.shape
    size = weights.shape[1]
    width = hidden.shape[0]
    chunk = pick_chunk(cells, 512)
    groups = split_rows(genes, 12)[1]
    row = column_blocks(1, chunk)
    per_gene = pl.BlockSpec((size, LANES), lambda i: (0, 0))
    return pl.pallas_call(
        functools.partial(likelihood_kernel, genes=genes, chunk=chunk, genes_all=genes_all),
        grid=(cells // chunk,),
        in_specs=[column_blocks(genes, chunk), column_blocks(width, chunk)]
        + [column_blocks(rows.shape[0], chunk), row]
        + [whole(a) for a in (rows, sample, valid, weights)]
        + [whole(a) for a in gene_tables],
        out_specs=[
            column_blocks(size, chunk),
            pl.BlockSpec((2, cells), lambda i: (0, 0)),
            column_blocks(width, chunk),
        ]
        + [per_gene] * 3,
        out_shape=[
            jax.ShapeDtypeStruct((size, cells), f32),
            jax.ShapeDtypeStruct((2, cells), f32),
            jax.ShapeDtypeStruct((width, cells), f32),
        ]
        + [jax.ShapeDtypeStruct((size, LANES), f32)] * 3,
        scratch_shapes=[pltpu.VMEM((HOT_DEPTH, chunk), bf16)]
        + [pltpu.VMEM((2, ROWS * groups, chunk), f32)] * 2
        + [pltpu.VMEM((ROWS * groups, chunk), bf16)] * 2
        + [pltpu.VMEM((lax.axis_size("gene"), 2, cells), f32), pltpu.SemaphoreType.DMA((2,))],
        compiler_params=talking(3),
        name="likelihood",
    )(counts_t, hidden, rows, share, rows, sample, valid, weights, *gene_tables)


def frequency_kernel(
    slopes_ref,
    hidden_ref,
    rows_ref,
    pull_ref,
    share_ref,
    other_ref,
    weight_ref,
    second_ref,
    dropout_ref,
    theta_ref,
    scale_ref,
    grad_hidden_ref,
    grad_weight_ref,
    genes_ref,
    long_ref,
    even_ref,
    odd_ref,
    even_grad_ref,
    odd_grad_ref,
    grad_bias_ref,
    *,
    genes,
    chunk,
):
    full, groups, tail = split_rows(genes, 26)
    block = ROWS * groups
    blocks = full // groups
    size = weight_ref.shape[1]
    width = hidden_ref.shape[0]
    values, grads = (even_ref, odd_ref), (even_grad_ref, odd_grad_ref)

    @pl.when(pl.program_id(0) == 0)
    def _():
        grad_weight_ref[0] = jnp.zeros((size, LANES), f32)
        grad_weight_ref[1] = second_ref[...]
        grad_bias_ref[...] = jnp.zeros_like(grad_bias_ref)

    fill_hidden(long_ref, hidden_ref, rows_ref[0:1, :])
    pieces = logit_pieces(1, chunk)
    share = share_ref[...]
    pulled = pull_ref[0:1, :] * share

    def logits(i, rows, size, which):
        for _, columns in which:
            values[i][0:size, columns] = jnp.dot(
                weight_ref[0, rows, :], long_ref[:, columns], preferred_element_type=f32
            )

    def group(buffer, held, span):
        exponent = jnp.exp2(values[buffer][held, :] * (1.0 / ln2))
        grad = slopes_ref.at[span][held, :] * share - exponent * pulled
        grads[buffer][held, :] = grad.astype(bf16)
        grad_bias_ref.at[span][held, :] += fold_lanes(grad)

    def terms(buffer, number, carry, beside):
        span = pl.ds(pl.multiple_of(number * block, ROWS), block)
        for i in range(groups):
            for act in beside[i::groups]:
                act()
            group(buffer, slice(i * ROWS, (i + 1) * ROWS), span)
        return carry

    def back(i, rows, size):
        grad = grads[i][0:size, :]
        grad_weight_ref[0, rows, :] += lax.dot_general(
            grad, hidden_ref[...], (((1,), (1,)), ((), ())), preferred_element_type=f32
        )
        grad_hidden_ref[...] += lax.dot_general(
            weight_ref[0, rows, 0:width],
            grad,
            (((0,), (0,)), ((), ())),
            preferred_element_type=f32,
        )

    grad_hidden_ref[...] = other_ref[...]
    odd_grad_ref[...] = jnp.zeros_like(odd_grad_ref)
    sweep(blocks, block, groups, pieces, logits, terms, back, 0)
    if tail:
        rows = pl.ds(full * ROWS, ROWS)
        logits(1, rows, ROWS, pieces)
        group(1, slice(0, ROWS), rows)
        back(1, rows, ROWS)

    @pl.when(pl.program_id(0) == pl.num_programs(0) - 1)
    def _():
        ones = jnp.ones((ROWS, LANES), bf16)
        parts = (grad_bias_ref[...], dropout_ref[...], theta_ref[...] * scale_ref[...])
        for i, values in enumerate(parts):
            total = jnp.zeros((1, size), f32)
            for _ in range(3):
                piece = values.astype(bf16)
                values = values - piece.astype(f32)
                total = total + lax.dot_general(
                    ones, piece, (((1,), (1,)), ((), ())), preferred_element_type=f32
                )[0:1]
            genes_ref[i : i + 1, :] = total
        genes_ref[3:4, :] = jnp.zeros((1, size), f32)


def frequency(slopes, hidden, rows, pull, share, other, weights, second, dropout, theta, scale, genes):
    size, cells = slopes.shape
    width = hidden.shape[0]
    chunk = pick_chunk(cells, 1024)
    groups = split_rows(genes, 26)[1]
    row = column_blocks(1, chunk)
    wide = column_blocks(width, chunk)
    return pl.pallas_call(
        functools.partial(frequency_kernel, genes=genes, chunk=chunk),
        grid=(cells // chunk,),
        in_specs=[column_blocks(size, chunk), wide, column_blocks(rows.shape[0], chunk)]
        + [column_blocks(2, chunk), row, wide, whole(weights)]
        + [whole(a) for a in (second, dropout, theta, scale)],
        out_specs=[
            wide,
            pl.BlockSpec((2, size, LANES), lambda i: (0, 0, 0)),
            pl.BlockSpec((4, size), lambda i: (0, 0)),
        ],
        out_shape=[
            jax.ShapeDtypeStruct((width, cells), f32),
            jax.ShapeDtypeStruct((2, size, LANES), f32),
            jax.ShapeDtypeStruct((4, size), f32),
        ],
        scratch_shapes=[pltpu.VMEM((HOT_DEPTH, chunk), bf16)]
        + [pltpu.VMEM((ROWS * groups, chunk), f32)] * 2
        + [pltpu.VMEM((ROWS * groups, chunk), bf16)] * 2
        + [pltpu.VMEM((size, LANES), f32)],
        compiler_params=PARAMS,
        name="frequency",
    )(slopes, hidden, rows, pull, share, other, weights, second, dropout, theta, scale)


def local(
    counts,
    batch_index,
    valid_mask,
    noise_draw,
    encoder_weight,
    output_weight,
    gene_vectors,
    batch_shift,
    layer_norm_params,
    head_weight,
    head_bias,
    decoder_input,
    encoder_weight_momentum,
    output_weight_momentum,
    gene_vectors_momentum,
    batch_shift_momentum,
    norm_params_momentum,
    head_weight_momentum,
    head_bias_momentum,
    decoder_input_momentum,
    encoder_weight_average,
    output_weight_average,
    gene_vectors_average,
    batch_shift_average,
    norm_params_average,
    head_weight_average,
    head_bias_average,
    decoder_input_average,
):
    cells, genes = counts.shape
    gene_devices = lax.axis_size("gene")
    genes_all = genes * gene_devices
    latent = head_bias.shape[0] // 2
    batches = batch_shift.shape[0]

    def by_gene(array):
        return jnp.transpose(array, (2, 0, 1)).reshape(2 * genes, -1)

    counts_t = counts.T
    output_rows = by_gene(output_weight)

    pad = 16
    small_weights = (
        layer_norm_params,
        head_bias[None, :],
        decoder_input,
        head_weight.T,
        batch_shift,
    )
    index, valid, noise = batch_index[None, :], valid_mask[None, :], noise_draw.T

    encoded, weights, *gene_tables = encode(counts_t, encoder_weight, output_rows, gene_vectors)
    hidden2, centered2, sample, share, stats, centered1, heads, pack = middle(
        encoded, index, valid, noise, small_weights, batches, pad, genes_all
    )
    rows = totals(hidden2, weights, sample, genes)
    slopes, pull, grad_hidden2, grad_out1, grad_bias1, grad_theta = likelihood(
        counts_t, hidden2, rows, share, sample, valid, weights, gene_tables, genes_all
    )
    cell_loss = pull[1]

    grad_hidden2, grad_out, grad_genes = frequency(
        slopes,
        hidden2,
        rows,
        pull,
        share,
        grad_hidden2,
        weights,
        grad_out1,
        grad_bias1,
        grad_theta,
        gene_tables[0],
        genes,
    )
    grad_pre16, small, norm_rows, grad_out, grad_genes = middle_back(
        grad_hidden2,
        centered2,
        sample,
        index,
        valid,
        noise,
        pack,
        stats,
        centered1,
        heads,
        grad_out,
        grad_genes,
        batches,
    )
    grad_encoder, small, grad_out = encoder_grad(counts_t, grad_pre16, small, grad_out)
    states = [
        (encoder, by_gene(output), vectors, shift, norms, head.T, bias[None, :], mixing)
        for encoder, output, vectors, shift, norms, head, bias, mixing in (
            (
                encoder_weight,
                output_weight,
                gene_vectors,
                batch_shift,
                layer_norm_params,
                head_weight,
                head_bias,
                decoder_input,
            ),
            (
                encoder_weight_momentum,
                output_weight_momentum,
                gene_vectors_momentum,
                batch_shift_momentum,
                norm_params_momentum,
                head_weight_momentum,
                head_bias_momentum,
                decoder_input_momentum,
            ),
            (
                encoder_weight_average,
                output_weight_average,
                gene_vectors_average,
                batch_shift_average,
                norm_params_average,
                head_weight_average,
                head_bias_average,
                decoder_input_average,
            ),
        )
    ]
    input_grad, fresh = finish(
        grad_pre16,
        grad_encoder,
        grad_out,
        grad_genes,
        small,
        norm_rows,
        states,
        pad,
        latent,
        batches,
    )
    results = []
    for encoder, output, vectors, shift, norms, head, bias, mixing in fresh:
        output = jnp.transpose(output.reshape(genes, 2, -1), (1, 2, 0))
        results += [encoder, output, vectors, shift, norms, head.T, bias[0], mixing]
    return (cell_loss, input_grad.T, *results)


def solution(mesh):
    cells, genes = P("cell"), P("gene", None)
    weight_specs = (genes, P(None, None, "gene"), P(None, "gene"), P(), P(), P(), P(), P())
    return jax.shard_map(
        local,
        mesh=mesh,
        in_specs=(P("cell", "gene"), cells, cells, P("cell", None)) + weight_specs * 3,
        out_specs=(cells, P("cell", "gene")) + weight_specs * 3,
        check_vma=False,
    )
```
